32 devices in a mesh: dp: 8 (over z, y), heads: 4 (over x, core).
Axes of the slice: x: 2, y: 2, z: 4, core: 2. Of those that a mesh axis runs over, the one named last changes fastest.
Arguments:
- content_in: bfloat16 [12288, 768], P(('dp', 'heads')), may hold values from -6 to 6
- query_in: bfloat16 [12288, 768], P(('dp', 'heads')), may hold values from -6 to 6
- content_grad: bfloat16 [12288, 768], P(('dp', 'heads')), may hold values from -6 to 6
- query_grad: bfloat16 [12288, 768], P(('dp', 'heads')), may hold values from -6 to 6
- segment_ids: int32 [24, 512], P('dp'), may hold values from 0 to 1
- doc_lengths: int32 [24, 8], P('dp'), may hold values from 1 to 256, 512 in all within a row
- factor_order: int32 [24, 512], P('dp'), may hold values from 0 to 511, each once within a row
- attn_proj: float32 [4, 768, 768], P(None, 'dp', 'heads'), may hold values from -0.21875 to 0.21875
- attn_proj_first: float32 [4, 768, 768], P(None, 'dp', 'heads'), may hold values from -0.00061035156 to 0.00061035156
- attn_proj_second: float32 [4, 768, 768], P(None, 'dp', 'heads'), may hold values from 6.511719e-11 to 1.041875e-09
- out_proj: float32 [768, 768], P('heads', 'dp'), may hold values from -0.875 to 0.875
- out_proj_first: float32 [768, 768], P('heads', 'dp'), may hold values from -0.00061035156 to 0.00061035156
- out_proj_second: float32 [768, 768], P('heads', 'dp'), may hold values from 6.511719e-11 to 1.041875e-09
- up_proj: float32 [768, 3072], P('dp', 'heads'), may hold values from -0.21875 to 0.21875
- up_proj_first: float32 [768, 3072], P('dp', 'heads'), may hold values from -0.00061035156 to 0.00061035156
- up_proj_second: float32 [768, 3072], P('dp', 'heads'), may hold values from 6.511719e-11 to 1.041875e-09
- down_proj: float32 [3072, 768], P('heads', 'dp'), may hold values from -0.109375 to 0.109375
- down_proj_first: float32 [3072, 768], P('heads', 'dp'), may hold values from -0.00061035156 to 0.00061035156
- down_proj_second: float32 [3072, 768], P('heads', 'dp'), may hold values from 6.511719e-11 to 1.041875e-09
- head_bias: float32 [5, 12, 64], P(None, 'heads'), may hold values from -3 to 3
- head_bias_first: float32 [5, 12, 64], P(None, 'heads'), may hold values from -0.00061035156 to 0.00061035156
- head_bias_second: float32 [5, 12, 64], P(None, 'heads'), may hold values from 1.3023438e-10 to 5.209375e-10
- up_bias: float32 [3072], P('heads'), may hold values from -3 to 3
- up_bias_first: float32 [3072], P('heads'), may hold values from -0.00036621094 to 0.00036621094
- up_bias_second: float32 [3072], P('heads'), may hold values from 5.2093753e-11 to 2.0837501e-10
- norm_param: float32 [5, 768], replicated, may hold values from -2 to 2
- norm_param_first: float32 [5, 768], replicated, may hold values from -0.0017089844 to 0.0017089844
- norm_param_second: float32 [5, 768], replicated, may hold values from 6.511719e-10 to 1.041875e-08
Outputs:
- content_out: bfloat16 [12288, 768], P(('dp', 'heads'))
- query_out: bfloat16 [12288, 768], P(('dp', 'heads'))
- content_in_grad: float32 [12288, 768], P(('dp', 'heads'))
- query_in_grad: float32 [12288, 768], P(('dp', 'heads'))
- grad_norm: float32 [], replicated
- attn_proj_grad: float32 [4, 768, 768], P(None, 'dp', 'heads')
- attn_proj_first_new: float32 [4, 768, 768], P(None, 'dp', 'heads')
- attn_proj_second_new: float32 [4, 768, 768], P(None, 'dp', 'heads')
- attn_proj_new: float32 [4, 768, 768], P(None, 'dp', 'heads')
- out_proj_grad: float32 [768, 768], P('heads', 'dp')
- out_proj_first_new: float32 [768, 768], P('heads', 'dp')
- out_proj_second_new: float32 [768, 768], P('heads', 'dp')
- out_proj_new: float32 [768, 768], P('heads', 'dp')
- up_proj_grad: float32 [768, 3072], P('dp', 'heads')
- up_proj_first_new: float32 [768, 3072], P('dp', 'heads')
- up_proj_second_new: float32 [768, 3072], P('dp', 'heads')
- up_proj_new: float32 [768, 3072], P('dp', 'heads')
- down_proj_grad: float32 [3072, 768], P('heads', 'dp')
- down_proj_first_new: float32 [3072, 768], P('heads', 'dp')
- down_proj_second_new: float32 [3072, 768], P('heads', 'dp')
- down_proj_new: float32 [3072, 768], P('heads', 'dp')
- head_bias_grad: float32 [5, 12, 64], P(None, 'heads')
- head_bias_first_new: float32 [5, 12, 64], P(None, 'heads')
- head_bias_second_new: float32 [5, 12, 64], P(None, 'heads')
- head_bias_new: float32 [5, 12, 64], P(None, 'heads')
- up_bias_grad: float32 [3072], P('heads')
- up_bias_first_new: float32 [3072], P('heads')
- up_bias_second_new: float32 [3072], P('heads')
- up_bias_new: float32 [3072], P('heads')
- norm_param_grad: float32 [5, 768], replicated
- norm_param_first_new: float32 [5, 768], replicated
- norm_param_second_new: float32 [5, 768], replicated
- norm_param_new: float32 [5, 768], replicated
The draws below stay inside these ranges and needn't reach their ends.
Inputs may be any that keep to these rules, and one draw needn't show every extreme that they name: `doc_lengths`: each row's 8 lengths sum to 512, and the largest is exactly 256. `factor_order`: each row holds every position of 0 to 511 once.
All inputs are finite; a program needn't handle non-finite values.
Results may differ from the reference program's by a relative error of at most 0.018.
Values may be sent and summed in bfloat16 or wider, within the bound.
A program may use at most 192 MiB of HBM per device.

```python
import math
import jax
import jax.numpy as jnp
import numpy as np
from jax import lax

D = 768
NH = 12
DH = 64
FF = 3072
SEQ = 512
NDOC = 8
STEP = 10
ROWS = 24
TOKENS = 12288
NPARAM = 7678464


def draw_content_in(key, part):
    key = jax.random.fold_in(key, 11)
    column = jnp.arange(D, dtype=jnp.float32) / (D - 1)
    scaling = 0.8 + 0.6 * column
    sample = jax.random.truncated_normal(key, -4.0, 4.0, (TOKENS, D), jnp.float32)
    return (sample * scaling[None, :]).astype(jnp.bfloat16)


def draw_norm_param(key, part):
    key = jax.random.fold_in(key, 23)
    column = jnp.arange(D, dtype=jnp.float32) / (D - 1)
    jitter = jax.random.truncated_normal(key, -3.0, 3.0, (5, D), jnp.float32)
    rising = 0.8 + 0.6 * column
    gain_rows = rising[None, :] * (1.0 + 0.1 * jitter)
    biases = 0.3 * jitter
    return jnp.stack([gain_rows[0], biases[1], biases[2], gain_rows[3], biases[4]])


def with_ends(array, rng, low, largest):
    dims = array.shape
    spot = [jax.random.randint(jax.random.fold_in(rng, axis), (), 0, dims[axis]) for axis in range(len(dims))]
    array = array.at[tuple(spot)].set(low)
    longest = dims.index(max(dims))
    spot[longest] = (spot[longest] + 1) % dims[longest]
    return array.at[tuple(spot)].set(largest)


def shard_levels(key, shape, shards, low, largest):
    level = 1.0
    for dim, parts in shards:
        heights = jax.random.uniform(jax.random.fold_in(jax.random.fold_in(key, 6), dim), (parts,), jnp.float32, low / len(shards), largest / len(shards))
        level = level * jnp.repeat(jnp.exp(heights), shape[dim] // parts).reshape((-1,) + (1,) * (len(shape) - 1 - dim))
    return level


def profile(count, total, bound, slope):
    loads = [(1 << 20) // math.isqrt(rank ** slope) + 1 for rank in range(2, count + 1)]
    spare, counts = total - bound - (count - 1), [1] * (count - 1)
    while spare > 0:
        movable = [i for i in range(count - 1) if counts[i] < bound]
        mass, left = sum([loads[i] for i in movable]), spare
        for i in movable:
            extra = min(bound - counts[i], max(1, left * loads[i] // mass), spare)
            counts[i] = counts[i] + extra
            spare = spare - extra
    return np.array([bound] + counts)


def ragged_sizes(key, amount, total, most, slope):
    if amount == 2:
        one = jax.random.randint(key, (), max(1, total - most), min(most, total - 1) + 1)
        return jnp.stack([one, total - one])
    tallies = jnp.asarray(profile(amount, total, most, slope), jnp.int32)
    twos = (amount - 1) // 2
    giver, receiver = tallies[1:1 + 2 * twos:2], tallies[2:2 + 2 * twos:2]
    margin = jnp.minimum(giver - 1, most - receiver)
    passed = jax.random.randint(jax.random.fold_in(key, 1), (twos,), 0, 1 << 20) % (margin + 1)
    tallies = tallies.at[1:1 + 2 * twos:2].set(giver - passed).at[2:2 + 2 * twos:2].set(receiver + passed)
    return tallies[jax.random.permutation(jax.random.fold_in(key, 2), amount)]


def gaussian(stream_key, dims, spread, reach, shards=(), kind=jnp.bfloat16):
    drawn = spread * jax.random.normal(stream_key, dims, jnp.float32)
    if shards:
        drawn = drawn * shard_levels(stream_key, dims, shards, -0.22, 0.18)
    return jnp.clip(drawn, -reach, reach).astype(kind)


def setup_inputs(seed: int = 0) -> dict:
    keys = jax.random.split(jax.random.key(seed), 29)
    return {
        "content_in": draw_content_in(jax.random.fold_in(keys[28], 71), 0),
        "query_in": gaussian(keys[1], (TOKENS, D), 1.0, 6.0, ((0, 32),)),
        "content_grad": gaussian(keys[2], (TOKENS, D), 1.0, 6.0, ((0, 32),)),
        "query_grad": gaussian(keys[3], (TOKENS, D), 1.0, 6.0, ((0, 32),)),
        "segment_ids": with_ends(jax.random.randint(keys[4], (ROWS, SEQ), 0, 2), jax.random.fold_in(keys[4], 1), 0, 1).astype(jnp.int32),
        "doc_lengths": jax.vmap(lambda own: ragged_sizes(own, NDOC, SEQ, SEQ // 2, 2))(jax.random.split(keys[5], ROWS)).reshape((ROWS, NDOC)).astype(jnp.int32),
        "factor_order": jax.vmap(lambda own: jax.random.permutation(own, SEQ))(jax.random.split(keys[6], ROWS)).reshape((ROWS, SEQ)).astype(jnp.int32),
        "attn_proj": gaussian(keys[7], (4, D, NH * DH), D ** -0.5, 0.21875, ((1, 8), (2, 4)), jnp.float32),
        "attn_proj_first": gaussian(keys[8], (4, D, NH * DH), (0.11 / NPARAM ** 0.5), 0.00061035156, ((1, 8), (2, 4)), jnp.float32),
        "attn_proj_second": jnp.clip(jnp.exp(math.log(1.0418750306939728e-09) - 2.7725887 * jax.random.uniform(keys[9], (4, D, NH * DH), jnp.float32) ** shard_levels(keys[9], (4, D, NH * DH), ((1, 8), (2, 4)), -0.2, 0.2)), 6.51171894183733e-11, 1.0418750306939728e-09),
        "out_proj": gaussian(keys[10], (NH * DH, D), (NH * DH // 16) ** -0.5, 0.875, ((0, 4), (1, 8)), jnp.float32),
        "out_proj_first": gaussian(keys[11], (NH * DH, D), (0.11 / NPARAM ** 0.5), 0.00061035156, ((0, 4), (1, 8)), jnp.float32),
        "out_proj_second": jnp.clip(jnp.exp(math.log(1.0418750306939728e-09) - 2.7725887 * jax.random.uniform(keys[12], (NH * DH, D), jnp.float32) ** shard_levels(keys[12], (NH * DH, D), ((0, 4), (1, 8)), -0.2, 0.2)), 6.51171894183733e-11, 1.0418750306939728e-09),
        "up_proj": gaussian(keys[13], (D, FF), D ** -0.5, 0.21875, ((0, 8), (1, 4)), jnp.float32),
        "up_proj_first": gaussian(keys[14], (D, FF), (0.11 / NPARAM ** 0.5), 0.00061035156, ((0, 8), (1, 4)), jnp.float32),
        "up_proj_second": jnp.clip(jnp.exp(math.log(1.0418750306939728e-09) - 2.7725887 * jax.random.uniform(keys[15], (D, FF), jnp.float32) ** shard_levels(keys[15], (D, FF), ((0, 8), (1, 4)), -0.2, 0.2)), 6.51171894183733e-11, 1.0418750306939728e-09),
        "down_proj": gaussian(keys[16], (FF, D), FF ** -0.5, 0.109375, ((0, 4), (1, 8)), jnp.float32),
        "down_proj_first": gaussian(keys[17], (FF, D), (0.11 / NPARAM ** 0.5), 0.00061035156, ((0, 4), (1, 8)), jnp.float32),
        "down_proj_second": jnp.clip(jnp.exp(math.log(1.0418750306939728e-09) - 2.7725887 * jax.random.uniform(keys[18], (FF, D), jnp.float32) ** shard_levels(keys[18], (FF, D), ((0, 4), (1, 8)), -0.2, 0.2)), 6.51171894183733e-11, 1.0418750306939728e-09),
        "head_bias": gaussian(keys[19], (5, NH, DH), 0.5, 3.0, ((1, 4),), jnp.float32),
        "head_bias_first": gaussian(keys[20], (5, NH, DH), (0.11 / NPARAM ** 0.5), 0.00061035156, ((1, 4),), jnp.float32),
        "head_bias_second": jnp.clip(jnp.exp(math.log(5.209375153469864e-10) - 1.3862944 * jax.random.uniform(keys[21], (5, NH, DH), jnp.float32) ** shard_levels(keys[21], (5, NH, DH), ((1, 4),), -0.2, 0.2)), 1.302343788367466e-10, 5.209375153469864e-10),
        "up_bias": gaussian(keys[22], (FF,), 0.3, 3.0, ((0, 4),), jnp.float32),
        "up_bias_first": gaussian(keys[23], (FF,), (0.07 / NPARAM ** 0.5), 0.00036621094, ((0, 4),), jnp.float32),
        "up_bias_second": jnp.clip(jnp.exp(math.log(2.0837501168990968e-10) - 1.3862944 * jax.random.uniform(keys[24], (FF,), jnp.float32) ** shard_levels(keys[24], (FF,), ((0, 4),), -0.2, 0.2)), 5.209375292247742e-11, 2.0837501168990968e-10),
        "norm_param": draw_norm_param(jax.random.fold_in(keys[28], 71), 0),
        "norm_param_first": gaussian(keys[26], (5, D), (0.3 / NPARAM ** 0.5), 0.0017089844, (), jnp.float32),
        "norm_param_second": jnp.clip(jnp.exp(jax.random.uniform(keys[27], (5, D), jnp.float32, math.log(6.51171894183733e-10), math.log(1.0418750306939728e-08))), 6.51171894183733e-10, 1.0418750306939728e-08),
    }


HIGH_PRECISION = lax.Precision.HIGHEST
NORM_EPSILON = 1e-05
CLIP_NORM = 1.0
MATRIX_RATE = 0.08
VECTOR_RATE = 0.5
BETA_ONE = 0.9
BETA_TWO = 0.999
ADAM_EPSILON = 1e-08
WEIGHT_DECAY = 0.01
MASKED_SCORE = -1e+30

@jax.custom_vjp
def low(v):
    return lax.optimization_barrier(v.astype(jnp.bfloat16)).astype(jnp.float32)

@jax.custom_vjp
def low_back(v):
    return v

def low_keep(v):
    return (low(v), None)

def low_pass(kept, grad):
    return (grad,)

def back_keep(v):
    return (v, None)

def back_low(kept, grad):
    return (low(grad),)
low.defvjp(low_keep, low_pass)
low_back.defvjp(back_keep, back_low)

def matmul(left, right):
    return jnp.dot(left, right, precision=HIGH_PRECISION, preferred_element_type=jnp.float32)

def layer_norm(values, gain_row, bias_row):
    row_mean = lax.optimization_barrier(jnp.mean(values, -1, keepdims=True))
    centred = values - row_mean
    row_var = lax.optimization_barrier(jnp.mean(centred * centred, -1, keepdims=True))
    return centred * lax.rsqrt(row_var + NORM_EPSILON) * gain_row + bias_row

def position_table(length, width):
    distance = (length - jnp.arange(2 * length)).astype(jnp.float32)
    frequency = 1.0 / 10000.0 ** (jnp.arange(0, width, 2).astype(jnp.float32) / width)
    angles = distance[:, None] * frequency[None, :]
    return jnp.concatenate([jnp.sin(angles), jnp.cos(angles)], -1)

def rel_shift(wide_scores):
    length = wide_scores.shape[-2]
    leading = wide_scores.shape[:-2]
    flattened = wide_scores.reshape(leading + (2 * length * length,))[..., length:]
    return flattened.reshape(leading + (length, 2 * length - 1))[..., :length]

def pair_masks(segment, lengths, order):
    length = segment.shape[-1]
    places = jnp.arange(length, dtype=jnp.int32)
    doc_ends = jnp.cumsum(lengths, -1).astype(jnp.int32)
    document = lax.optimization_barrier(jnp.sum((places[:, None] >= doc_ends[None, :]).astype(jnp.int32), -1))
    ranking = lax.optimization_barrier(jnp.sum(jnp.where(order[:, None] == places[None, :], places[:, None], 0), 0))
    same_doc = document[:, None] == document[None, :]
    allow_content = same_doc & (ranking[None, :] <= ranking[:, None])
    allow_query = same_doc & (ranking[None, :] < ranking[:, None])
    differ = (segment[:, None] != segment[None, :]).astype(jnp.float32)
    return (allow_content, allow_query, differ)

def score_all(query_now, keys_now, relative, head_bias, differ):
    scale = query_now.shape[-1] ** (-0.5)
    content = jnp.einsum('ihd,jhd->hij', query_now, keys_now, precision=HIGH_PRECISION)
    content = content + jnp.einsum('jhd,hd->hj', keys_now, head_bias[0], precision=HIGH_PRECISION)[:, None, :]
    position = jnp.einsum('ihd,phd->hip', query_now, relative, precision=HIGH_PRECISION)
    position = position + jnp.einsum('phd,hd->hp', relative, head_bias[1], precision=HIGH_PRECISION)[:, None, :]
    segment = jnp.einsum('ihd,shd->hsi', query_now + head_bias[2], head_bias[3:5], precision=HIGH_PRECISION)
    seg_term = segment[:, 0, :, None] + differ[None] * (segment[:, 1, :, None] - segment[:, 0, :, None])
    return (content + rel_shift(position) + seg_term) * scale

def forward(weights, content, query, pair_sets):
    attn_proj, out_proj, up_proj, down_proj, head_bias, up_bias, norm_param = weights
    allow_content, allow_query, differ = pair_sets
    queries = low(low_back(matmul(content, attn_proj[0])))
    keys_all = low(low_back(matmul(content, attn_proj[1])))
    values_all = low(low_back(matmul(content, attn_proj[2])))
    query_g = low(low_back(matmul(query, attn_proj[0])))
    table = low(position_table(SEQ, D))
    seq_shape = (ROWS, SEQ, NH, DH)

    @jax.checkpoint
    def per_sequence(items):
        query_c, key_s, value_s, query_q, allow_c, allow_q, differ_s = items
        relative = low(low_back(matmul(table, attn_proj[3]))).reshape(2 * SEQ, NH, DH)
        attended = []
        for query_now, allowed in ((query_c, allow_c), (query_q, allow_q)):
            scores = low_back(score_all(query_now, key_s, relative, head_bias, differ_s))
            highest = jnp.maximum(lax.optimization_barrier(jnp.max(jnp.where(allowed, scores, MASKED_SCORE), -1)), 0.0)
            weights_exp = jnp.exp(jnp.where(allowed, scores - highest[..., None], MASKED_SCORE))
            totals = jnp.exp(-highest) + lax.optimization_barrier(jnp.sum(weights_exp, -1))
            chances = low(weights_exp / totals[..., None])
            mixed = jnp.einsum('hij,jhd->ihd', chances, value_s, precision=HIGH_PRECISION)
            attended.append(low(low_back(mixed.reshape(SEQ, NH * DH))))
        return (attended[0], attended[1])
    attended_c, attended_q = lax.map(per_sequence, (queries.reshape(seq_shape), keys_all.reshape(seq_shape), values_all.reshape(seq_shape), query_g.reshape(seq_shape), allow_content, allow_query, differ))
    results = []
    for source, attended in ((content, attended_c), (query, attended_q)):
        attended = attended.reshape(TOKENS, NH * DH)
        middle = layer_norm(source + low_back(matmul(attended, out_proj)), norm_param[0], norm_param[1])
        hidden = low(jax.nn.gelu(low_back(matmul(low(middle), up_proj) + up_bias), approximate=True))
        results.append(layer_norm(middle + low_back(matmul(hidden, down_proj)) + norm_param[2], norm_param[3], norm_param[4]))
    return (results[0], results[1])

def adam_step(master, first, second, gradient, factor, decayed):
    clipped = gradient * factor
    new_first = BETA_ONE * first + (1.0 - BETA_ONE) * clipped
    new_second = BETA_TWO * second + (1.0 - BETA_TWO) * clipped * clipped
    first_hat = new_first / (1.0 - BETA_ONE ** STEP)
    second_hat = new_second / (1.0 - BETA_TWO ** STEP)
    update = first_hat / (jnp.sqrt(second_hat) + ADAM_EPSILON)
    if decayed:
        update = update + WEIGHT_DECAY * master
        return (new_first, new_second, master - MATRIX_RATE * update)
    return (new_first, new_second, master - VECTOR_RATE * update)

def reference(content_in, query_in, content_grad, query_grad, segment_ids, doc_lengths, factor_order, attn_proj, attn_proj_first, attn_proj_second, out_proj, out_proj_first, out_proj_second, up_proj, up_proj_first, up_proj_second, down_proj, down_proj_first, down_proj_second, head_bias, head_bias_first, head_bias_second, up_bias, up_bias_first, up_bias_second, norm_param, norm_param_first, norm_param_second):
    pair_sets = jax.vmap(pair_masks)(segment_ids, doc_lengths, factor_order)
    used = (attn_proj.astype(jnp.bfloat16).astype(jnp.float32), out_proj.astype(jnp.bfloat16).astype(jnp.float32), up_proj.astype(jnp.bfloat16).astype(jnp.float32), down_proj.astype(jnp.bfloat16).astype(jnp.float32), head_bias, up_bias, norm_param)

    def run(weights, content, query):
        return forward(weights, content, query, pair_sets)
    primal, pullback = jax.vjp(run, used, content_in.astype(jnp.float32), query_in.astype(jnp.float32))
    weight_grads, content_in_grad, query_in_grad = pullback((content_grad.astype(jnp.float32), query_grad.astype(jnp.float32)))
    grad_norm = jnp.sqrt(sum((jnp.sum(gradient * gradient) for gradient in weight_grads)))
    factor = CLIP_NORM / jnp.maximum(grad_norm, CLIP_NORM)
    attn_grad, out_grad, up_grad, down_grad, head_grad, bias_grad, norm_grad = weight_grads
    attn_first, attn_second, attn_new = adam_step(attn_proj, attn_proj_first, attn_proj_second, attn_grad, factor, True)
    out_first, out_second, out_new = adam_step(out_proj, out_proj_first, out_proj_second, out_grad, factor, True)
    up_first, up_second, up_new = adam_step(up_proj, up_proj_first, up_proj_second, up_grad, factor, True)
    down_first, down_second, down_new = adam_step(down_proj, down_proj_first, down_proj_second, down_grad, factor, True)
    head_first, head_second, head_new = adam_step(head_bias, head_bias_first, head_bias_second, head_grad, factor, False)
    bias_first, bias_second, bias_new = adam_step(up_bias, up_bias_first, up_bias_second, bias_grad, factor, False)
    norm_first, norm_second, norm_new = adam_step(norm_param, norm_param_first, norm_param_second, norm_grad, factor, False)
    return (primal[0].astype(jnp.bfloat16), primal[1].astype(jnp.bfloat16), content_in_grad, query_in_grad, grad_norm, attn_grad, attn_first, attn_second, attn_new, out_grad, out_first, out_second, out_new, up_grad, up_first, up_second, up_new, down_grad, down_first, down_second, down_new, head_grad, head_first, head_second, head_new, bias_grad, bias_first, bias_second, bias_new, norm_grad, norm_first, norm_second, norm_new)
```

```python
import functools

import jax
import jax.numpy as jnp
import ml_dtypes
import numpy as np
from jax import lax
from jax.experimental import pallas as pl
from jax.experimental.pallas import tpu as pltpu
from jax.sharding import PartitionSpec as P

STEP = 10


HIGH_PRECISION = lax.Precision.HIGHEST
NORM_EPSILON = 1e-05
CLIP_NORM = 1.0
MATRIX_RATE = 0.08
VECTOR_RATE = 0.5
BETA_ONE = 0.9
BETA_TWO = 0.999
ADAM_EPSILON = 1e-08
WEIGHT_DECAY = 0.01
MASKED_SCORE = -1e30
LOG2E = 1.4426950408889634
VMEM_LIMIT = 56 << 20


def position_table(length, width):
    distance = length // 2 - np.arange(length)
    frequency = 10000.0 ** (-np.arange(0, width, 2) / width)
    angles = distance[:, None] * frequency[None, :]
    return np.concatenate([np.sin(angles), np.cos(angles)], -1).astype(np.float32).astype(ml_dtypes.bfloat16)


def dot(left, right):
    return lax.dot_general(left, right, (((1,), (0,)), ((), ())), preferred_element_type=jnp.float32)


def dot_nt(left, right):
    return lax.dot_general(left, right, (((1,), (1,)), ((), ())), preferred_element_type=jnp.float32)


def split_pair(values):
    high = values.astype(jnp.bfloat16)
    low = (values - high.astype(jnp.float32)).astype(jnp.bfloat16)
    return jnp.concatenate([high, low], -1)


def row_facts(segment_ids, doc_lengths, factor_order):
    rows, length = segment_ids.shape
    places = jnp.arange(length, dtype=jnp.int32)
    counts = doc_lengths.shape[1]
    earlier = jnp.arange(counts)[:, None] <= jnp.arange(counts)[None, :]
    ends = jnp.sum(jnp.where(earlier[None], doc_lengths[:, :, None], 0), 1)
    start = jnp.sum(jnp.where(doc_lengths == length // 2, ends - doc_lengths, 0), -1)
    token = (places[None] + start[:, None]) % length
    document = jnp.sum((token[:, :, None] >= ends[:, None, :]).astype(jnp.int32), -1)
    ranking = jnp.sum(
        jnp.where(factor_order[:, :, None] == token[:, None, :], places[None, :, None], 0), 1
    )
    segment = jnp.sum(
        jnp.where(places[None, :, None] == token[:, None, :], segment_ids[:, :, None], 0), 1
    )
    base = document * length
    zero = jnp.zeros_like(base)
    facts = jnp.stack([base + ranking, base, segment, token, zero, zero, zero, zero], 1)
    facts = facts.astype(jnp.float32)
    return facts, jnp.swapaxes(facts, 1, 2)


def roll_matrix(token_col, length):
    lanes = lax.broadcasted_iota(jnp.int32, (length, length), 1).astype(jnp.float32)
    return jnp.where(token_col == lanes, 1.0, 0.0).astype(jnp.bfloat16)


def unroll_matrix(token_row, length):
    places = lax.broadcasted_iota(jnp.int32, (length, length), 0).astype(jnp.float32)
    return jnp.where(token_row == places, 1.0, 0.0).astype(jnp.bfloat16)


def write_masks(mask_ref, facts_row, facts_col, half):
    for block in range(2):
        part = slice(block * half, (block + 1) * half)
        code_i, base_i = facts_col[part, 0:1], facts_col[part, 1:2]
        code_j = facts_row[0:1, part]
        same = code_j >= base_i
        mask_ref[0, block] = jnp.where(same & (code_j <= code_i), 0.0, MASKED_SCORE)
        mask_ref[1, block] = jnp.where(same & (code_j < code_i), 0.0, MASKED_SCORE)


def query_sides(query, bias, segment_col, factor):
    wide = query.astype(jnp.float32)
    with_u = split_pair((wide + bias[0]) * factor)
    with_w = split_pair((wide + bias[1]) * factor)
    with_c = wide + bias[2]
    same = jnp.sum(with_c * bias[3], -1, keepdims=True) * factor
    change = jnp.sum(with_c * (bias[4] - bias[3]), -1, keepdims=True) * factor
    return with_u, with_w, with_c, same + change * segment_col, change * (1.0 - 2.0 * segment_col)


def block_scores(with_u, with_w, keys_twice, relative_twice, half):
    content = dot_nt(with_u, keys_twice)
    position = dot_nt(with_w, relative_twice)
    return content + pltpu.roll(position, half, 1, stride=1, stride_axis=0)[:, :half]


def attention_forward_kernel(
    head_size, content_ref, query_ref, weight_ref, table_ref, bias_ref, row_ref, col_ref,
    proj_ref, mixed_ref, logsum_ref, relative_ref, mask_ref,
):
    length = content_ref.shape[0]
    half = length // 2
    width = weight_ref.shape[-1]
    heads = width // head_size
    factor = head_size ** (-0.5) * LOG2E

    @pl.when(pl.program_id(0) == 0)
    def _():
        relative_ref[...] = dot(table_ref[...], weight_ref[3]).astype(jnp.bfloat16)

    facts_row, facts_col = row_ref[0], col_ref[0]
    write_masks(mask_ref, facts_row, facts_col, half)
    roll = roll_matrix(facts_col[:, 3:4], length)
    unroll = unroll_matrix(facts_row[3:4, :], length)
    content, query = content_ref[...], query_ref[...]
    joined = jnp.concatenate(
        [
            dot(content, weight_ref[0]).astype(jnp.bfloat16),
            dot(content, weight_ref[1]).astype(jnp.bfloat16),
            dot(content, weight_ref[2]).astype(jnp.bfloat16),
            dot(query, weight_ref[0]).astype(jnp.bfloat16),
        ],
        -1,
    )
    proj_ref[0] = dot(roll, joined).astype(jnp.bfloat16)
    segment_col, segment_row = facts_col[:, 2:3], facts_row[2:3, :]
    mixed = [[None] * heads, [None] * heads]
    for head in range(heads):
        cols = lambda kind: slice(kind * width + head * head_size, kind * width + (head + 1) * head_size)
        bias = [bias_ref[kind : kind + 1, head * head_size : (head + 1) * head_size] for kind in range(5)]
        keys, values = proj_ref[0, :, cols(1)], proj_ref[0, :, cols(2)]
        keys_twice = jnp.concatenate([keys, keys], -1)
        relative = relative_ref[:, head * head_size : (head + 1) * head_size]
        relative_twice = jnp.concatenate([relative, relative], -1)
        for stream in range(2):
            with_u, with_w, _, own, slope = query_sides(
                proj_ref[0, :, cols(3 * stream)], bias, segment_col, factor
            )
            pieces = []
            for block in range(2):
                part = slice(block * half, (block + 1) * half)
                scores = block_scores(
                    with_u[part], with_w[part], keys_twice[part], relative_twice, half
                )
                scores = scores + own[part] + slope[part] * segment_row[:, part] + mask_ref[stream, block]
                highest = jnp.maximum(jnp.max(scores, -1, keepdims=True), 0.0)
                weights = jnp.exp2(scores - highest)
                totals = jnp.exp2(-highest) + jnp.sum(weights, -1, keepdims=True)
                pieces.append(dot(weights.astype(jnp.bfloat16), values[part]) / totals)
                index = stream * heads + head
                logsum_ref[0, part, index : index + 1] = highest + jnp.log2(totals)
            mixed[stream][head] = jnp.concatenate(pieces, 0).astype(jnp.bfloat16)
    both = jnp.concatenate(mixed[0] + mixed[1], -1)
    both = dot(unroll, both).astype(jnp.bfloat16)
    mixed_ref[0] = both[:, :width]
    mixed_ref[1] = both[:, width:]


def attention_forward(content_rows, query_rows, projection, table, head_bias, facts):
    rows, length = facts[0].shape[0], facts[0].shape[2]
    tokens, depth = content_rows.shape
    width = projection.shape[-1]
    head_size = head_bias.shape[-1]
    half = length // 2
    full = lambda *shape: pl.BlockSpec(shape, lambda r: (0,) * len(shape))
    return pl.pallas_call(
        functools.partial(attention_forward_kernel, head_size),
        grid=(rows,),
        in_specs=[
            pl.BlockSpec((length, depth), lambda r: (r, 0)),
            pl.BlockSpec((length, depth), lambda r: (r, 0)),
            full(4, depth, width),
            full(length, depth),
            full(5, width),
            pl.BlockSpec((1, 8, length), lambda r: (r, 0, 0)),
            pl.BlockSpec((1, length, 8), lambda r: (r, 0, 0)),
        ],
        out_specs=[
            pl.BlockSpec((1, length, 4 * width), lambda r: (r, 0, 0)),
            pl.BlockSpec((2, length, width), lambda r: (0, r, 0)),
            pl.BlockSpec((1, length, 8), lambda r: (r, 0, 0)),
        ],
        out_shape=[
            jax.ShapeDtypeStruct((rows, length, 4 * width), jnp.bfloat16),
            jax.ShapeDtypeStruct((2, tokens, width), jnp.bfloat16),
            jax.ShapeDtypeStruct((rows, length, 8), jnp.float32),
        ],
        scratch_shapes=[
            pltpu.VMEM((length, width), jnp.bfloat16),
            pltpu.VMEM((2, 2, half, half), jnp.float32),
        ],
        compiler_params=pltpu.CompilerParams(vmem_limit_bytes=VMEM_LIMIT),
    )(content_rows, query_rows, projection, table, head_bias.reshape(5, width), *facts)


def attention_backward_kernel(
    head_size, content_ref, query_ref, weight_ref, table_ref, turned_ref, bias_ref, row_ref, col_ref,
    proj_ref, logsum_ref, upper_ref,
    dinput_ref, dweight_ref, dhead_ref,
    relative_ref, backward_ref, mask_ref, drel_ref, dcols_ref, dkeys_ref, dvalues_ref,
):
    length = content_ref.shape[0]
    half = length // 2
    width = weight_ref.shape[-1]
    heads = width // head_size
    scale = head_size ** (-0.5)
    factor = scale * LOG2E
    row = pl.program_id(0)

    @pl.when(row == 0)
    def _():
        relative_ref[...] = dot(table_ref[...], weight_ref[3]).astype(jnp.bfloat16)
        backward_ref[...] = dot(turned_ref[...], weight_ref[3]).astype(jnp.bfloat16)
        drel_ref[...] = jnp.zeros_like(drel_ref)
        dweight_ref[...] = jnp.zeros_like(dweight_ref)
        dhead_ref[...] = jnp.zeros_like(dhead_ref)

    facts_row, facts_col = row_ref[0], col_ref[0]
    write_masks(mask_ref, facts_row, facts_col, half)
    roll = roll_matrix(facts_col[:, 3:4], length)
    upper = dot(roll, jnp.concatenate([upper_ref[0], upper_ref[1]], -1)).astype(jnp.bfloat16)
    segment_col, segment_row = facts_col[:, 2:3], facts_row[2:3, :]
    down = lax.broadcasted_iota(jnp.int32, (half, half), 0)
    along = lax.broadcasted_iota(jnp.int32, (half, half), 1)
    mirror = jnp.where(down + along == half - 1, 1.0, 0.0).astype(jnp.bfloat16)
    lane = lax.broadcasted_iota(jnp.int32, (length, head_size), 1)
    extra = jnp.where(lane == 0, segment_col, jnp.where(lane == 1, 1.0, 0.0)).astype(jnp.bfloat16)
    for head in range(heads):
        own_cols = slice(head * head_size, (head + 1) * head_size)
        cols = lambda kind: slice(kind * width + head * head_size, kind * width + (head + 1) * head_size)
        bias = [bias_ref[kind : kind + 1, own_cols] for kind in range(5)]
        keys, values = proj_ref[0, :, cols(1)], proj_ref[0, :, cols(2)]
        keys_twice = jnp.concatenate([keys, keys], -1)
        keys_extra = jnp.concatenate([keys, extra], -1)
        relative = relative_ref[:, own_cols]
        relative_twice = jnp.concatenate([relative, relative], -1)
        backward = backward_ref[:, own_cols]
        heads_sums = [jnp.zeros((1, head_size), jnp.float32) for _ in range(5)]
        for stream in range(2):
            with_u, with_w, with_c, own, slope = query_sides(
                proj_ref[0, :, cols(3 * stream)], bias, segment_col, factor
            )
            index = stream * heads + head
            own = own - logsum_ref[0, :, index : index + 1]
            upper_now = upper[:, index * head_size : (index + 1) * head_size]
            with_u_t, with_w_t, upper_t = with_u.T, with_w.T, upper_now.T
            dquery = []
            for block in range(2):
                part = slice(block * half, (block + 1) * half)
                scores = block_scores(
                    with_u[part], with_w[part], keys_twice[part], relative_twice, half
                )
                scores = scores + own[part] + slope[part] * segment_row[:, part] + mask_ref[stream, block]
                chances = jnp.exp2(scores)
                dchance = dot_nt(upper_now[part], values[part])
                centre = jnp.sum(chances * dchance, -1, keepdims=True)
                dscore = (chances * (dchance - centre)).astype(jnp.bfloat16)
                dvalue_part = dot(upper_t[:, part], chances.astype(jnp.bfloat16))
                by_key = dot(dscore, keys_extra[part])
                turned = dot(dscore, mirror)
                wide = pltpu.roll(
                    jnp.concatenate([turned, jnp.zeros((half, half), jnp.float32)], -1),
                    0, 1, stride=1, stride_axis=0,
                ).astype(jnp.bfloat16)
                by_place = dot(wide, backward)
                dkey_part = dot(with_u_t[:, part], dscore)
                dkey_part = dkey_part[:head_size] + dkey_part[head_size:]
                drel_part = dot(with_w_t[:, part], wide)
                drel_ref[own_cols] += drel_part[:head_size] + drel_part[head_size:]
                if stream == 0:
                    dkeys_ref[own_cols, part] = dkey_part
                    dvalues_ref[own_cols, part] = dvalue_part
                else:
                    dkeys_ref[own_cols, part] += dkey_part
                    dvalues_ref[own_cols, part] += dvalue_part
                with_seg, total = by_key[:, head_size : head_size + 1], by_key[:, head_size + 1 : head_size + 2]
                seg_i = segment_col[part]
                seg_one = with_seg + seg_i * (total - 2.0 * with_seg)
                seg_zero = total - seg_one
                by_key = by_key[:, :head_size]
                by_segment = seg_zero * bias[3] + seg_one * bias[4]
                dquery.append((by_key + by_place + by_segment) * scale)
                for kind, term in enumerate(
                    (by_key, by_place, by_segment, seg_zero * with_c[part], seg_one * with_c[part])
                ):
                    heads_sums[kind] = heads_sums[kind] + jnp.sum(term, 0, keepdims=True)
            dcols_ref[:, cols(stream)] = jnp.concatenate(dquery, 0).astype(jnp.bfloat16)
        for kind in range(5):
            dhead_ref[kind : kind + 1, own_cols] += heads_sums[kind] * scale
    dcols_ref[:, 2 * width : 3 * width] = (dkeys_ref[...] * (1.0 / LOG2E)).astype(jnp.bfloat16).T
    dcols_ref[:, 3 * width :] = dvalues_ref[...].astype(jnp.bfloat16).T
    unroll = unroll_matrix(facts_row[3:4, :], length)
    joined = dot(unroll, dcols_ref[...]).astype(jnp.bfloat16)
    joined_t = joined.T
    content, query = content_ref[...], query_ref[...]
    dweight_ref[0] += dot(joined_t[:width], content) + dot(joined_t[width : 2 * width], query)
    dweight_ref[1] += dot(joined_t[2 * width : 3 * width], content)
    dweight_ref[2] += dot(joined_t[3 * width :], content)
    dinput_ref[0] = (
        dot_nt(joined[:, :width], weight_ref[0])
        + dot_nt(joined[:, 2 * width : 3 * width], weight_ref[1])
        + dot_nt(joined[:, 3 * width :], weight_ref[2])
    ).astype(jnp.bfloat16)
    dinput_ref[1] = dot_nt(joined[:, width : 2 * width], weight_ref[0]).astype(jnp.bfloat16)

    @pl.when(row == pl.num_programs(0) - 1)
    def _():
        drel = drel_ref[...] * (1.0 / LOG2E)
        high = drel.astype(jnp.bfloat16)
        low = (drel - high.astype(jnp.float32)).astype(jnp.bfloat16)
        dweight_ref[3] = dot(high, turned_ref[...]) + dot(low, turned_ref[...])


def attention_backward(content_rows, query_rows, projection, tables, head_bias, facts, proj, logsum, upper):
    rows, length = facts[0].shape[0], facts[0].shape[2]
    tokens, depth = content_rows.shape
    width = projection.shape[-1]
    head_size = head_bias.shape[-1]
    half = length // 2
    full = lambda *shape: pl.BlockSpec(shape, lambda r: (0,) * len(shape))
    return pl.pallas_call(
        functools.partial(attention_backward_kernel, head_size),
        grid=(rows,),
        in_specs=[
            pl.BlockSpec((length, depth), lambda r: (r, 0)),
            pl.BlockSpec((length, depth), lambda r: (r, 0)),
            full(4, depth, width),
            full(length, depth),
            full(length, depth),
            full(5, width),
            pl.BlockSpec((1, 8, length), lambda r: (r, 0, 0)),
            pl.BlockSpec((1, length, 8), lambda r: (r, 0, 0)),
            pl.BlockSpec((1, length, 4 * width), lambda r: (r, 0, 0)),
            pl.BlockSpec((1, length, 8), lambda r: (r, 0, 0)),
            pl.BlockSpec((2, length, width), lambda r: (0, r, 0)),
        ],
        out_specs=[
            pl.BlockSpec((2, length, depth), lambda r: (0, r, 0)),
            full(4, width, depth),
            full(5, width),
        ],
        out_shape=[
            jax.ShapeDtypeStruct((2, tokens, depth), jnp.bfloat16),
            jax.ShapeDtypeStruct((4, width, depth), jnp.float32),
            jax.ShapeDtypeStruct((5, width), jnp.float32),
        ],
        scratch_shapes=[
            pltpu.VMEM((length, width), jnp.bfloat16),
            pltpu.VMEM((length, width), jnp.bfloat16),
            pltpu.VMEM((2, 2, half, half), jnp.float32),
            pltpu.VMEM((width, length), jnp.float32),
            pltpu.VMEM((length, 4 * width), jnp.bfloat16),
            pltpu.VMEM((width, length), jnp.float32),
            pltpu.VMEM((width, length), jnp.float32),
        ],
        compiler_params=pltpu.CompilerParams(vmem_limit_bytes=VMEM_LIMIT),
    )(content_rows, query_rows, projection, *tables, head_bias.reshape(5, width), *facts, proj, logsum, upper)


def layer_norm_parts(values, gain_row, bias_row):
    row_mean = jnp.mean(values, -1, keepdims=True)
    centred = values - row_mean
    row_var = jnp.mean(centred * centred, -1, keepdims=True)
    inverse = lax.rsqrt(row_var + NORM_EPSILON)
    normed = centred * inverse
    return (normed * gain_row + bias_row, normed, inverse)


def layer_norm_back(upstream, normed, inverse, gain_row):
    scaled = upstream * gain_row
    first_mean = jnp.mean(scaled, -1, keepdims=True)
    second_mean = jnp.mean(scaled * normed, -1, keepdims=True)
    return inverse * (scaled - first_mean - normed * second_mean)


def gelu_back(before, upstream):
    return jax.vjp(lambda inner: jax.nn.gelu(inner, approximate=True), before)[1](upstream)[0]


def adam_step(master, first, second, gradient, factor, decayed):
    clipped = gradient * factor
    new_first = BETA_ONE * first + (1.0 - BETA_ONE) * clipped
    new_second = BETA_TWO * second + (1.0 - BETA_TWO) * clipped * clipped
    first_hat = new_first / (1.0 - BETA_ONE**STEP)
    second_hat = new_second / (1.0 - BETA_TWO**STEP)
    update = first_hat / (jnp.sqrt(second_hat) + ADAM_EPSILON)
    if decayed:
        update = update + WEIGHT_DECAY * master
        return (new_first, new_second, master - MATRIX_RATE * update)
    return (new_first, new_second, master - VECTOR_RATE * update)


def local(
    content_in,
    query_in,
    content_grad,
    query_grad,
    segment_ids,
    doc_lengths,
    factor_order,
    attn_proj,
    attn_proj_first,
    attn_proj_second,
    out_proj,
    out_proj_first,
    out_proj_second,
    up_proj,
    up_proj_first,
    up_proj_second,
    down_proj,
    down_proj_first,
    down_proj_second,
    head_bias,
    head_bias_first,
    head_bias_second,
    up_bias,
    up_bias_first,
    up_bias_second,
    norm_param,
    norm_param_first,
    norm_param_second,
):
    local_rows, width = content_in.shape
    sequences, length = segment_ids.shape
    local_heads, head_size = (head_bias.shape[1], head_bias.shape[2])
    hidden_cols = up_bias.shape[0]
    projection, out_weight, up_weight, down_weight = (
        lax.all_gather(attn_proj.astype(jnp.bfloat16), "dp", axis=1, tiled=True),
        lax.all_gather(out_proj.astype(jnp.bfloat16), "dp", axis=1, tiled=True),
        lax.all_gather(up_proj.astype(jnp.bfloat16), "dp", axis=0, tiled=True),
        lax.all_gather(down_proj.astype(jnp.bfloat16), "dp", axis=1, tiled=True),
    )
    content_rows, query_rows = (
        lax.all_gather(content_in, "heads", axis=0, tiled=True),
        lax.all_gather(query_in, "heads", axis=0, tiled=True),
    )
    table = position_table(length, width)
    tables = (jnp.asarray(table), jnp.asarray(table[::-1].copy()))
    facts = row_facts(segment_ids, doc_lengths, factor_order)
    proj, mixed, logsum = attention_forward(
        content_rows, query_rows, projection, tables[0], head_bias, facts
    )
    attended_c, attended_q = mixed[0], mixed[1]
    rows_c = attended_c
    rows_q = attended_q
    attention_sum = lax.psum_scatter(
        jnp.concatenate(
            [
                jnp.dot(rows_c, out_weight, preferred_element_type=jnp.float32),
                jnp.dot(rows_q, out_weight, preferred_element_type=jnp.float32),
            ],
            1,
        ),
        "heads",
        scatter_dimension=0,
        tiled=True,
    )
    middle_c, normed1_c, inverse1_c = layer_norm_parts(
        content_in.astype(jnp.float32) + attention_sum[:, :width], norm_param[0], norm_param[1]
    )
    middle_q, normed1_q, inverse1_q = layer_norm_parts(
        query_in.astype(jnp.float32) + attention_sum[:, width:], norm_param[0], norm_param[1]
    )
    middle_rows_c, middle_rows_q = (
        lax.all_gather(middle_c.astype(jnp.bfloat16), "heads", axis=0, tiled=True),
        lax.all_gather(middle_q.astype(jnp.bfloat16), "heads", axis=0, tiled=True),
    )
    before_c = jnp.dot(middle_rows_c, up_weight, preferred_element_type=jnp.float32) + up_bias
    before_q = jnp.dot(middle_rows_q, up_weight, preferred_element_type=jnp.float32) + up_bias
    hidden_c = jax.nn.gelu(before_c, approximate=True).astype(jnp.bfloat16)
    hidden_q = jax.nn.gelu(before_q, approximate=True).astype(jnp.bfloat16)
    rows_c = hidden_c
    rows_q = hidden_q
    feed_sum = lax.psum_scatter(
        jnp.concatenate(
            [
                jnp.dot(rows_c, down_weight, preferred_element_type=jnp.float32),
                jnp.dot(rows_q, down_weight, preferred_element_type=jnp.float32),
            ],
            1,
        ).astype(jnp.bfloat16),
        "heads",
        scatter_dimension=0,
        tiled=True,
    ).astype(jnp.float32)
    final_c, normed2_c, inverse2_c = layer_norm_parts(
        middle_c + feed_sum[:, :width] + norm_param[2], norm_param[3], norm_param[4]
    )
    final_q, normed2_q, inverse2_q = layer_norm_parts(
        middle_q + feed_sum[:, width:] + norm_param[2], norm_param[3], norm_param[4]
    )
    upstream_c = content_grad.astype(jnp.float32)
    upstream_q = query_grad.astype(jnp.float32)
    dfinal_c = layer_norm_back(upstream_c, normed2_c, inverse2_c, norm_param[3])
    dfinal_q = layer_norm_back(upstream_q, normed2_q, inverse2_q, norm_param[3])
    gain2_grad = jnp.sum(upstream_c * normed2_c, 0) + jnp.sum(upstream_q * normed2_q, 0)
    bias2_grad = jnp.sum(upstream_c, 0) + jnp.sum(upstream_q, 0)
    outbias_grad = jnp.sum(dfinal_c, 0) + jnp.sum(dfinal_q, 0)
    back_c, back_q = (
        lax.all_gather(dfinal_c.astype(jnp.bfloat16), "heads", axis=0, tiled=True),
        lax.all_gather(dfinal_q.astype(jnp.bfloat16), "heads", axis=0, tiled=True),
    )
    down_grad = jnp.einsum(
        "tf,td->fd", hidden_c, back_c, preferred_element_type=jnp.float32
    ) + jnp.einsum("tf,td->fd", hidden_q, back_q, preferred_element_type=jnp.float32)
    dbefore_c = gelu_back(
        before_c, jnp.einsum("td,fd->tf", back_c, down_weight, preferred_element_type=jnp.float32)
    ).astype(jnp.bfloat16)
    dbefore_q = gelu_back(
        before_q, jnp.einsum("td,fd->tf", back_q, down_weight, preferred_element_type=jnp.float32)
    ).astype(jnp.bfloat16)
    upbias_local = jnp.sum(dbefore_c.astype(jnp.float32), 0) + jnp.sum(
        dbefore_q.astype(jnp.float32), 0
    )
    up_grad = jnp.einsum(
        "td,tf->df", middle_rows_c, dbefore_c, preferred_element_type=jnp.float32
    ) + jnp.einsum("td,tf->df", middle_rows_q, dbefore_q, preferred_element_type=jnp.float32)
    rows_c = dbefore_c
    rows_q = dbefore_q
    feed_back = lax.psum_scatter(
        jnp.concatenate(
            [
                jnp.einsum("tf,df->td", rows_c, up_weight, preferred_element_type=jnp.float32),
                jnp.einsum("tf,df->td", rows_q, up_weight, preferred_element_type=jnp.float32),
            ],
            1,
        ).astype(jnp.bfloat16),
        "heads",
        scatter_dimension=0,
        tiled=True,
    ).astype(jnp.float32)
    dmiddle_c = dfinal_c + feed_back[:, :width]
    dmiddle_q = dfinal_q + feed_back[:, width:]
    dresid_c = layer_norm_back(dmiddle_c, normed1_c, inverse1_c, norm_param[0])
    dresid_q = layer_norm_back(dmiddle_q, normed1_q, inverse1_q, norm_param[0])
    gain1_grad = jnp.sum(dmiddle_c * normed1_c, 0) + jnp.sum(dmiddle_q * normed1_q, 0)
    bias1_grad = jnp.sum(dmiddle_c, 0) + jnp.sum(dmiddle_q, 0)
    dattn_c, dattn_q = (
        lax.all_gather(dresid_c.astype(jnp.bfloat16), "heads", axis=0, tiled=True),
        lax.all_gather(dresid_q.astype(jnp.bfloat16), "heads", axis=0, tiled=True),
    )
    out_grad = jnp.einsum(
        "te,td->ed", attended_c, dattn_c, preferred_element_type=jnp.float32
    ) + jnp.einsum("te,td->ed", attended_q, dattn_q, preferred_element_type=jnp.float32)
    dmixed_c = jnp.einsum(
        "td,ed->te", dattn_c, out_weight, preferred_element_type=jnp.float32
    ).astype(jnp.bfloat16)
    dmixed_q = jnp.einsum(
        "td,ed->te", dattn_q, out_weight, preferred_element_type=jnp.float32
    ).astype(jnp.bfloat16)

    dinput, dweight, head_local = attention_backward(
        content_rows, query_rows, projection, tables, head_bias, facts, proj, logsum,
        jnp.stack([dmixed_c, dmixed_q]),
    )
    head_local = head_local.reshape(head_bias.shape)
    proj_grad = jnp.swapaxes(dweight, 1, 2)
    input_back = lax.psum_scatter(
        jnp.concatenate([dinput[0], dinput[1]], 1),
        "heads",
        scatter_dimension=0,
        tiled=True,
    ).astype(jnp.float32)
    content_in_grad = dresid_c + input_back[:, :width]
    query_in_grad = dresid_q + input_back[:, width:]
    proj_share, out_share, up_share, down_share = (
        lax.psum_scatter(proj_grad, "dp", scatter_dimension=1, tiled=True),
        lax.psum_scatter(out_grad, "dp", scatter_dimension=1, tiled=True),
        lax.psum_scatter(up_grad, "dp", scatter_dimension=0, tiled=True),
        lax.psum_scatter(down_grad, "dp", scatter_dimension=1, tiled=True),
    )
    heads_count = lax.axis_size("heads")
    head_index = lax.axis_index("heads")
    head_full = jnp.zeros((5, local_heads * heads_count, head_size), jnp.float32)
    head_full = lax.dynamic_update_slice_in_dim(head_full, head_local, head_index * local_heads, 1)
    bias_full = jnp.zeros((hidden_cols * heads_count,), jnp.float32)
    bias_full = lax.dynamic_update_slice_in_dim(
        bias_full, upbias_local, head_index * hidden_cols, 0
    )
    norm_local = jnp.stack([gain1_grad, bias1_grad, outbias_grad, gain2_grad, bias2_grad])
    head_sum, bias_sum, norm_sum = lax.psum((head_full, bias_full, norm_local), ("dp", "heads"))
    head_grad = lax.dynamic_slice_in_dim(head_sum, head_index * local_heads, local_heads, 1)
    bias_grad = lax.dynamic_slice_in_dim(bias_sum, head_index * hidden_cols, hidden_cols, 0)
    devices = lax.axis_size("dp") * heads_count
    shared_squares = (
        jnp.sum(head_sum * head_sum) + jnp.sum(bias_sum * bias_sum) + jnp.sum(norm_sum * norm_sum)
    )
    local_squares = (
        jnp.sum(proj_share * proj_share)
        + jnp.sum(out_share * out_share)
        + jnp.sum(up_share * up_share)
        + jnp.sum(down_share * down_share)
        + shared_squares / devices
    )
    grad_norm = jnp.sqrt(lax.psum(local_squares, ("dp", "heads")))
    factor = CLIP_NORM / jnp.maximum(grad_norm, CLIP_NORM)
    attn_first, attn_second, attn_new = adam_step(
        attn_proj, attn_proj_first, attn_proj_second, proj_share, factor, True
    )
    out_first, out_second, out_new = adam_step(
        out_proj, out_proj_first, out_proj_second, out_share, factor, True
    )
    up_first, up_second, up_new = adam_step(
        up_proj, up_proj_first, up_proj_second, up_share, factor, True
    )
    down_first, down_second, down_new = adam_step(
        down_proj, down_proj_first, down_proj_second, down_share, factor, True
    )
    head_first, head_second, head_new = adam_step(
        head_bias, head_bias_first, head_bias_second, head_grad, factor, False
    )
    bias_first, bias_second, bias_new = adam_step(
        up_bias, up_bias_first, up_bias_second, bias_grad, factor, False
    )
    norm_first, norm_second, norm_new = adam_step(
        norm_param, norm_param_first, norm_param_second, norm_sum, factor, False
    )
    return (
        final_c.astype(jnp.bfloat16),
        final_q.astype(jnp.bfloat16),
        content_in_grad,
        query_in_grad,
        grad_norm,
        proj_share,
        attn_first,
        attn_second,
        attn_new,
        out_share,
        out_first,
        out_second,
        out_new,
        up_share,
        up_first,
        up_second,
        up_new,
        down_share,
        down_first,
        down_second,
        down_new,
        head_grad,
        head_first,
        head_second,
        head_new,
        bias_grad,
        bias_first,
        bias_second,
        bias_new,
        norm_sum,
        norm_first,
        norm_second,
        norm_new,
    )


def solution(mesh):
    return jax.shard_map(
        local,
        mesh=mesh,
        in_specs=(
            P(("dp", "heads"), None),
            P(("dp", "heads"), None),
            P(("dp", "heads"), None),
            P(("dp", "heads"), None),
            P("dp", None),
            P("dp", None),
            P("dp", None),
            P(None, "dp", "heads"),
            P(None, "dp", "heads"),
            P(None, "dp", "heads"),
            P("heads", "dp"),
            P("heads", "dp"),
            P("heads", "dp"),
            P("dp", "heads"),
            P("dp", "heads"),
            P("dp", "heads"),
            P("heads", "dp"),
            P("heads", "dp"),
            P("heads", "dp"),
            P(None, "heads", None),
            P(None, "heads", None),
            P(None, "heads", None),
            P("heads"),
            P("heads"),
            P("heads"),
            P(),
            P(),
            P(),
        ),
        out_specs=(
            P(("dp", "heads"), None),
            P(("dp", "heads"), None),
            P(("dp", "heads"), None),
            P(("dp", "heads"), None),
            P(),
            P(None, "dp", "heads"),
            P(None, "dp", "heads"),
            P(None, "dp", "heads"),
            P(None, "dp", "heads"),
            P("heads", "dp"),
            P("heads", "dp"),
            P("heads", "dp"),
            P("heads", "dp"),
            P("dp", "heads"),
            P("dp", "heads"),
            P("dp", "heads"),
            P("dp", "heads"),
            P("heads", "dp"),
            P("heads", "dp"),
            P("heads", "dp"),
            P("heads", "dp"),
            P(None, "heads", None),
            P(None, "heads", None),
            P(None, "heads", None),
            P(None, "heads", None),
            P("heads"),
            P("heads"),
            P("heads"),
            P("heads"),
            P(),
            P(),
            P(),
            P(),
        ),
        check_vma=False,
    )
```

```python
import functools

import jax
import jax.numpy as jnp
import ml_dtypes
import numpy as np
from jax import lax
from jax.experimental import pallas as pl
from jax.experimental.pallas import tpu as pltpu
from jax.sharding import PartitionSpec as P

STEP = 10


NORM_EPSILON = 1e-05
CLIP_NORM = 1.0
MATRIX_RATE = 0.08
VECTOR_RATE = 0.5
BETA_ONE = 0.9
BETA_TWO = 0.999
ADAM_EPSILON = 1e-08
WEIGHT_DECAY = 0.01
MASKED_SCORE = -1e30
GELU_FACTOR = 0.7978845608028654
GELU_CUBIC = 0.044715
LOG2E = 1.4426950408889634
VMEM_LIMIT = 56 << 20


def position_table(length, width):
    distance = length // 2 - np.arange(length)
    frequency = 10000.0 ** (-np.arange(0, width, 2) / width)
    angles = distance[:, None] * frequency[None, :]
    return np.concatenate([np.sin(angles), np.cos(angles)], -1).astype(np.float32).astype(ml_dtypes.bfloat16)


def dot(left, right):
    return lax.dot_general(left, right, (((1,), (0,)), ((), ())), preferred_element_type=jnp.float32)


def dot_nt(left, right):
    return lax.dot_general(left, right, (((1,), (1,)), ((), ())), preferred_element_type=jnp.float32)


def split_pair(values):
    high = values.astype(jnp.bfloat16)
    low = (values - high.astype(jnp.float32)).astype(jnp.bfloat16)
    return jnp.concatenate([high, low], -1)


def row_facts(segment_ids, doc_lengths, factor_order):
    rows, length = segment_ids.shape
    places = jnp.arange(length, dtype=jnp.int32)
    counts = doc_lengths.shape[1]
    earlier = jnp.arange(counts)[:, None] <= jnp.arange(counts)[None, :]
    ends = jnp.sum(jnp.where(earlier[None], doc_lengths[:, :, None], 0), 1)
    start = jnp.sum(jnp.where(doc_lengths == length // 2, ends - doc_lengths, 0), -1)
    token = (places[None] + start[:, None]) % length
    document = jnp.sum((token[:, :, None] >= ends[:, None, :]).astype(jnp.int32), -1)
    ranking = jnp.sum(
        jnp.where(factor_order[:, :, None] == token[:, None, :], places[None, :, None], 0), 1
    )
    segment = jnp.sum(
        jnp.where(places[None, :, None] == token[:, None, :], segment_ids[:, :, None], 0), 1
    )
    base = document * length
    zero = jnp.zeros_like(base)
    facts = jnp.stack([base + ranking, base, segment, token, zero, zero, zero, zero], 1)
    facts = facts.astype(jnp.float32)
    return facts, jnp.swapaxes(facts, 1, 2)


def roll_matrix(token_col, length):
    lanes = lax.broadcasted_iota(jnp.int32, (length, length), 1).astype(jnp.float32)
    return jnp.where(token_col == lanes, 1.0, 0.0).astype(jnp.bfloat16)


def unroll_matrix(token_row, length):
    places = lax.broadcasted_iota(jnp.int32, (length, length), 0).astype(jnp.float32)
    return jnp.where(token_row == places, 1.0, 0.0).astype(jnp.bfloat16)


def write_masks(mask_ref, facts_row, facts_col, half):
    for block in range(2):
        part = slice(block * half, (block + 1) * half)
        code_i, base_i = facts_col[part, 0:1], facts_col[part, 1:2]
        code_j = facts_row[0:1, part]
        same = code_j >= base_i
        mask_ref[0, block] = jnp.where(same & (code_j <= code_i), 0.0, MASKED_SCORE)
        mask_ref[1, block] = jnp.where(same & (code_j < code_i), 0.0, MASKED_SCORE)


def query_sides(query, bias, segment_col, factor):
    wide = query.astype(jnp.float32)
    with_u = split_pair((wide + bias[0]) * factor)
    with_w = split_pair((wide + bias[1]) * factor)
    with_c = wide + bias[2]
    same = jnp.sum(with_c * bias[3], -1, keepdims=True) * factor
    change = jnp.sum(with_c * (bias[4] - bias[3]), -1, keepdims=True) * factor
    return with_u, with_w, with_c, same + change * segment_col, change * (1.0 - 2.0 * segment_col)


def block_scores(with_u, with_w, keys_twice, relative_twice, half):
    content = dot_nt(with_u, keys_twice)
    position = dot_nt(with_w, relative_twice)
    return content + pltpu.roll(position, half, 1, stride=1, stride_axis=0)[:, :half]


def start_pieces(pieces, place, sems, base):
    copies = []
    for index, piece in enumerate(pieces):
        copy = pltpu.make_async_copy(piece, place(index), sems.at[base + index])
        copy.start()
        copies.append(copy)
    return copies


def start_inputs(content_pieces, query_pieces, weight_pieces, content_ref, query_ref, weight_ref, sems):
    heads_here, dp_here = lax.axis_index("heads"), lax.axis_index("dp")
    tokens, rows = content_pieces[0].shape[0], weight_pieces[0].shape[1]

    def token_place(ref):
        return lambda k: ref.at[pl.ds(pl.multiple_of((heads_here ^ k) * tokens, tokens), tokens)]

    def weight_place(k):
        if len(weight_pieces) == 1:
            return weight_ref
        return weight_ref.at[:, pl.ds(pl.multiple_of((dp_here ^ k) * rows, rows), rows)]

    copies = start_pieces(weight_pieces, weight_place, sems, 0)
    base = len(weight_pieces)
    copies += start_pieces(content_pieces, token_place(content_ref), sems, base)
    base += len(content_pieces)
    return copies + start_pieces(query_pieces, token_place(query_ref), sems, base)


def greet(axis, masks):
    barrier = pltpu.get_barrier_semaphore()
    for mask in masks:
        pl.semaphore_signal(
            barrier, inc=1, device_id={axis: lax.axis_index(axis) ^ mask}, device_id_type=pl.DeviceIdType.MESH
        )
    pl.semaphore_wait(barrier, len(masks))


def send_pieces(full_ref, pieces, send_sems, recv_sems, base):
    tokens = pieces[0].shape[1]
    here = lax.axis_index("heads")
    copies = []
    for k, piece in enumerate(pieces):
        part = full_ref.at[:, pl.ds(pl.multiple_of((here ^ k) * tokens, tokens), tokens)]
        if k == 0:
            copy = pltpu.make_async_copy(part, piece, send_sems.at[base])
        else:
            copy = pltpu.make_async_remote_copy(
                part, piece, send_sems.at[base + k], recv_sems.at[k],
                device_id={"heads": here ^ k}, device_id_type=pl.DeviceIdType.MESH,
            )
        copy.start()
        copies.append(copy)
    for copy in copies:
        copy.wait()


def attention_forward_kernel(head_size, group, parts, *refs):
    content_pieces, query_pieces, refs = refs[:group], refs[group : 2 * group], refs[2 * group :]
    weight_pieces, refs = refs[:parts], refs[parts:]
    table_ref, bias_ref, row_ref, col_ref, proj_ref, logsum_ref = refs[:6]
    mixed_pieces, refs = refs[6 : 6 + group], refs[6 + group :]
    content_all, query_all, weight_ref, mixed_ref, relative_ref, mask_ref, sems, recv_sems = refs
    length = row_ref.shape[2]
    half = length // 2
    width = weight_ref.shape[-1]
    heads = width // head_size
    factor = head_size ** (-0.5) * LOG2E
    row = pl.program_id(0)

    @pl.when(row == 0)
    def _():
        copies = start_inputs(
            content_pieces, query_pieces, weight_pieces, content_all, query_all, weight_ref, sems
        )
        greet("heads", range(1, group))
        for copy in copies:
            copy.wait()
        relative_ref[...] = dot(table_ref[...], weight_ref[3]).astype(jnp.bfloat16)

    here = pl.ds(pl.multiple_of(row * length, length), length)
    content_ref, query_ref = content_all.at[here], query_all.at[here]

    facts_row, facts_col = row_ref[0], col_ref[0]
    write_masks(mask_ref, facts_row, facts_col, half)
    roll = roll_matrix(facts_col[:, 3:4], length)
    unroll = unroll_matrix(facts_row[3:4, :], length)
    content, query = content_ref[...], query_ref[...]
    joined = jnp.concatenate(
        [
            dot(content, weight_ref[0]).astype(jnp.bfloat16),
            dot(content, weight_ref[1]).astype(jnp.bfloat16),
            dot(content, weight_ref[2]).astype(jnp.bfloat16),
            dot(query, weight_ref[0]).astype(jnp.bfloat16),
        ],
        -1,
    )
    proj_ref[0] = dot(roll, joined).astype(jnp.bfloat16)
    segment_col, segment_row = facts_col[:, 2:3], facts_row[2:3, :]
    mixed = [[None] * heads, [None] * heads]
    for head in range(heads):
        cols = lambda kind: slice(kind * width + head * head_size, kind * width + (head + 1) * head_size)
        bias = [bias_ref[kind : kind + 1, head * head_size : (head + 1) * head_size] for kind in range(5)]
        keys, values = proj_ref[0, :, cols(1)], proj_ref[0, :, cols(2)]
        keys_twice = jnp.concatenate([keys, keys], -1)
        relative = relative_ref[:, head * head_size : (head + 1) * head_size]
        relative_twice = jnp.concatenate([relative, relative], -1)
        for stream in range(2):
            with_u, with_w, _, own, slope = query_sides(
                proj_ref[0, :, cols(3 * stream)], bias, segment_col, factor
            )
            pieces = []
            for block in range(2):
                part = slice(block * half, (block + 1) * half)
                scores = block_scores(
                    with_u[part], with_w[part], keys_twice[part], relative_twice, half
                )
                scores = scores + own[part] + slope[part] * segment_row[:, part] + mask_ref[stream, block]
                highest = jnp.maximum(jnp.max(scores, -1, keepdims=True), 0.0)
                weights = jnp.exp2(scores - highest)
                totals = jnp.exp2(-highest) + jnp.sum(weights, -1, keepdims=True)
                pieces.append(dot(weights.astype(jnp.bfloat16), values[part]) / totals)
                index = stream * heads + head
                logsum_ref[0, part, index : index + 1] = highest + jnp.log2(totals)
            mixed[stream][head] = jnp.concatenate(pieces, 0).astype(jnp.bfloat16)
    both = jnp.concatenate(mixed[0] + mixed[1], -1)
    both = dot(unroll, both).astype(jnp.bfloat16)
    mixed_ref[0, here] = both[:, :width]
    mixed_ref[1, here] = both[:, width:]

    @pl.when(row == pl.num_programs(0) - 1)
    def _():
        send_pieces(mixed_ref, mixed_pieces, sems, recv_sems, 2 * group + parts)


def attention_forward(content_pieces, query_pieces, weight_pieces, table, head_bias, facts):
    rows, length = facts[0].shape[0], facts[0].shape[2]
    group, parts = len(content_pieces), len(weight_pieces)
    own, depth = content_pieces[0].shape
    tokens = own * group
    width = weight_pieces[0].shape[-1]
    head_size = head_bias.shape[-1]
    half = length // 2
    full = lambda *shape: pl.BlockSpec(shape, lambda r: (0,) * len(shape))
    outside = pl.BlockSpec(memory_space=pl.ANY)
    results = pl.pallas_call(
        functools.partial(attention_forward_kernel, head_size, group, parts),
        grid=(rows,),
        in_specs=[outside] * (2 * group + parts)
        + [
            full(length, depth),
            full(5, width),
            pl.BlockSpec((1, 8, length), lambda r: (r, 0, 0)),
            pl.BlockSpec((1, length, 8), lambda r: (r, 0, 0)),
        ],
        out_specs=[
            pl.BlockSpec((1, length, 4 * width), lambda r: (r, 0, 0)),
            pl.BlockSpec((1, length, 8), lambda r: (r, 0, 0)),
        ]
        + [outside] * group,
        out_shape=[
            jax.ShapeDtypeStruct((rows, length, 4 * width), jnp.bfloat16),
            jax.ShapeDtypeStruct((rows, length, 8), jnp.float32),
        ]
        + [jax.ShapeDtypeStruct((2, own, width), jnp.bfloat16)] * group,
        scratch_shapes=[
            pltpu.VMEM((tokens, depth), jnp.bfloat16),
            pltpu.VMEM((tokens, depth), jnp.bfloat16),
            pltpu.VMEM((4, depth, width), jnp.bfloat16),
            pltpu.VMEM((2, tokens, width), jnp.bfloat16),
            pltpu.VMEM((length, width), jnp.bfloat16),
            pltpu.VMEM((2, 2, half, half), jnp.float32),
            pltpu.SemaphoreType.DMA((3 * group + parts,)),
            pltpu.SemaphoreType.DMA((group,)),
        ],
        compiler_params=pltpu.CompilerParams(
            vmem_limit_bytes=VMEM_LIMIT, collective_id=0, has_side_effects=True
        ),
    )(*content_pieces, *query_pieces, *weight_pieces, table, head_bias.reshape(5, width), *facts)
    return results[0], results[1], results[2:]


def attention_backward_kernel(head_size, group, parts, *refs):
    content_pieces, query_pieces, refs = refs[:group], refs[group : 2 * group], refs[2 * group :]
    weight_pieces, refs = refs[:parts], refs[parts:]
    upper_pieces, refs = refs[:group], refs[group:]
    table_ref, turned_ref, bias_ref, row_ref, col_ref, proj_ref, logsum_ref = refs[:7]
    dinput_pieces, refs = refs[7 : 7 + group], refs[7 + group :]
    dweight_pieces, dhead_ref, refs = refs[:parts], refs[parts], refs[parts + 1 :]
    content_all, query_all, weight_ref, upper_all, dinput_ref, dweight_ref = refs[:6]
    relative_ref, backward_ref, mask_ref, drel_ref, dcols_ref, dkeys_ref, dvalues_ref, sems = refs[6:]
    length = row_ref.shape[2]
    half = length // 2
    width = weight_ref.shape[-1]
    heads = width // head_size
    scale = head_size ** (-0.5)
    factor = scale * LOG2E
    row = pl.program_id(0)
    heads_here, dp_here = lax.axis_index("heads"), lax.axis_index("dp")

    @pl.when(row == 0)
    def _():
        copies = start_inputs(
            content_pieces, query_pieces, weight_pieces, content_all, query_all, weight_ref, sems
        )
        tokens = upper_pieces[0].shape[1]
        copies += start_pieces(
            upper_pieces,
            lambda k: upper_all.at[:, pl.ds(pl.multiple_of((heads_here ^ k) * tokens, tokens), tokens)],
            sems,
            2 * group + parts,
        )
        for copy in copies:
            copy.wait()
        relative_ref[...] = dot(table_ref[...], weight_ref[3]).astype(jnp.bfloat16)
        backward_ref[...] = dot(turned_ref[...], weight_ref[3]).astype(jnp.bfloat16)
        drel_ref[...] = jnp.zeros_like(drel_ref)
        dweight_ref[...] = jnp.zeros_like(dweight_ref)
        dhead_ref[...] = jnp.zeros_like(dhead_ref)

    here = pl.ds(pl.multiple_of(row * length, length), length)
    content_ref, query_ref = content_all.at[here], query_all.at[here]
    facts_row, facts_col = row_ref[0], col_ref[0]
    write_masks(mask_ref, facts_row, facts_col, half)
    roll = roll_matrix(facts_col[:, 3:4], length)
    upper = dot(roll, jnp.concatenate([upper_all[0, here], upper_all[1, here]], -1)).astype(jnp.bfloat16)
    segment_col, segment_row = facts_col[:, 2:3], facts_row[2:3, :]
    down = lax.broadcasted_iota(jnp.int32, (half, half), 0)
    along = lax.broadcasted_iota(jnp.int32, (half, half), 1)
    mirror = jnp.where(down + along == half - 1, 1.0, 0.0).astype(jnp.bfloat16)
    lane = lax.broadcasted_iota(jnp.int32, (length, head_size), 1)
    extra = jnp.where(lane == 0, segment_col, jnp.where(lane == 1, 1.0, 0.0)).astype(jnp.bfloat16)
    for head in range(heads):
        own_cols = slice(head * head_size, (head + 1) * head_size)
        cols = lambda kind: slice(kind * width + head * head_size, kind * width + (head + 1) * head_size)
        bias = [bias_ref[kind : kind + 1, own_cols] for kind in range(5)]
        keys, values = proj_ref[0, :, cols(1)], proj_ref[0, :, cols(2)]
        keys_twice = jnp.concatenate([keys, keys], -1)
        keys_extra = jnp.concatenate([keys, extra], -1)
        relative = relative_ref[:, own_cols]
        relative_twice = jnp.concatenate([relative, relative], -1)
        backward = backward_ref[:, own_cols]
        heads_sums = [jnp.zeros((1, head_size), jnp.float32) for _ in range(5)]
        for stream in range(2):
            with_u, with_w, with_c, own, slope = query_sides(
                proj_ref[0, :, cols(3 * stream)], bias, segment_col, factor
            )
            index = stream * heads + head
            own = own - logsum_ref[0, :, index : index + 1]
            upper_now = upper[:, index * head_size : (index + 1) * head_size]
            with_u_t, with_w_t, upper_t = with_u.T, with_w.T, upper_now.T
            dquery = []
            for block in range(2):
                part = slice(block * half, (block + 1) * half)
                scores = block_scores(
                    with_u[part], with_w[part], keys_twice[part], relative_twice, half
                )
                scores = scores + own[part] + slope[part] * segment_row[:, part] + mask_ref[stream, block]
                chances = jnp.exp2(scores)
                dchance = dot_nt(upper_now[part], values[part])
                centre = jnp.sum(chances * dchance, -1, keepdims=True)
                dscore = (chances * (dchance - centre)).astype(jnp.bfloat16)
                dvalue_part = dot(upper_t[:, part], chances.astype(jnp.bfloat16))
                by_key = dot(dscore, keys_extra[part])
                turned = dot(dscore, mirror)
                wide = pltpu.roll(
                    jnp.concatenate([turned, jnp.zeros((half, half), jnp.float32)], -1),
                    0, 1, stride=1, stride_axis=0,
                ).astype(jnp.bfloat16)
                by_place = dot(wide, backward)
                dkey_part = dot(with_u_t[:, part], dscore)
                dkey_part = dkey_part[:head_size] + dkey_part[head_size:]
                drel_part = dot(with_w_t[:, part], wide)
                drel_ref[own_cols] += drel_part[:head_size] + drel_part[head_size:]
                if stream == 0:
                    dkeys_ref[own_cols, part] = dkey_part
                    dvalues_ref[own_cols, part] = dvalue_part
                else:
                    dkeys_ref[own_cols, part] += dkey_part
                    dvalues_ref[own_cols, part] += dvalue_part
                with_seg, total = by_key[:, head_size : head_size + 1], by_key[:, head_size + 1 : head_size + 2]
                seg_i = segment_col[part]
                seg_one = with_seg + seg_i * (total - 2.0 * with_seg)
                seg_zero = total - seg_one
                by_key = by_key[:, :head_size]
                by_segment = seg_zero * bias[3] + seg_one * bias[4]
                dquery.append((by_key + by_place + by_segment) * scale)
                for kind, term in enumerate(
                    (by_key, by_place, by_segment, seg_zero * with_c[part], seg_one * with_c[part])
                ):
                    heads_sums[kind] = heads_sums[kind] + jnp.sum(term, 0, keepdims=True)
            dcols_ref[:, cols(stream)] = jnp.concatenate(dquery, 0).astype(jnp.bfloat16)
        for kind in range(5):
            dhead_ref[kind : kind + 1, own_cols] += heads_sums[kind] * scale
    dcols_ref[:, 2 * width : 3 * width] = (dkeys_ref[...] * (1.0 / LOG2E)).astype(jnp.bfloat16).T
    dcols_ref[:, 3 * width :] = dvalues_ref[...].astype(jnp.bfloat16).T
    unroll = unroll_matrix(facts_row[3:4, :], length)
    joined = dot(unroll, dcols_ref[...]).astype(jnp.bfloat16)
    joined_t = joined.T
    content, query = content_ref[...], query_ref[...]
    dweight_ref[0] += dot(joined_t[:width], content) + dot(joined_t[width : 2 * width], query)
    dweight_ref[1] += dot(joined_t[2 * width : 3 * width], content)
    dweight_ref[2] += dot(joined_t[3 * width :], content)
    dinput_ref[0, here] = (
        dot_nt(joined[:, :width], weight_ref[0])
        + dot_nt(joined[:, 2 * width : 3 * width], weight_ref[1])
        + dot_nt(joined[:, 3 * width :], weight_ref[2])
    ).astype(jnp.bfloat16)
    dinput_ref[1, here] = dot_nt(joined[:, width : 2 * width], weight_ref[0]).astype(jnp.bfloat16)

    @pl.when(row == pl.num_programs(0) - 1)
    def _():
        drel = drel_ref[...] * (1.0 / LOG2E)
        high = drel.astype(jnp.bfloat16)
        low = (drel - high.astype(jnp.float32)).astype(jnp.bfloat16)
        dweight_ref[3] = dot(high, turned_ref[...]) + dot(low, turned_ref[...])
        tokens, pick = dinput_pieces[0].shape[1], dweight_pieces[0].shape[1]
        for k in range(group):
            part = pl.ds(pl.multiple_of((heads_here ^ k) * tokens, tokens), tokens)
            dinput_pieces[k][...] = dinput_ref[:, part]
        for kind in range(4):
            content_all[: weight_ref.shape[1], :width] = dweight_ref[kind].astype(jnp.bfloat16).T
            for k in range(parts):
                start = (dp_here ^ k) * pick if parts > 1 else 0
                dweight_pieces[k][kind] = content_all[pl.ds(pl.multiple_of(start, pick), pick), :width]


def attention_backward(
    content_pieces, query_pieces, weight_pieces, tables, head_bias, facts, proj, logsum, upper_pieces
):
    rows, length = facts[0].shape[0], facts[0].shape[2]
    group, parts = len(content_pieces), len(weight_pieces)
    own, depth = content_pieces[0].shape
    tokens = own * group
    width = weight_pieces[0].shape[-1]
    head_size = head_bias.shape[-1]
    half = length // 2
    full = lambda *shape: pl.BlockSpec(shape, lambda r: (0,) * len(shape))
    outside = pl.BlockSpec(memory_space=pl.ANY)
    results = pl.pallas_call(
        functools.partial(attention_backward_kernel, head_size, group, parts),
        grid=(rows,),
        in_specs=[outside] * (3 * group + parts)
        + [
            full(length, depth),
            full(length, depth),
            full(5, width),
            pl.BlockSpec((1, 8, length), lambda r: (r, 0, 0)),
            pl.BlockSpec((1, length, 8), lambda r: (r, 0, 0)),
            pl.BlockSpec((1, length, 4 * width), lambda r: (r, 0, 0)),
            pl.BlockSpec((1, length, 8), lambda r: (r, 0, 0)),
        ],
        out_specs=[full(2, own, depth)] * group
        + [full(*piece.shape) for piece in weight_pieces]
        + [full(5, width)],
        out_shape=[jax.ShapeDtypeStruct((2, own, depth), jnp.bfloat16)] * group
        + [jax.ShapeDtypeStruct(piece.shape, jnp.bfloat16) for piece in weight_pieces]
        + [jax.ShapeDtypeStruct((5, width), jnp.float32)],
        scratch_shapes=[
            pltpu.VMEM((tokens, depth), jnp.bfloat16),
            pltpu.VMEM((tokens, depth), jnp.bfloat16),
            pltpu.VMEM((4, depth, width), jnp.bfloat16),
            pltpu.VMEM((2, tokens, width), jnp.bfloat16),
            pltpu.VMEM((2, tokens, depth), jnp.bfloat16),
            pltpu.VMEM((4, width, depth), jnp.float32),
            pltpu.VMEM((length, width), jnp.bfloat16),
            pltpu.VMEM((length, width), jnp.bfloat16),
            pltpu.VMEM((2, 2, half, half), jnp.float32),
            pltpu.VMEM((width, length), jnp.float32),
            pltpu.VMEM((length, 4 * width), jnp.bfloat16),
            pltpu.VMEM((width, length), jnp.float32),
            pltpu.VMEM((width, length), jnp.float32),
            pltpu.SemaphoreType.DMA((3 * group + parts,)),
        ],
        compiler_params=pltpu.CompilerParams(vmem_limit_bytes=VMEM_LIMIT),
    )(
        *content_pieces, *query_pieces, *weight_pieces, *upper_pieces, *tables,
        head_bias.reshape(5, width), *facts, proj, logsum,
    )
    return results[:group], results[group : group + parts], results[-1]


def norm_parts(values):
    centred = values - jnp.mean(values, -1, keepdims=True)
    inverse = lax.rsqrt(jnp.mean(centred * centred, -1, keepdims=True) + NORM_EPSILON)
    return centred * inverse, inverse


def norm_back(upstream, normed, inverse, gain):
    scaled = upstream * gain
    first = jnp.mean(scaled, -1, keepdims=True)
    second = jnp.mean(scaled * normed, -1, keepdims=True)
    return inverse * (scaled - first - normed * second)


def column_sum(values):
    return jnp.sum(values, 0, keepdims=True)


def feed_kernel(group, *refs):
    mixed_pieces, refs = refs[:group], refs[group:]
    bias_pieces, refs = refs[:group], refs[group:]
    content_ref, query_ref, dcontent_ref, dquery_ref, norm_ref, up_hbm, down_hbm, out_hbm = refs[:8]
    content_out, query_out, dresid_ref, refs = refs[8], refs[9], refs[10], refs[11:]
    dmixed_pieces, refs = refs[:group], refs[group:]
    dup_hbm, ddown_hbm, dout_ref, dsmall_ref, refs = refs[0], refs[1], refs[2], refs[3], refs[4:]
    up_ref, down_ref, out_ref, hidden_ref, slope_ref, bias_ref = refs[:6]
    low_ref, low_t_ref, normed_ref, total_ref, sems = refs[6:]
    own, depth = content_ref.shape
    tokens = 2 * own
    here = lax.axis_index("heads")
    loads = [
        pltpu.make_async_copy(out_hbm.at[:, j], out_ref.at[j], sems.at[j]) for j in range(group)
    ]
    loads += [
        pltpu.make_async_copy(up_hbm.at[:, j], up_ref.at[j], sems.at[group + j]) for j in range(group)
    ]
    loads += [
        pltpu.make_async_copy(down_hbm.at[:, j], down_ref.at[j], sems.at[2 * group + j])
        for j in range(group)
    ]
    for load in loads:
        load.start()
    for k in range(group):
        bias_ref[here ^ k] = bias_pieces[k][...]
    gain_one, bias_one, bias_out, gain_two, bias_two = [norm_ref[i : i + 1] for i in range(5)]
    for load in loads[:group]:
        load.wait()
    hidden = up_ref.shape[-1]

    def out_block(k):
        return out_ref[here ^ k].reshape(depth, out_ref.shape[-1])

    total = jnp.concatenate([content_ref[...], query_ref[...]], 0).astype(jnp.float32)
    for k in range(group):
        total = total + dot_nt(mixed_pieces[k][...].reshape(tokens, -1), out_block(k))
    normed, inverse_one = norm_parts(total)
    normed_ref[...] = normed
    middle = normed * gain_one + bias_one
    low_ref[...] = middle.astype(jnp.bfloat16)
    low_t_ref[...] = low_ref[...].T
    total_ref[...] = middle + bias_out
    for load in loads[group:]:
        load.wait()

    def forward(j, carry):
        before = dot(low_ref[...], up_ref[j].reshape(depth, hidden)) + bias_ref[j]
        square = before * before
        bent = jnp.tanh(GELU_FACTOR * before * (1.0 + GELU_CUBIC * square))
        half_up = 0.5 * (1.0 + bent)
        hidden_now = (before * half_up).astype(jnp.bfloat16)
        slope_ref[j] = half_up + 0.5 * before * (1.0 - bent * bent) * GELU_FACTOR * (
            1.0 + 3.0 * GELU_CUBIC * square
        )
        hidden_ref[j] = hidden_now.reshape(hidden_ref.shape[1:])
        total_ref[...] += dot_nt(hidden_now, down_ref[j].reshape(depth, hidden))
        return carry

    lax.fori_loop(0, group, forward, 0)
    normed_two, inverse_two = norm_parts(total_ref[...])
    result = (normed_two * gain_two + bias_two).astype(jnp.bfloat16)
    content_out[...] = result[:own]
    query_out[...] = result[own:]
    upstream = jnp.concatenate([dcontent_ref[...], dquery_ref[...]], 0).astype(jnp.float32)
    dsmall_ref[group + 3 : group + 4] = column_sum(upstream * normed_two)
    dsmall_ref[group + 4 : group + 5] = column_sum(upstream)
    dfinal = norm_back(upstream, normed_two, inverse_two, gain_two)
    dsmall_ref[group + 2 : group + 3] = column_sum(dfinal)
    total_ref[...] = dfinal
    dlow = dfinal.astype(jnp.bfloat16)
    dlow_t = dlow.T

    def backward(j, carry):
        hidden_now = hidden_ref[j].reshape(tokens, hidden)
        down_now = down_ref[j].reshape(depth, hidden)
        dhidden = dot(dlow, down_now)
        down_ref[j] = dot(dlow_t, hidden_now).astype(jnp.bfloat16).reshape(down_ref.shape[1:])
        dbefore = (dhidden * slope_ref[j]).astype(jnp.bfloat16)
        dsmall_ref[pl.ds(j, 1)] = column_sum(dbefore.astype(jnp.float32))
        total_ref[...] += dot_nt(dbefore, up_ref[j].reshape(depth, hidden))
        up_ref[j] = dot(low_t_ref[...], dbefore).astype(jnp.bfloat16).reshape(up_ref.shape[1:])
        return carry

    lax.fori_loop(0, group, backward, 0)
    stores = [
        pltpu.make_async_copy(up_ref.at[j], dup_hbm.at[:, j], sems.at[group + j]) for j in range(group)
    ]
    stores += [
        pltpu.make_async_copy(down_ref.at[j], ddown_hbm.at[:, j], sems.at[2 * group + j])
        for j in range(group)
    ]
    for store in stores:
        store.start()
    dmiddle = total_ref[...]
    normed = normed_ref[...]
    dsmall_ref[group : group + 1] = column_sum(dmiddle * normed)
    dsmall_ref[group + 1 : group + 2] = column_sum(dmiddle)
    dresid = norm_back(dmiddle, normed, inverse_one, gain_one)
    dresid_ref[...] = dresid.reshape(dresid_ref.shape)
    dlow = dresid.astype(jnp.bfloat16)
    dlow_t = dlow.T
    for k in range(group):
        mixed = mixed_pieces[k][...].reshape(tokens, -1)
        dmixed_pieces[k][...] = (
            dot(dlow, out_block(k)).astype(jnp.bfloat16).reshape(dmixed_pieces[k].shape)
        )
        dout_ref[here ^ k] = dot(dlow_t, mixed).astype(jnp.bfloat16).reshape(dout_ref.shape[1:])
    dsmall_ref[group + 5 :] = jnp.zeros((dsmall_ref.shape[0] - group - 5, depth), jnp.float32)
    for store in stores:
        store.wait()


def feed_layer(mixed_pieces, bias_pieces, content, query, dcontent, dquery, norm_param, up, down, out):
    group = len(mixed_pieces)
    own, depth = content.shape
    parts, _, pick, hidden = up.shape
    width = out.shape[-1]
    inside = pl.BlockSpec(memory_space=pltpu.VMEM)
    outside = pl.BlockSpec(memory_space=pl.ANY)
    tokens = 2 * own
    results = pl.pallas_call(
        functools.partial(feed_kernel, group),
        in_specs=[inside] * (2 * group + 5) + [outside] * 3,
        out_specs=[inside] * (3 + group) + [outside, outside, inside, inside],
        out_shape=[
            jax.ShapeDtypeStruct((own, depth), jnp.bfloat16),
            jax.ShapeDtypeStruct((own, depth), jnp.bfloat16),
            jax.ShapeDtypeStruct((2, own, depth), jnp.float32),
        ]
        + [jax.ShapeDtypeStruct((2, own, width), jnp.bfloat16)] * group
        + [
            jax.ShapeDtypeStruct(up.shape, jnp.bfloat16),
            jax.ShapeDtypeStruct(down.shape, jnp.bfloat16),
            jax.ShapeDtypeStruct((group, parts, pick, width), jnp.bfloat16),
            jax.ShapeDtypeStruct((16, depth), jnp.float32),
        ],
        scratch_shapes=[
            pltpu.VMEM((group, parts, pick, hidden), jnp.bfloat16),
            pltpu.VMEM((group, parts, pick, hidden), jnp.bfloat16),
            pltpu.VMEM((group, parts, pick, width), jnp.bfloat16),
            pltpu.VMEM((group, tokens, hidden), jnp.bfloat16),
            pltpu.VMEM((group, tokens, hidden), jnp.float32),
            pltpu.VMEM((group, 1, hidden), jnp.float32),
            pltpu.VMEM((tokens, depth), jnp.bfloat16),
            pltpu.VMEM((depth, tokens), jnp.bfloat16),
            pltpu.VMEM((tokens, depth), jnp.float32),
            pltpu.VMEM((tokens, depth), jnp.float32),
            pltpu.SemaphoreType.DMA((3 * group,)),
        ],
        compiler_params=pltpu.CompilerParams(vmem_limit_bytes=VMEM_LIMIT),
    )(*mixed_pieces, *bias_pieces, content, query, dcontent, dquery, norm_param, up, down, out)
    return results[0], results[1], results[2], results[3 : 3 + group], results[3 + group :]


def exchange(value, axis, mask):
    return lax.ppermute(value, axis, [(i, i ^ mask) for i in range(lax.axis_size(axis))])


def total_over(value, axis):
    mask = 1
    while mask < lax.axis_size(axis):
        value = value + exchange(value, axis, mask)
        mask = 2 * mask
    return value


def gather_heads(own):
    far = exchange(own, "heads", 2)
    return [own, exchange(own, "heads", 1), far, exchange(far, "heads", 1)]


def spread(pieces):
    return [pieces[0]] + [exchange(pieces[k], "heads", k) for k in range(1, len(pieces))]


def by_pieces(pick):
    return lax.axis_size("dp") <= 8 and pick % 16 == 0


def gather_projection(own):
    if not by_pieces(own.shape[1]):
        return [lax.all_gather(own, "dp", axis=1, tiled=True)]
    pieces = {0: own}
    mask = lax.axis_size("dp") // 2
    while mask:
        for k in sorted(pieces):
            pieces[k ^ mask] = exchange(pieces[k], "dp", mask)
        mask = mask // 2
    return [pieces[k] for k in range(len(pieces))]


def reduce_projection(pieces):
    if len(pieces) == 1:
        return lax.psum_scatter(pieces[0], "dp", scatter_dimension=1, tiled=True).astype(jnp.float32)
    total = pieces[0].astype(jnp.float32)
    for k in range(1, len(pieces)):
        total = total + exchange(pieces[k], "dp", k).astype(jnp.float32)
    return total


def gather_all(own):
    dp, heads = lax.axis_size("dp"), lax.axis_size("heads")
    rows, columns = own.shape
    full = lax.all_gather(own, ("dp", "heads"), axis=0, tiled=False).reshape(dp, heads, rows, columns)
    if by_pieces(rows):
        return full
    return jnp.swapaxes(full, 0, 1).reshape(1, heads, dp * rows, columns)


def scatter_all(full):
    dp, heads = lax.axis_size("dp"), lax.axis_size("heads")
    parts, _, rows, columns = full.shape
    if parts == 1:
        rows = rows // dp
        full = jnp.swapaxes(full.reshape(heads, dp, rows, columns), 0, 1)
    full = full.reshape(dp * heads * rows, columns)
    return lax.psum_scatter(full, ("dp", "heads"), scatter_dimension=0, tiled=True).astype(jnp.float32)


def adam_step(master, first, second, gradient, factor, decayed):
    clipped = gradient * factor
    new_first = BETA_ONE * first + (1.0 - BETA_ONE) * clipped
    new_second = BETA_TWO * second + (1.0 - BETA_TWO) * clipped * clipped
    first_hat = new_first / (1.0 - BETA_ONE**STEP)
    second_hat = new_second / (1.0 - BETA_TWO**STEP)
    update = first_hat / (jnp.sqrt(second_hat) + ADAM_EPSILON)
    if decayed:
        update = update + WEIGHT_DECAY * master
        return (new_first, new_second, master - MATRIX_RATE * update)
    return (new_first, new_second, master - VECTOR_RATE * update)


def local(
    content_in,
    query_in,
    content_grad,
    query_grad,
    segment_ids,
    doc_lengths,
    factor_order,
    attn_proj,
    attn_proj_first,
    attn_proj_second,
    out_proj,
    out_proj_first,
    out_proj_second,
    up_proj,
    up_proj_first,
    up_proj_second,
    down_proj,
    down_proj_first,
    down_proj_second,
    head_bias,
    head_bias_first,
    head_bias_second,
    up_bias,
    up_bias_first,
    up_bias_second,
    norm_param,
    norm_param_first,
    norm_param_second,
):
    width = content_in.shape[1]
    length = segment_ids.shape[1]
    local_heads, head_size = (head_bias.shape[1], head_bias.shape[2])
    weight_pieces = gather_projection(attn_proj.astype(jnp.bfloat16))
    content_pieces = gather_heads(content_in)
    query_pieces = gather_heads(query_in)
    bias_pieces = [up_bias[None]] + [exchange(up_bias[None], "heads", k) for k in range(1, 4)]
    out_full = gather_all(out_proj.T.astype(jnp.bfloat16))
    up_full = gather_all(up_proj.astype(jnp.bfloat16))
    down_full = gather_all(down_proj.T.astype(jnp.bfloat16))
    table = position_table(length, width)
    tables = (jnp.asarray(table), jnp.asarray(table[::-1].copy()))
    facts = row_facts(segment_ids, doc_lengths, factor_order)
    proj, logsum, mixed_pieces = attention_forward(
        content_pieces, query_pieces, weight_pieces, tables[0], head_bias, facts
    )
    content_out, query_out, dresid, dmixed_pieces, (dup, ddown, dout, dsmall) = feed_layer(
        mixed_pieces, bias_pieces, content_in, query_in, content_grad, query_grad, norm_param,
        up_full, down_full, out_full,
    )
    dinput_pieces, dweight_pieces, dhead = attention_backward(
        content_pieces, query_pieces, weight_pieces, tables, head_bias, facts, proj, logsum,
        spread(dmixed_pieces),
    )
    small_sum = total_over(total_over(dsmall, "heads"), "dp")
    up_share = scatter_all(dup)
    down_share = scatter_all(ddown).T
    out_share = scatter_all(jnp.swapaxes(dout, 0, 1)).T
    proj_share = reduce_projection(dweight_pieces)
    head_grad = total_over(dhead, "dp").reshape(head_bias.shape)
    near = exchange(dinput_pieces[1], "heads", 1).astype(jnp.float32)
    far = exchange(dinput_pieces[3], "heads", 1).astype(jnp.float32)
    far = (dinput_pieces[2].astype(jnp.float32) + far).astype(jnp.bfloat16)
    far = exchange(far, "heads", 2).astype(jnp.float32)
    input_grad = dresid + dinput_pieces[0].astype(jnp.float32) + near + far
    heads_count, head_index = lax.axis_size("heads"), lax.axis_index("heads")
    bias_sum, norm_sum = small_sum[:heads_count], small_sum[heads_count : heads_count + 5]
    bias_grad = lax.dynamic_slice_in_dim(bias_sum, head_index, 1, 0)[0]
    dp_count = lax.axis_size("dp")
    local_squares = (
        jnp.sum(proj_share * proj_share)
        + jnp.sum(out_share * out_share)
        + jnp.sum(up_share * up_share)
        + jnp.sum(down_share * down_share)
        + jnp.sum(head_grad * head_grad) / dp_count
        + (jnp.sum(bias_sum * bias_sum) + jnp.sum(norm_sum * norm_sum)) / (dp_count * heads_count)
    )
    grad_norm = jnp.sqrt(total_over(total_over(local_squares.reshape(1, 1), "heads"), "dp"))[0, 0]
    factor = CLIP_NORM / jnp.maximum(grad_norm, CLIP_NORM)
    attn_first, attn_second, attn_new = adam_step(
        attn_proj, attn_proj_first, attn_proj_second, proj_share, factor, True
    )
    out_first, out_second, out_new = adam_step(
        out_proj, out_proj_first, out_proj_second, out_share, factor, True
    )
    up_first, up_second, up_new = adam_step(
        up_proj, up_proj_first, up_proj_second, up_share, factor, True
    )
    down_first, down_second, down_new = adam_step(
        down_proj, down_proj_first, down_proj_second, down_share, factor, True
    )
    head_first, head_second, head_new = adam_step(
        head_bias, head_bias_first, head_bias_second, head_grad, factor, False
    )
    bias_first, bias_second, bias_new = adam_step(
        up_bias, up_bias_first, up_bias_second, bias_grad, factor, False
    )
    norm_first, norm_second, norm_new = adam_step(
        norm_param, norm_param_first, norm_param_second, norm_sum, factor, False
    )
    return (
        content_out,
        query_out,
        input_grad[0],
        input_grad[1],
        grad_norm,
        proj_share,
        attn_first,
        attn_second,
        attn_new,
        out_share,
        out_first,
        out_second,
        out_new,
        up_share,
        up_first,
        up_second,
        up_new,
        down_share,
        down_first,
        down_second,
        down_new,
        head_grad,
        head_first,
        head_second,
        head_new,
        bias_grad,
        bias_first,
        bias_second,
        bias_new,
        norm_sum,
        norm_first,
        norm_second,
        norm_new,
    )


def solution(mesh):
    return jax.shard_map(
        local,
        mesh=mesh,
        in_specs=(
            P(("dp", "heads"), None),
            P(("dp", "heads"), None),
            P(("dp", "heads"), None),
            P(("dp", "heads"), None),
            P("dp", None),
            P("dp", None),
            P("dp", None),
            P(None, "dp", "heads"),
            P(None, "dp", "heads"),
            P(None, "dp", "heads"),
            P("heads", "dp"),
            P("heads", "dp"),
            P("heads", "dp"),
            P("dp", "heads"),
            P("dp", "heads"),
            P("dp", "heads"),
            P("heads", "dp"),
            P("heads", "dp"),
            P("heads", "dp"),
            P(None, "heads", None),
            P(None, "heads", None),
            P(None, "heads", None),
            P("heads"),
            P("heads"),
            P("heads"),
            P(),
            P(),
            P(),
        ),
        out_specs=(
            P(("dp", "heads"), None),
            P(("dp", "heads"), None),
            P(("dp", "heads"), None),
            P(("dp", "heads"), None),
            P(),
            P(None, "dp", "heads"),
            P(None, "dp", "heads"),
            P(None, "dp", "heads"),
            P(None, "dp", "heads"),
            P("heads", "dp"),
            P("heads", "dp"),
            P("heads", "dp"),
            P("heads", "dp"),
            P("dp", "heads"),
            P("dp", "heads"),
            P("dp", "heads"),
            P("dp", "heads"),
            P("heads", "dp"),
            P("heads", "dp"),
            P("heads", "dp"),
            P("heads", "dp"),
            P(None, "heads", None),
            P(None, "heads", None),
            P(None, "heads", None),
            P(None, "heads", None),
            P("heads"),
            P("heads"),
            P("heads"),
            P("heads"),
            P(),
            P(),
            P(),
            P(),
        ),
        check_vma=False,
    )
```

```python
import functools

import jax
import jax.numpy as jnp
import ml_dtypes
import numpy as np
from jax import lax
from jax.experimental import pallas as pl
from jax.experimental.pallas import tpu as pltpu
from jax.sharding import PartitionSpec as P

STEP = 10


NORM_EPSILON = 1e-05
CLIP_NORM = 1.0
MATRIX_RATE = 0.08
VECTOR_RATE = 0.5
BETA_ONE = 0.9
BETA_TWO = 0.999
ADAM_EPSILON = 1e-08
WEIGHT_DECAY = 0.01
MASKED_SCORE = -1e30
GELU_FACTOR = 0.7978845608028654
GELU_CUBIC = 0.044715
LOG2E = 1.4426950408889634
VMEM_LIMIT = 56 << 20


def position_table(length, width):
    distance = length // 2 - np.arange(length)
    frequency = 10000.0 ** (-np.arange(0, width, 2) / width)
    angles = distance[:, None] * frequency[None, :]
    return np.concatenate([np.sin(angles), np.cos(angles)], -1).astype(np.float32).astype(ml_dtypes.bfloat16)


def dot(left, right):
    return lax.dot_general(left, right, (((1,), (0,)), ((), ())), preferred_element_type=jnp.float32)


def dot_nt(left, right):
    return lax.dot_general(left, right, (((1,), (1,)), ((), ())), preferred_element_type=jnp.float32)


def split_pair(values):
    high = values.astype(jnp.bfloat16)
    low = (values - high.astype(jnp.float32)).astype(jnp.bfloat16)
    return jnp.concatenate([high, low], -1)


def row_facts(segment_ids, doc_lengths, factor_order):
    rows, length = segment_ids.shape
    places = jnp.arange(length, dtype=jnp.int32)
    counts = doc_lengths.shape[1]
    earlier = jnp.arange(counts)[:, None] <= jnp.arange(counts)[None, :]
    ends = jnp.sum(jnp.where(earlier[None], doc_lengths[:, :, None], 0), 1)
    start = jnp.sum(jnp.where(doc_lengths == length // 2, ends - doc_lengths, 0), -1)
    token = (places[None] + start[:, None]) % length
    document = jnp.sum((token[:, :, None] >= ends[:, None, :]).astype(jnp.int32), -1)
    ranking = jnp.sum(
        jnp.where(factor_order[:, :, None] == token[:, None, :], places[None, :, None], 0), 1
    )
    segment = jnp.sum(
        jnp.where(places[None, :, None] == token[:, None, :], segment_ids[:, :, None], 0), 1
    )
    base = document * length
    zero = jnp.zeros_like(base)
    facts = jnp.stack([base + ranking, base, segment, token, zero, zero, zero, zero], 1)
    facts = facts.astype(jnp.float32)
    return facts, jnp.swapaxes(facts, 1, 2)


def roll_matrix(token_col, length):
    lanes = lax.broadcasted_iota(jnp.int32, (length, length), 1).astype(jnp.float32)
    return jnp.where(token_col == lanes, 1.0, 0.0).astype(jnp.bfloat16)


def unroll_matrix(token_row, length):
    places = lax.broadcasted_iota(jnp.int32, (length, length), 0).astype(jnp.float32)
    return jnp.where(token_row == places, 1.0, 0.0).astype(jnp.bfloat16)


def write_masks(mask_ref, facts_row, facts_col, half):
    for block in range(2):
        part = slice(block * half, (block + 1) * half)
        code_i, base_i = facts_col[part, 0:1], facts_col[part, 1:2]
        code_j = facts_row[0:1, part]
        same = code_j >= base_i
        mask_ref[0, block] = jnp.where(same & (code_j <= code_i), 0.0, MASKED_SCORE)
        mask_ref[1, block] = jnp.where(same & (code_j < code_i), 0.0, MASKED_SCORE)


def query_sides(query, bias, segment_col, factor):
    wide = query.astype(jnp.float32)
    with_u = split_pair((wide + bias[0]) * factor)
    with_w = split_pair((wide + bias[1]) * factor)
    with_c = wide + bias[2]
    same = jnp.sum(with_c * bias[3], -1, keepdims=True) * factor
    change = jnp.sum(with_c * (bias[4] - bias[3]), -1, keepdims=True) * factor
    return with_u, with_w, with_c, same + change * segment_col, change * (1.0 - 2.0 * segment_col)


def block_scores(with_u, with_w, keys_twice, relative_twice, half):
    content = dot_nt(with_u, keys_twice)
    position = dot_nt(with_w, relative_twice)
    return content + pltpu.roll(position, half, 1, stride=1, stride_axis=0)[:, :half]


def start_pieces(pieces, place, sems, base):
    copies = []
    for index, piece in enumerate(pieces):
        copy = pltpu.make_async_copy(piece, place(index), sems.at[base + index])
        copy.start()
        copies.append(copy)
    return copies


def start_inputs(content_pieces, query_pieces, weight_pieces, content_ref, query_ref, weight_ref, sems):
    heads_here, dp_here = lax.axis_index("heads"), lax.axis_index("dp")
    tokens, rows = content_pieces[0].shape[0], weight_pieces[0].shape[1]

    def token_place(ref):
        return lambda k: ref.at[pl.ds(pl.multiple_of((heads_here ^ k) * tokens, tokens), tokens)]

    def weight_place(k):
        if len(weight_pieces) == 1:
            return weight_ref
        return weight_ref.at[:, pl.ds(pl.multiple_of((dp_here ^ k) * rows, rows), rows)]

    copies = start_pieces(weight_pieces, weight_place, sems, 0)
    base = len(weight_pieces)
    copies += start_pieces(content_pieces, token_place(content_ref), sems, base)
    base += len(content_pieces)
    return copies + start_pieces(query_pieces, token_place(query_ref), sems, base)


def greet(axis, masks):
    barrier = pltpu.get_barrier_semaphore()
    for mask in masks:
        pl.semaphore_signal(
            barrier, inc=1, device_id={axis: lax.axis_index(axis) ^ mask}, device_id_type=pl.DeviceIdType.MESH
        )
    pl.semaphore_wait(barrier, len(masks))


def send_pieces(full_ref, pieces, send_sems, recv_sems, base):
    tokens = pieces[0].shape[1]
    here = lax.axis_index("heads")
    copies = []
    for k, piece in enumerate(pieces):
        part = full_ref.at[:, pl.ds(pl.multiple_of((here ^ k) * tokens, tokens), tokens)]
        if k == 0:
            copy = pltpu.make_async_copy(part, piece, send_sems.at[base])
        else:
            copy = pltpu.make_async_remote_copy(
                part, piece, send_sems.at[base + k], recv_sems.at[k],
                device_id={"heads": here ^ k}, device_id_type=pl.DeviceIdType.MESH,
            )
        copy.start()
        copies.append(copy)
    for copy in copies:
        copy.wait()


def attention_forward_kernel(head_size, group, parts, *refs):
    content_pieces, query_pieces, refs = refs[:group], refs[group : 2 * group], refs[2 * group :]
    weight_pieces, refs = refs[:parts], refs[parts:]
    table_ref, bias_ref, row_ref, col_ref, proj_ref, logsum_ref = refs[:6]
    mixed_pieces, refs = refs[6 : 6 + group], refs[6 + group :]
    content_all, query_all, weight_ref, mixed_ref, relative_ref, mask_ref, sems, recv_sems = refs
    length = row_ref.shape[2]
    half = length // 2
    width = weight_ref.shape[-1]
    heads = width // head_size
    factor = head_size ** (-0.5) * LOG2E
    row = pl.program_id(0)

    @pl.when(row == 0)
    def _():
        copies = start_inputs(
            content_pieces, query_pieces, weight_pieces, content_all, query_all, weight_ref, sems
        )
        greet("heads", range(1, group))
        for copy in copies:
            copy.wait()
        relative_ref[...] = dot(table_ref[...], weight_ref[3]).astype(jnp.bfloat16)

    here = pl.ds(pl.multiple_of(row * length, length), length)
    content_ref, query_ref = content_all.at[here], query_all.at[here]

    facts_row, facts_col = row_ref[0], col_ref[0]
    write_masks(mask_ref, facts_row, facts_col, half)
    roll = roll_matrix(facts_col[:, 3:4], length)
    unroll = unroll_matrix(facts_row[3:4, :], length)
    content, query = content_ref[...], query_ref[...]
    joined = jnp.concatenate(
        [
            dot(content, weight_ref[0]).astype(jnp.bfloat16),
            dot(content, weight_ref[1]).astype(jnp.bfloat16),
            dot(content, weight_ref[2]).astype(jnp.bfloat16),
            dot(query, weight_ref[0]).astype(jnp.bfloat16),
        ],
        -1,
    )
    proj_ref[0] = dot(roll, joined).astype(jnp.bfloat16)
    segment_col, segment_row = facts_col[:, 2:3], facts_row[2:3, :]
    mixed = [[None] * heads, [None] * heads]
    for head in range(heads):
        cols = lambda kind: slice(kind * width + head * head_size, kind * width + (head + 1) * head_size)
        bias = [bias_ref[kind : kind + 1, head * head_size : (head + 1) * head_size] for kind in range(5)]
        keys, values = proj_ref[0, :, cols(1)], proj_ref[0, :, cols(2)]
        keys_twice = jnp.concatenate([keys, keys], -1)
        relative = relative_ref[:, head * head_size : (head + 1) * head_size]
        relative_twice = jnp.concatenate([relative, relative], -1)
        for stream in range(2):
            with_u, with_w, _, own, slope = query_sides(
                proj_ref[0, :, cols(3 * stream)], bias, segment_col, factor
            )
            pieces = []
            for block in range(2):
                part = slice(block * half, (block + 1) * half)
                scores = block_scores(
                    with_u[part], with_w[part], keys_twice[part], relative_twice, half
                )
                scores = scores + own[part] + slope[part] * segment_row[:, part] + mask_ref[stream, block]
                highest = jnp.maximum(jnp.max(scores, -1, keepdims=True), 0.0)
                weights = jnp.exp2(scores - highest)
                totals = jnp.exp2(-highest) + jnp.sum(weights, -1, keepdims=True)
                pieces.append(dot(weights.astype(jnp.bfloat16), values[part]) / totals)
                index = stream * heads + head
                logsum_ref[0, part, index : index + 1] = highest + jnp.log2(totals)
            mixed[stream][head] = jnp.concatenate(pieces, 0).astype(jnp.bfloat16)
    both = jnp.concatenate(mixed[0] + mixed[1], -1)
    both = dot(unroll, both).astype(jnp.bfloat16)
    mixed_ref[0, here] = both[:, :width]
    mixed_ref[1, here] = both[:, width:]

    @pl.when(row == pl.num_programs(0) - 1)
    def _():
        send_pieces(mixed_ref, mixed_pieces, sems, recv_sems, 2 * group + parts)


def attention_forward(content_pieces, query_pieces, weight_pieces, table, head_bias, facts):
    rows, length = facts[0].shape[0], facts[0].shape[2]
    group, parts = len(content_pieces), len(weight_pieces)
    own, depth = content_pieces[0].shape
    tokens = own * group
    width = weight_pieces[0].shape[-1]
    head_size = head_bias.shape[-1]
    half = length // 2
    full = lambda *shape: pl.BlockSpec(shape, lambda r: (0,) * len(shape))
    outside = pl.BlockSpec(memory_space=pl.ANY)
    results = pl.pallas_call(
        functools.partial(attention_forward_kernel, head_size, group, parts),
        grid=(rows,),
        in_specs=[outside] * (2 * group + parts)
        + [
            full(length, depth),
            full(5, width),
            pl.BlockSpec((1, 8, length), lambda r: (r, 0, 0)),
            pl.BlockSpec((1, length, 8), lambda r: (r, 0, 0)),
        ],
        out_specs=[
            pl.BlockSpec((1, length, 4 * width), lambda r: (r, 0, 0)),
            pl.BlockSpec((1, length, 8), lambda r: (r, 0, 0)),
        ]
        + [outside] * group,
        out_shape=[
            jax.ShapeDtypeStruct((rows, length, 4 * width), jnp.bfloat16),
            jax.ShapeDtypeStruct((rows, length, 8), jnp.float32),
        ]
        + [jax.ShapeDtypeStruct((2, own, width), jnp.bfloat16)] * group,
        scratch_shapes=[
            pltpu.VMEM((tokens, depth), jnp.bfloat16),
            pltpu.VMEM((tokens, depth), jnp.bfloat16),
            pltpu.VMEM((4, depth, width), jnp.bfloat16),
            pltpu.VMEM((2, tokens, width), jnp.bfloat16),
            pltpu.VMEM((length, width), jnp.bfloat16),
            pltpu.VMEM((2, 2, half, half), jnp.float32),
            pltpu.SemaphoreType.DMA((3 * group + parts,)),
            pltpu.SemaphoreType.DMA((group,)),
        ],
        compiler_params=pltpu.CompilerParams(
            vmem_limit_bytes=VMEM_LIMIT, collective_id=0, has_side_effects=True
        ),
    )(*content_pieces, *query_pieces, *weight_pieces, table, head_bias.reshape(5, width), *facts)
    return results[0], results[1], results[2:]


class Links:
    def __init__(self, send_sems, recv_sems):
        self.send_sems, self.recv_sems, self.used = send_sems, recv_sems, 0

    def push(self, source, place, axis, distance):
        index = self.used
        self.used = index + 1
        return pltpu.make_async_remote_copy(
            source, place, self.send_sems.at[index], self.recv_sems.at[index],
            device_id={axis: lax.axis_index(axis) ^ distance}, device_id_type=pl.DeviceIdType.MESH,
        )


def add_planes(place, first, second):
    def one(z, carry):
        place[z] = (first(z).astype(jnp.float32) + second[z].astype(jnp.float32)).astype(place.dtype)
        return carry

    lax.fori_loop(0, place.shape[0], one, 0)


class Scatter:
    def __init__(self, links, sems, sem, source, order, refs):
        self.kept, self.got, self.got_two, self.got_last = refs
        self.order = order
        heads_here, dp_here = lax.axis_index("heads"), lax.axis_index("dp")
        x, y, z = heads_here >> 1, dp_here & 1, dp_here >> 1
        if order == "xy":
            own, other, first, second, self.mine = source.at[:, :, x], source.at[:, :, 1 - x], ("heads", 2), ("dp", 1), y
        else:
            own, other, first, second, self.mine = source.at[:, y], source.at[:, 1 - y], ("dp", 1), ("heads", 2), x
        self.load = pltpu.make_async_copy(own, self.kept, sems.at[sem])
        self.copy = links.push(other, self.got, *first)
        self.copy_two = links.push(self.kept.at[:, 1 - self.mine], self.got_two, *second)
        self.place = z
        self.copies_last = [
            links.push(self.got_two.at[z ^ m], self.got_last.at[m - 1], "dp", 2 * m)
            for m in range(1, source.shape[0])
        ]

    def begin(self):
        self.load.start()
        self.copy.start()

    def second(self):
        self.load.wait()
        self.copy.wait()
        add_planes(self.kept, lambda z: self.kept[z], self.got)
        self.copy_two.start()

    def third(self):
        self.copy_two.wait()
        add_planes(self.got_two, lambda z: self.kept[z, self.mine], self.got_two)
        for copy in self.copies_last:
            copy.start()

    def last(self):
        for copy in self.copies_last:
            copy.wait()
        total = self.got_two[self.place].astype(jnp.float32)
        for index in range(self.got_last.shape[0]):
            total = total + self.got_last[index].astype(jnp.float32)
        return total


def square_sum(values):
    return jnp.sum(jnp.sum(values * values, -1, keepdims=True), 0, keepdims=True)


def attention_backward_kernel(head_size, group, parts, fast, *refs):
    content_pieces, query_pieces, refs = refs[:group], refs[group : 2 * group], refs[2 * group :]
    weight_pieces, refs = refs[:parts], refs[parts:]
    upper_pieces, dresid_hbm, refs = refs[:group], refs[group], refs[group + 1 :]
    table_ref, turned_ref, bias_ref, row_ref, col_ref, proj_ref, logsum_ref = refs[:7]
    sources, small_ref, refs = refs[7:10], refs[10], refs[11:]
    outputs, refs = refs[:9] if fast else refs[:4], refs[9:] if fast else refs[4:]
    content_grad_ref, query_grad_ref, dhead_ref = outputs[:3]
    content_all, query_all, weight_ref, upper_all, dinput_ref, dweight_ref = refs[:6]
    relative_ref, backward_ref, mask_ref, drel_ref, dcols_ref, dkeys_ref, dvalues_ref = refs[6:13]
    dwide_ref, near_ref, cross_ref, far_ref, dresid_ref, dhead_own, refs = *refs[13:19], refs[19:]
    sems, send_sems, recv_sems, refs = *refs[:3], refs[3:]
    rows, length = row_ref.shape[0], row_ref.shape[2]
    half = length // 2
    depth, width = weight_ref.shape[1:]
    heads = width // head_size
    scale = head_size ** (-0.5)
    factor = scale * LOG2E
    heads_here, dp_here = lax.axis_index("heads"), lax.axis_index("dp")
    chip = heads_here >> 1
    tokens = upper_pieces[0].shape[1]
    links = Links(send_sems, recv_sems)

    def token_part(k):
        return pl.ds(pl.multiple_of((heads_here ^ k) * tokens, tokens), tokens)

    copies = start_inputs(
        content_pieces, query_pieces, weight_pieces, content_all, query_all, weight_ref, sems
    )
    copies += start_pieces([upper_pieces[0]], lambda k: upper_all.at[:, token_part(0)], sems, 2 * group + parts)
    dresid_copy = pltpu.make_async_copy(dresid_hbm, dresid_ref, sems.at[2 * group + parts + 1])
    dresid_copy.start()
    barrier = pltpu.get_barrier_semaphore()
    peers = [("heads", k) for k in range(1, group)] + [("dp", k) for k in range(1, parts)]
    for axis, k in peers:
        pl.semaphore_signal(
            barrier, inc=1, device_id={axis: lax.axis_index(axis) ^ k}, device_id_type=pl.DeviceIdType.MESH
        )
    pl.semaphore_wait(barrier, len(peers))
    upper_copies = [
        links.push(upper_pieces[k], upper_all.at[:, token_part(0)], "heads", k) for k in range(1, group)
    ]
    for copy in upper_copies:
        copy.start()
    if fast:
        scatters = [
            Scatter(links, sems, 2 * group + parts + 2 + n, sources[n], order, refs[4 * n : 4 * n + 4])
            for n, order in enumerate(("xy", "yx", "yx"))
        ]
        small_got, small_more, small_mid, dweight_got, dweight_more, head_got, tile_ref, tile_got, tile_more = refs[12:]
        for scatter in scatters:
            scatter.begin()
        small_first = [links.push(small_ref, small_got.at[heads_here], "heads", k) for k in range(1, group)]
        for copy in small_first:
            copy.start()
        small_got[heads_here] = small_ref[...]
        small_second = [links.push(small_mid, small_more.at[dp_here], "dp", k) for k in range(1, parts)]
    for copy in copies:
        copy.wait()
    upper_copies[0].wait()
    relative_ref[...] = dot(table_ref[...], weight_ref[3]).astype(jnp.bfloat16)
    backward_ref[...] = dot(turned_ref[...], weight_ref[3]).astype(jnp.bfloat16)
    drel_ref[...] = jnp.zeros_like(drel_ref)
    dweight_ref[...] = jnp.zeros_like(dweight_ref)
    dhead_own[...] = jnp.zeros_like(dhead_own)

    def after(step, place, body):
        if fast:
            @pl.when(step == place)
            def _():
                body()

    def small_middle():
        for copy in small_first:
            copy.wait()
        total = small_got[0]
        for k in range(1, group):
            total = total + small_got[k]
        small_mid[...] = total
        small_more[dp_here] = total
        for copy in small_second:
            copy.start()

    def one_row(step, carry):
        row = jnp.where(step == 0, 0, rows - step)
        row = jnp.where(chip == 0, row, rows - 1 - row)

        @pl.when(step == 1)
        def _():
            for copy in upper_copies[1:]:
                copy.wait()

        row_part(step, row)
        return carry

    def row_part(step, row):
        here = pl.ds(pl.multiple_of(row * length, length), length)
        content_ref, query_ref = content_all.at[here], query_all.at[here]
        facts_row, facts_col = row_ref[row], col_ref[row]
        write_masks(mask_ref, facts_row, facts_col, half)
        roll = roll_matrix(facts_col[:, 3:4], length)
        upper = dot(roll, jnp.concatenate([upper_all[0, here], upper_all[1, here]], -1)).astype(jnp.bfloat16)
        segment_col, segment_row = facts_col[:, 2:3], facts_row[2:3, :]
        down = lax.broadcasted_iota(jnp.int32, (half, half), 0)
        along = lax.broadcasted_iota(jnp.int32, (half, half), 1)
        mirror = jnp.where(down + along == half - 1, 1.0, 0.0).astype(jnp.bfloat16)
        lane = lax.broadcasted_iota(jnp.int32, (length, head_size), 1)
        extra = jnp.where(lane == 0, segment_col, jnp.where(lane == 1, 1.0, 0.0)).astype(jnp.bfloat16)
        for head in range(heads):
            own_cols = slice(head * head_size, (head + 1) * head_size)
            cols = lambda kind: slice(kind * width + head * head_size, kind * width + (head + 1) * head_size)
            bias = [bias_ref[kind : kind + 1, own_cols] for kind in range(5)]
            keys, values = proj_ref[row, :, cols(1)], proj_ref[row, :, cols(2)]
            keys_twice = jnp.concatenate([keys, keys], -1)
            keys_extra = jnp.concatenate([keys, extra], -1)
            relative = relative_ref[:, own_cols]
            relative_twice = jnp.concatenate([relative, relative], -1)
            backward = backward_ref[:, own_cols]
            heads_sums = [jnp.zeros((1, head_size), jnp.float32) for _ in range(5)]
            for stream in range(2):
                with_u, with_w, with_c, own, slope = query_sides(
                    proj_ref[row, :, cols(3 * stream)], bias, segment_col, factor
                )
                index = stream * heads + head
                own = own - logsum_ref[row, :, index : index + 1]
                upper_now = upper[:, index * head_size : (index + 1) * head_size]
                with_u_t, with_w_t, upper_t = with_u.T, with_w.T, upper_now.T
                dquery = []
                for block in range(2):
                    part = slice(block * half, (block + 1) * half)
                    scores = block_scores(
                        with_u[part], with_w[part], keys_twice[part], relative_twice, half
                    )
                    scores = scores + own[part] + slope[part] * segment_row[:, part] + mask_ref[stream, block]
                    chances = jnp.exp2(scores)
                    dchance = dot_nt(upper_now[part], values[part])
                    centre = jnp.sum(chances * dchance, -1, keepdims=True)
                    dscore = (chances * (dchance - centre)).astype(jnp.bfloat16)
                    dvalue_part = dot(upper_t[:, part], chances.astype(jnp.bfloat16))
                    by_key = dot(dscore, keys_extra[part])
                    turned = dot(dscore, mirror)
                    wide = pltpu.roll(
                        jnp.concatenate([turned, jnp.zeros((half, half), jnp.float32)], -1),
                        0, 1, stride=1, stride_axis=0,
                    ).astype(jnp.bfloat16)
                    by_place = dot(wide, backward)
                    dkey_part = dot(with_u_t[:, part], dscore)
                    dkey_part = dkey_part[:head_size] + dkey_part[head_size:]
                    drel_part = dot(with_w_t[:, part], wide)
                    drel_ref[own_cols] += drel_part[:head_size] + drel_part[head_size:]
                    if stream == 0:
                        dkeys_ref[own_cols, part] = dkey_part
                        dvalues_ref[own_cols, part] = dvalue_part
                    else:
                        dkeys_ref[own_cols, part] += dkey_part
                        dvalues_ref[own_cols, part] += dvalue_part
                    with_seg, total = by_key[:, head_size : head_size + 1], by_key[:, head_size + 1 : head_size + 2]
                    seg_i = segment_col[part]
                    seg_one = with_seg + seg_i * (total - 2.0 * with_seg)
                    seg_zero = total - seg_one
                    by_key = by_key[:, :head_size]
                    by_segment = seg_zero * bias[3] + seg_one * bias[4]
                    dquery.append((by_key + by_place + by_segment) * scale)
                    for kind, term in enumerate(
                        (by_key, by_place, by_segment, seg_zero * with_c[part], seg_one * with_c[part])
                    ):
                        heads_sums[kind] = heads_sums[kind] + jnp.sum(term, 0, keepdims=True)
                dcols_ref[:, cols(stream)] = jnp.concatenate(dquery, 0).astype(jnp.bfloat16)
            for kind in range(5):
                dhead_own[kind : kind + 1, own_cols] += heads_sums[kind] * scale
            if fast and head == 0:
                after(step, 1, small_middle)
            if fast and head == heads - 1:
                after(step, 1, lambda: [scatter.second() for scatter in scatters[1:]])
                after(step, 2, lambda: [scatter.third() for scatter in scatters])
        dcols_ref[:, 2 * width : 3 * width] = (dkeys_ref[...] * (1.0 / LOG2E)).astype(jnp.bfloat16).T
        dcols_ref[:, 3 * width :] = dvalues_ref[...].astype(jnp.bfloat16).T
        unroll = unroll_matrix(facts_row[3:4, :], length)
        joined = dot(unroll, dcols_ref[...]).astype(jnp.bfloat16)
        joined_t = joined.T
        content, query = content_ref[...], query_ref[...]
        dweight_ref[0] += dot(joined_t[:width], content) + dot(joined_t[width : 2 * width], query)
        dweight_ref[1] += dot(joined_t[2 * width : 3 * width], content)
        dweight_ref[2] += dot(joined_t[3 * width :], content)
        dinput_ref[0, here] = (
            dot_nt(joined[:, :width], weight_ref[0])
            + dot_nt(joined[:, 2 * width : 3 * width], weight_ref[1])
            + dot_nt(joined[:, 3 * width :], weight_ref[2])
        ).astype(jnp.bfloat16)
        dinput_ref[1, here] = dot_nt(joined[:, width : 2 * width], weight_ref[0]).astype(jnp.bfloat16)
        if fast:
            after(step, 1, scatters[0].second)

    lax.fori_loop(0, rows, one_row, 0)
    drel = drel_ref[...] * (1.0 / LOG2E)
    high = drel.astype(jnp.bfloat16)
    low = (drel - high.astype(jnp.float32)).astype(jnp.bfloat16)
    dweight_ref[3] = dot(high, turned_ref[...]) + dot(low, turned_ref[...])
    cross = [
        links.push(dinput_ref.at[n, token_part(3)], cross_ref.at[n], "heads", 1) for n in range(2)
    ]
    near = [links.push(dinput_ref.at[n, token_part(1)], near_ref.at[n], "heads", 1) for n in range(2)]
    far = [links.push(cross_ref.at[n], far_ref.at[n], "heads", 2) for n in range(2)]
    for copy in cross + near:
        copy.start()
    for kind in range(4):
        turned = dweight_ref[kind].astype(jnp.bfloat16).T
        dwide_ref[kind] = turned.reshape(dwide_ref.shape[1:])
    if fast:
        place_y, place_z = dp_here & 1, dp_here >> 1
        dweight_first = links.push(dwide_ref.at[:, :, 1 - place_y], dweight_got, "dp", 1)
        dweight_first.start()
        head_copies = [links.push(dhead_own, head_got.at[dp_here], "dp", k) for k in range(1, parts)]
        for copy in head_copies:
            copy.start()
        head_got[dp_here] = dhead_own[...]
    for n in range(2):
        cross[n].wait()
        both = cross_ref[n].astype(jnp.float32) + dinput_ref[n, token_part(2)].astype(jnp.float32)
        cross_ref[n] = both.astype(jnp.bfloat16)
        far[n].start()
    if fast:
        dweight_first.wait()
        dweight_second = []
        for kind in range(4):
            dweight_got[kind] = (
                dweight_got[kind].astype(jnp.float32) + dwide_ref[kind, :, place_y].astype(jnp.float32)
            ).astype(jnp.bfloat16)
        for m in range(1, 4):
            dweight_second.append(
                links.push(dweight_got.at[:, place_z ^ m], dweight_more.at[m - 1], "dp", 2 * m)
            )
            dweight_second[-1].start()
        up_share, down_share, out_share, proj_share, small_sum, norm_ref = outputs[3:]
        squares = jnp.zeros((1, 1), jnp.float32)
        for copy in small_second:
            copy.wait()
        total = small_more[0]
        for k in range(1, parts):
            total = total + small_more[k]
        small_sum[...] = total
        squares = squares + square_sum(total) / (group * parts)
        for copy in head_copies:
            copy.wait()
        total = head_got[0]
        for k in range(1, parts):
            total = total + head_got[k]
        dhead_ref[...] = total
        squares = squares + square_sum(total) / parts
        for scatter, share in zip(scatters, (up_share, down_share, out_share)):
            share[...] = scatter.last()
            squares = squares + square_sum(share[...])
        for copy in dweight_second:
            copy.wait()
        for kind in range(4):
            total = dweight_got[kind, place_z].astype(jnp.float32)
            for m in range(1, 4):
                total = total + dweight_more[m - 1, kind].astype(jnp.float32)
            proj_share[kind] = total
            squares = squares + square_sum(total)
        tile_ref[...] = jnp.broadcast_to(squares, tile_ref.shape)
        tile_got[heads_here] = tile_ref[...]
        tile_first = [links.push(tile_ref, tile_got.at[heads_here], "heads", k) for k in range(1, group)]
        for copy in tile_first:
            copy.start()
    else:
        dhead_ref[...] = dhead_own[...]
        outputs[3][...] = dwide_ref[...]
    if fast:
        for copy in tile_first:
            copy.wait()
        total = tile_got[0]
        for k in range(1, group):
            total = total + tile_got[k]
        tile_more[dp_here] = total
        tile_ref[...] = total
        tile_second = [links.push(tile_ref, tile_more.at[dp_here], "dp", k) for k in range(1, parts)]
        for copy in tile_second:
            copy.start()
    dresid_copy.wait()
    for n, place in enumerate((content_grad_ref, query_grad_ref)):
        near[n].wait()
        far[n].wait()
        place[...] = (
            dresid_ref[n]
            + dinput_ref[n, token_part(0)].astype(jnp.float32)
            + near_ref[n].astype(jnp.float32)
            + far_ref[n].astype(jnp.float32)
        )
    if fast:
        for copy in tile_second:
            copy.wait()
        total = tile_more[0]
        for k in range(1, parts):
            total = total + tile_more[k]
        norm_ref[...] = jnp.sqrt(total)


def attention_backward(
    content_pieces, query_pieces, weight_pieces, tables, head_bias, facts, proj, logsum, upper_pieces,
    dresid, gradients, small,
):
    rows, length = facts[0].shape[0], facts[0].shape[2]
    group, parts = len(content_pieces), len(weight_pieces)
    fast = parts > 1
    own, depth = content_pieces[0].shape
    tokens = own * group
    pick, width = weight_pieces[0].shape[1:]
    head_size = head_bias.shape[-1]
    half = length // 2
    inside = pl.BlockSpec(memory_space=pltpu.VMEM)
    outside = pl.BlockSpec(memory_space=pl.ANY)
    bfloat, float32 = jnp.bfloat16, jnp.float32
    out_shape = [
        jax.ShapeDtypeStruct((own, depth), float32),
        jax.ShapeDtypeStruct((own, depth), float32),
        jax.ShapeDtypeStruct((8, width), float32),
    ]
    lanes = max(2 * parts, 2)
    wide_shape = (4, parts // 2, 2, pick, width) if fast else (4, pick, width)
    scratch = [
        pltpu.VMEM((tokens, depth), bfloat),
        pltpu.VMEM((tokens, depth), bfloat),
        pltpu.VMEM((4, depth, width), bfloat),
        pltpu.VMEM((2, tokens, width), bfloat),
        pltpu.VMEM((2, tokens, depth), bfloat),
        pltpu.VMEM((4, width, depth), float32),
        pltpu.VMEM((length, width), bfloat),
        pltpu.VMEM((length, width), bfloat),
        pltpu.VMEM((2, 2, half, half), float32),
        pltpu.VMEM((width, length), float32),
        pltpu.VMEM((length, 4 * width), bfloat),
        pltpu.VMEM((width, length), float32),
        pltpu.VMEM((width, length), float32),
        pltpu.VMEM(wide_shape, bfloat),
        pltpu.VMEM((2, own, depth), bfloat),
        pltpu.VMEM((2, own, depth), bfloat),
        pltpu.VMEM((2, own, depth), bfloat),
        pltpu.VMEM((2, own, depth), float32),
        pltpu.VMEM((8, width), float32),
        pltpu.SemaphoreType.DMA((2 * group + parts + 5,)),
        pltpu.SemaphoreType.DMA((64,)),
        pltpu.SemaphoreType.DMA((64,)),
    ]
    if fast:
        planes = parts // 2
        columns = [gradient.shape[-1] for gradient in gradients]
        out_shape += [jax.ShapeDtypeStruct((pick, c), float32) for c in columns]
        out_shape += [
            jax.ShapeDtypeStruct((4, pick, width), float32),
            jax.ShapeDtypeStruct(small.shape, float32),
            jax.ShapeDtypeStruct((8, 128), float32),
        ]
        gradients = [g.reshape(planes, 2, group // 2, pick, g.shape[-1]) for g in gradients]
        for c in columns:
            scratch += [
                pltpu.VMEM((planes, 2, pick, c), bfloat),
                pltpu.VMEM((planes, 2, pick, c), bfloat),
                pltpu.VMEM((planes, pick, c), bfloat),
                pltpu.VMEM((planes - 1, pick, c), bfloat),
            ]
        scratch += [
            pltpu.VMEM((group,) + small.shape, float32),
            pltpu.VMEM((parts,) + small.shape, float32),
            pltpu.VMEM(small.shape, float32),
            pltpu.VMEM((4, planes, pick, width), bfloat),
            pltpu.VMEM((planes - 1, 4, pick, width), bfloat),
            pltpu.VMEM((parts, 8, width), float32),
            pltpu.VMEM((8, 128), float32),
            pltpu.VMEM((group, 8, 128), float32),
            pltpu.VMEM((parts, 8, 128), float32),
        ]
    else:
        out_shape += [jax.ShapeDtypeStruct(wide_shape, bfloat)]
    return pl.pallas_call(
        functools.partial(attention_backward_kernel, head_size, group, parts, fast),
        in_specs=[outside] * (3 * group + parts + 1) + [inside] * 7 + [outside] * 3 + [inside],
        out_specs=[inside] * len(out_shape),
        out_shape=out_shape,
        scratch_shapes=scratch,
        compiler_params=pltpu.CompilerParams(
            vmem_limit_bytes=VMEM_LIMIT, collective_id=2, has_side_effects=True
        ),
    )(
        *content_pieces, *query_pieces, *weight_pieces, *upper_pieces, dresid, *tables,
        head_bias.reshape(5, width), *facts, proj, logsum, *gradients, small,
    )


def norm_parts(values):
    centred = values - jnp.mean(values, -1, keepdims=True)
    inverse = lax.rsqrt(jnp.mean(centred * centred, -1, keepdims=True) + NORM_EPSILON)
    return centred * inverse, inverse


def norm_back(upstream, normed, inverse, gain):
    scaled = upstream * gain
    first = jnp.mean(scaled, -1, keepdims=True)
    second = jnp.mean(scaled * normed, -1, keepdims=True)
    return inverse * (scaled - first - normed * second)


def column_sum(values):
    return jnp.sum(values, 0, keepdims=True)


def feed_kernel(group, *refs):
    mixed_pieces, refs = refs[:group], refs[group:]
    bias_pieces, refs = refs[:group], refs[group:]
    content_ref, query_ref, dcontent_ref, dquery_ref, norm_ref, up_hbm, down_hbm, out_hbm = refs[:8]
    content_out, query_out, dresid_ref, refs = refs[8], refs[9], refs[10], refs[11:]
    dmixed_pieces, refs = refs[:group], refs[group:]
    dup_hbm, ddown_hbm, dout_ref, dsmall_ref, refs = refs[0], refs[1], refs[2], refs[3], refs[4:]
    up_ref, down_ref, out_ref, hidden_ref, slope_ref, bias_ref = refs[:6]
    low_ref, low_t_ref, normed_ref, total_ref, up_got, down_got, out_got, out_sent = refs[6:14]
    sems, send_sems, recv_sems = refs[14:]
    own, depth = content_ref.shape
    tokens = 2 * own
    here = lax.axis_index("heads")
    core = here & 1
    chips = group // 2
    loads = [
        pltpu.make_async_copy(out_hbm.at[:, j], out_ref.at[j], sems.at[j]) for j in range(group)
    ]
    loads += [
        pltpu.make_async_copy(up_hbm.at[:, j], up_ref.at[j], sems.at[group + j]) for j in range(group)
    ]
    loads += [
        pltpu.make_async_copy(down_hbm.at[:, j], down_ref.at[j], sems.at[2 * group + j])
        for j in range(group)
    ]
    for load in loads:
        load.start()
    greet("heads", [1])
    for k in range(group):
        bias_ref[here ^ k] = bias_pieces[k][...]
    gain_one, bias_one, bias_out, gain_two, bias_two = [norm_ref[i : i + 1] for i in range(5)]
    for load in loads[:group]:
        load.wait()
    hidden = up_ref.shape[-1]

    def out_block(k):
        return out_ref[here ^ k].reshape(depth, out_ref.shape[-1])

    total = jnp.concatenate([content_ref[...], query_ref[...]], 0).astype(jnp.float32)
    for k in range(group):
        total = total + dot_nt(mixed_pieces[k][...].reshape(tokens, -1), out_block(k))
    normed, inverse_one = norm_parts(total)
    normed_ref[...] = normed
    middle = normed * gain_one + bias_one
    low_ref[...] = middle.astype(jnp.bfloat16)
    low_t_ref[...] = low_ref[...].T
    total_ref[...] = middle + bias_out
    for load in loads[group:]:
        load.wait()

    def forward(j, carry):
        for part in (slice(0, own), slice(own, tokens)):
            before = dot(low_ref[part], up_ref[j].reshape(depth, hidden)) + bias_ref[j]
            square = before * before
            bent = jnp.tanh(GELU_FACTOR * before * (1.0 + GELU_CUBIC * square))
            half_up = 0.5 * (1.0 + bent)
            hidden_now = (before * half_up).astype(jnp.bfloat16)
            slope_ref[j, part] = half_up + 0.5 * before * (1.0 - bent * bent) * GELU_FACTOR * (
                1.0 + 3.0 * GELU_CUBIC * square
            )
            hidden_ref[j, part] = hidden_now
            total_ref[part] += dot_nt(hidden_now, down_ref[j].reshape(depth, hidden))
        return carry

    lax.fori_loop(0, group, forward, 0)
    normed_two, inverse_two = norm_parts(total_ref[...])
    result = (normed_two * gain_two + bias_two).astype(jnp.bfloat16)
    content_out[...] = result[:own]
    query_out[...] = result[own:]
    upstream = jnp.concatenate([dcontent_ref[...], dquery_ref[...]], 0).astype(jnp.float32)
    dsmall_ref[group + 3 : group + 4] = column_sum(upstream * normed_two)
    dsmall_ref[group + 4 : group + 5] = column_sum(upstream)
    dfinal = norm_back(upstream, normed_two, inverse_two, gain_two)
    dsmall_ref[group + 2 : group + 3] = column_sum(dfinal)
    total_ref[...] = dfinal
    dlow = dfinal.astype(jnp.bfloat16)
    dlow_t = dlow.T

    def to_sibling(source, place, index):
        return pltpu.make_async_remote_copy(
            source, place, send_sems.at[index], recv_sems.at[index],
            device_id={"heads": here ^ 1}, device_id_type=pl.DeviceIdType.MESH,
        )

    def back_block(j):
        ddown = dot(dlow_t, hidden_ref[j])
        bias_grad = jnp.zeros((1, hidden), jnp.float32)
        for part in (slice(0, own), slice(own, tokens)):
            dhidden = dot(dlow[part], down_ref[j].reshape(depth, hidden))
            dbefore = (dhidden * slope_ref[j, part]).astype(jnp.bfloat16)
            bias_grad = bias_grad + column_sum(dbefore.astype(jnp.float32))
            total_ref[part] += dot_nt(dbefore, up_ref[j].reshape(depth, hidden))
            hidden_ref[j, part] = dbefore
        dsmall_ref[pl.ds(j, 1)] = bias_grad
        return dot(low_t_ref[...], hidden_ref[j]), ddown

    def sent(chip):
        j = 2 * chip + 1 - core
        return [
            to_sibling(up_ref.at[j], up_got.at[chip], 2 * chip),
            to_sibling(down_ref.at[j], down_got.at[chip], 2 * chip + 1),
        ]

    def kept(chip):
        j = 2 * chip + core
        return [
            pltpu.make_async_copy(up_ref.at[j], dup_hbm.at[:, chip], sems.at[chip]),
            pltpu.make_async_copy(down_ref.at[j], ddown_hbm.at[:, chip], sems.at[group + chip]),
        ]

    def backward_sent(chip, carry):
        j = 2 * chip + 1 - core
        dup, ddown = back_block(j)
        up_ref[j] = dup.astype(jnp.bfloat16).reshape(up_ref.shape[1:])
        down_ref[j] = ddown.astype(jnp.bfloat16).reshape(down_ref.shape[1:])
        for copy in sent(chip):
            copy.start()
        return carry

    def backward_kept(chip, carry):
        j = 2 * chip + core
        dup, ddown = back_block(j)
        for copy in sent(chip):
            copy.wait_recv()
        dup = dup + up_got[chip].astype(jnp.float32).reshape(depth, hidden)
        ddown = ddown + down_got[chip].astype(jnp.float32).reshape(depth, hidden)
        up_ref[j] = dup.astype(jnp.bfloat16).reshape(up_ref.shape[1:])
        down_ref[j] = ddown.astype(jnp.bfloat16).reshape(down_ref.shape[1:])
        for copy in kept(chip):
            copy.start()
        return carry

    lax.fori_loop(0, chips, backward_sent, 0)
    lax.fori_loop(0, chips, backward_kept, 0)
    dmiddle = total_ref[...]
    normed = normed_ref[...]
    dsmall_ref[group : group + 1] = column_sum(dmiddle * normed)
    dsmall_ref[group + 1 : group + 2] = column_sum(dmiddle)
    dresid = norm_back(dmiddle, normed, inverse_one, gain_one)
    total_ref[...] = dresid
    dresid_copy = pltpu.make_async_copy(total_ref, dresid_ref, sems.at[0])
    dresid_copy.start()
    dlow = dresid.astype(jnp.bfloat16)
    dlow_t = dlow.T
    out_copies = [
        to_sibling(out_sent.at[chip], out_got.at[chip], 2 * chips + chip) for chip in range(chips)
    ]
    for chip in range(chips):
        k = 2 * chip + 1
        mixed = mixed_pieces[k][...].reshape(tokens, -1)
        out_sent[chip] = dot(dlow_t, mixed).astype(jnp.bfloat16).reshape(out_sent.shape[1:])
        out_copies[chip].start()
    for k in range(group):
        dmixed_pieces[k][...] = (
            dot(dlow, out_block(k)).astype(jnp.bfloat16).reshape(dmixed_pieces[k].shape)
        )
    for chip in range(chips):
        k = 2 * chip
        mixed = mixed_pieces[k][...].reshape(tokens, -1)
        dout = dot(dlow_t, mixed)
        out_copies[chip].wait_recv()
        dout = dout + out_got[chip].astype(jnp.float32).reshape(dout.shape)
        dout_ref[:, (here ^ k) >> 1] = dout.astype(jnp.bfloat16).reshape(out_sent.shape[1:])
    dsmall_ref[group + 5 :] = jnp.zeros((dsmall_ref.shape[0] - group - 5, depth), jnp.float32)
    dresid_copy.wait()
    for chip in range(chips):
        for copy in sent(chip):
            copy.wait_send()
        out_copies[chip].wait_send()
        for copy in kept(chip):
            copy.wait()


def feed_layer(mixed_pieces, bias_pieces, content, query, dcontent, dquery, norm_param, up, down, out):
    group = len(mixed_pieces)
    own, depth = content.shape
    parts, _, pick, hidden = up.shape
    width = out.shape[-1]
    inside = pl.BlockSpec(memory_space=pltpu.VMEM)
    outside = pl.BlockSpec(memory_space=pl.ANY)
    tokens = 2 * own
    results = pl.pallas_call(
        functools.partial(feed_kernel, group),
        in_specs=[inside] * (2 * group + 5) + [outside] * 3,
        out_specs=[inside, inside, outside] + [inside] * group + [outside, outside, inside, inside],
        out_shape=[
            jax.ShapeDtypeStruct((own, depth), jnp.bfloat16),
            jax.ShapeDtypeStruct((own, depth), jnp.bfloat16),
            jax.ShapeDtypeStruct((tokens, depth), jnp.float32),
        ]
        + [jax.ShapeDtypeStruct((2, own, width), jnp.bfloat16)] * group
        + [
            jax.ShapeDtypeStruct((parts, group // 2, pick, hidden), jnp.bfloat16),
            jax.ShapeDtypeStruct((parts, group // 2, pick, hidden), jnp.bfloat16),
            jax.ShapeDtypeStruct((parts, group // 2, pick, width), jnp.bfloat16),
            jax.ShapeDtypeStruct((16, depth), jnp.float32),
        ],
        scratch_shapes=[
            pltpu.VMEM((group, parts, pick, hidden), jnp.bfloat16),
            pltpu.VMEM((group, parts, pick, hidden), jnp.bfloat16),
            pltpu.VMEM((group, parts, pick, width), jnp.bfloat16),
            pltpu.VMEM((group, tokens, hidden), jnp.bfloat16),
            pltpu.VMEM((group, tokens, hidden), jnp.float32),
            pltpu.VMEM((group, 1, hidden), jnp.float32),
            pltpu.VMEM((tokens, depth), jnp.bfloat16),
            pltpu.VMEM((depth, tokens), jnp.bfloat16),
            pltpu.VMEM((tokens, depth), jnp.float32),
            pltpu.VMEM((tokens, depth), jnp.float32),
            pltpu.VMEM((group // 2, parts, pick, hidden), jnp.bfloat16),
            pltpu.VMEM((group // 2, parts, pick, hidden), jnp.bfloat16),
            pltpu.VMEM((group // 2, parts, pick, width), jnp.bfloat16),
            pltpu.VMEM((group // 2, parts, pick, width), jnp.bfloat16),
            pltpu.SemaphoreType.DMA((3 * group,)),
            pltpu.SemaphoreType.DMA((3 * group // 2,)),
            pltpu.SemaphoreType.DMA((3 * group // 2,)),
        ],
        compiler_params=pltpu.CompilerParams(
            vmem_limit_bytes=VMEM_LIMIT, collective_id=1, has_side_effects=True
        ),
    )(*mixed_pieces, *bias_pieces, content, query, dcontent, dquery, norm_param, up, down, out)
    return results[0], results[1], results[2].reshape(2, own, depth), results[3 : 3 + group], results[3 + group :]


def exchange(value, axis, mask):
    return lax.ppermute(value, axis, [(i, i ^ mask) for i in range(lax.axis_size(axis))])


def total_over(value, axis):
    mask = 1
    while mask < lax.axis_size(axis):
        value = value + exchange(value, axis, mask)
        mask = 2 * mask
    return value


def gather_heads(own):
    far = exchange(own, "heads", 2)
    return [own, exchange(own, "heads", 1), far, exchange(far, "heads", 1)]


def by_pieces(pick):
    return lax.axis_size("dp") <= 8 and pick % 16 == 0


def gather_projection(own):
    if not by_pieces(own.shape[1]):
        return [lax.all_gather(own, "dp", axis=1, tiled=True)]
    pieces = {0: own}
    mask = lax.axis_size("dp") // 2
    while mask:
        for k in sorted(pieces):
            pieces[k ^ mask] = exchange(pieces[k], "dp", mask)
        mask = mask // 2
    return [pieces[k] for k in range(len(pieces))]


def reduce_projection(pieces):
    return lax.psum_scatter(pieces[0], "dp", scatter_dimension=1, tiled=True).astype(jnp.float32)


def gather_all(own):
    dp, heads = lax.axis_size("dp"), lax.axis_size("heads")
    rows, columns = own.shape
    full = lax.all_gather(own, ("dp", "heads"), axis=0, tiled=False).reshape(dp, heads, rows, columns)
    if by_pieces(rows):
        return full
    return jnp.swapaxes(full, 0, 1).reshape(1, heads, dp * rows, columns)


def scatter_all(full):
    chip = lax.axis_index("heads") // 2
    mine = lax.dynamic_index_in_dim(full[0], chip, 0, False)
    theirs = lax.dynamic_index_in_dim(full[0], 1 - chip, 0, False)
    mine = mine.astype(jnp.float32) + exchange(theirs, "heads", 2).astype(jnp.float32)
    return lax.psum_scatter(mine, "dp", scatter_dimension=0, tiled=True)


def adam_step(master, first, second, gradient, factor, decayed):
    clipped = gradient * factor
    new_first = BETA_ONE * first + (1.0 - BETA_ONE) * clipped
    new_second = BETA_TWO * second + (1.0 - BETA_TWO) * clipped * clipped
    first_hat = new_first / (1.0 - BETA_ONE**STEP)
    second_hat = new_second / (1.0 - BETA_TWO**STEP)
    update = first_hat / (jnp.sqrt(second_hat) + ADAM_EPSILON)
    if decayed:
        update = update + WEIGHT_DECAY * master
        return (new_first, new_second, master - MATRIX_RATE * update)
    return (new_first, new_second, master - VECTOR_RATE * update)


def local(
    content_in,
    query_in,
    content_grad,
    query_grad,
    segment_ids,
    doc_lengths,
    factor_order,
    attn_proj,
    attn_proj_first,
    attn_proj_second,
    out_proj,
    out_proj_first,
    out_proj_second,
    up_proj,
    up_proj_first,
    up_proj_second,
    down_proj,
    down_proj_first,
    down_proj_second,
    head_bias,
    head_bias_first,
    head_bias_second,
    up_bias,
    up_bias_first,
    up_bias_second,
    norm_param,
    norm_param_first,
    norm_param_second,
):
    width = content_in.shape[1]
    length = segment_ids.shape[1]
    local_heads, head_size = (head_bias.shape[1], head_bias.shape[2])
    weight_pieces = gather_projection(attn_proj.astype(jnp.bfloat16))
    content_pieces = gather_heads(content_in)
    query_pieces = gather_heads(query_in)
    bias_pieces = [up_bias[None]] + [exchange(up_bias[None], "heads", k) for k in range(1, 4)]
    out_full = gather_all(out_proj.T.astype(jnp.bfloat16))
    up_full = gather_all(up_proj.astype(jnp.bfloat16))
    down_full = gather_all(down_proj.T.astype(jnp.bfloat16))
    table = position_table(length, width)
    tables = (jnp.asarray(table), jnp.asarray(table[::-1].copy()))
    facts = row_facts(segment_ids, doc_lengths, factor_order)
    proj, logsum, mixed_pieces = attention_forward(
        content_pieces, query_pieces, weight_pieces, tables[0], head_bias, facts
    )
    content_out, query_out, dresid, dmixed_pieces, (dup, ddown, dout, dsmall) = feed_layer(
        mixed_pieces, bias_pieces, content_in, query_in, content_grad, query_grad, norm_param,
        up_full, down_full, out_full,
    )
    backward = attention_backward(
        content_pieces, query_pieces, weight_pieces, tables, head_bias, facts, proj, logsum,
        dmixed_pieces, dresid, (dup, ddown, dout), dsmall,
    )
    heads_count, head_index = lax.axis_size("heads"), lax.axis_index("heads")
    if len(weight_pieces) > 1:
        input_grad, dhead = backward[:2], backward[2]
        up_share, down_share, out_share, proj_share, small_sum, norm_tile = backward[3:]
        grad_norm = norm_tile[0, 0]
    else:
        input_grad, dhead = backward[:2], total_over(backward[2], "dp")
        proj_share = reduce_projection([backward[3]])
        up_share, down_share, out_share = scatter_all(dup), scatter_all(ddown), scatter_all(dout)
        small_sum = total_over(total_over(dsmall, "heads"), "dp")
        squares = sum(jnp.sum(share * share) for share in (up_share, down_share, out_share, proj_share))
        squares = squares + jnp.sum(dhead * dhead) / lax.axis_size("dp")
        squares = squares + jnp.sum(small_sum * small_sum) / (lax.axis_size("dp") * heads_count)
        grad_norm = jnp.sqrt(total_over(total_over(squares.reshape(1, 1), "heads"), "dp"))[0, 0]
    down_share, out_share = down_share.T, out_share.T
    head_grad = dhead[:5].reshape(head_bias.shape)
    bias_sum, norm_sum = small_sum[:heads_count], small_sum[heads_count : heads_count + 5]
    bias_grad = lax.dynamic_slice_in_dim(bias_sum, head_index, 1, 0)[0]
    factor = CLIP_NORM / jnp.maximum(grad_norm, CLIP_NORM)
    attn_first, attn_second, attn_new = adam_step(
        attn_proj, attn_proj_first, attn_proj_second, proj_share, factor, True
    )
    out_first, out_second, out_new = adam_step(
        out_proj, out_proj_first, out_proj_second, out_share, factor, True
    )
    up_first, up_second, up_new = adam_step(
        up_proj, up_proj_first, up_proj_second, up_share, factor, True
    )
    down_first, down_second, down_new = adam_step(
        down_proj, down_proj_first, down_proj_second, down_share, factor, True
    )
    head_first, head_second, head_new = adam_step(
        head_bias, head_bias_first, head_bias_second, head_grad, factor, False
    )
    bias_first, bias_second, bias_new = adam_step(
        up_bias, up_bias_first, up_bias_second, bias_grad, factor, False
    )
    norm_first, norm_second, norm_new = adam_step(
        norm_param, norm_param_first, norm_param_second, norm_sum, factor, False
    )
    return (
        content_out,
        query_out,
        input_grad[0],
        input_grad[1],
        grad_norm,
        proj_share,
        attn_first,
        attn_second,
        attn_new,
        out_share,
        out_first,
        out_second,
        out_new,
        up_share,
        up_first,
        up_second,
        up_new,
        down_share,
        down_first,
        down_second,
        down_new,
        head_grad,
        head_first,
        head_second,
        head_new,
        bias_grad,
        bias_first,
        bias_second,
        bias_new,
        norm_sum,
        norm_first,
        norm_second,
        norm_new,
    )


def solution(mesh):
    return jax.shard_map(
        local,
        mesh=mesh,
        in_specs=(
            P(("dp", "heads"), None),
            P(("dp", "heads"), None),
            P(("dp", "heads"), None),
            P(("dp", "heads"), None),
            P("dp", None),
            P("dp", None),
            P("dp", None),
            P(None, "dp", "heads"),
            P(None, "dp", "heads"),
            P(None, "dp", "heads"),
            P("heads", "dp"),
            P("heads", "dp"),
            P("heads", "dp"),
            P("dp", "heads"),
            P("dp", "heads"),
            P("dp", "heads"),
            P("heads", "dp"),
            P("heads", "dp"),
            P("heads", "dp"),
            P(None, "heads", None),
            P(None, "heads", None),
            P(None, "heads", None),
            P("heads"),
            P("heads"),
            P("heads"),
            P(),
            P(),
            P(),
        ),
        out_specs=(
            P(("dp", "heads"), None),
            P(("dp", "heads"), None),
            P(("dp", "heads"), None),
            P(("dp", "heads"), None),
            P(),
            P(None, "dp", "heads"),
            P(None, "dp", "heads"),
            P(None, "dp", "heads"),
            P(None, "dp", "heads"),
            P("heads", "dp"),
            P("heads", "dp"),
            P("heads", "dp"),
            P("heads", "dp"),
            P("dp", "heads"),
            P("dp", "heads"),
            P("dp", "heads"),
            P("dp", "heads"),
            P("heads", "dp"),
            P("heads", "dp"),
            P("heads", "dp"),
            P("heads", "dp"),
            P(None, "heads", None),
            P(None, "heads", None),
            P(None, "heads", None),
            P(None, "heads", None),
            P("heads"),
            P("heads"),
            P("heads"),
            P("heads"),
            P(),
            P(),
            P(),
            P(),
        ),
        check_vma=False,
    )
```

```python
import functools

import jax
import jax.numpy as jnp
import ml_dtypes
import numpy as np
from jax import lax
from jax.experimental import pallas as pl
from jax.experimental.pallas import tpu as pltpu
from jax.sharding import PartitionSpec as P

STEP = 10


NORM_EPSILON = 1e-05
CLIP_NORM = 1.0
MATRIX_RATE = 0.08
VECTOR_RATE = 0.5
BETA_ONE = 0.9
BETA_TWO = 0.999
ADAM_EPSILON = 1e-08
WEIGHT_DECAY = 0.01
MASKED_SCORE = -1e30
GELU_FACTOR = 0.7978845608028654
GELU_CUBIC = 0.044715
LOG2E = 1.4426950408889634
VMEM_LIMIT = 56 << 20


def position_table(length, width):
    distance = length // 2 - np.arange(length)
    frequency = 10000.0 ** (-np.arange(0, width, 2) / width)
    angles = distance[:, None] * frequency[None, :]
    return np.concatenate([np.sin(angles), np.cos(angles)], -1).astype(np.float32).astype(ml_dtypes.bfloat16)


def dot(left, right):
    return lax.dot_general(left, right, (((1,), (0,)), ((), ())), preferred_element_type=jnp.float32)


def dot_nt(left, right):
    return lax.dot_general(left, right, (((1,), (1,)), ((), ())), preferred_element_type=jnp.float32)


def split_pair(values):
    high = values.astype(jnp.bfloat16)
    low = (values - high.astype(jnp.float32)).astype(jnp.bfloat16)
    return jnp.concatenate([high, low], -1)


def roll_matrix(token_col, length):
    lanes = lax.broadcasted_iota(jnp.int32, (length, length), 1).astype(jnp.float32)
    return jnp.where(token_col == lanes, 1.0, 0.0).astype(jnp.bfloat16)


def unroll_matrix(token_row, length):
    places = lax.broadcasted_iota(jnp.int32, (length, length), 0).astype(jnp.float32)
    return jnp.where(token_row == places, 1.0, 0.0).astype(jnp.bfloat16)


def write_masks(mask_ref, facts_row, facts_col, half):
    for block in range(2):
        part = slice(block * half, (block + 1) * half)
        code_i, base_i = facts_col[part, 0:1], facts_col[part, 1:2]
        code_j = facts_row[0:1, part]
        same = code_j >= base_i
        mask_ref[0, block] = jnp.where(same & (code_j <= code_i), 0.0, MASKED_SCORE)
        mask_ref[1, block] = jnp.where(same & (code_j < code_i), 0.0, MASKED_SCORE)


def query_sides(query, bias, segment_col, factor):
    wide = query.astype(jnp.float32)
    with_u = split_pair((wide + bias[0]) * factor)
    with_w = split_pair((wide + bias[1]) * factor)
    with_c = wide + bias[2]
    same = jnp.sum(with_c * bias[3], -1, keepdims=True) * factor
    change = jnp.sum(with_c * (bias[4] - bias[3]), -1, keepdims=True) * factor
    return with_u, with_w, with_c, same + change * segment_col, change * (1.0 - 2.0 * segment_col)


def block_scores(with_u, with_w, keys_twice, relative_twice, half):
    content = dot_nt(with_u, keys_twice)
    position = dot_nt(with_w, relative_twice)
    return content + pltpu.roll(position, half, 1, stride=1, stride_axis=0)[:, :half]


def greet(axis, masks):
    barrier = pltpu.get_barrier_semaphore()
    for mask in masks:
        pl.semaphore_signal(
            barrier, inc=1, device_id={axis: lax.axis_index(axis) ^ mask}, device_id_type=pl.DeviceIdType.MESH
        )
    pl.semaphore_wait(barrier, len(masks))


class Links:
    def __init__(self, send_sems, recv_sems):
        self.send_sems, self.recv_sems, self.used = send_sems, recv_sems, 0

    def push(self, source, place, axis, distance):
        index = self.used
        self.used = index + 1
        return pltpu.make_async_remote_copy(
            source, place, self.send_sems.at[index], self.recv_sems.at[index],
            device_id={axis: lax.axis_index(axis) ^ distance}, device_id_type=pl.DeviceIdType.MESH,
        )


def add_planes(place, first, second):
    def one(z, carry):
        place[z] = (first(z).astype(jnp.float32) + second[z].astype(jnp.float32)).astype(place.dtype)
        return carry

    lax.fori_loop(0, place.shape[0], one, 0)


class Scatter:
    def __init__(self, links, sems, sem, source, order, refs):
        self.kept, self.got, self.got_two, self.got_last = refs
        self.order = order
        heads_here, dp_here = lax.axis_index("heads"), lax.axis_index("dp")
        x, y, z = heads_here >> 1, dp_here & 1, dp_here >> 1
        if order == "xy":
            own, other, first, second, self.mine = source.at[:, :, x], source.at[:, :, 1 - x], ("heads", 2), ("dp", 1), y
        else:
            own, other, first, second, self.mine = source.at[:, y], source.at[:, 1 - y], ("dp", 1), ("heads", 2), x
        self.load = pltpu.make_async_copy(own, self.kept, sems.at[sem])
        self.copy = links.push(other, self.got, *first)
        self.copy_two = links.push(self.kept.at[:, 1 - self.mine], self.got_two, *second)
        self.place = z
        self.copies_last = [
            links.push(self.got_two.at[z ^ m], self.got_last.at[m - 1], "dp", 2 * m)
            for m in range(1, source.shape[0])
        ]

    def begin(self):
        self.load.start()
        self.copy.start()

    def second(self):
        self.load.wait()
        self.copy.wait()
        add_planes(self.kept, lambda z: self.kept[z], self.got)
        self.copy_two.start()

    def third(self):
        self.copy_two.wait()
        add_planes(self.got_two, lambda z: self.kept[z, self.mine], self.got_two)
        for copy in self.copies_last:
            copy.start()

    def last(self):
        for copy in self.copies_last:
            copy.wait()
        total = self.got_two[self.place].astype(jnp.float32)
        for index in range(self.got_last.shape[0]):
            total = total + self.got_last[index].astype(jnp.float32)
        return total


def square_sum(values):
    return jnp.sum(jnp.sum(values * values, -1, keepdims=True), 0, keepdims=True)


class Gather:
    def __init__(self, links, sem, full, own, rows, order):
        heads_here, dp_here = lax.axis_index("heads"), lax.axis_index("dp")
        x, core, y, z = heads_here >> 1, heads_here & 1, dp_here & 1, dp_here >> 1

        def same(*place):
            part = full.at[place + (rows,)]
            return part, part

        everything = slice(None)
        planes = full.shape[0]
        mine = full.at[z, y, x, core, rows]
        self.keep = pltpu.make_async_copy(own.at[rows], mine, sem)
        self.along_z = [links.push(own.at[rows], mine, "dp", 2 * m) for m in range(1, planes)]
        column = same(everything, y, x, core)
        across = ("heads", 2), ("dp", 1)
        if order == "xy":
            near, wide = same(everything, y, 1 - x, core), same(everything, y, everything, core)
            last = same(everything, 1 - y, everything, core)
        else:
            near, wide = same(everything, 1 - y, x, core), same(everything, everything, x, core)
            last = same(everything, everything, 1 - x, core)
            across = across[1], across[0]
        self.first = links.push(*column, *across[0])
        self.second = links.push(*wide, *across[1])
        self.to_sibling = [links.push(*part, "heads", 1) for part in (column, near, last)]

    def begin(self):
        self.keep.start()
        for copy in self.along_z:
            copy.start()

    def step_one(self):
        self.keep.wait()
        for copy in self.along_z:
            copy.wait()
        self.first.start()
        self.to_sibling[0].start()

    def step_two(self):
        self.first.wait()
        self.second.start()
        self.to_sibling[1].start()

    def step_three(self):
        self.second.wait()
        self.to_sibling[2].start()

    def finish(self):
        for copy in self.to_sibling:
            copy.wait()


def write_facts(lengths_ref, order_ref, segment_ref, row_ref, col_ref):
    rows, length = order_ref.shape
    down = lax.broadcasted_iota(jnp.int32, (length, length), 0).astype(jnp.float32)
    along = lax.broadcasted_iota(jnp.int32, (length, length), 1).astype(jnp.float32)
    places_col, places_row = down[:, 0:1], along[0:1, :]
    row_ref[...] = jnp.zeros_like(row_ref)
    col_ref[...] = jnp.zeros_like(col_ref)

    def as_column(values):
        return jnp.sum(jnp.where(down == along, values, 0.0), 1, keepdims=True)

    for row in range(rows):
        ends, start, end = [], 0, 0
        for document in range(lengths_ref.shape[1]):
            count = lengths_ref[row, document]
            start = start + (count == length // 2).astype(jnp.int32) * end
            end = end + count
            ends.append(end.astype(jnp.float32))
        start = start.astype(jnp.float32)
        order = order_ref[row : row + 1].astype(jnp.float32)
        segment = segment_ref[row : row + 1].astype(jnp.float32)
        order_col, segment_col = as_column(order), as_column(segment)
        for place, turned in ((places_row, False), (places_col, True)):
            token = place + start
            token = jnp.where(token >= length, token - length, token)
            base = jnp.zeros_like(token)
            for end in ends:
                base = base + jnp.where(token >= end, float(length), 0.0)
            if turned:
                rank = jnp.sum(jnp.where(order == token, along, 0.0), 1, keepdims=True)
                kind = jnp.sum(jnp.where(along == token, segment, 0.0), 1, keepdims=True)
                for index, values in enumerate((base + rank, base, kind, token)):
                    col_ref[row, :, index : index + 1] = values
            else:
                rank = jnp.sum(jnp.where(order_col == token, down, 0.0), 0, keepdims=True)
                kind = jnp.sum(jnp.where(down == token, segment_col, 0.0), 0, keepdims=True)
                for index, values in enumerate((base + rank, base, kind, token)):
                    row_ref[row, index : index + 1] = values


def turn(values):
    size = values.shape[1]
    same = lax.broadcasted_iota(jnp.int32, (size, size), 0) == lax.broadcasted_iota(jnp.int32, (size, size), 1)
    identity = jnp.where(same, 1.0, 0.0).astype(jnp.bfloat16)
    return dot_nt(identity, values.astype(jnp.bfloat16)).astype(jnp.bfloat16)


def attention_forward_kernel(head_size, group, parts, fast, *refs):
    content_hbm, query_hbm, weight_in, up_in, down_in, out_in, bias_in, refs = *refs[:7], refs[7:]
    lengths_ref, order_ref, segment_ref, table_ref, head_ref, refs = *refs[:5], refs[5:]
    proj_ref, logsum_ref, row_ref, col_ref, bias_all, refs = *refs[:5], refs[5:]
    mixed_pieces, refs = refs[:group], refs[group:]
    content_out, query_out, weight_out, refs = *refs[:3], refs[3:]
    if fast:
        up_all, down_all, out_all, refs = *refs[:3], refs[3:]
    content_all, query_all, weight_ref, mixed_ref, relative_ref, mask_ref, refs = *refs[:6], refs[6:]
    sems, send_sems, recv_sems, refs = *refs[:3], refs[3:]
    rows, length = row_ref.shape[0], row_ref.shape[2]
    half = length // 2
    tokens, depth = content_hbm.shape
    width = weight_ref.shape[-1]
    heads = width // head_size
    factor = head_size ** (-0.5) * LOG2E
    heads_here, dp_here = lax.axis_index("heads"), lax.axis_index("dp")
    chip = heads_here >> 1
    links = Links(send_sems, recv_sems)

    def token_part(k):
        return pl.ds(pl.multiple_of((heads_here ^ k) * tokens, tokens), tokens)

    streams = ((content_hbm, content_all), (query_hbm, query_all))
    local = [pltpu.make_async_copy(own, full.at[token_part(0)], sems.at[n]) for n, (own, full) in enumerate(streams)]
    if not fast:
        local.append(pltpu.make_async_copy(weight_in, weight_ref, sems.at[2]))
    for copy in local:
        copy.start()
    barrier = pltpu.get_barrier_semaphore()
    peers = [("heads", k) for k in range(1, group)] + [("dp", k) for k in range(1, parts)]
    for axis, k in peers:
        pl.semaphore_signal(
            barrier, inc=1, device_id={axis: lax.axis_index(axis) ^ k}, device_id_type=pl.DeviceIdType.MESH
        )
    if fast:
        weight_send, up_send, down_send, out_send = refs
        weight_send[...] = weight_in[...].astype(jnp.bfloat16)
    pl.semaphore_wait(barrier, len(peers))
    far = [links.push(own, full.at[token_part(0)], "heads", 2) for own, full in streams]
    near = [links.push(own, full.at[token_part(0)], "heads", 1) for own, full in streams]
    passed = [links.push(full.at[token_part(2)], full.at[token_part(2)], "heads", 1) for _, full in streams]
    bias_copies = [links.push(bias_in, bias_all.at[heads_here], "heads", k) for k in range(1, group)]
    for copy in far + near + bias_copies:
        copy.start()
    if fast:
        y, z = dp_here & 1, dp_here >> 1
        weight_z, weight_y = [], []
        for pair in (slice(0, 2), slice(2, 4)):
            mine = weight_ref.at[pair, z, y]
            weight_z.append([links.push(weight_send.at[pair], mine, "dp", 2 * m) for m in range(1, parts // 2)])
            column = weight_ref.at[pair, :, y]
            weight_y.append(links.push(column, column, "dp", 1))
            for copy in weight_z[-1]:
                copy.start()
        weight_ref[:, z, y] = weight_send[...]
        up_send[...] = up_in[...].astype(jnp.bfloat16)
        down_send[...] = turn(down_in[...])
        out_send[...] = turn(out_in[...])
        pick = up_send.shape[0]
        early, late = pl.ds(0, pick // 2), pl.ds(pick // 2, pick // 2)
        up_one = Gather(links, sems.at[3], up_all, up_send, early, "xy")
        up_two = Gather(links, sems.at[4], up_all, up_send, late, "xy")
        down_one = Gather(links, sems.at[5], down_all, down_send, early, "yx")
        down_two = Gather(links, sems.at[6], down_all, down_send, late, "xy")
        out_one = Gather(links, sems.at[7], out_all, out_send, pl.ds(0, pick), "yx")
        gathers = (up_one, up_two, down_one, down_two, out_one)
    bias_all[heads_here] = bias_in[...]
    write_facts(lengths_ref, order_ref, segment_ref, row_ref, col_ref)
    if fast:
        for first, second in zip(weight_z, weight_y):
            for copy in first:
                copy.wait()
            second.start()
        down_one.begin()
        out_one.begin()
        for copy in weight_y[:1]:
            copy.wait()
        up_one.begin()
        weight_y[1].wait()
    for copy in local + near:
        copy.wait()

    def weight(kind):
        return weight_ref[kind].reshape(depth, width)

    saves = [
        pltpu.make_async_copy(content_all, content_out, sems.at[0]),
        pltpu.make_async_copy(query_all, query_out, sems.at[1]),
        pltpu.make_async_copy(weight_ref, weight_out, sems.at[2]),
    ]
    saves[2].start()
    relative_ref[...] = dot(table_ref[...], weight(3)).astype(jnp.bfloat16)

    def pass_on():
        for arrived, onward in zip(far, passed):
            arrived.wait()
            onward.start()

    def nothing():
        pass

    events = {(0, 0): [pass_on]}
    if fast:
        events = {
            (0, 0): [pass_on, down_one.step_one, up_two.begin],
            (0, 1): [up_one.step_one, down_two.begin],
            (0, 2): [out_one.step_one, down_one.step_two],
            (1, 0): [up_one.step_two, up_two.step_one],
            (1, 1): [down_two.step_one, out_one.step_two],
            (1, 2): [up_two.step_two, down_one.step_three],
            (2, 0): [down_two.step_two, up_one.step_three],
            (2, 1): [out_one.step_three],
        }

    def one_row(step, carry):
        row = jnp.where(step == 0, 0, rows - step)
        row = jnp.where(chip == 0, row, rows - 1 - row)

        @pl.when(step == 1)
        def _():
            for copy in passed:
                copy.wait()
            for save in saves[:2]:
                save.start()

        here = pl.ds(pl.multiple_of(row * length, length), length)
        facts_row, facts_col = row_ref[row], col_ref[row]
        write_masks(mask_ref, facts_row, facts_col, half)
        roll = roll_matrix(facts_col[:, 3:4], length)
        unroll = unroll_matrix(facts_row[3:4, :], length)
        content, query = content_all[here], query_all[here]
        joined = jnp.concatenate(
            [
                dot(content, weight(0)).astype(jnp.bfloat16),
                dot(content, weight(1)).astype(jnp.bfloat16),
                dot(content, weight(2)).astype(jnp.bfloat16),
                dot(query, weight(0)).astype(jnp.bfloat16),
            ],
            -1,
        )
        proj_ref[row] = dot(roll, joined).astype(jnp.bfloat16)
        segment_col, segment_row = facts_col[:, 2:3], facts_row[2:3, :]
        mixed = [[None] * heads, [None] * heads]
        for head in range(heads):
            cols = lambda kind: slice(kind * width + head * head_size, kind * width + (head + 1) * head_size)
            own_cols = slice(head * head_size, (head + 1) * head_size)
            bias = [head_ref[kind : kind + 1, own_cols] for kind in range(5)]
            keys, values = proj_ref[row, :, cols(1)], proj_ref[row, :, cols(2)]
            keys_twice = jnp.concatenate([keys, keys], -1)
            relative = relative_ref[:, own_cols]
            relative_twice = jnp.concatenate([relative, relative], -1)
            for stream in range(2):
                with_u, with_w, _, own, slope = query_sides(
                    proj_ref[row, :, cols(3 * stream)], bias, segment_col, factor
                )
                pieces = []
                for block in range(2):
                    part = slice(block * half, (block + 1) * half)
                    scores = block_scores(
                        with_u[part], with_w[part], keys_twice[part], relative_twice, half
                    )
                    scores = scores + own[part] + slope[part] * segment_row[:, part] + mask_ref[stream, block]
                    highest = jnp.maximum(jnp.max(scores, -1, keepdims=True), 0.0)
                    weights = jnp.exp2(scores - highest)
                    totals = jnp.exp2(-highest) + jnp.sum(weights, -1, keepdims=True)
                    pieces.append(dot(weights.astype(jnp.bfloat16), values[part]) / totals)
                    index = stream * heads + head
                    logsum_ref[row, part, index : index + 1] = highest + jnp.log2(totals)
                mixed[stream][head] = jnp.concatenate(pieces, 0).astype(jnp.bfloat16)
            for when, actions in events.items():
                if when[1] == head:
                    @pl.when(step == when[0])
                    def _():
                        for action in actions:
                            action()
        both = jnp.concatenate(mixed[0] + mixed[1], -1)
        both = dot(unroll, both).astype(jnp.bfloat16)
        mixed_ref[0, here] = both[:, :width]
        mixed_ref[1, here] = both[:, width:]
        return carry

    lax.fori_loop(0, rows, one_row, 0)
    keep = pltpu.make_async_copy(mixed_ref.at[:, token_part(0)], mixed_pieces[0], sems.at[8])
    keep.start()
    sends = [
        links.push(mixed_ref.at[:, token_part(k)], mixed_pieces[k], "heads", k) for k in (2, 3, 1)[: group - 1]
    ]
    for copy in sends:
        copy.start()
    if fast:
        up_two.step_three()
        down_two.step_three()
    for copy in [keep] + saves + sends + bias_copies:
        copy.wait()
    if fast:
        for gather in gathers:
            gather.finish()


def attention_forward(
    content, query, attn_proj, up_proj, down_proj, out_proj, up_bias, doc_lengths, factor_order, segment_ids,
    table, head_bias,
):
    rows, length = segment_ids.shape
    group, parts = lax.axis_size("heads"), lax.axis_size("dp")
    fast = by_pieces(attn_proj.shape[1])
    own, depth = content.shape
    tokens = own * group
    pick, width = attn_proj.shape[1:]
    hidden = up_proj.shape[1]
    head_size = head_bias.shape[-1]
    half = length // 2
    inside = pl.BlockSpec(memory_space=pltpu.VMEM)
    outside = pl.BlockSpec(memory_space=pl.ANY)
    scalars = pl.BlockSpec(memory_space=pltpu.SMEM)
    bfloat, float32 = jnp.bfloat16, jnp.float32
    weight_shape = (4, parts // 2, 2, pick, width) if fast else (4, depth, width)
    out_shape = [
        jax.ShapeDtypeStruct((rows, length, 4 * width), bfloat),
        jax.ShapeDtypeStruct((rows, length, 8), float32),
        jax.ShapeDtypeStruct((rows, 8, length), float32),
        jax.ShapeDtypeStruct((rows, length, 8), float32),
        jax.ShapeDtypeStruct((group, 1, hidden), float32),
    ]
    out_specs = [inside] * 5 + [outside] * (group + 3)
    out_shape += [jax.ShapeDtypeStruct((2, own, width), bfloat)] * group
    out_shape += [jax.ShapeDtypeStruct((tokens, depth), bfloat)] * 2
    out_shape += [jax.ShapeDtypeStruct(weight_shape, bfloat)]
    scratch = [
        pltpu.VMEM((tokens, depth), bfloat),
        pltpu.VMEM((tokens, depth), bfloat),
        pltpu.VMEM(weight_shape, bfloat),
        pltpu.VMEM((2, tokens, width), bfloat),
        pltpu.VMEM((length, width), bfloat),
        pltpu.VMEM((2, 2, half, half), float32),
        pltpu.SemaphoreType.DMA((9,)),
        pltpu.SemaphoreType.DMA((72,)),
        pltpu.SemaphoreType.DMA((72,)),
    ]
    if fast:
        weight_spec = inside
        out_specs += [outside] * 3
        out_shape += [
            jax.ShapeDtypeStruct((parts // 2, 2, group // 2, 2, pick, c), bfloat) for c in (hidden, hidden, width)
        ]
        scratch += [
            pltpu.VMEM((4, pick, width), bfloat),
            pltpu.VMEM((pick, hidden), bfloat),
            pltpu.VMEM((pick, hidden), bfloat),
            pltpu.VMEM((pick, width), bfloat),
        ]
    else:
        weight_spec = outside
        attn_proj = lax.all_gather(attn_proj.astype(bfloat), "dp", axis=1, tiled=True)
    results = pl.pallas_call(
        functools.partial(attention_forward_kernel, head_size, group, parts if fast else 1, fast),
        in_specs=[outside, outside, weight_spec] + [inside] * 4 + [scalars] + [inside] * 4,
        out_specs=out_specs,
        out_shape=out_shape,
        scratch_shapes=scratch,
        compiler_params=pltpu.CompilerParams(
            vmem_limit_bytes=VMEM_LIMIT, collective_id=0, has_side_effects=True
        ),
    )(
        content, query, attn_proj, up_proj, down_proj, out_proj, up_bias[None], doc_lengths, factor_order,
        segment_ids, table, head_bias.reshape(5, width),
    )
    proj, logsum, facts_row, facts_col, bias_all = results[:5]
    mixed_pieces, results = results[5 : 5 + group], results[5 + group :]
    content_all, query_all, weight_all = results[:3]
    if fast:
        wide = [full.reshape(parts, group, pick, full.shape[-1]) for full in results[3:]]
    else:
        wide = [gather_all(m) for m in (up_proj.astype(bfloat), down_proj.T.astype(bfloat), out_proj.T.astype(bfloat))]
    kept = (content_all, query_all, weight_all, (facts_row, facts_col), proj, logsum)
    return kept, bias_all, mixed_pieces, wide


def attention_backward_kernel(head_size, group, parts, fast, *refs):
    content_hbm, query_hbm, weight_hbm, refs = *refs[:3], refs[3:]
    upper_pieces, dresid_hbm, refs = refs[:group], refs[group], refs[group + 1 :]
    table_ref, turned_ref, bias_ref, row_ref, col_ref, proj_ref, logsum_ref = refs[:7]
    sources, small_ref, refs = refs[7:10], refs[10], refs[11:]
    outputs, refs = refs[:9] if fast else refs[:4], refs[9:] if fast else refs[4:]
    content_grad_ref, query_grad_ref, dhead_ref = outputs[:3]
    content_all, query_all, weight_ref, upper_all, dinput_ref, dweight_ref = refs[:6]
    relative_ref, backward_ref, mask_ref, drel_ref, dcols_ref, dkeys_ref, dvalues_ref = refs[6:13]
    dwide_ref, near_ref, cross_ref, far_ref, dresid_ref, dhead_own, refs = *refs[13:19], refs[19:]
    sems, send_sems, recv_sems, refs = *refs[:3], refs[3:]
    rows, length = row_ref.shape[0], row_ref.shape[2]
    half = length // 2
    depth, width = content_all.shape[1], weight_ref.shape[-1]
    heads = width // head_size
    scale = head_size ** (-0.5)
    factor = scale * LOG2E
    heads_here, dp_here = lax.axis_index("heads"), lax.axis_index("dp")
    chip = heads_here >> 1
    tokens = upper_pieces[0].shape[1]
    links = Links(send_sems, recv_sems)

    def token_part(k):
        return pl.ds(pl.multiple_of((heads_here ^ k) * tokens, tokens), tokens)

    copies = [
        pltpu.make_async_copy(content_hbm, content_all, sems.at[0]),
        pltpu.make_async_copy(query_hbm, query_all, sems.at[1]),
        pltpu.make_async_copy(weight_hbm, weight_ref, sems.at[2]),
        pltpu.make_async_copy(upper_pieces[0], upper_all.at[:, token_part(0)], sems.at[3]),
    ]
    for copy in copies:
        copy.start()
    dresid_copy = pltpu.make_async_copy(dresid_hbm, dresid_ref, sems.at[4])
    dresid_copy.start()

    def weight(kind):
        return weight_ref[kind].reshape(depth, width)

    barrier = pltpu.get_barrier_semaphore()
    peers = [("heads", k) for k in range(1, group)] + [("dp", k) for k in range(1, parts)]
    for axis, k in peers:
        pl.semaphore_signal(
            barrier, inc=1, device_id={axis: lax.axis_index(axis) ^ k}, device_id_type=pl.DeviceIdType.MESH
        )
    pl.semaphore_wait(barrier, len(peers))
    upper_copies = [
        links.push(upper_pieces[k], upper_all.at[:, token_part(0)], "heads", k) for k in range(1, group)
    ]
    for copy in upper_copies:
        copy.start()
    if fast:
        scatters = [
            Scatter(links, sems, 5 + n, sources[n], order, refs[4 * n : 4 * n + 4])
            for n, order in enumerate(("xy", "yx", "yx"))
        ]
        small_got, small_more, small_mid, dweight_got, dweight_more, head_got, tile_ref, tile_got, tile_more = refs[12:]
        for scatter in scatters:
            scatter.begin()
        small_first = [links.push(small_ref, small_got.at[heads_here], "heads", k) for k in range(1, group)]
        for copy in small_first:
            copy.start()
        small_got[heads_here] = small_ref[...]
        small_second = [links.push(small_mid, small_more.at[dp_here], "dp", k) for k in range(1, parts)]
    for copy in copies:
        copy.wait()
    upper_copies[0].wait()
    relative_ref[...] = dot(table_ref[...], weight(3)).astype(jnp.bfloat16)
    backward_ref[...] = dot(turned_ref[...], weight(3)).astype(jnp.bfloat16)
    drel_ref[...] = jnp.zeros_like(drel_ref)
    dweight_ref[...] = jnp.zeros_like(dweight_ref)
    dhead_own[...] = jnp.zeros_like(dhead_own)

    def after(step, place, body):
        if fast:
            @pl.when(step == place)
            def _():
                body()

    def small_middle():
        for copy in small_first:
            copy.wait()
        total = small_got[0]
        for k in range(1, group):
            total = total + small_got[k]
        small_mid[...] = total
        small_more[dp_here] = total
        for copy in small_second:
            copy.start()

    def one_row(step, carry):
        row = jnp.where(step == 0, 0, rows - step)
        row = jnp.where(chip == 0, row, rows - 1 - row)

        @pl.when(step == 1)
        def _():
            for copy in upper_copies[1:]:
                copy.wait()

        row_part(step, row)
        return carry

    def row_part(step, row):
        here = pl.ds(pl.multiple_of(row * length, length), length)
        content_ref, query_ref = content_all.at[here], query_all.at[here]
        facts_row, facts_col = row_ref[row], col_ref[row]
        write_masks(mask_ref, facts_row, facts_col, half)
        roll = roll_matrix(facts_col[:, 3:4], length)
        upper = dot(roll, jnp.concatenate([upper_all[0, here], upper_all[1, here]], -1)).astype(jnp.bfloat16)
        segment_col, segment_row = facts_col[:, 2:3], facts_row[2:3, :]
        down = lax.broadcasted_iota(jnp.int32, (half, half), 0)
        along = lax.broadcasted_iota(jnp.int32, (half, half), 1)
        mirror = jnp.where(down + along == half - 1, 1.0, 0.0).astype(jnp.bfloat16)
        lane = lax.broadcasted_iota(jnp.int32, (length, head_size), 1)
        extra = jnp.where(lane == 0, segment_col, jnp.where(lane == 1, 1.0, 0.0)).astype(jnp.bfloat16)
        for head in range(heads):
            own_cols = slice(head * head_size, (head + 1) * head_size)
            cols = lambda kind: slice(kind * width + head * head_size, kind * width + (head + 1) * head_size)
            bias = [bias_ref[kind : kind + 1, own_cols] for kind in range(5)]
            keys, values = proj_ref[row, :, cols(1)], proj_ref[row, :, cols(2)]
            keys_twice = jnp.concatenate([keys, keys], -1)
            keys_extra = jnp.concatenate([keys, extra], -1)
            relative = relative_ref[:, own_cols]
            relative_twice = jnp.concatenate([relative, relative], -1)
            backward = backward_ref[:, own_cols]
            heads_sums = [jnp.zeros((1, head_size), jnp.float32) for _ in range(5)]
            for stream in range(2):
                with_u, with_w, with_c, own, slope = query_sides(
                    proj_ref[row, :, cols(3 * stream)], bias, segment_col, factor
                )
                index = stream * heads + head
                own = own - logsum_ref[row, :, index : index + 1]
                upper_now = upper[:, index * head_size : (index + 1) * head_size]
                with_u_t, with_w_t, upper_t = with_u.T, with_w.T, upper_now.T
                dquery = []
                for block in range(2):
                    part = slice(block * half, (block + 1) * half)
                    scores = block_scores(
                        with_u[part], with_w[part], keys_twice[part], relative_twice, half
                    )
                    scores = scores + own[part] + slope[part] * segment_row[:, part] + mask_ref[stream, block]
                    chances = jnp.exp2(scores)
                    dchance = dot_nt(upper_now[part], values[part])
                    centre = jnp.sum(chances * dchance, -1, keepdims=True)
                    dscore = (chances * (dchance - centre)).astype(jnp.bfloat16)
                    dvalue_part = dot(upper_t[:, part], chances.astype(jnp.bfloat16))
                    by_key = dot(dscore, keys_extra[part])
                    turned = dot(dscore, mirror)
                    wide = pltpu.roll(
                        jnp.concatenate([turned, jnp.zeros((half, half), jnp.float32)], -1),
                        0, 1, stride=1, stride_axis=0,
                    ).astype(jnp.bfloat16)
                    by_place = dot(wide, backward)
                    dkey_part = dot(with_u_t[:, part], dscore)
                    dkey_part = dkey_part[:head_size] + dkey_part[head_size:]
                    drel_part = dot(with_w_t[:, part], wide)
                    drel_ref[own_cols] += drel_part[:head_size] + drel_part[head_size:]
                    if stream == 0:
                        dkeys_ref[own_cols, part] = dkey_part
                        dvalues_ref[own_cols, part] = dvalue_part
                    else:
                        dkeys_ref[own_cols, part] += dkey_part
                        dvalues_ref[own_cols, part] += dvalue_part
                    with_seg, total = by_key[:, head_size : head_size + 1], by_key[:, head_size + 1 : head_size + 2]
                    seg_i = segment_col[part]
                    seg_one = with_seg + seg_i * (total - 2.0 * with_seg)
                    seg_zero = total - seg_one
                    by_key = by_key[:, :head_size]
                    by_segment = seg_zero * bias[3] + seg_one * bias[4]
                    dquery.append((by_key + by_place + by_segment) * scale)
                    for kind, term in enumerate(
                        (by_key, by_place, by_segment, seg_zero * with_c[part], seg_one * with_c[part])
                    ):
                        heads_sums[kind] = heads_sums[kind] + jnp.sum(term, 0, keepdims=True)
                dcols_ref[:, cols(stream)] = jnp.concatenate(dquery, 0).astype(jnp.bfloat16)
            for kind in range(5):
                dhead_own[kind : kind + 1, own_cols] += heads_sums[kind] * scale
            if fast and head == 0:
                after(step, 1, small_middle)
            if fast and head == heads - 1:
                after(step, 1, lambda: [scatter.second() for scatter in scatters[1:]])
                after(step, 2, lambda: [scatter.third() for scatter in scatters])
        dcols_ref[:, 2 * width : 3 * width] = (dkeys_ref[...] * (1.0 / LOG2E)).astype(jnp.bfloat16).T
        dcols_ref[:, 3 * width :] = dvalues_ref[...].astype(jnp.bfloat16).T
        unroll = unroll_matrix(facts_row[3:4, :], length)
        joined = dot(unroll, dcols_ref[...]).astype(jnp.bfloat16)
        joined_t = joined.T
        content, query = content_ref[...], query_ref[...]
        dweight_ref[0] += dot(joined_t[:width], content) + dot(joined_t[width : 2 * width], query)
        dweight_ref[1] += dot(joined_t[2 * width : 3 * width], content)
        dweight_ref[2] += dot(joined_t[3 * width :], content)
        dinput_ref[0, here] = (
            dot_nt(joined[:, :width], weight(0))
            + dot_nt(joined[:, 2 * width : 3 * width], weight(1))
            + dot_nt(joined[:, 3 * width :], weight(2))
        ).astype(jnp.bfloat16)
        dinput_ref[1, here] = dot_nt(joined[:, width : 2 * width], weight(0)).astype(jnp.bfloat16)
        if fast:
            after(step, 1, scatters[0].second)

    lax.fori_loop(0, rows, one_row, 0)
    drel = drel_ref[...] * (1.0 / LOG2E)
    high = drel.astype(jnp.bfloat16)
    low = (drel - high.astype(jnp.float32)).astype(jnp.bfloat16)
    dweight_ref[3] = dot(high, turned_ref[...]) + dot(low, turned_ref[...])
    cross = [
        links.push(dinput_ref.at[n, token_part(3)], cross_ref.at[n], "heads", 1) for n in range(2)
    ]
    near = [links.push(dinput_ref.at[n, token_part(1)], near_ref.at[n], "heads", 1) for n in range(2)]
    far = [links.push(cross_ref.at[n], far_ref.at[n], "heads", 2) for n in range(2)]
    for copy in cross + near:
        copy.start()
    for kind in range(4):
        turned = dweight_ref[kind].astype(jnp.bfloat16).T
        dwide_ref[kind] = turned.reshape(dwide_ref.shape[1:])
    if fast:
        place_y, place_z = dp_here & 1, dp_here >> 1
        dweight_first = links.push(dwide_ref.at[:, :, 1 - place_y], dweight_got, "dp", 1)
        dweight_first.start()
        head_copies = [links.push(dhead_own, head_got.at[dp_here], "dp", k) for k in range(1, parts)]
        for copy in head_copies:
            copy.start()
        head_got[dp_here] = dhead_own[...]
    for n in range(2):
        cross[n].wait()
        both = cross_ref[n].astype(jnp.float32) + dinput_ref[n, token_part(2)].astype(jnp.float32)
        cross_ref[n] = both.astype(jnp.bfloat16)
        far[n].start()
    if fast:
        dweight_first.wait()
        dweight_second = []
        for kind in range(4):
            dweight_got[kind] = (
                dweight_got[kind].astype(jnp.float32) + dwide_ref[kind, :, place_y].astype(jnp.float32)
            ).astype(jnp.bfloat16)
        for m in range(1, 4):
            dweight_second.append(
                links.push(dweight_got.at[:, place_z ^ m], dweight_more.at[m - 1], "dp", 2 * m)
            )
            dweight_second[-1].start()
        up_share, down_share, out_share, proj_share, small_sum, norm_ref = outputs[3:]
        squares = jnp.zeros((1, 1), jnp.float32)
        for copy in small_second:
            copy.wait()
        total = small_more[0]
        for k in range(1, parts):
            total = total + small_more[k]
        small_sum[...] = total
        squares = squares + square_sum(total) / (group * parts)
        for copy in head_copies:
            copy.wait()
        total = head_got[0]
        for k in range(1, parts):
            total = total + head_got[k]
        dhead_ref[...] = total
        squares = squares + square_sum(total) / parts
        for scatter, share in zip(scatters, (up_share, down_share, out_share)):
            share[...] = scatter.last()
            squares = squares + square_sum(share[...])
        for copy in dweight_second:
            copy.wait()
        for kind in range(4):
            total = dweight_got[kind, place_z].astype(jnp.float32)
            for m in range(1, 4):
                total = total + dweight_more[m - 1, kind].astype(jnp.float32)
            proj_share[kind] = total
            squares = squares + square_sum(total)
        tile_ref[...] = jnp.broadcast_to(squares, tile_ref.shape)
        tile_got[heads_here] = tile_ref[...]
        tile_first = [links.push(tile_ref, tile_got.at[heads_here], "heads", k) for k in range(1, group)]
        for copy in tile_first:
            copy.start()
    else:
        dhead_ref[...] = dhead_own[...]
        outputs[3][...] = dwide_ref[...]
    if fast:
        for copy in tile_first:
            copy.wait()
        total = tile_got[0]
        for k in range(1, group):
            total = total + tile_got[k]
        tile_more[dp_here] = total
        tile_ref[...] = total
        tile_second = [links.push(tile_ref, tile_more.at[dp_here], "dp", k) for k in range(1, parts)]
        for copy in tile_second:
            copy.start()
    dresid_copy.wait()
    for n, place in enumerate((content_grad_ref, query_grad_ref)):
        near[n].wait()
        far[n].wait()
        place[...] = (
            dresid_ref[n]
            + dinput_ref[n, token_part(0)].astype(jnp.float32)
            + near_ref[n].astype(jnp.float32)
            + far_ref[n].astype(jnp.float32)
        )
    if fast:
        for copy in tile_second:
            copy.wait()
        total = tile_more[0]
        for k in range(1, parts):
            total = total + tile_more[k]
        norm_ref[...] = jnp.sqrt(total)


def attention_backward(
    kept, tables, head_bias, upper_pieces, dresid, gradients, small
):
    content_all, query_all, weight_all, facts, proj, logsum = kept
    rows, length = facts[0].shape[0], facts[0].shape[2]
    group = len(upper_pieces)
    fast = weight_all.ndim == 5
    tokens, depth = content_all.shape
    own = tokens // group
    pick, width = weight_all.shape[-2:]
    parts = depth // pick
    head_size = head_bias.shape[-1]
    half = length // 2
    inside = pl.BlockSpec(memory_space=pltpu.VMEM)
    outside = pl.BlockSpec(memory_space=pl.ANY)
    bfloat, float32 = jnp.bfloat16, jnp.float32
    out_shape = [
        jax.ShapeDtypeStruct((own, depth), float32),
        jax.ShapeDtypeStruct((own, depth), float32),
        jax.ShapeDtypeStruct((8, width), float32),
    ]
    wide_shape = (4, parts // 2, 2, pick, width) if fast else (4, pick, width)
    scratch = [
        pltpu.VMEM((tokens, depth), bfloat),
        pltpu.VMEM((tokens, depth), bfloat),
        pltpu.VMEM(weight_all.shape, bfloat),
        pltpu.VMEM((2, tokens, width), bfloat),
        pltpu.VMEM((2, tokens, depth), bfloat),
        pltpu.VMEM((4, width, depth), float32),
        pltpu.VMEM((length, width), bfloat),
        pltpu.VMEM((length, width), bfloat),
        pltpu.VMEM((2, 2, half, half), float32),
        pltpu.VMEM((width, length), float32),
        pltpu.VMEM((length, 4 * width), bfloat),
        pltpu.VMEM((width, length), float32),
        pltpu.VMEM((width, length), float32),
        pltpu.VMEM(wide_shape, bfloat),
        pltpu.VMEM((2, own, depth), bfloat),
        pltpu.VMEM((2, own, depth), bfloat),
        pltpu.VMEM((2, own, depth), bfloat),
        pltpu.VMEM((2, own, depth), float32),
        pltpu.VMEM((8, width), float32),
        pltpu.SemaphoreType.DMA((8,)),
        pltpu.SemaphoreType.DMA((64,)),
        pltpu.SemaphoreType.DMA((64,)),
    ]
    if fast:
        planes = parts // 2
        columns = [gradient.shape[-1] for gradient in gradients]
        out_shape += [jax.ShapeDtypeStruct((pick, c), float32) for c in columns]
        out_shape += [
            jax.ShapeDtypeStruct((4, pick, width), float32),
            jax.ShapeDtypeStruct(small.shape, float32),
            jax.ShapeDtypeStruct((8, 128), float32),
        ]
        gradients = [g.reshape(planes, 2, group // 2, pick, g.shape[-1]) for g in gradients]
        for c in columns:
            scratch += [
                pltpu.VMEM((planes, 2, pick, c), bfloat),
                pltpu.VMEM((planes, 2, pick, c), bfloat),
                pltpu.VMEM((planes, pick, c), bfloat),
                pltpu.VMEM((planes - 1, pick, c), bfloat),
            ]
        scratch += [
            pltpu.VMEM((group,) + small.shape, float32),
            pltpu.VMEM((parts,) + small.shape, float32),
            pltpu.VMEM(small.shape, float32),
            pltpu.VMEM((4, planes, pick, width), bfloat),
            pltpu.VMEM((planes - 1, 4, pick, width), bfloat),
            pltpu.VMEM((parts, 8, width), float32),
            pltpu.VMEM((8, 128), float32),
            pltpu.VMEM((group, 8, 128), float32),
            pltpu.VMEM((parts, 8, 128), float32),
        ]
    else:
        out_shape += [jax.ShapeDtypeStruct(wide_shape, bfloat)]
    return pl.pallas_call(
        functools.partial(attention_backward_kernel, head_size, group, parts, fast),
        in_specs=[outside] * (group + 4) + [inside] * 7 + [outside] * 3 + [inside],
        out_specs=[inside] * len(out_shape),
        out_shape=out_shape,
        scratch_shapes=scratch,
        compiler_params=pltpu.CompilerParams(
            vmem_limit_bytes=VMEM_LIMIT, collective_id=2, has_side_effects=True
        ),
    )(
        content_all, query_all, weight_all, *upper_pieces, dresid, *tables,
        head_bias.reshape(5, width), *facts, proj, logsum, *gradients, small,
    )


def norm_parts(values):
    centred = values - jnp.mean(values, -1, keepdims=True)
    inverse = lax.rsqrt(jnp.mean(centred * centred, -1, keepdims=True) + NORM_EPSILON)
    return centred * inverse, inverse


def norm_back(upstream, normed, inverse, gain):
    scaled = upstream * gain
    first = jnp.mean(scaled, -1, keepdims=True)
    second = jnp.mean(scaled * normed, -1, keepdims=True)
    return inverse * (scaled - first - normed * second)


def column_sum(values):
    return jnp.sum(values, 0, keepdims=True)


def feed_kernel(group, *refs):
    mixed_pieces, refs = refs[:group], refs[group:]
    bias_ref, refs = refs[0], refs[1:]
    content_ref, query_ref, dcontent_ref, dquery_ref, norm_ref, up_hbm, down_hbm, out_hbm = refs[:8]
    content_out, query_out, dresid_ref, refs = refs[8], refs[9], refs[10], refs[11:]
    dmixed_pieces, refs = refs[:group], refs[group:]
    dup_hbm, ddown_hbm, dout_ref, dsmall_ref, refs = refs[0], refs[1], refs[2], refs[3], refs[4:]
    up_ref, down_ref, out_ref, hidden_ref, slope_ref = refs[:5]
    low_ref, low_t_ref, normed_ref, total_ref, up_got, down_got, out_got, out_sent = refs[5:13]
    sems, send_sems, recv_sems = refs[13:]
    own, depth = content_ref.shape
    tokens = 2 * own
    here = lax.axis_index("heads")
    core = here & 1
    chips = group // 2
    loads = [
        pltpu.make_async_copy(out_hbm.at[:, j], out_ref.at[j], sems.at[j]) for j in range(group)
    ]
    loads += [
        pltpu.make_async_copy(up_hbm.at[:, j], up_ref.at[j], sems.at[group + j]) for j in range(group)
    ]
    loads += [
        pltpu.make_async_copy(down_hbm.at[:, j], down_ref.at[j], sems.at[2 * group + j])
        for j in range(group)
    ]
    for load in loads:
        load.start()
    greet("heads", [1])
    gain_one, bias_one, bias_out, gain_two, bias_two = [norm_ref[i : i + 1] for i in range(5)]
    for load in loads[:group]:
        load.wait()
    hidden = up_ref.shape[-1]

    def out_block(k):
        return out_ref[here ^ k].reshape(depth, out_ref.shape[-1])

    total = jnp.concatenate([content_ref[...], query_ref[...]], 0).astype(jnp.float32)
    for k in range(group):
        total = total + dot_nt(mixed_pieces[k][...].reshape(tokens, -1), out_block(k))
    normed, inverse_one = norm_parts(total)
    normed_ref[...] = normed
    middle = normed * gain_one + bias_one
    low_ref[...] = middle.astype(jnp.bfloat16)
    low_t_ref[...] = low_ref[...].T
    total_ref[...] = middle + bias_out
    for load in loads[group:]:
        load.wait()

    def forward(j, carry):
        for part in (slice(0, own), slice(own, tokens)):
            before = dot(low_ref[part], up_ref[j].reshape(depth, hidden)) + bias_ref[j]
            square = before * before
            bent = jnp.tanh(GELU_FACTOR * before * (1.0 + GELU_CUBIC * square))
            half_up = 0.5 * (1.0 + bent)
            hidden_now = (before * half_up).astype(jnp.bfloat16)
            slope_ref[j, part] = half_up + 0.5 * before * (1.0 - bent * bent) * GELU_FACTOR * (
                1.0 + 3.0 * GELU_CUBIC * square
            )
            hidden_ref[j, part] = hidden_now
            total_ref[part] += dot_nt(hidden_now, down_ref[j].reshape(depth, hidden))
        return carry

    lax.fori_loop(0, group, forward, 0)
    normed_two, inverse_two = norm_parts(total_ref[...])
    result = (normed_two * gain_two + bias_two).astype(jnp.bfloat16)
    content_out[...] = result[:own]
    query_out[...] = result[own:]
    upstream = jnp.concatenate([dcontent_ref[...], dquery_ref[...]], 0).astype(jnp.float32)
    dsmall_ref[group + 3 : group + 4] = column_sum(upstream * normed_two)
    dsmall_ref[group + 4 : group + 5] = column_sum(upstream)
    dfinal = norm_back(upstream, normed_two, inverse_two, gain_two)
    dsmall_ref[group + 2 : group + 3] = column_sum(dfinal)
    total_ref[...] = dfinal
    dlow = dfinal.astype(jnp.bfloat16)
    dlow_t = dlow.T

    def to_sibling(source, place, index):
        return pltpu.make_async_remote_copy(
            source, place, send_sems.at[index], recv_sems.at[index],
            device_id={"heads": here ^ 1}, device_id_type=pl.DeviceIdType.MESH,
        )

    def back_block(j):
        ddown = dot(dlow_t, hidden_ref[j])
        bias_grad = jnp.zeros((1, hidden), jnp.float32)
        for part in (slice(0, own), slice(own, tokens)):
            dhidden = dot(dlow[part], down_ref[j].reshape(depth, hidden))
            dbefore = (dhidden * slope_ref[j, part]).astype(jnp.bfloat16)
            bias_grad = bias_grad + column_sum(dbefore.astype(jnp.float32))
            total_ref[part] += dot_nt(dbefore, up_ref[j].reshape(depth, hidden))
            hidden_ref[j, part] = dbefore
        dsmall_ref[pl.ds(j, 1)] = bias_grad
        return dot(low_t_ref[...], hidden_ref[j]), ddown

    def sent(chip):
        j = 2 * chip + 1 - core
        return [
            to_sibling(up_ref.at[j], up_got.at[chip], 2 * chip),
            to_sibling(down_ref.at[j], down_got.at[chip], 2 * chip + 1),
        ]

    def kept(chip):
        j = 2 * chip + core
        return [
            pltpu.make_async_copy(up_ref.at[j], dup_hbm.at[:, chip], sems.at[chip]),
            pltpu.make_async_copy(down_ref.at[j], ddown_hbm.at[:, chip], sems.at[group + chip]),
        ]

    def backward_sent(chip, carry):
        j = 2 * chip + 1 - core
        dup, ddown = back_block(j)
        up_ref[j] = dup.astype(jnp.bfloat16).reshape(up_ref.shape[1:])
        down_ref[j] = ddown.astype(jnp.bfloat16).reshape(down_ref.shape[1:])
        for copy in sent(chip):
            copy.start()
        return carry

    def backward_kept(chip, carry):
        j = 2 * chip + core
        dup, ddown = back_block(j)
        for copy in sent(chip):
            copy.wait_recv()
        dup = dup + up_got[chip].astype(jnp.float32).reshape(depth, hidden)
        ddown = ddown + down_got[chip].astype(jnp.float32).reshape(depth, hidden)
        up_ref[j] = dup.astype(jnp.bfloat16).reshape(up_ref.shape[1:])
        down_ref[j] = ddown.astype(jnp.bfloat16).reshape(down_ref.shape[1:])
        for copy in kept(chip):
            copy.start()
        return carry

    lax.fori_loop(0, chips, backward_sent, 0)
    lax.fori_loop(0, chips, backward_kept, 0)
    dmiddle = total_ref[...]
    normed = normed_ref[...]
    dsmall_ref[group : group + 1] = column_sum(dmiddle * normed)
    dsmall_ref[group + 1 : group + 2] = column_sum(dmiddle)
    dresid = norm_back(dmiddle, normed, inverse_one, gain_one)
    total_ref[...] = dresid
    dresid_copy = pltpu.make_async_copy(total_ref, dresid_ref, sems.at[0])
    dresid_copy.start()
    dlow = dresid.astype(jnp.bfloat16)
    dlow_t = dlow.T
    out_copies = [
        to_sibling(out_sent.at[chip], out_got.at[chip], 2 * chips + chip) for chip in range(chips)
    ]
    for chip in range(chips):
        k = 2 * chip + 1
        mixed = mixed_pieces[k][...].reshape(tokens, -1)
        out_sent[chip] = dot(dlow_t, mixed).astype(jnp.bfloat16).reshape(out_sent.shape[1:])
        out_copies[chip].start()
    for k in range(group):
        dmixed_pieces[k][...] = (
            dot(dlow, out_block(k)).astype(jnp.bfloat16).reshape(dmixed_pieces[k].shape)
        )
    for chip in range(chips):
        k = 2 * chip
        mixed = mixed_pieces[k][...].reshape(tokens, -1)
        dout = dot(dlow_t, mixed)
        out_copies[chip].wait_recv()
        dout = dout + out_got[chip].astype(jnp.float32).reshape(dout.shape)
        dout_ref[:, (here ^ k) >> 1] = dout.astype(jnp.bfloat16).reshape(out_sent.shape[1:])
    dsmall_ref[group + 5 :] = jnp.zeros((dsmall_ref.shape[0] - group - 5, depth), jnp.float32)
    dresid_copy.wait()
    for chip in range(chips):
        for copy in sent(chip):
            copy.wait_send()
        out_copies[chip].wait_send()
        for copy in kept(chip):
            copy.wait()


def feed_layer(mixed_pieces, bias_all, content, query, dcontent, dquery, norm_param, up, down, out):
    group = len(mixed_pieces)
    own, depth = content.shape
    parts, _, pick, hidden = up.shape
    width = out.shape[-1]
    inside = pl.BlockSpec(memory_space=pltpu.VMEM)
    outside = pl.BlockSpec(memory_space=pl.ANY)
    tokens = 2 * own
    results = pl.pallas_call(
        functools.partial(feed_kernel, group),
        in_specs=[inside] * (group + 6) + [outside] * 3,
        out_specs=[inside, inside, outside] + [inside] * group + [outside, outside, inside, inside],
        out_shape=[
            jax.ShapeDtypeStruct((own, depth), jnp.bfloat16),
            jax.ShapeDtypeStruct((own, depth), jnp.bfloat16),
            jax.ShapeDtypeStruct((tokens, depth), jnp.float32),
        ]
        + [jax.ShapeDtypeStruct((2, own, width), jnp.bfloat16)] * group
        + [
            jax.ShapeDtypeStruct((parts, group // 2, pick, hidden), jnp.bfloat16),
            jax.ShapeDtypeStruct((parts, group // 2, pick, hidden), jnp.bfloat16),
            jax.ShapeDtypeStruct((parts, group // 2, pick, width), jnp.bfloat16),
            jax.ShapeDtypeStruct((16, depth), jnp.float32),
        ],
        scratch_shapes=[
            pltpu.VMEM((group, parts, pick, hidden), jnp.bfloat16),
            pltpu.VMEM((group, parts, pick, hidden), jnp.bfloat16),
            pltpu.VMEM((group, parts, pick, width), jnp.bfloat16),
            pltpu.VMEM((group, tokens, hidden), jnp.bfloat16),
            pltpu.VMEM((group, tokens, hidden), jnp.float32),
            pltpu.VMEM((tokens, depth), jnp.bfloat16),
            pltpu.VMEM((depth, tokens), jnp.bfloat16),
            pltpu.VMEM((tokens, depth), jnp.float32),
            pltpu.VMEM((tokens, depth), jnp.float32),
            pltpu.VMEM((group // 2, parts, pick, hidden), jnp.bfloat16),
            pltpu.VMEM((group // 2, parts, pick, hidden), jnp.bfloat16),
            pltpu.VMEM((group // 2, parts, pick, width), jnp.bfloat16),
            pltpu.VMEM((group // 2, parts, pick, width), jnp.bfloat16),
            pltpu.SemaphoreType.DMA((3 * group,)),
            pltpu.SemaphoreType.DMA((3 * group // 2,)),
            pltpu.SemaphoreType.DMA((3 * group // 2,)),
        ],
        compiler_params=pltpu.CompilerParams(
            vmem_limit_bytes=VMEM_LIMIT, collective_id=1, has_side_effects=True
        ),
    )(*mixed_pieces, bias_all, content, query, dcontent, dquery, norm_param, up, down, out)
    return results[0], results[1], results[2].reshape(2, own, depth), results[3 : 3 + group], results[3 + group :]


def exchange(value, axis, mask):
    return lax.ppermute(value, axis, [(i, i ^ mask) for i in range(lax.axis_size(axis))])


def total_over(value, axis):
    mask = 1
    while mask < lax.axis_size(axis):
        value = value + exchange(value, axis, mask)
        mask = 2 * mask
    return value


def by_pieces(pick):
    return lax.axis_size("dp") <= 8 and pick % 16 == 0


def reduce_projection(pieces):
    return lax.psum_scatter(pieces[0], "dp", scatter_dimension=1, tiled=True).astype(jnp.float32)


def gather_all(own):
    dp, heads = lax.axis_size("dp"), lax.axis_size("heads")
    rows, columns = own.shape
    full = lax.all_gather(own, ("dp", "heads"), axis=0, tiled=False).reshape(dp, heads, rows, columns)
    if by_pieces(rows):
        return full
    return jnp.swapaxes(full, 0, 1).reshape(1, heads, dp * rows, columns)


def scatter_all(full):
    chip = lax.axis_index("heads") // 2
    mine = lax.dynamic_index_in_dim(full[0], chip, 0, False)
    theirs = lax.dynamic_index_in_dim(full[0], 1 - chip, 0, False)
    mine = mine.astype(jnp.float32) + exchange(theirs, "heads", 2).astype(jnp.float32)
    return lax.psum_scatter(mine, "dp", scatter_dimension=0, tiled=True)


def adam_step(master, first, second, gradient, factor, decayed):
    clipped = gradient * factor
    new_first = BETA_ONE * first + (1.0 - BETA_ONE) * clipped
    new_second = BETA_TWO * second + (1.0 - BETA_TWO) * clipped * clipped
    first_hat = new_first / (1.0 - BETA_ONE**STEP)
    second_hat = new_second / (1.0 - BETA_TWO**STEP)
    update = first_hat / (jnp.sqrt(second_hat) + ADAM_EPSILON)
    if decayed:
        update = update + WEIGHT_DECAY * master
        return (new_first, new_second, master - MATRIX_RATE * update)
    return (new_first, new_second, master - VECTOR_RATE * update)


def local(
    content_in,
    query_in,
    content_grad,
    query_grad,
    segment_ids,
    doc_lengths,
    factor_order,
    attn_proj,
    attn_proj_first,
    attn_proj_second,
    out_proj,
    out_proj_first,
    out_proj_second,
    up_proj,
    up_proj_first,
    up_proj_second,
    down_proj,
    down_proj_first,
    down_proj_second,
    head_bias,
    head_bias_first,
    head_bias_second,
    up_bias,
    up_bias_first,
    up_bias_second,
    norm_param,
    norm_param_first,
    norm_param_second,
):
    width = content_in.shape[1]
    length = segment_ids.shape[1]
    table = position_table(length, width)
    tables = (jnp.asarray(table), jnp.asarray(table[::-1].copy()))
    kept, bias_all, mixed_pieces, (up_full, down_full, out_full) = attention_forward(
        content_in, query_in, attn_proj, up_proj, down_proj, out_proj, up_bias, doc_lengths, factor_order,
        segment_ids, tables[0], head_bias,
    )
    content_out, query_out, dresid, dmixed_pieces, (dup, ddown, dout, dsmall) = feed_layer(
        mixed_pieces, bias_all, content_in, query_in, content_grad, query_grad, norm_param,
        up_full, down_full, out_full,
    )
    backward = attention_backward(
        kept, tables, head_bias, dmixed_pieces, dresid, (dup, ddown, dout), dsmall
    )
    heads_count, head_index = lax.axis_size("heads"), lax.axis_index("heads")
    if by_pieces(attn_proj.shape[1]):
        input_grad, dhead = backward[:2], backward[2]
        up_share, down_share, out_share, proj_share, small_sum, norm_tile = backward[3:]
        grad_norm = norm_tile[0, 0]
    else:
        input_grad, dhead = backward[:2], total_over(backward[2], "dp")
        proj_share = reduce_projection([backward[3]])
        up_share, down_share, out_share = scatter_all(dup), scatter_all(ddown), scatter_all(dout)
        small_sum = total_over(total_over(dsmall, "heads"), "dp")
        squares = sum(jnp.sum(share * share) for share in (up_share, down_share, out_share, proj_share))
        squares = squares + jnp.sum(dhead * dhead) / lax.axis_size("dp")
        squares = squares + jnp.sum(small_sum * small_sum) / (lax.axis_size("dp") * heads_count)
        grad_norm = jnp.sqrt(total_over(total_over(squares.reshape(1, 1), "heads"), "dp"))[0, 0]
    down_share, out_share = down_share.T, out_share.T
    head_grad = dhead[:5].reshape(head_bias.shape)
    bias_sum, norm_sum = small_sum[:heads_count], small_sum[heads_count : heads_count + 5]
    bias_grad = lax.dynamic_slice_in_dim(bias_sum, head_index, 1, 0)[0]
    factor = CLIP_NORM / jnp.maximum(grad_norm, CLIP_NORM)
    attn_first, attn_second, attn_new = adam_step(
        attn_proj, attn_proj_first, attn_proj_second, proj_share, factor, True
    )
    out_first, out_second, out_new = adam_step(
        out_proj, out_proj_first, out_proj_second, out_share, factor, True
    )
    up_first, up_second, up_new = adam_step(
        up_proj, up_proj_first, up_proj_second, up_share, factor, True
    )
    down_first, down_second, down_new = adam_step(
        down_proj, down_proj_first, down_proj_second, down_share, factor, True
    )
    head_first, head_second, head_new = adam_step(
        head_bias, head_bias_first, head_bias_second, head_grad, factor, False
    )
    bias_first, bias_second, bias_new = adam_step(
        up_bias, up_bias_first, up_bias_second, bias_grad, factor, False
    )
    norm_first, norm_second, norm_new = adam_step(
        norm_param, norm_param_first, norm_param_second, norm_sum, factor, False
    )
    return (
        content_out,
        query_out,
        input_grad[0],
        input_grad[1],
        grad_norm,
        proj_share,
        attn_first,
        attn_second,
        attn_new,
        out_share,
        out_first,
        out_second,
        out_new,
        up_share,
        up_first,
        up_second,
        up_new,
        down_share,
        down_first,
        down_second,
        down_new,
        head_grad,
        head_first,
        head_second,
        head_new,
        bias_grad,
        bias_first,
        bias_second,
        bias_new,
        norm_sum,
        norm_first,
        norm_second,
        norm_new,
    )


def solution(mesh):
    return jax.shard_map(
        local,
        mesh=mesh,
        in_specs=(
            P(("dp", "heads"), None),
            P(("dp", "heads"), None),
            P(("dp", "heads"), None),
            P(("dp", "heads"), None),
            P("dp", None),
            P("dp", None),
            P("dp", None),
            P(None, "dp", "heads"),
            P(None, "dp", "heads"),
            P(None, "dp", "heads"),
            P("heads", "dp"),
            P("heads", "dp"),
            P("heads", "dp"),
            P("dp", "heads"),
            P("dp", "heads"),
            P("dp", "heads"),
            P("heads", "dp"),
            P("heads", "dp"),
            P("heads", "dp"),
            P(None, "heads", None),
            P(None, "heads", None),
            P(None, "heads", None),
            P("heads"),
            P("heads"),
            P("heads"),
            P(),
            P(),
            P(),
        ),
        out_specs=(
            P(("dp", "heads"), None),
            P(("dp", "heads"), None),
            P(("dp", "heads"), None),
            P(("dp", "heads"), None),
            P(),
            P(None, "dp", "heads"),
            P(None, "dp", "heads"),
            P(None, "dp", "heads"),
            P(None, "dp", "heads"),
            P("heads", "dp"),
            P("heads", "dp"),
            P("heads", "dp"),
            P("heads", "dp"),
            P("dp", "heads"),
            P("dp", "heads"),
            P("dp", "heads"),
            P("dp", "heads"),
            P("heads", "dp"),
            P("heads", "dp"),
            P("heads", "dp"),
            P("heads", "dp"),
            P(None, "heads", None),
            P(None, "heads", None),
            P(None, "heads", None),
            P(None, "heads", None),
            P("heads"),
            P("heads"),
            P("heads"),
            P("heads"),
            P(),
            P(),
            P(),
            P(),
        ),
        check_vma=False,
    )
```

```python
import functools

import jax
import jax.numpy as jnp
import ml_dtypes
import numpy as np
from jax import lax
from jax.experimental import pallas as pl
from jax.experimental.pallas import tpu as pltpu
from jax.sharding import PartitionSpec as P

STEP = 10


NORM_EPSILON = 1e-05
CLIP_NORM = 1.0
MATRIX_RATE = 0.08
VECTOR_RATE = 0.5
BETA_ONE = 0.9
BETA_TWO = 0.999
ADAM_EPSILON = 1e-08
WEIGHT_DECAY = 0.01
MASKED_SCORE = -1e30
GELU_FACTOR = 0.7978845608028654
GELU_CUBIC = 0.044715
LOG2E = 1.4426950408889634
VMEM_LIMIT = 56 << 20


def position_table(length, width):
    distance = length // 2 - np.arange(length)
    frequency = 10000.0 ** (-np.arange(0, width, 2) / width)
    angles = distance[:, None] * frequency[None, :]
    return np.concatenate([np.sin(angles), np.cos(angles)], -1).astype(np.float32).astype(ml_dtypes.bfloat16)


def dot(left, right):
    return lax.dot_general(left, right, (((1,), (0,)), ((), ())), preferred_element_type=jnp.float32)


def dot_nt(left, right):
    return lax.dot_general(left, right, (((1,), (1,)), ((), ())), preferred_element_type=jnp.float32)


def split_pair(values):
    high = values.astype(jnp.bfloat16)
    low = (values - high.astype(jnp.float32)).astype(jnp.bfloat16)
    return jnp.concatenate([high, low], -1)


def roll_matrix(token_col, length):
    lanes = lax.broadcasted_iota(jnp.int32, (length, length), 1).astype(jnp.float32)
    return jnp.where(token_col == lanes, 1.0, 0.0).astype(jnp.bfloat16)


def unroll_matrix(token_row, length):
    places = lax.broadcasted_iota(jnp.int32, (length, length), 0).astype(jnp.float32)
    return jnp.where(token_row == places, 1.0, 0.0).astype(jnp.bfloat16)


def write_masks(mask_ref, facts_row, facts_col, half):
    for block in range(2):
        part = slice(block * half, (block + 1) * half)
        code_i, base_i = facts_col[part, 0:1], facts_col[part, 1:2]
        code_j = facts_row[0:1, part]
        same = code_j >= base_i
        mask_ref[0, block] = jnp.where(same & (code_j <= code_i), 0.0, MASKED_SCORE)
        mask_ref[1, block] = jnp.where(same & (code_j < code_i), 0.0, MASKED_SCORE)


def query_sides(query, bias, segment_col, factor):
    wide = query.astype(jnp.float32)
    with_u = split_pair((wide + bias[0]) * factor)
    with_w = split_pair((wide + bias[1]) * factor)
    with_c = wide + bias[2]
    same = jnp.sum(with_c * bias[3], -1, keepdims=True) * factor
    change = jnp.sum(with_c * (bias[4] - bias[3]), -1, keepdims=True) * factor
    return with_u, with_w, with_c, same + change * segment_col, change * (1.0 - 2.0 * segment_col)


def block_scores(with_u, with_w, keys_twice, relative_twice, half):
    content = dot_nt(with_u, keys_twice)
    position = dot_nt(with_w, relative_twice)
    return content + pltpu.roll(position, half, 1, stride=1, stride_axis=0)[:, :half]


def greet(axis, masks):
    barrier = pltpu.get_barrier_semaphore()
    for mask in masks:
        pl.semaphore_signal(
            barrier, inc=1, device_id={axis: lax.axis_index(axis) ^ mask}, device_id_type=pl.DeviceIdType.MESH
        )
    pl.semaphore_wait(barrier, len(masks))


class Links:
    def __init__(self, send_sems, recv_sems):
        self.send_sems, self.recv_sems, self.used = send_sems, recv_sems, 0

    def push(self, source, place, axis, distance):
        index = self.used
        self.used = index + 1
        return pltpu.make_async_remote_copy(
            source, place, self.send_sems.at[index], self.recv_sems.at[index],
            device_id={axis: lax.axis_index(axis) ^ distance}, device_id_type=pl.DeviceIdType.MESH,
        )


def add_planes(place, first, second):
    def one(z, carry):
        place[z] = (first(z).astype(jnp.float32) + second[z].astype(jnp.float32)).astype(place.dtype)
        return carry

    lax.fori_loop(0, place.shape[0], one, 0)


class Scatter:
    def __init__(self, links, sem, source, rows, order, refs):
        self.kept, self.got, self.got_two, self.got_last = refs
        heads_here, dp_here = lax.axis_index("heads"), lax.axis_index("dp")
        x, y, z = heads_here >> 1, dp_here & 1, dp_here >> 1
        if order == "xy":
            own, other, first, second, self.mine = source.at[:, :, x, rows], source.at[:, :, 1 - x, rows], ("heads", 2), ("dp", 1), y
        else:
            own, other, first, second, self.mine = source.at[:, y, :, rows], source.at[:, 1 - y, :, rows], ("dp", 1), ("heads", 2), x
        self.load = pltpu.make_async_copy(own, self.kept, sem)
        self.copy = links.push(other, self.got, *first)
        self.copy_two = links.push(self.kept.at[:, 1 - self.mine], self.got_two, *second)
        self.place = z
        self.copies_last = [
            links.push(self.got_two.at[z ^ m], self.got_last.at[m - 1], "dp", 2 * m)
            for m in range(1, source.shape[0])
        ]

    def begin(self):
        self.load.start()
        self.copy.start()

    def second(self):
        self.load.wait()
        self.copy.wait()
        add_planes(self.kept, lambda z: self.kept[z], self.got)
        self.copy_two.start()

    def third(self):
        self.copy_two.wait()
        add_planes(self.got_two, lambda z: self.kept[z, self.mine], self.got_two)
        for copy in self.copies_last:
            copy.start()

    def last(self):
        for copy in self.copies_last:
            copy.wait()
        total = self.got_two[self.place].astype(jnp.float32)
        for index in range(self.got_last.shape[0]):
            total = total + self.got_last[index].astype(jnp.float32)
        return total


def square_sum(values):
    return jnp.sum(jnp.sum(values * values, -1, keepdims=True), 0, keepdims=True)


def unit_copies(links, source, places, starts, size, base):
    heads_here = lax.axis_index("heads")
    own = places.shape[1]
    copies = []
    for start in starts:
        owner = start // own
        distance = owner ^ heads_here
        index = links.used
        links.used = index + 1
        copies.append(
            pltpu.make_async_remote_copy(
                source.at[pl.ds(pl.multiple_of(start, size), size)],
                places.at[distance, pl.ds(pl.multiple_of(start - owner * own, size), size)],
                links.send_sems.at[index], links.recv_sems.at[base + distance],
                device_id={"heads": owner}, device_id_type=pl.DeviceIdType.MESH,
            )
        )
    return copies


class Gather:
    def __init__(self, links, sem, full, own, rows, order):
        heads_here, dp_here = lax.axis_index("heads"), lax.axis_index("dp")
        x, core, y, z = heads_here >> 1, heads_here & 1, dp_here & 1, dp_here >> 1

        def same(*place):
            part = full.at[place + (rows,)]
            return part, part

        everything = slice(None)
        planes = full.shape[0]
        mine = full.at[z, y, x, core, rows]
        self.keep = pltpu.make_async_copy(own.at[rows], mine, sem)
        self.along_z = [links.push(own.at[rows], mine, "dp", 2 * m) for m in range(1, planes)]
        column = same(everything, y, x, core)
        across = ("heads", 2), ("dp", 1)
        if order == "xy":
            near, wide = same(everything, y, 1 - x, core), same(everything, y, everything, core)
            last = same(everything, 1 - y, everything, core)
        else:
            near, wide = same(everything, 1 - y, x, core), same(everything, everything, x, core)
            last = same(everything, everything, 1 - x, core)
            across = across[1], across[0]
        self.first = links.push(*column, *across[0])
        self.second = links.push(*wide, *across[1])
        self.to_sibling = [links.push(*part, "heads", 1) for part in (column, near, last)]

    def begin(self):
        self.keep.start()
        for copy in self.along_z:
            copy.start()

    def step_one(self):
        self.keep.wait()
        for copy in self.along_z:
            copy.wait()
        self.first.start()
        self.to_sibling[0].start()

    def step_two(self):
        self.first.wait()
        self.second.start()
        self.to_sibling[1].start()

    def step_three(self):
        self.second.wait()
        self.to_sibling[2].start()

    def finish(self):
        for copy in self.to_sibling:
            copy.wait()


def write_facts(lengths_ref, order_ref, segment_ref, row_ref, col_ref):
    rows, length = order_ref.shape
    down = lax.broadcasted_iota(jnp.int32, (length, length), 0).astype(jnp.float32)
    along = lax.broadcasted_iota(jnp.int32, (length, length), 1).astype(jnp.float32)
    places_col, places_row = down[:, 0:1], along[0:1, :]
    row_ref[...] = jnp.zeros_like(row_ref)
    col_ref[...] = jnp.zeros_like(col_ref)

    def as_column(values):
        return jnp.sum(jnp.where(down == along, values, 0.0), 1, keepdims=True)

    for row in range(rows):
        ends, start, end = [], 0, 0
        for document in range(lengths_ref.shape[1]):
            count = lengths_ref[row, document]
            start = start + (count == length // 2).astype(jnp.int32) * end
            end = end + count
            ends.append(end.astype(jnp.float32))
        start = start.astype(jnp.float32)
        order = order_ref[row : row + 1].astype(jnp.float32)
        segment = segment_ref[row : row + 1].astype(jnp.float32)
        order_col, segment_col = as_column(order), as_column(segment)
        for place, turned in ((places_row, False), (places_col, True)):
            token = place + start
            token = jnp.where(token >= length, token - length, token)
            base = jnp.zeros_like(token)
            for end in ends:
                base = base + jnp.where(token >= end, float(length), 0.0)
            if turned:
                rank = jnp.sum(jnp.where(order == token, along, 0.0), 1, keepdims=True)
                kind = jnp.sum(jnp.where(along == token, segment, 0.0), 1, keepdims=True)
                for index, values in enumerate((base + rank, base, kind, token)):
                    col_ref[row, :, index : index + 1] = values
            else:
                rank = jnp.sum(jnp.where(order_col == token, down, 0.0), 0, keepdims=True)
                kind = jnp.sum(jnp.where(down == token, segment_col, 0.0), 0, keepdims=True)
                for index, values in enumerate((base + rank, base, kind, token)):
                    row_ref[row, index : index + 1] = values


def turn(values):
    size = values.shape[1]
    same = lax.broadcasted_iota(jnp.int32, (size, size), 0) == lax.broadcasted_iota(jnp.int32, (size, size), 1)
    identity = jnp.where(same, 1.0, 0.0).astype(jnp.bfloat16)
    return dot_nt(identity, values.astype(jnp.bfloat16)).astype(jnp.bfloat16)


def attention_forward_kernel(head_size, group, parts, fast, *refs):
    content_hbm, query_hbm, weight_in, up_in, down_in, out_in, bias_in, refs = *refs[:7], refs[7:]
    lengths_ref, order_ref, segment_ref, table_ref, head_ref, refs = *refs[:5], refs[5:]
    proj_ref, row_ref, col_ref, bias_all, refs = *refs[:4], refs[4:]
    mixed_pieces, refs = refs[0], refs[1:]
    content_out, query_out, weight_out, chance_out, refs = *refs[:4], refs[4:]
    if fast:
        up_all, down_all, out_all, refs = *refs[:3], refs[3:]
    content_all, query_all, weight_ref, mixed_ref, relative_ref, mask_ref, chance_ref, refs = *refs[:7], refs[7:]
    sems, send_sems, recv_sems, refs = *refs[:3], refs[3:]
    rows, length = row_ref.shape[0], row_ref.shape[2]
    half = length // 2
    tokens, depth = content_hbm.shape
    width = weight_ref.shape[-1] // 4
    heads = width // head_size
    factor = head_size ** (-0.5) * LOG2E
    heads_here, dp_here = lax.axis_index("heads"), lax.axis_index("dp")
    chip = heads_here >> 1
    links = Links(send_sems, recv_sems)

    def token_part(k):
        return pl.ds(pl.multiple_of((heads_here ^ k) * tokens, tokens), tokens)

    streams = ((content_hbm, content_all), (query_hbm, query_all))
    local = [pltpu.make_async_copy(own, full.at[token_part(0)], sems.at[n]) for n, (own, full) in enumerate(streams)]
    if not fast:
        local.append(pltpu.make_async_copy(weight_in, weight_ref, sems.at[2]))
    for copy in local:
        copy.start()
    barrier = pltpu.get_barrier_semaphore()
    peers = [("heads", k) for k in range(1, group)] + [("dp", k) for k in range(1, parts)]
    for axis, k in peers:
        pl.semaphore_signal(
            barrier, inc=1, device_id={axis: lax.axis_index(axis) ^ k}, device_id_type=pl.DeviceIdType.MESH
        )
    if fast:
        weight_send, up_send, down_send, out_send = refs
        weight_send[...] = jnp.concatenate([weight_in[kind] for kind in range(4)], -1).astype(jnp.bfloat16)
    pl.semaphore_wait(barrier, len(peers))
    far = [links.push(own, full.at[token_part(0)], "heads", 2) for own, full in streams]
    near = [links.push(own, full.at[token_part(0)], "heads", 1) for own, full in streams]
    passed = [links.push(full.at[token_part(2)], full.at[token_part(2)], "heads", 1) for _, full in streams]
    bias_copies = [links.push(bias_in, bias_all.at[heads_here], "heads", k) for k in range(1, group)]
    for copy in far + near + bias_copies:
        copy.start()
    if fast:
        y, z = dp_here & 1, dp_here >> 1
        weight_z, weight_y = [], []
        for pair in (pl.ds(0, 2 * width), pl.ds(2 * width, 2 * width)):
            mine = weight_ref.at[z, y, :, pair]
            weight_z.append([links.push(weight_send.at[:, pair], mine, "dp", 2 * m) for m in range(1, parts // 2)])
            column = weight_ref.at[:, y, :, pair]
            weight_y.append(links.push(column, column, "dp", 1))
            for copy in weight_z[-1]:
                copy.start()
        weight_ref[z, y] = weight_send[...]
        up_send[...] = up_in[...].astype(jnp.bfloat16)
        down_send[...] = down_in[...].astype(jnp.bfloat16)
        out_send[...] = turn(out_in[...])
        pick = up_send.shape[0]
        early, late = pl.ds(0, pick // 2), pl.ds(pick // 2, pick // 2)
        up_one = Gather(links, sems.at[3], up_all, up_send, early, "xy")
        up_two = Gather(links, sems.at[4], up_all, up_send, late, "xy")
        down_one = Gather(links, sems.at[5], down_all, down_send, early, "yx")
        down_two = Gather(links, sems.at[6], down_all, down_send, late, "xy")
        out_one = Gather(links, sems.at[7], out_all, out_send, pl.ds(0, pick), "yx")
        gathers = (up_one, up_two, down_one, down_two, out_one)
    bias_all[heads_here] = bias_in[...]
    write_facts(lengths_ref, order_ref, segment_ref, row_ref, col_ref)
    if fast:
        for first, second in zip(weight_z, weight_y):
            for copy in first:
                copy.wait()
            second.start()
        down_one.begin()
        out_one.begin()
        for copy in weight_y[:1]:
            copy.wait()
        up_one.begin()
        weight_y[1].wait()
    for copy in local + near:
        copy.wait()

    def weight(first, last):
        return weight_ref[..., first * width : last * width].reshape(depth, (last - first) * width)

    saves = [
        pltpu.make_async_copy(content_all, content_out, sems.at[0]),
        pltpu.make_async_copy(query_all, query_out, sems.at[1]),
        pltpu.make_async_copy(weight_ref, weight_out, sems.at[2]),
    ]
    saves[2].start()
    relative_ref[...] = dot(table_ref[...], weight(3, 4)).astype(jnp.bfloat16)

    def pass_on():
        for arrived, onward in zip(far, passed):
            arrived.wait()
            onward.start()

    def nothing():
        pass

    events = {(0, 0): [pass_on]}
    if fast:
        events = {
            (0, 0): [pass_on, down_one.step_one, up_two.begin],
            (0, 1): [up_one.step_one, down_two.begin],
            (0, 2): [out_one.step_one, down_one.step_two],
            (1, 0): [up_one.step_two, up_two.step_one],
            (1, 1): [down_two.step_one, out_one.step_two],
            (1, 2): [up_two.step_two, down_one.step_three],
            (2, 0): [down_two.step_two, up_one.step_three],
            (2, 1): [out_one.step_three],
        }

    def one_row(step, carry):
        row = jnp.where(step == 0, 0, rows - step)
        row = jnp.where(chip == 0, row, rows - 1 - row)

        @pl.when(step == 1)
        def _():
            for copy in passed:
                copy.wait()
            for save in saves[:2]:
                save.start()

        here = pl.ds(pl.multiple_of(row * length, length), length)
        facts_row, facts_col = row_ref[row], col_ref[row]
        write_masks(mask_ref, facts_row, facts_col, half)
        roll = roll_matrix(facts_col[:, 3:4], length)
        unroll = unroll_matrix(facts_row[3:4, :], length)
        content, query = content_all[here], query_all[here]
        joined = jnp.concatenate(
            [
                dot(content, weight(0, 3)).astype(jnp.bfloat16),
                dot(query, weight(0, 1)).astype(jnp.bfloat16),
            ],
            -1,
        )
        proj_ref[row] = dot(roll, joined).astype(jnp.bfloat16)
        segment_col, segment_row = facts_col[:, 2:3], facts_row[2:3, :]
        mixed = [[None] * heads, [None] * heads]
        for head in range(heads):
            cols = lambda kind: slice(kind * width + head * head_size, kind * width + (head + 1) * head_size)
            own_cols = slice(head * head_size, (head + 1) * head_size)
            bias = [head_ref[kind, head : head + 1] for kind in range(5)]
            keys, values = proj_ref[row, :, cols(1)], proj_ref[row, :, cols(2)]
            keys_twice = jnp.concatenate([keys, keys], -1)
            relative = relative_ref[:, own_cols]
            relative_twice = jnp.concatenate([relative, relative], -1)
            for stream in range(2):
                with_u, with_w, _, own, slope = query_sides(
                    proj_ref[row, :, cols(3 * stream)], bias, segment_col, factor
                )
                pieces = []
                for block in range(2):
                    part = slice(block * half, (block + 1) * half)
                    scores = block_scores(
                        with_u[part], with_w[part], keys_twice[part], relative_twice, half
                    )
                    scores = scores + own[part] + slope[part] * segment_row[:, part] + mask_ref[stream, block]
                    highest = jnp.maximum(jnp.max(scores, -1, keepdims=True), 0.0)
                    weights = jnp.exp2(scores - highest)
                    totals = jnp.exp2(-highest) + jnp.sum(weights, -1, keepdims=True)
                    chances = (weights * (1.0 / totals)).astype(jnp.bfloat16)
                    chance_ref[row, stream * heads + head, block] = chances
                    pieces.append(dot(chances, values[part]))
                mixed[stream][head] = jnp.concatenate(pieces, 0).astype(jnp.bfloat16)
            for when, actions in events.items():
                if when[1] == head:
                    @pl.when(step == when[0])
                    def _():
                        for action in actions:
                            action()
        both = jnp.concatenate(mixed[0] + mixed[1], -1)
        mixed_ref[here] = dot(unroll, both).astype(jnp.bfloat16)
        chance_copy(row).start()

        @pl.when(step == 1)
        def _():
            for copy in far_units:
                copy.start()

        return carry

    def chance_copy(row):
        return pltpu.make_async_copy(chance_ref.at[row], chance_out.at[row], sems.at[9 + row])

    unit = half // 2
    far_row = jnp.where(chip == 0, (rows - 1) * length, 0)
    far_middle = jnp.where(chip == 0, length + half, length)
    base = links.used
    links.used = base + group
    far_units = unit_copies(links, mixed_ref, mixed_pieces, [far_row + n * unit for n in range(4)], unit, base)
    middle_units = unit_copies(links, mixed_ref, mixed_pieces, [far_middle + n * unit for n in range(2)], unit, base)
    far_pieces = [
        pltpu.make_async_remote_copy(
            mixed_pieces.at[k], mixed_pieces.at[k], send_sems.at[base + k], recv_sems.at[base + k],
            device_id={"heads": heads_here ^ k}, device_id_type=pl.DeviceIdType.MESH,
        )
        for k in (2, 3)
    ]
    lax.fori_loop(0, rows, one_row, 0)
    for copy in middle_units:
        copy.start()
    keep = pltpu.make_async_copy(mixed_ref.at[token_part(0)], mixed_pieces.at[0], sems.at[8])
    keep.start()
    sends = [links.push(mixed_ref.at[token_part(1)], mixed_pieces.at[1], "heads", 1)]
    for copy in sends:
        copy.start()
    if fast:
        up_two.step_three()
        down_two.step_three()
    for copy in [keep] + saves + sends + bias_copies:
        copy.wait()
    for copy in far_units + middle_units:
        copy.wait_send()
    for row in range(rows):
        chance_copy(row).wait()
    for piece in far_pieces:
        piece.wait_recv()
    if fast:
        for gather in gathers:
            gather.finish()


def attention_forward(
    content, query, attn_proj, up_proj, down_proj, out_proj, up_bias, doc_lengths, factor_order, segment_ids,
    table, head_bias,
):
    rows, length = segment_ids.shape
    group, parts = lax.axis_size("heads"), lax.axis_size("dp")
    fast = by_pieces(attn_proj.shape[1])
    own, depth = content.shape
    tokens = own * group
    pick, width = attn_proj.shape[1:]
    hidden = up_proj.shape[1]
    head_size = head_bias.shape[-1]
    half = length // 2
    inside = pl.BlockSpec(memory_space=pltpu.VMEM)
    outside = pl.BlockSpec(memory_space=pl.ANY)
    scalars = pl.BlockSpec(memory_space=pltpu.SMEM)
    bfloat, float32 = jnp.bfloat16, jnp.float32
    weight_shape = (parts // 2, 2, pick, 4 * width) if fast else (depth, 4 * width)
    out_shape = [
        jax.ShapeDtypeStruct((rows, length, 4 * width), bfloat),
        jax.ShapeDtypeStruct((rows, 8, length), float32),
        jax.ShapeDtypeStruct((rows, length, 8), float32),
        jax.ShapeDtypeStruct((group, 1, hidden), float32),
    ]
    out_specs = [inside] * 4 + [outside] * 5
    out_shape += [jax.ShapeDtypeStruct((group, own, 2 * width), bfloat)]
    out_shape += [jax.ShapeDtypeStruct((tokens, depth), bfloat)] * 2
    out_shape += [jax.ShapeDtypeStruct(weight_shape, bfloat)]
    chance_shape = (rows, 2 * width // head_size, 2, half, half)
    out_shape += [jax.ShapeDtypeStruct(chance_shape, bfloat)]
    scratch = [
        pltpu.VMEM((tokens, depth), bfloat),
        pltpu.VMEM((tokens, depth), bfloat),
        pltpu.VMEM(weight_shape, bfloat),
        pltpu.VMEM((tokens, 2 * width), bfloat),
        pltpu.VMEM((length, width), bfloat),
        pltpu.VMEM((2, 2, half, half), float32),
        pltpu.VMEM(chance_shape, bfloat),
        pltpu.SemaphoreType.DMA((9 + rows,)),
        pltpu.SemaphoreType.DMA((72,)),
        pltpu.SemaphoreType.DMA((72,)),
    ]
    if fast:
        weight_spec = inside
        out_specs += [outside] * 3
        out_shape += [
            jax.ShapeDtypeStruct((parts // 2, 2, group // 2, 2, pick, c), bfloat) for c in (hidden, hidden, width)
        ]
        scratch += [
            pltpu.VMEM((pick, 4 * width), bfloat),
            pltpu.VMEM((pick, hidden), bfloat),
            pltpu.VMEM((pick, hidden), bfloat),
            pltpu.VMEM((pick, width), bfloat),
        ]
    else:
        weight_spec = outside
        attn_proj = lax.all_gather(attn_proj.astype(bfloat), "dp", axis=1, tiled=True)
        attn_proj = jnp.swapaxes(attn_proj, 0, 1).reshape(weight_shape)
    results = pl.pallas_call(
        functools.partial(attention_forward_kernel, head_size, group, parts if fast else 1, fast),
        in_specs=[outside, outside, weight_spec] + [inside] * 4 + [scalars] + [inside] * 4,
        out_specs=out_specs,
        out_shape=out_shape,
        scratch_shapes=scratch,
        compiler_params=pltpu.CompilerParams(
            vmem_limit_bytes=VMEM_LIMIT, collective_id=0, has_side_effects=True
        ),
    )(
        content, query, attn_proj, up_proj, down_proj.T, out_proj, up_bias[None], doc_lengths, factor_order,
        segment_ids, table, head_bias,
    )
    proj, facts_row, facts_col, bias_all, mixed_pieces = results[:5]
    content_all, query_all, weight_all, chance_all = results[5:9]
    if fast:
        wide = [full.reshape(parts, group, pick, full.shape[-1]) for full in results[9:]]
    else:
        wide = [gather_all(m) for m in (up_proj.astype(bfloat), down_proj.T.astype(bfloat), out_proj.T.astype(bfloat))]
    kept = (content_all, query_all, weight_all, chance_all, (facts_row, facts_col), proj)
    return kept, bias_all, mixed_pieces, wide


def attention_backward_kernel(head_size, group, parts, fast, *refs):
    content_hbm, query_hbm, weight_hbm, chance_hbm, refs = *refs[:4], refs[4:]
    upper_pieces, dresid_hbm, refs = refs[0], refs[1], refs[2:]
    turned_ref, bias_ref, row_ref, col_ref, proj_ref = refs[:5]
    sources, small_ref, refs = refs[5:8], refs[8], refs[9:]
    outputs, refs = refs[:9] if fast else refs[:4], refs[9:] if fast else refs[4:]
    content_grad_ref, query_grad_ref, dhead_ref = outputs[:3]
    content_all, query_all, weight_ref, upper_all, dinput_ref, dweight_ref = refs[:6]
    chance_ref, backward_ref, drel_ref, dcols_ref, dkeys_ref, dvalues_ref = refs[6:12]
    dwide_ref, side_ref, cross_ref, swap_ref, dresid_ref, dhead_own, refs = *refs[12:18], refs[18:]
    sems, send_sems, recv_sems, refs = *refs[:3], refs[3:]
    rows, length = row_ref.shape[0], row_ref.shape[2]
    half = length // 2
    depth, width = content_all.shape[1], weight_ref.shape[-1] // 4
    heads = width // head_size
    scale = head_size ** (-0.5)
    heads_here, dp_here = lax.axis_index("heads"), lax.axis_index("dp")
    chip = heads_here >> 1
    tokens = upper_pieces.shape[1]
    links = Links(send_sems, recv_sems)

    def token_part(k):
        return pl.ds(pl.multiple_of((heads_here ^ k) * tokens, tokens), tokens)

    copies = [
        pltpu.make_async_copy(content_hbm, content_all, sems.at[0]),
        pltpu.make_async_copy(query_hbm, query_all, sems.at[1]),
        pltpu.make_async_copy(weight_hbm, weight_ref, sems.at[2]),
        pltpu.make_async_copy(chance_hbm, chance_ref, sems.at[10]),
        pltpu.make_async_copy(upper_pieces.at[0], upper_all.at[token_part(0)], sems.at[3]),
    ]
    for copy in copies:
        copy.start()
    dresid_copy = pltpu.make_async_copy(dresid_hbm, dresid_ref, sems.at[4])
    dresid_copy.start()

    def weight(first, last):
        return weight_ref[..., first * width : last * width].reshape(depth, (last - first) * width)

    barrier = pltpu.get_barrier_semaphore()
    peers = [("heads", k) for k in range(1, group)] + [("dp", k) for k in range(1, parts)]
    for axis, k in peers:
        pl.semaphore_signal(
            barrier, inc=1, device_id={axis: lax.axis_index(axis) ^ k}, device_id_type=pl.DeviceIdType.MESH
        )
    pl.semaphore_wait(barrier, len(peers))
    upper_copies = [
        links.push(upper_pieces.at[k], upper_all.at[token_part(0)], "heads", k) for k in range(1, group)
    ]
    for copy in upper_copies:
        copy.start()
    if fast:
        pick = sources[0].shape[3]
        early, late, full = pl.ds(0, pick // 2), pl.ds(pick // 2, pick // 2), pl.ds(0, pick)
        plan = ((0, early, "yx"), (0, late, "yx"), (1, early, "yx"), (1, late, "xy"), (2, full, "yx"))
        scatters = [
            Scatter(links, sems.at[5 + n], sources[which], part, order, refs[4 * n : 4 * n + 4])
            for n, (which, part, order) in enumerate(plan)
        ]
        up_one, up_two, down_one, down_two, out_one = scatters
        small_got, small_more, small_mid, dweight_got, dweight_more, head_got, tile_ref, tile_got, tile_more = refs[20:]
        up_one.begin()
        small_first = [links.push(small_ref, small_got.at[heads_here], "heads", k) for k in range(1, group)]
        for copy in small_first:
            copy.start()
        small_got[heads_here] = small_ref[...]
        small_second = [links.push(small_mid, small_more.at[dp_here], "dp", k) for k in range(1, parts)]
    for copy in copies:
        copy.wait()
    upper_copies[0].wait()
    backward_ref[...] = dot(turned_ref[...], weight(3, 4)).astype(jnp.bfloat16)
    drel_ref[...] = jnp.zeros_like(drel_ref)
    dweight_ref[...] = jnp.zeros_like(dweight_ref)
    dhead_own[...] = jnp.zeros_like(dhead_own)
    bias_cols = [bias_ref[kind].T for kind in range(2)]
    ones = jnp.ones((16, length), jnp.bfloat16)

    def act(condition, actions):
        @pl.when(condition)
        def _():
            for action in actions:
                action()

    def span(start, size):
        return pl.ds(pl.multiple_of(start, size), size)

    def sides(first, size, slot):
        mine, other = span(first + core * size, size), span(first + (1 - core) * size, size)
        landed = side_ref.at[:, pl.ds(slot, size)]
        return links.push(dinput_ref.at[:, other], landed, "heads", 1), mine, landed

    def add_side(side, landed=None):
        copy, mine, place = side
        copy.wait()
        for n in range(2):
            dinput_ref[n, mine] = (
                dinput_ref[n, mine].astype(jnp.float32) + place[n].astype(jnp.float32)
            ).astype(jnp.bfloat16)

    core, unit = heads_here & 1, half // 2
    own_first = jnp.where(chip == 0, 0, (rows - 1) * length)
    far_first = jnp.where(chip == 0, (rows - 1) * length, 0)
    own_middle = jnp.where(chip == 0, length, length + half)
    far_middle = jnp.where(chip == 0, length + half, length)
    own_side, far_side = sides(own_first, half, 0), sides(far_first, half, half)
    own_side_two, far_side_two = sides(own_middle, unit, 2 * half), sides(far_middle, unit, 2 * half + unit)
    across = [
        (links.push(dinput_ref.at[:, side[1]], cross_ref.at[:, place], "heads", 2), mine[1], cross_ref.at[:, place])
        for side, mine, place in (
            (far_side, own_side, pl.ds(0, half)), (far_side_two, own_side_two, pl.ds(half, unit))
        )
    ]
    swap_part = span(2 * half + 5 * unit * chip - half * core, unit)
    swap_got = span(2 * half + 5 * unit * chip - half * (1 - core), unit)
    swap = links.push(dinput_ref.at[:, swap_part], swap_ref, "heads", 1)

    def far_over():
        add_side(far_side)
        across[0][0].start()

    def small_middle():
        for copy in small_first:
            copy.wait()
        total = small_got[0]
        for k in range(1, group):
            total = total + small_got[k]
        small_mid[...] = total
        small_more[dp_here] = total
        for copy in small_second:
            copy.start()

    events = {
        (0, heads): [own_side[0].start],
        (1, heads): [far_side[0].start],
        (2, 0): [far_over, lambda: add_side(own_side)],
    }
    if fast:
        for place, actions in {
            (0, 0): [up_two.begin],
            (0, 1): [down_two.begin],
            (0, 2): [up_one.second, down_one.begin],
            (0, heads): [out_one.begin],
            (1, 0): [small_middle, up_two.second, up_one.third],
            (1, 1): [down_two.second],
            (1, 2): [up_two.third, down_one.second],
            (1, heads): [out_one.second],
            (2, 0): [down_two.third],
            (2, 1): [down_one.third],
            (2, 2): [out_one.third],
        }.items():
            events[place] = events.get(place, []) + actions

    def one_row(step, carry):
        row = jnp.where(step == 0, 0, rows - step)
        row = jnp.where(chip == 0, row, rows - 1 - row)

        @pl.when(step == 1)
        def _():
            for copy in upper_copies[1:]:
                copy.wait()

        row_part(step, row)
        return carry

    def row_part(step, row):
        here = pl.ds(pl.multiple_of(row * length, length), length)
        content_ref, query_ref = content_all.at[here], query_all.at[here]
        facts_row, facts_col = row_ref[row], col_ref[row]
        roll = roll_matrix(facts_col[:, 3:4], length)
        upper = dot(roll, upper_all[here]).astype(jnp.bfloat16)
        segment_col = facts_col[:, 2:3]
        down = lax.broadcasted_iota(jnp.int32, (half, half), 0)
        along = lax.broadcasted_iota(jnp.int32, (half, half), 1)
        mirror = jnp.where(down + along == half - 1, 1.0, 0.0).astype(jnp.bfloat16)
        lane = lax.broadcasted_iota(jnp.int32, (length, head_size), 1)
        extra = jnp.where(lane == 0, segment_col, jnp.where(lane == 1, 1.0, 0.0)).astype(jnp.bfloat16)
        for head in range(heads):
            own_cols = slice(head * head_size, (head + 1) * head_size)
            cols = lambda kind: slice(kind * width + head * head_size, kind * width + (head + 1) * head_size)
            bias = [bias_ref[kind, head : head + 1] for kind in range(5)]
            keys, values = proj_ref[row, :, cols(1)], proj_ref[row, :, cols(2)]
            keys_extra = jnp.concatenate([keys, extra], -1)
            backward = backward_ref[:, own_cols]
            u_col, w_col = (turned_bias[:, head : head + 1] for turned_bias in bias_cols)
            heads_sums = [jnp.zeros((1, head_size), jnp.float32) for _ in range(5)]
            for stream in range(2):
                query_now = proj_ref[row, :, cols(3 * stream)]
                with_c = query_now.astype(jnp.float32) + bias[2]
                index = stream * heads + head
                upper_now = upper[:, index * head_size : (index + 1) * head_size]
                query_t, upper_t = jnp.concatenate([query_now.T, ones], 0), upper_now.T
                dquery = []
                for block in range(2):
                    part = slice(block * half, (block + 1) * half)
                    low_chances = chance_ref[row, index, block]
                    chances = low_chances.astype(jnp.float32)
                    weighted = chances * dot_nt(upper_now[part], values[part])
                    centre = jnp.sum(weighted, -1, keepdims=True)
                    dscore = (weighted - chances * centre).astype(jnp.bfloat16)
                    dvalue_part = dot(upper_t[:, part], low_chances)
                    by_key = dot(dscore, keys_extra[part])
                    turned = dot(dscore, mirror)
                    wide = pltpu.roll(
                        jnp.concatenate([turned, jnp.zeros((half, half), jnp.float32)], -1),
                        0, 1, stride=1, stride_axis=0,
                    ).astype(jnp.bfloat16)
                    by_place = dot(wide, backward)
                    dkey_part = dot(query_t[:, part], dscore)
                    dkey_part = dkey_part[:head_size] + u_col * dkey_part[head_size : head_size + 1]
                    drel_part = dot(query_t[:, part], wide)
                    drel_ref[own_cols] += drel_part[:head_size] + w_col * drel_part[head_size : head_size + 1]
                    if stream == 0:
                        dkeys_ref[own_cols, part] = dkey_part
                        dvalues_ref[own_cols, part] = dvalue_part
                    else:
                        dkeys_ref[own_cols, part] += dkey_part
                        dvalues_ref[own_cols, part] += dvalue_part
                    with_seg, total = by_key[:, head_size : head_size + 1], by_key[:, head_size + 1 : head_size + 2]
                    seg_i = segment_col[part]
                    seg_one = with_seg + seg_i * (total - 2.0 * with_seg)
                    seg_zero = total - seg_one
                    by_key = by_key[:, :head_size]
                    by_segment = seg_zero * bias[3] + seg_one * bias[4]
                    dquery.append((by_key + by_place + by_segment) * scale)
                    for kind, term in enumerate(
                        (by_key, by_place, by_segment, seg_zero * with_c[part], seg_one * with_c[part])
                    ):
                        heads_sums[kind] = heads_sums[kind] + jnp.sum(term, 0, keepdims=True)
                dcols_ref[:, cols(3 * stream)] = jnp.concatenate(dquery, 0).astype(jnp.bfloat16)
            for kind in range(5):
                dhead_own[kind : kind + 1, own_cols] += heads_sums[kind] * scale
            for when, actions in events.items():
                if when[1] == head:
                    act(step == when[0], actions)
        dcols_ref[:, width : 2 * width] = (dkeys_ref[...] * scale).astype(jnp.bfloat16).T
        dcols_ref[:, 2 * width : 3 * width] = dvalues_ref[...].astype(jnp.bfloat16).T
        unroll = unroll_matrix(facts_row[3:4, :], length)
        joined = dot(unroll, dcols_ref[...]).astype(jnp.bfloat16)
        joined_t = joined.T
        content, query = content_ref[...], query_ref[...]
        dweight_ref[: 3 * width] += dot(joined_t[: 3 * width], content)
        dweight_ref[:width] += dot(joined_t[3 * width :], query)
        dinput_ref[0, here] = dot_nt(joined[:, : 3 * width], weight(0, 3)).astype(jnp.bfloat16)
        dinput_ref[1, here] = dot_nt(joined[:, 3 * width :], weight(0, 1)).astype(jnp.bfloat16)
        for when, actions in events.items():
            if when[1] == heads:
                act(step == when[0], actions)

    lax.fori_loop(0, rows, one_row, 0)
    for side in (far_side_two, own_side_two):
        side[0].start()
    drel = drel_ref[...] * scale
    high = drel.astype(jnp.bfloat16)
    low = (drel - high.astype(jnp.float32)).astype(jnp.bfloat16)
    dweight_ref[3 * width :] = dot(high, turned_ref[...]) + dot(low, turned_ref[...])
    dwide_ref[...] = dweight_ref[...].astype(jnp.bfloat16).T.reshape(dwide_ref.shape)
    if fast:
        place_y, place_z = dp_here & 1, dp_here >> 1
        dweight_first = links.push(dwide_ref.at[:, 1 - place_y], dweight_got, "dp", 1)
        dweight_first.start()
        head_copies = [links.push(dhead_own, head_got.at[dp_here], "dp", k) for k in range(1, parts)]
        for copy in head_copies:
            copy.start()
        head_got[dp_here] = dhead_own[...]
    add_side(far_side_two)
    across[1][0].start()
    add_side(own_side_two)
    if fast:
        dweight_first.wait()
        add_planes(dweight_got, lambda z: dwide_ref[z, place_y], dweight_got)
        dweight_second = [
            links.push(dweight_got.at[place_z ^ m], dweight_more.at[m - 1], "dp", 2 * m) for m in range(1, 4)
        ]
        for copy in dweight_second:
            copy.start()
    for side in across:
        add_side(side)
    swap.start()
    if fast:
        up_share, down_share, out_share, proj_share, small_sum, norm_ref = outputs[3:]
        squares = jnp.zeros((1, 1), jnp.float32)
        for copy in small_second:
            copy.wait()
        total = small_more[0]
        for k in range(1, parts):
            total = total + small_more[k]
        small_sum[...] = total
        squares = squares + square_sum(total) / (group * parts)
        for copy in head_copies:
            copy.wait()
        total = head_got[0]
        for k in range(1, parts):
            total = total + head_got[k]
        dhead_ref[...] = total
        squares = squares + square_sum(total) / parts
        for (which, part, _), scatter in zip(plan, scatters):
            total = scatter.last()
            (up_share, down_share, out_share)[which][part] = total
            squares = squares + square_sum(total)
        for copy in dweight_second:
            copy.wait()
        total = dweight_got[place_z].astype(jnp.float32)
        for m in range(1, 4):
            total = total + dweight_more[m - 1].astype(jnp.float32)
        proj_share[...] = total
        squares = squares + square_sum(total)
        tile_ref[...] = jnp.broadcast_to(squares, tile_ref.shape)
        tile_got[heads_here] = tile_ref[...]
        tile_first = [links.push(tile_ref, tile_got.at[heads_here], "heads", k) for k in range(1, group)]
        for copy in tile_first:
            copy.start()
    else:
        dhead_ref[...] = dhead_own[...]
        outputs[3][...] = dwide_ref[...]
    if fast:
        for copy in tile_first:
            copy.wait()
        total = tile_got[0]
        for k in range(1, group):
            total = total + tile_got[k]
        tile_more[dp_here] = total
        tile_ref[...] = total
        tile_second = [links.push(tile_ref, tile_more.at[dp_here], "dp", k) for k in range(1, parts)]
        for copy in tile_second:
            copy.start()
    dresid_copy.wait()
    swap.wait()
    dinput_ref[:, swap_got] = swap_ref[...]
    for n, place in enumerate((content_grad_ref, query_grad_ref)):
        place[...] = dresid_ref[n] + dinput_ref[n, token_part(0)].astype(jnp.float32)
    if fast:
        for copy in tile_second:
            copy.wait()
        total = tile_more[0]
        for k in range(1, parts):
            total = total + tile_more[k]
        norm_ref[...] = jnp.sqrt(total)


def attention_backward(
    kept, table, head_bias, upper, dresid, gradients, small
):
    content_all, query_all, weight_all, chance_all, facts, proj = kept
    rows, length = facts[0].shape[0], facts[0].shape[2]
    group = upper.shape[0]
    fast = weight_all.ndim == 4
    tokens, depth = content_all.shape
    own = tokens // group
    pick, width = weight_all.shape[-2], weight_all.shape[-1] // 4
    parts = depth // pick
    head_size = head_bias.shape[-1]
    half = length // 2
    inside = pl.BlockSpec(memory_space=pltpu.VMEM)
    outside = pl.BlockSpec(memory_space=pl.ANY)
    bfloat, float32 = jnp.bfloat16, jnp.float32
    out_shape = [
        jax.ShapeDtypeStruct((own, depth), float32),
        jax.ShapeDtypeStruct((own, depth), float32),
        jax.ShapeDtypeStruct((8, width), float32),
    ]
    wide_shape = weight_all.shape
    scratch = [
        pltpu.VMEM((tokens, depth), bfloat),
        pltpu.VMEM((tokens, depth), bfloat),
        pltpu.VMEM(weight_all.shape, bfloat),
        pltpu.VMEM((tokens, 2 * width), bfloat),
        pltpu.VMEM((2, tokens, depth), bfloat),
        pltpu.VMEM((4 * width, depth), float32),
        pltpu.VMEM(chance_all.shape, bfloat),
        pltpu.VMEM((length, width), bfloat),
        pltpu.VMEM((width, length), float32),
        pltpu.VMEM((length, 4 * width), bfloat),
        pltpu.VMEM((width, length), float32),
        pltpu.VMEM((width, length), float32),
        pltpu.VMEM(wide_shape, bfloat),
        pltpu.VMEM((2, 2 * own, depth), bfloat),
        pltpu.VMEM((2, own, depth), bfloat),
        pltpu.VMEM((2, half // 2, depth), bfloat),
        pltpu.VMEM((2, own, depth), float32),
        pltpu.VMEM((8, width), float32),
        pltpu.SemaphoreType.DMA((11,)),
        pltpu.SemaphoreType.DMA((80,)),
        pltpu.SemaphoreType.DMA((80,)),
    ]
    if fast:
        planes = parts // 2
        columns = [gradient.shape[-1] for gradient in gradients]
        out_shape += [jax.ShapeDtypeStruct((pick, c), float32) for c in columns]
        out_shape += [
            jax.ShapeDtypeStruct((pick, 4 * width), float32),
            jax.ShapeDtypeStruct(small.shape, float32),
            jax.ShapeDtypeStruct((8, 128), float32),
        ]
        gradients = [g.reshape(planes, 2, group // 2, pick, g.shape[-1]) for g in gradients]
        sizes = [(pick // 2, columns[0])] * 2 + [(pick // 2, columns[1])] * 2 + [(pick, columns[2])]
        for size in sizes:
            scratch += [
                pltpu.VMEM((planes, 2) + size, bfloat),
                pltpu.VMEM((planes, 2) + size, bfloat),
                pltpu.VMEM((planes,) + size, bfloat),
                pltpu.VMEM((planes - 1,) + size, bfloat),
            ]
        scratch += [
            pltpu.VMEM((group,) + small.shape, float32),
            pltpu.VMEM((parts,) + small.shape, float32),
            pltpu.VMEM(small.shape, float32),
            pltpu.VMEM((planes, pick, 4 * width), bfloat),
            pltpu.VMEM((planes - 1, pick, 4 * width), bfloat),
            pltpu.VMEM((parts, 8, width), float32),
            pltpu.VMEM((8, 128), float32),
            pltpu.VMEM((group, 8, 128), float32),
            pltpu.VMEM((parts, 8, 128), float32),
        ]
    else:
        out_shape += [jax.ShapeDtypeStruct(wide_shape, bfloat)]
    return pl.pallas_call(
        functools.partial(attention_backward_kernel, head_size, group, parts, fast),
        in_specs=[outside] * 6 + [inside] * 5 + [outside] * 3 + [inside],
        out_specs=[inside] * len(out_shape),
        out_shape=out_shape,
        scratch_shapes=scratch,
        compiler_params=pltpu.CompilerParams(
            vmem_limit_bytes=VMEM_LIMIT, collective_id=2, has_side_effects=True
        ),
    )(
        content_all, query_all, weight_all, chance_all, upper, dresid, table,
        head_bias, *facts, proj, *gradients, small,
    )


def norm_parts(values):
    centred = values - jnp.mean(values, -1, keepdims=True)
    inverse = lax.rsqrt(jnp.mean(centred * centred, -1, keepdims=True) + NORM_EPSILON)
    return centred * inverse, inverse


def norm_back(upstream, normed, inverse, gain):
    scaled = upstream * gain
    first = jnp.mean(scaled, -1, keepdims=True)
    second = jnp.mean(scaled * normed, -1, keepdims=True)
    return inverse * (scaled - first - normed * second)


def column_sum(values):
    return jnp.sum(values, 0, keepdims=True)


def feed_kernel(group, *refs):
    mixed_ref, refs = refs[0], refs[1:]
    bias_ref, refs = refs[0], refs[1:]
    content_ref, query_ref, dcontent_ref, dquery_ref, norm_ref, up_hbm, down_hbm, out_hbm = refs[:8]
    content_out, query_out, dresid_ref, refs = refs[8], refs[9], refs[10], refs[11:]
    dmixed_ref, refs = refs[0], refs[1:]
    dup_hbm, ddown_hbm, dout_ref, dsmall_ref, refs = refs[0], refs[1], refs[2], refs[3], refs[4:]
    up_ref, down_ref, out_ref, hidden_ref, slope_ref = refs[:5]
    low_ref, low_t_ref, normed_ref, total_ref, up_got, down_got, out_got, out_sent = refs[5:13]
    sems, send_sems, recv_sems = refs[13:]
    own, depth = content_ref.shape
    tokens = 2 * own
    here = lax.axis_index("heads")
    core = here & 1
    chips = group // 2
    loads = [
        pltpu.make_async_copy(out_hbm.at[:, j], out_ref.at[j], sems.at[j]) for j in range(group)
    ]
    loads += [
        pltpu.make_async_copy(up_hbm.at[:, j], up_ref.at[j], sems.at[group + j]) for j in range(group)
    ]
    loads += [
        pltpu.make_async_copy(down_hbm.at[:, j], down_ref.at[j], sems.at[2 * group + j])
        for j in range(group)
    ]
    for load in loads:
        load.start()
    greet("heads", [1])
    gain_one, bias_one, bias_out, gain_two, bias_two = [norm_ref[i : i + 1] for i in range(5)]
    for load in loads[:group]:
        load.wait()
    hidden = up_ref.shape[-1]

    def mixed_piece(k):
        both = mixed_ref[k]
        return jnp.concatenate([both[:, : both.shape[1] // 2], both[:, both.shape[1] // 2 :]], 0)

    def out_block(k):
        return out_ref[here ^ k].reshape(depth, out_ref.shape[-1])

    total = jnp.concatenate([content_ref[...], query_ref[...]], 0).astype(jnp.float32)
    for k in range(group):
        total = total + dot_nt(mixed_piece(k), out_block(k))
    normed, inverse_one = norm_parts(total)
    normed_ref[...] = normed
    middle = normed * gain_one + bias_one
    low_ref[...] = middle.astype(jnp.bfloat16)
    low_t_ref[...] = low_ref[...].T
    total_ref[...] = middle + bias_out
    for load in loads[group:]:
        load.wait()

    def forward(j, carry):
        for part in (slice(0, own), slice(own, tokens)):
            before = dot(low_ref[part], up_ref[j].reshape(depth, hidden)) + bias_ref[j]
            square = before * before
            bent = jnp.tanh(GELU_FACTOR * before * (1.0 + GELU_CUBIC * square))
            half_up = 0.5 * (1.0 + bent)
            hidden_now = (before * half_up).astype(jnp.bfloat16)
            slope_ref[j, part] = half_up + 0.5 * before * (1.0 - bent * bent) * GELU_FACTOR * (
                1.0 + 3.0 * GELU_CUBIC * square
            )
            hidden_ref[j, part] = hidden_now
            total_ref[part] += dot_nt(hidden_now, down_ref[j].reshape(depth, hidden))
        return carry

    lax.fori_loop(0, group, forward, 0)
    normed_two, inverse_two = norm_parts(total_ref[...])
    result = (normed_two * gain_two + bias_two).astype(jnp.bfloat16)
    content_out[...] = result[:own]
    query_out[...] = result[own:]
    upstream = jnp.concatenate([dcontent_ref[...], dquery_ref[...]], 0).astype(jnp.float32)
    dsmall_ref[group + 3 : group + 4] = column_sum(upstream * normed_two)
    dsmall_ref[group + 4 : group + 5] = column_sum(upstream)
    dfinal = norm_back(upstream, normed_two, inverse_two, gain_two)
    dsmall_ref[group + 2 : group + 3] = column_sum(dfinal)
    total_ref[...] = dfinal
    dlow = dfinal.astype(jnp.bfloat16)
    dlow_t = dlow.T

    def to_sibling(source, place, index):
        return pltpu.make_async_remote_copy(
            source, place, send_sems.at[index], recv_sems.at[index],
            device_id={"heads": here ^ 1}, device_id_type=pl.DeviceIdType.MESH,
        )

    def back_block(j):
        ddown = dot(dlow_t, hidden_ref[j])
        bias_grad = jnp.zeros((1, hidden), jnp.float32)
        for part in (slice(0, own), slice(own, tokens)):
            dhidden = dot(dlow[part], down_ref[j].reshape(depth, hidden))
            dbefore = (dhidden * slope_ref[j, part]).astype(jnp.bfloat16)
            bias_grad = bias_grad + column_sum(dbefore.astype(jnp.float32))
            total_ref[part] += dot_nt(dbefore, up_ref[j].reshape(depth, hidden))
            hidden_ref[j, part] = dbefore
        dsmall_ref[pl.ds(j, 1)] = bias_grad
        return dot(low_t_ref[...], hidden_ref[j]), ddown

    def sent(chip):
        j = 2 * chip + 1 - core
        return [
            to_sibling(up_ref.at[j], up_got.at[chip], 2 * chip),
            to_sibling(down_ref.at[j], down_got.at[chip], 2 * chip + 1),
        ]

    def kept(chip):
        j = 2 * chip + core
        return [
            pltpu.make_async_copy(up_ref.at[j], dup_hbm.at[:, chip], sems.at[chip]),
            pltpu.make_async_copy(down_ref.at[j], ddown_hbm.at[:, chip], sems.at[group + chip]),
        ]

    def backward_sent(chip, carry):
        j = 2 * chip + 1 - core
        dup, ddown = back_block(j)
        up_ref[j] = dup.astype(jnp.bfloat16).reshape(up_ref.shape[1:])
        down_ref[j] = ddown.astype(jnp.bfloat16).reshape(down_ref.shape[1:])
        for copy in sent(chip):
            copy.start()
        return carry

    def backward_kept(chip, carry):
        j = 2 * chip + core
        dup, ddown = back_block(j)
        for copy in sent(chip):
            copy.wait_recv()
        dup = dup + up_got[chip].astype(jnp.float32).reshape(depth, hidden)
        ddown = ddown + down_got[chip].astype(jnp.float32).reshape(depth, hidden)
        up_ref[j] = dup.astype(jnp.bfloat16).reshape(up_ref.shape[1:])
        down_ref[j] = ddown.astype(jnp.bfloat16).reshape(down_ref.shape[1:])
        for copy in kept(chip):
            copy.start()
        return carry

    lax.fori_loop(0, chips, backward_sent, 0)
    lax.fori_loop(0, chips, backward_kept, 0)
    dmiddle = total_ref[...]
    normed = normed_ref[...]
    dsmall_ref[group : group + 1] = column_sum(dmiddle * normed)
    dsmall_ref[group + 1 : group + 2] = column_sum(dmiddle)
    dresid = norm_back(dmiddle, normed, inverse_one, gain_one)
    total_ref[...] = dresid
    dresid_copy = pltpu.make_async_copy(total_ref, dresid_ref, sems.at[0])
    dresid_copy.start()
    dlow = dresid.astype(jnp.bfloat16)
    dlow_t = dlow.T
    out_copies = [
        to_sibling(out_sent.at[chip], out_got.at[chip], 2 * chips + chip) for chip in range(chips)
    ]
    for chip in range(chips):
        k = 2 * chip + 1
        mixed = mixed_piece(k)
        out_sent[chip] = dot(dlow_t, mixed).astype(jnp.bfloat16).reshape(out_sent.shape[1:])
        out_copies[chip].start()
    for k in range(group):
        dmixed = dot(dlow, out_block(k)).astype(jnp.bfloat16)
        dmixed_ref[k] = jnp.concatenate([dmixed[:own], dmixed[own:]], -1)
    for chip in range(chips):
        k = 2 * chip
        mixed = mixed_piece(k)
        dout = dot(dlow_t, mixed)
        out_copies[chip].wait_recv()
        dout = dout + out_got[chip].astype(jnp.float32).reshape(dout.shape)
        dout_ref[:, (here ^ k) >> 1] = dout.astype(jnp.bfloat16).reshape(out_sent.shape[1:])
    dsmall_ref[group + 5 :] = jnp.zeros((dsmall_ref.shape[0] - group - 5, depth), jnp.float32)
    dresid_copy.wait()
    for chip in range(chips):
        for copy in sent(chip):
            copy.wait_send()
        out_copies[chip].wait_send()
        for copy in kept(chip):
            copy.wait()


def feed_layer(mixed, bias_all, content, query, dcontent, dquery, norm_param, up, down, out):
    group = mixed.shape[0]
    own, depth = content.shape
    parts, _, pick, hidden = up.shape
    width = out.shape[-1]
    inside = pl.BlockSpec(memory_space=pltpu.VMEM)
    outside = pl.BlockSpec(memory_space=pl.ANY)
    tokens = 2 * own
    results = pl.pallas_call(
        functools.partial(feed_kernel, group),
        in_specs=[inside] * 7 + [outside] * 3,
        out_specs=[inside, inside, outside, inside, outside, outside, inside, inside],
        out_shape=[
            jax.ShapeDtypeStruct((own, depth), jnp.bfloat16),
            jax.ShapeDtypeStruct((own, depth), jnp.bfloat16),
            jax.ShapeDtypeStruct((tokens, depth), jnp.float32),
        ]
        + [
            jax.ShapeDtypeStruct((group, own, 2 * width), jnp.bfloat16),
            jax.ShapeDtypeStruct((parts, group // 2, pick, hidden), jnp.bfloat16),
            jax.ShapeDtypeStruct((parts, group // 2, pick, hidden), jnp.bfloat16),
            jax.ShapeDtypeStruct((parts, group // 2, pick, width), jnp.bfloat16),
            jax.ShapeDtypeStruct((16, depth), jnp.float32),
        ],
        scratch_shapes=[
            pltpu.VMEM((group, parts, pick, hidden), jnp.bfloat16),
            pltpu.VMEM((group, parts, pick, hidden), jnp.bfloat16),
            pltpu.VMEM((group, parts, pick, width), jnp.bfloat16),
            pltpu.VMEM((group, tokens, hidden), jnp.bfloat16),
            pltpu.VMEM((group, tokens, hidden), jnp.float32),
            pltpu.VMEM((tokens, depth), jnp.bfloat16),
            pltpu.VMEM((depth, tokens), jnp.bfloat16),
            pltpu.VMEM((tokens, depth), jnp.float32),
            pltpu.VMEM((tokens, depth), jnp.float32),
            pltpu.VMEM((group // 2, parts, pick, hidden), jnp.bfloat16),
            pltpu.VMEM((group // 2, parts, pick, hidden), jnp.bfloat16),
            pltpu.VMEM((group // 2, parts, pick, width), jnp.bfloat16),
            pltpu.VMEM((group // 2, parts, pick, width), jnp.bfloat16),
            pltpu.SemaphoreType.DMA((3 * group,)),
            pltpu.SemaphoreType.DMA((3 * group // 2,)),
            pltpu.SemaphoreType.DMA((3 * group // 2,)),
        ],
        compiler_params=pltpu.CompilerParams(
            vmem_limit_bytes=VMEM_LIMIT, collective_id=1, has_side_effects=True
        ),
    )(mixed, bias_all, content, query, dcontent, dquery, norm_param, up, down, out)
    return results[0], results[1], results[2].reshape(2, own, depth), results[3], results[4:]


def exchange(value, axis, mask):
    return lax.ppermute(value, axis, [(i, i ^ mask) for i in range(lax.axis_size(axis))])


def total_over(value, axis):
    mask = 1
    while mask < lax.axis_size(axis):
        value = value + exchange(value, axis, mask)
        mask = 2 * mask
    return value


def by_pieces(pick):
    return lax.axis_size("dp") <= 8 and pick % 16 == 0


def reduce_projection(full):
    return lax.psum_scatter(full, "dp", scatter_dimension=0, tiled=True).astype(jnp.float32)


def gather_all(own):
    dp, heads = lax.axis_size("dp"), lax.axis_size("heads")
    rows, columns = own.shape
    full = lax.all_gather(own, ("dp", "heads"), axis=0, tiled=False).reshape(dp, heads, rows, columns)
    if by_pieces(rows):
        return full
    return jnp.swapaxes(full, 0, 1).reshape(1, heads, dp * rows, columns)


def scatter_all(full):
    chip = lax.axis_index("heads") // 2
    mine = lax.dynamic_index_in_dim(full[0], chip, 0, False)
    theirs = lax.dynamic_index_in_dim(full[0], 1 - chip, 0, False)
    mine = mine.astype(jnp.float32) + exchange(theirs, "heads", 2).astype(jnp.float32)
    return lax.psum_scatter(mine, "dp", scatter_dimension=0, tiled=True)


def adam_parts(master, first, second, gradient, factor, decayed):
    clipped = gradient * factor
    new_first = BETA_ONE * first + (1.0 - BETA_ONE) * clipped
    new_second = BETA_TWO * second + (1.0 - BETA_TWO) * clipped * clipped
    first_hat = new_first * (1.0 / (1.0 - BETA_ONE**STEP))
    second_hat = new_second * (1.0 / (1.0 - BETA_TWO**STEP))
    update = first_hat / (jnp.sqrt(second_hat) + ADAM_EPSILON)
    if decayed:
        update = update + WEIGHT_DECAY * master
        return new_first, new_second, master - MATRIX_RATE * update
    return new_first, new_second, master - VECTOR_RATE * update


def update_kernel(group, *refs):
    kept, refs = refs[:4], refs[4:]
    up_share, down_share, out_share, proj_share, dhead_ref, small_ref, norm_ref, refs = *refs[:7], refs[7:]
    weights, refs = refs[:21], refs[21:]
    placed, refs = refs[:4], refs[4:]
    results, grad_norm, stages, sems = refs[:28], refs[28], refs[29:33], refs[33]
    loads = [pltpu.make_async_copy(a, b, sems.at[n]) for n, (a, b) in enumerate(zip(kept, stages))]
    stores = [pltpu.make_async_copy(a, b, sems.at[4 + n]) for n, (a, b) in enumerate(zip(stages, placed))]
    for copy in loads:
        copy.start()
    norm = norm_ref[0:1, 0:1]
    grad_norm[...] = norm
    factor = CLIP_NORM / jnp.maximum(norm, CLIP_NORM)

    def put(index, gradient, decayed, place=lambda ref: ref[...], store=None):
        values = adam_parts(*(place(ref) for ref in weights[3 * index : 3 * index + 3]), gradient, factor, decayed)
        for ref, value in zip(results[4 * index : 4 * index + 4], (gradient,) + values):
            if store is None:
                ref[...] = value
            else:
                store(ref, value)

    width = proj_share.shape[1] // 4
    for kind in range(4):
        def store(ref, value, kind=kind):
            ref[kind] = value

        put(0, proj_share[:, kind * width : (kind + 1) * width], True, lambda ref, kind=kind: ref[kind], store)
    for load, store in zip(loads, stores):
        load.wait()
        store.start()
    put(1, out_share[...].T, True)
    put(2, up_share[...], True)
    put(3, down_share[...], True)
    heads, size = weights[12].shape[1:]
    for head in range(heads):
        def store(ref, value, head=head):
            ref[:, head, :] = value

        put(4, dhead_ref[:5, head * size : (head + 1) * size], False, lambda ref, head=head: ref[:, head, :], store)
    put(5, small_ref[pl.ds(lax.axis_index("heads"), 1)], False)
    put(6, small_ref[group : group + 5], False)
    for store in stores:
        store.wait()


def update_layer(kept, shares, dhead, small_sum, norm_tile, weights):
    inside = pl.BlockSpec(memory_space=pltpu.VMEM)
    outside = pl.BlockSpec(memory_space=pl.ANY)
    up_share, down_share, out_share, proj_share = shares
    out_shape = [jax.ShapeDtypeStruct(a.shape, a.dtype) for a in kept]
    for index in range(7):
        out_shape += [jax.ShapeDtypeStruct(weights[3 * index].shape, jnp.float32)] * 4
    out_shape.append(jax.ShapeDtypeStruct((1, 1), jnp.float32))
    results = pl.pallas_call(
        functools.partial(update_kernel, lax.axis_size("heads")),
        in_specs=[outside] * 4 + [inside] * 28,
        out_specs=[outside] * 4 + [inside] * 29,
        out_shape=out_shape,
        scratch_shapes=[pltpu.VMEM(a.shape, a.dtype) for a in kept] + [pltpu.SemaphoreType.DMA((8,))],
        compiler_params=pltpu.CompilerParams(vmem_limit_bytes=VMEM_LIMIT),
    )(*kept, up_share, down_share, out_share, proj_share, dhead, small_sum, norm_tile, *weights)
    return results[:4], results[4:32], results[32]


def local(
    content_in,
    query_in,
    content_grad,
    query_grad,
    segment_ids,
    doc_lengths,
    factor_order,
    attn_proj,
    attn_proj_first,
    attn_proj_second,
    out_proj,
    out_proj_first,
    out_proj_second,
    up_proj,
    up_proj_first,
    up_proj_second,
    down_proj,
    down_proj_first,
    down_proj_second,
    head_bias,
    head_bias_first,
    head_bias_second,
    up_bias,
    up_bias_first,
    up_bias_second,
    norm_param,
    norm_param_first,
    norm_param_second,
):
    width = content_in.shape[1]
    length = segment_ids.shape[1]
    table = position_table(length, width)
    tables = (jnp.asarray(table), jnp.asarray(table[::-1].copy()))
    kept, bias_all, mixed_pieces, (up_full, down_full, out_full) = attention_forward(
        content_in, query_in, attn_proj, up_proj, down_proj, out_proj, up_bias, doc_lengths, factor_order,
        segment_ids, tables[0], head_bias,
    )
    content_out, query_out, dresid, dmixed_pieces, (dup, ddown, dout, dsmall) = feed_layer(
        mixed_pieces, bias_all, content_in, query_in, content_grad, query_grad, norm_param,
        up_full, down_full, out_full,
    )
    backward = attention_backward(
        kept, tables[1], head_bias, dmixed_pieces, dresid, (dup, ddown, dout), dsmall
    )
    input_grad = backward[:2]
    if by_pieces(attn_proj.shape[1]):
        dhead = backward[2]
        up_share, down_share, out_share, proj_share, small_sum, norm_tile = backward[3:]
    else:
        dp_count, heads_count = lax.axis_size("dp"), lax.axis_size("heads")
        dhead = total_over(backward[2], "dp")
        proj_share = reduce_projection(backward[3])
        up_share, down_share, out_share = scatter_all(dup), scatter_all(ddown), scatter_all(dout)
        small_sum = total_over(total_over(dsmall, "heads"), "dp")
        squares = sum(jnp.sum(share * share) for share in (up_share, down_share, out_share, proj_share))
        squares = squares + jnp.sum(dhead * dhead) / dp_count
        squares = squares + jnp.sum(small_sum * small_sum) / (dp_count * heads_count)
        norm = jnp.sqrt(total_over(total_over(squares.reshape(1, 1), "heads"), "dp"))
        norm_tile = jnp.broadcast_to(norm, (8, 128))
    moments = (
        (attn_proj, attn_proj_first, attn_proj_second),
        (out_proj, out_proj_first, out_proj_second),
        (up_proj, up_proj_first, up_proj_second),
        (down_proj.T, down_proj_first.T, down_proj_second.T),
        (head_bias, head_bias_first, head_bias_second),
        (up_bias[None], up_bias_first[None], up_bias_second[None]),
        (norm_param, norm_param_first, norm_param_second),
    )
    placed, updated, grad_norm = update_layer(
        (content_out, query_out) + tuple(input_grad),
        (up_share, down_share, out_share, proj_share),
        dhead, small_sum, norm_tile, [array for group in moments for array in group],
    )
    updated = list(updated)
    for index in range(12, 16):
        updated[index] = updated[index].T
    for index in range(20, 24):
        updated[index] = updated[index].reshape(-1)
    return (*placed, grad_norm[0, 0], *updated)


def solution(mesh):
    return jax.shard_map(
        local,
        mesh=mesh,
        in_specs=(
            P(("dp", "heads"), None),
            P(("dp", "heads"), None),
            P(("dp", "heads"), None),
            P(("dp", "heads"), None),
            P("dp", None),
            P("dp", None),
            P("dp", None),
            P(None, "dp", "heads"),
            P(None, "dp", "heads"),
            P(None, "dp", "heads"),
            P("heads", "dp"),
            P("heads", "dp"),
            P("heads", "dp"),
            P("dp", "heads"),
            P("dp", "heads"),
            P("dp", "heads"),
            P("heads", "dp"),
            P("heads", "dp"),
            P("heads", "dp"),
            P(None, "heads", None),
            P(None, "heads", None),
            P(None, "heads", None),
            P("heads"),
            P("heads"),
            P("heads"),
            P(),
            P(),
            P(),
        ),
        out_specs=(
            P(("dp", "heads"), None),
            P(("dp", "heads"), None),
            P(("dp", "heads"), None),
            P(("dp", "heads"), None),
            P(),
            P(None, "dp", "heads"),
            P(None, "dp", "heads"),
            P(None, "dp", "heads"),
            P(None, "dp", "heads"),
            P("heads", "dp"),
            P("heads", "dp"),
            P("heads", "dp"),
            P("heads", "dp"),
            P("dp", "heads"),
            P("dp", "heads"),
            P("dp", "heads"),
            P("dp", "heads"),
            P("heads", "dp"),
            P("heads", "dp"),
            P("heads", "dp"),
            P("heads", "dp"),
            P(None, "heads", None),
            P(None, "heads", None),
            P(None, "heads", None),
            P(None, "heads", None),
            P("heads"),
            P("heads"),
            P("heads"),
            P("heads"),
            P(),
            P(),
            P(),
            P(),
        ),
        check_vma=False,
    )
```

```python
import functools

import jax
import jax.numpy as jnp
import ml_dtypes
import numpy as np
from jax import lax
from jax.experimental import pallas as pl
from jax.experimental.pallas import tpu as pltpu
from jax.sharding import PartitionSpec as P

STEP = 10


NORM_EPSILON = 1e-05
CLIP_NORM = 1.0
MATRIX_RATE = 0.08
VECTOR_RATE = 0.5
BETA_ONE = 0.9
BETA_TWO = 0.999
ADAM_EPSILON = 1e-08
WEIGHT_DECAY = 0.01
MASKED_SCORE = -1e30
GELU_FACTOR = 0.7978845608028654
GELU_CUBIC = 0.044715
LOG2E = 1.4426950408889634
VMEM_LIMIT = 56 << 20


def position_table(length, width):
    distance = length // 2 - np.arange(length)
    frequency = 10000.0 ** (-np.arange(0, width, 2) / width)
    angles = distance[:, None] * frequency[None, :]
    return np.concatenate([np.sin(angles), np.cos(angles)], -1).astype(np.float32).astype(ml_dtypes.bfloat16)


def dot(left, right):
    return lax.dot_general(left, right, (((1,), (0,)), ((), ())), preferred_element_type=jnp.float32)


def dot_nt(left, right):
    return lax.dot_general(left, right, (((1,), (1,)), ((), ())), preferred_element_type=jnp.float32)


def split_pair(values):
    high = values.astype(jnp.bfloat16)
    low = (values - high.astype(jnp.float32)).astype(jnp.bfloat16)
    return jnp.concatenate([high, low], -1)


def roll_matrix(token_col, length):
    lanes = lax.broadcasted_iota(jnp.int32, (length, length), 1).astype(jnp.float32)
    return jnp.where(token_col == lanes, 1.0, 0.0).astype(jnp.bfloat16)


def unroll_matrix(token_row, length):
    places = lax.broadcasted_iota(jnp.int32, (length, length), 0).astype(jnp.float32)
    return jnp.where(token_row == places, 1.0, 0.0).astype(jnp.bfloat16)


def write_masks(mask_ref, facts_row, facts_col, half):
    for block in range(2):
        part = slice(block * half, (block + 1) * half)
        code_i, base_i = facts_col[part, 0:1], facts_col[part, 1:2]
        code_j = facts_row[0:1, part]
        same = code_j >= base_i
        mask_ref[0, block] = jnp.where(same & (code_j <= code_i), 0.0, MASKED_SCORE)
        mask_ref[1, block] = jnp.where(same & (code_j < code_i), 0.0, MASKED_SCORE)


def query_sides(query, bias, segment_col, factor):
    wide = query.astype(jnp.float32)
    with_u = split_pair((wide + bias[0]) * factor)
    with_w = split_pair((wide + bias[1]) * factor)
    with_c = wide + bias[2]
    same = jnp.sum(with_c * bias[3], -1, keepdims=True) * factor
    change = jnp.sum(with_c * (bias[4] - bias[3]), -1, keepdims=True) * factor
    return with_u, with_w, with_c, same + change * segment_col, change * (1.0 - 2.0 * segment_col)


def block_scores(with_u, with_w, keys_twice, relative_twice, half):
    content = dot_nt(with_u, keys_twice)
    position = dot_nt(with_w, relative_twice)
    return content + pltpu.roll(position, half, 1, stride=1, stride_axis=0)[:, :half]


def greet(axis, masks):
    barrier = pltpu.get_barrier_semaphore()
    for mask in masks:
        pl.semaphore_signal(
            barrier, inc=1, device_id={axis: lax.axis_index(axis) ^ mask}, device_id_type=pl.DeviceIdType.MESH
        )
    pl.semaphore_wait(barrier, len(masks))


class Links:
    def __init__(self, send_sems, recv_sems):
        self.send_sems, self.recv_sems, self.used = send_sems, recv_sems, 0

    def push(self, source, place, axis, distance):
        index = self.used
        self.used = index + 1
        return pltpu.make_async_remote_copy(
            source, place, self.send_sems.at[index], self.recv_sems.at[index],
            device_id={axis: lax.axis_index(axis) ^ distance}, device_id_type=pl.DeviceIdType.MESH,
        )


def add_planes(place, first, second):
    def one(z, carry):
        place[z] = (first(z).astype(jnp.float32) + second[z].astype(jnp.float32)).astype(place.dtype)
        return carry

    lax.fori_loop(0, place.shape[0], one, 0)


class Scatter:
    def __init__(self, links, sem, source, rows, order, refs):
        self.kept, self.got, self.got_two, self.got_last = refs
        heads_here, dp_here = lax.axis_index("heads"), lax.axis_index("dp")
        x, y, z = heads_here >> 1, dp_here & 1, dp_here >> 1
        if order == "xy":
            own, other, first, second, self.mine = source.at[:, :, x, rows], source.at[:, :, 1 - x, rows], ("heads", 2), ("dp", 1), y
        else:
            own, other, first, second, self.mine = source.at[:, y, :, rows], source.at[:, 1 - y, :, rows], ("dp", 1), ("heads", 2), x
        self.load = pltpu.make_async_copy(own, self.kept, sem)
        self.copy = links.push(other, self.got, *first)
        self.copy_two = links.push(self.kept.at[:, 1 - self.mine], self.got_two, *second)
        self.place = z
        self.copies_last = [
            links.push(self.got_two.at[z ^ m], self.got_last.at[m - 1], "dp", 2 * m)
            for m in range(1, source.shape[0])
        ]

    def begin(self):
        self.load.start()
        self.copy.start()

    def second(self):
        self.load.wait()
        self.copy.wait()
        add_planes(self.kept, lambda z: self.kept[z], self.got)
        self.copy_two.start()

    def third(self):
        self.copy_two.wait()
        add_planes(self.got_two, lambda z: self.kept[z, self.mine], self.got_two)
        for copy in self.copies_last:
            copy.start()

    def last(self):
        for copy in self.copies_last:
            copy.wait()
        total = self.got_two[self.place].astype(jnp.float32)
        for index in range(self.got_last.shape[0]):
            total = total + self.got_last[index].astype(jnp.float32)
        return total


def square_sum(values):
    return jnp.sum(jnp.sum(values * values, -1, keepdims=True), 0, keepdims=True)


def unit_copies(links, source, places, starts, size, base):
    heads_here = lax.axis_index("heads")
    own = places.shape[1]
    copies = []
    for start in starts:
        owner = start // own
        distance = owner ^ heads_here
        index = links.used
        links.used = index + 1
        copies.append(
            pltpu.make_async_remote_copy(
                source.at[pl.ds(pl.multiple_of(start, size), size)],
                places.at[distance, pl.ds(pl.multiple_of(start - owner * own, size), size)],
                links.send_sems.at[index], links.recv_sems.at[base + distance],
                device_id={"heads": owner}, device_id_type=pl.DeviceIdType.MESH,
            )
        )
    return copies


class Gather:
    def __init__(self, links, sem, full, own, rows, order):
        heads_here, dp_here = lax.axis_index("heads"), lax.axis_index("dp")
        x, core, y, z = heads_here >> 1, heads_here & 1, dp_here & 1, dp_here >> 1

        def same(*place):
            part = full.at[place + (rows,)]
            return part, part

        everything = slice(None)
        planes = full.shape[0]
        mine = full.at[z, y, x, core, rows]
        self.keep = pltpu.make_async_copy(own.at[rows], mine, sem)
        self.along_z = [links.push(own.at[rows], mine, "dp", 2 * m) for m in range(1, planes)]
        column = same(everything, y, x, core)
        across = ("heads", 2), ("dp", 1)
        if order == "xy":
            near, wide = same(everything, y, 1 - x, core), same(everything, y, everything, core)
            last = same(everything, 1 - y, everything, core)
        else:
            near, wide = same(everything, 1 - y, x, core), same(everything, everything, x, core)
            last = same(everything, everything, 1 - x, core)
            across = across[1], across[0]
        self.first = links.push(*column, *across[0])
        self.second = links.push(*wide, *across[1])
        self.to_sibling = [links.push(*part, "heads", 1) for part in (column, near, last)]

    def begin(self):
        self.keep.start()
        for copy in self.along_z:
            copy.start()

    def step_one(self):
        self.keep.wait()
        for copy in self.along_z:
            copy.wait()
        self.first.start()
        self.to_sibling[0].start()

    def step_two(self):
        self.first.wait()
        self.second.start()
        self.to_sibling[1].start()

    def step_three(self):
        self.second.wait()
        self.to_sibling[2].start()

    def finish(self):
        for copy in self.to_sibling:
            copy.wait()


def write_facts(lengths_ref, order_ref, segment_ref, row_ref, col_ref):
    rows, length = order_ref.shape
    down = lax.broadcasted_iota(jnp.int32, (length, length), 0).astype(jnp.float32)
    along = lax.broadcasted_iota(jnp.int32, (length, length), 1).astype(jnp.float32)
    places_col, places_row = down[:, 0:1], along[0:1, :]
    row_ref[...] = jnp.zeros_like(row_ref)
    col_ref[...] = jnp.zeros_like(col_ref)

    def as_column(values):
        return jnp.sum(jnp.where(down == along, values, 0.0), 1, keepdims=True)

    for row in range(rows):
        ends, start, end = [], 0, 0
        for document in range(lengths_ref.shape[1]):
            count = lengths_ref[row, document]
            start = start + (count == length // 2).astype(jnp.int32) * end
            end = end + count
            ends.append(end.astype(jnp.float32))
        start = start.astype(jnp.float32)
        order = order_ref[row : row + 1].astype(jnp.float32)
        segment = segment_ref[row : row + 1].astype(jnp.float32)
        order_col, segment_col = as_column(order), as_column(segment)
        for place, turned in ((places_row, False), (places_col, True)):
            token = place + start
            token = jnp.where(token >= length, token - length, token)
            base = jnp.zeros_like(token)
            for end in ends:
                base = base + jnp.where(token >= end, float(length), 0.0)
            if turned:
                rank = jnp.sum(jnp.where(order == token, along, 0.0), 1, keepdims=True)
                kind = jnp.sum(jnp.where(along == token, segment, 0.0), 1, keepdims=True)
                for index, values in enumerate((base + rank, base, kind, token)):
                    col_ref[row, :, index : index + 1] = values
            else:
                rank = jnp.sum(jnp.where(order_col == token, down, 0.0), 0, keepdims=True)
                kind = jnp.sum(jnp.where(down == token, segment_col, 0.0), 0, keepdims=True)
                for index, values in enumerate((base + rank, base, kind, token)):
                    row_ref[row, index : index + 1] = values


def turn(values):
    size = values.shape[1]
    same = lax.broadcasted_iota(jnp.int32, (size, size), 0) == lax.broadcasted_iota(jnp.int32, (size, size), 1)
    identity = jnp.where(same, 1.0, 0.0).astype(jnp.bfloat16)
    return dot_nt(identity, values.astype(jnp.bfloat16)).astype(jnp.bfloat16)


def attention_forward_kernel(head_size, group, parts, fast, *refs):
    content_hbm, query_hbm, weight_in, up_in, down_in, out_in, bias_in, refs = *refs[:7], refs[7:]
    lengths_ref, order_ref, segment_ref, table_ref, head_ref, refs = *refs[:5], refs[5:]
    proj_ref, row_ref, col_ref, bias_all, refs = *refs[:4], refs[4:]
    mixed_pieces, refs = refs[0], refs[1:]
    content_out, query_out, weight_out, chance_out, refs = *refs[:4], refs[4:]
    if fast:
        up_all, down_all, out_all, refs = *refs[:3], refs[3:]
    content_all, query_all, weight_ref, mixed_ref, relative_ref, mask_ref, chance_ref, refs = *refs[:7], refs[7:]
    sems, send_sems, recv_sems, refs = *refs[:3], refs[3:]
    rows, length = row_ref.shape[0], row_ref.shape[2]
    half = length // 2
    tokens, depth = content_hbm.shape
    width = weight_ref.shape[-1] // 4
    heads = width // head_size
    factor = head_size ** (-0.5) * LOG2E
    heads_here, dp_here = lax.axis_index("heads"), lax.axis_index("dp")
    chip = heads_here >> 1
    links = Links(send_sems, recv_sems)

    def token_part(k):
        return pl.ds(pl.multiple_of((heads_here ^ k) * tokens, tokens), tokens)

    streams = ((content_hbm, content_all), (query_hbm, query_all))
    local = [pltpu.make_async_copy(own, full.at[token_part(0)], sems.at[n]) for n, (own, full) in enumerate(streams)]
    if not fast:
        local.append(pltpu.make_async_copy(weight_in, weight_ref, sems.at[2]))
    for copy in local:
        copy.start()
    barrier = pltpu.get_barrier_semaphore()
    peers = [("heads", k) for k in range(1, group)] + [("dp", k) for k in range(1, parts)]
    for axis, k in peers:
        pl.semaphore_signal(
            barrier, inc=1, device_id={axis: lax.axis_index(axis) ^ k}, device_id_type=pl.DeviceIdType.MESH
        )
    if fast:
        weight_send, up_send, down_send, out_send = refs
        weight_send[...] = jnp.concatenate([weight_in[kind] for kind in range(4)], -1).astype(jnp.bfloat16)
    pl.semaphore_wait(barrier, len(peers))
    far = [links.push(own, full.at[token_part(0)], "heads", 2) for own, full in streams]
    near = [links.push(own, full.at[token_part(0)], "heads", 1) for own, full in streams]
    passed = [links.push(full.at[token_part(2)], full.at[token_part(2)], "heads", 1) for _, full in streams]
    bias_copies = [links.push(bias_in, bias_all.at[heads_here], "heads", k) for k in range(1, group)]
    for copy in far + near + bias_copies:
        copy.start()
    if fast:
        y, z = dp_here & 1, dp_here >> 1
        weight_z, weight_y = [], []
        for pair in (pl.ds(0, 2 * width), pl.ds(2 * width, 2 * width)):
            mine = weight_ref.at[z, y, :, pair]
            weight_z.append([links.push(weight_send.at[:, pair], mine, "dp", 2 * m) for m in range(1, parts // 2)])
            column = weight_ref.at[:, y, :, pair]
            weight_y.append(links.push(column, column, "dp", 1))
            for copy in weight_z[-1]:
                copy.start()
        weight_ref[z, y] = weight_send[...]
        up_send[...] = up_in[...].astype(jnp.bfloat16)
        down_send[...] = down_in[...].astype(jnp.bfloat16)
        out_send[...] = turn(out_in[...])
        pick = up_send.shape[0]
        early, late = pl.ds(0, pick // 2), pl.ds(pick // 2, pick // 2)
        up_one = Gather(links, sems.at[3], up_all, up_send, early, "xy")
        up_two = Gather(links, sems.at[4], up_all, up_send, late, "xy")
        down_one = Gather(links, sems.at[5], down_all, down_send, early, "yx")
        down_two = Gather(links, sems.at[6], down_all, down_send, late, "xy")
        out_one = Gather(links, sems.at[7], out_all, out_send, pl.ds(0, pick), "yx")
        gathers = (up_one, up_two, down_one, down_two, out_one)
    bias_all[heads_here] = bias_in[...]
    write_facts(lengths_ref, order_ref, segment_ref, row_ref, col_ref)
    if fast:
        for first, second in zip(weight_z, weight_y):
            for copy in first:
                copy.wait()
            second.start()
        down_one.begin()
        out_one.begin()
        for copy in weight_y[:1]:
            copy.wait()
        up_one.begin()
        weight_y[1].wait()
    for copy in local + near:
        copy.wait()

    def weight(first, last):
        return weight_ref[..., first * width : last * width].reshape(depth, (last - first) * width)

    saves = [
        pltpu.make_async_copy(content_all, content_out, sems.at[0]),
        pltpu.make_async_copy(query_all, query_out, sems.at[1]),
        pltpu.make_async_copy(weight_ref, weight_out, sems.at[2]),
    ]
    saves[2].start()
    relative_ref[...] = dot(table_ref[...], weight(3, 4)).astype(jnp.bfloat16)

    def pass_on():
        for arrived, onward in zip(far, passed):
            arrived.wait()
            onward.start()

    def nothing():
        pass

    events = {(0, 0): [pass_on]}
    if fast:
        events = {
            (0, 0): [pass_on, down_one.step_one, up_two.begin],
            (0, 1): [up_one.step_one, down_two.begin],
            (0, 2): [out_one.step_one, down_one.step_two],
            (1, 0): [up_one.step_two, up_two.step_one],
            (1, 1): [down_two.step_one, out_one.step_two],
            (1, 2): [up_two.step_two, down_one.step_three],
            (2, 0): [down_two.step_two, up_one.step_three],
            (2, 1): [out_one.step_three],
        }

    def one_row(step, carry):
        row = jnp.where(step == 0, 0, rows - step)
        row = jnp.where(chip == 0, row, rows - 1 - row)

        @pl.when(step == 1)
        def _():
            for copy in passed:
                copy.wait()
            for save in saves[:2]:
                save.start()

        here = pl.ds(pl.multiple_of(row * length, length), length)
        facts_row, facts_col = row_ref[row], col_ref[row]
        write_masks(mask_ref, facts_row, facts_col, half)
        roll = roll_matrix(facts_col[:, 3:4], length)
        unroll = unroll_matrix(facts_row[3:4, :], length)
        content, query = content_all[here], query_all[here]
        joined = jnp.concatenate(
            [
                dot(content, weight(0, 3)).astype(jnp.bfloat16),
                dot(query, weight(0, 1)).astype(jnp.bfloat16),
            ],
            -1,
        )
        proj_ref[row] = dot(roll, joined).astype(jnp.bfloat16)
        segment_col, segment_row = facts_col[:, 2:3], facts_row[2:3, :]
        mixed = [[None] * heads, [None] * heads]
        for head in range(heads):
            cols = lambda kind: slice(kind * width + head * head_size, kind * width + (head + 1) * head_size)
            own_cols = slice(head * head_size, (head + 1) * head_size)
            bias = [head_ref[kind, head : head + 1] for kind in range(5)]
            keys, values = proj_ref[row, :, cols(1)], proj_ref[row, :, cols(2)]
            keys_twice = jnp.concatenate([keys, keys], -1)
            relative = relative_ref[:, own_cols]
            relative_twice = jnp.concatenate([relative, relative], -1)
            for stream in range(2):
                with_u, with_w, _, own, slope = query_sides(
                    proj_ref[row, :, cols(3 * stream)], bias, segment_col, factor
                )
                pieces = []
                for block in range(2):
                    part = slice(block * half, (block + 1) * half)
                    scores = block_scores(
                        with_u[part], with_w[part], keys_twice[part], relative_twice, half
                    )
                    scores = scores + own[part] + slope[part] * segment_row[:, part] + mask_ref[stream, block]
                    highest = jnp.maximum(jnp.max(scores, -1, keepdims=True), 0.0)
                    weights = jnp.exp2(scores - highest)
                    totals = jnp.exp2(-highest) + jnp.sum(weights, -1, keepdims=True)
                    chances = (weights * (1.0 / totals)).astype(jnp.bfloat16)
                    chance_ref[row, stream * heads + head, block] = chances
                    pieces.append(dot(chances, values[part]))
                mixed[stream][head] = jnp.concatenate(pieces, 0).astype(jnp.bfloat16)
            for when, actions in events.items():
                if when[1] == head:
                    @pl.when(step == when[0])
                    def _():
                        for action in actions:
                            action()
        both = jnp.concatenate(mixed[0] + mixed[1], -1)
        mixed_ref[here] = dot(unroll, both).astype(jnp.bfloat16)
        chance_copy(row).start()

        @pl.when(step == 1)
        def _():
            for copy in far_units:
                copy.start()

        return carry

    def chance_copy(row):
        return pltpu.make_async_copy(chance_ref.at[row], chance_out.at[row], sems.at[9 + row])

    unit = half // 2
    far_row = jnp.where(chip == 0, (rows - 1) * length, 0)
    far_middle = jnp.where(chip == 0, length + half, length)
    base = links.used
    links.used = base + group
    far_units = unit_copies(links, mixed_ref, mixed_pieces, [far_row + n * unit for n in range(4)], unit, base)
    middle_units = unit_copies(links, mixed_ref, mixed_pieces, [far_middle + n * unit for n in range(2)], unit, base)
    far_pieces = [
        pltpu.make_async_remote_copy(
            mixed_pieces.at[k], mixed_pieces.at[k], send_sems.at[base + k], recv_sems.at[base + k],
            device_id={"heads": heads_here ^ k}, device_id_type=pl.DeviceIdType.MESH,
        )
        for k in (2, 3)
    ]
    lax.fori_loop(0, rows, one_row, 0)
    for copy in middle_units:
        copy.start()
    keep = pltpu.make_async_copy(mixed_ref.at[token_part(0)], mixed_pieces.at[0], sems.at[8])
    keep.start()
    sends = [links.push(mixed_ref.at[token_part(1)], mixed_pieces.at[1], "heads", 1)]
    for copy in sends:
        copy.start()
    if fast:
        up_two.step_three()
        down_two.step_three()
    for copy in [keep] + saves + sends + bias_copies:
        copy.wait()
    for copy in far_units + middle_units:
        copy.wait_send()
    for row in range(rows):
        chance_copy(row).wait()
    for piece in far_pieces:
        piece.wait_recv()
    if fast:
        for gather in gathers:
            gather.finish()


def attention_forward(
    content, query, attn_proj, up_proj, down_proj, out_proj, up_bias, doc_lengths, factor_order, segment_ids,
    table, head_bias,
):
    rows, length = segment_ids.shape
    group, parts = lax.axis_size("heads"), lax.axis_size("dp")
    fast = by_pieces(attn_proj.shape[1])
    own, depth = content.shape
    tokens = own * group
    pick, width = attn_proj.shape[1:]
    hidden = up_proj.shape[1]
    head_size = head_bias.shape[-1]
    half = length // 2
    inside = pl.BlockSpec(memory_space=pltpu.VMEM)
    outside = pl.BlockSpec(memory_space=pl.ANY)
    scalars = pl.BlockSpec(memory_space=pltpu.SMEM)
    bfloat, float32 = jnp.bfloat16, jnp.float32
    weight_shape = (parts // 2, 2, pick, 4 * width) if fast else (depth, 4 * width)
    out_shape = [
        jax.ShapeDtypeStruct((rows, length, 4 * width), bfloat),
        jax.ShapeDtypeStruct((rows, 8, length), float32),
        jax.ShapeDtypeStruct((rows, length, 8), float32),
        jax.ShapeDtypeStruct((group, 1, hidden), float32),
    ]
    out_specs = [inside] * 4 + [outside] * 5
    out_shape += [jax.ShapeDtypeStruct((group, own, 2 * width), bfloat)]
    out_shape += [jax.ShapeDtypeStruct((tokens, depth), bfloat)] * 2
    out_shape += [jax.ShapeDtypeStruct(weight_shape, bfloat)]
    chance_shape = (rows, 2 * width // head_size, 2, half, half)
    out_shape += [jax.ShapeDtypeStruct(chance_shape, bfloat)]
    scratch = [
        pltpu.VMEM((tokens, depth), bfloat),
        pltpu.VMEM((tokens, depth), bfloat),
        pltpu.VMEM(weight_shape, bfloat),
        pltpu.VMEM((tokens, 2 * width), bfloat),
        pltpu.VMEM((length, width), bfloat),
        pltpu.VMEM((2, 2, half, half), float32),
        pltpu.VMEM(chance_shape, bfloat),
        pltpu.SemaphoreType.DMA((9 + rows,)),
        pltpu.SemaphoreType.DMA((72,)),
        pltpu.SemaphoreType.DMA((72,)),
    ]
    if fast:
        weight_spec = inside
        out_specs += [outside] * 3
        out_shape += [
            jax.ShapeDtypeStruct((parts // 2, 2, group // 2, 2, pick, c), bfloat) for c in (hidden, hidden, width)
        ]
        scratch += [
            pltpu.VMEM((pick, 4 * width), bfloat),
            pltpu.VMEM((pick, hidden), bfloat),
            pltpu.VMEM((pick, hidden), bfloat),
            pltpu.VMEM((pick, width), bfloat),
        ]
    else:
        weight_spec = outside
        attn_proj = lax.all_gather(attn_proj.astype(bfloat), "dp", axis=1, tiled=True)
        attn_proj = jnp.swapaxes(attn_proj, 0, 1).reshape(weight_shape)
    results = pl.pallas_call(
        functools.partial(attention_forward_kernel, head_size, group, parts if fast else 1, fast),
        in_specs=[outside, outside, weight_spec] + [inside] * 4 + [scalars] + [inside] * 4,
        out_specs=out_specs,
        out_shape=out_shape,
        scratch_shapes=scratch,
        compiler_params=pltpu.CompilerParams(
            vmem_limit_bytes=VMEM_LIMIT, collective_id=0, has_side_effects=True
        ),
    )(
        content, query, attn_proj, up_proj, down_proj.T, out_proj, up_bias[None], doc_lengths, factor_order,
        segment_ids, table, head_bias,
    )
    proj, facts_row, facts_col, bias_all, mixed_pieces = results[:5]
    content_all, query_all, weight_all, chance_all = results[5:9]
    if fast:
        wide = [full.reshape(parts, group, pick, full.shape[-1]) for full in results[9:]]
    else:
        wide = [gather_all(m) for m in (up_proj.astype(bfloat), down_proj.T.astype(bfloat), out_proj.T.astype(bfloat))]
    kept = (content_all, query_all, weight_all, chance_all, (facts_row, facts_col), proj)
    return kept, bias_all, mixed_pieces, wide


def attention_backward_kernel(head_size, group, parts, fast, *refs):
    content_hbm, query_hbm, weight_hbm, chance_hbm, refs = *refs[:4], refs[4:]
    upper_pieces, dresid_hbm, refs = refs[0], refs[1], refs[2:]
    turned_ref, bias_ref, row_ref, col_ref, proj_ref = refs[:5]
    sources, small_ref, refs = refs[5:8], refs[8], refs[9:]
    outputs, refs = refs[:9] if fast else refs[:4], refs[9:] if fast else refs[4:]
    content_grad_ref, query_grad_ref, dhead_ref = outputs[:3]
    content_all, query_all, weight_ref, upper_all, dinput_ref, dweight_ref = refs[:6]
    chance_ref, backward_ref, drel_ref, dcols_ref, dkeys_ref, dvalues_ref = refs[6:12]
    dwide_ref, side_ref, cross_ref, swap_ref, dresid_ref, dhead_own, refs = *refs[12:18], refs[18:]
    sems, send_sems, recv_sems, refs = *refs[:3], refs[3:]
    rows, length = row_ref.shape[0], row_ref.shape[2]
    half = length // 2
    depth, width = content_all.shape[1], weight_ref.shape[-1] // 4
    heads = width // head_size
    scale = head_size ** (-0.5)
    heads_here, dp_here = lax.axis_index("heads"), lax.axis_index("dp")
    chip = heads_here >> 1
    tokens = upper_pieces.shape[1]
    links = Links(send_sems, recv_sems)

    def token_part(k):
        return pl.ds(pl.multiple_of((heads_here ^ k) * tokens, tokens), tokens)

    copies = [
        pltpu.make_async_copy(content_hbm, content_all, sems.at[0]),
        pltpu.make_async_copy(query_hbm, query_all, sems.at[1]),
        pltpu.make_async_copy(weight_hbm, weight_ref, sems.at[2]),
        pltpu.make_async_copy(chance_hbm, chance_ref, sems.at[10]),
        pltpu.make_async_copy(upper_pieces.at[0], upper_all.at[token_part(0)], sems.at[3]),
    ]
    for copy in copies:
        copy.start()
    dresid_copy = pltpu.make_async_copy(dresid_hbm, dresid_ref, sems.at[4])
    dresid_copy.start()

    def weight(first, last):
        return weight_ref[..., first * width : last * width].reshape(depth, (last - first) * width)

    barrier = pltpu.get_barrier_semaphore()
    peers = [("heads", k) for k in range(1, group)] + [("dp", k) for k in range(1, parts)]
    for axis, k in peers:
        pl.semaphore_signal(
            barrier, inc=1, device_id={axis: lax.axis_index(axis) ^ k}, device_id_type=pl.DeviceIdType.MESH
        )
    pl.semaphore_wait(barrier, len(peers))
    upper_copies = [
        links.push(upper_pieces.at[k], upper_all.at[token_part(0)], "heads", k) for k in range(1, group)
    ]
    for copy in upper_copies:
        copy.start()
    if fast:
        pick = sources[0].shape[3]
        early, late, full = pl.ds(0, pick // 2), pl.ds(pick // 2, pick // 2), pl.ds(0, pick)
        plan = ((0, early, "yx"), (0, late, "yx"), (1, early, "yx"), (1, late, "xy"), (2, full, "yx"))
        scatters = [
            Scatter(links, sems.at[5 + n], sources[which], part, order, refs[4 * n : 4 * n + 4])
            for n, (which, part, order) in enumerate(plan)
        ]
        up_one, up_two, down_one, down_two, out_one = scatters
        small_got, small_more, small_mid, dweight_got, dweight_more, head_got, tile_ref, tile_got, tile_more = refs[20:]
        up_one.begin()
        out_one.begin()
        small_first = [links.push(small_ref, small_got.at[heads_here], "heads", k) for k in range(1, group)]
        for copy in small_first:
            copy.start()
        small_got[heads_here] = small_ref[...]
        small_second = [links.push(small_mid, small_more.at[dp_here], "dp", k) for k in range(1, parts)]
    for copy in copies:
        copy.wait()
    upper_copies[0].wait()
    backward_ref[...] = dot(turned_ref[...], weight(3, 4)).astype(jnp.bfloat16)
    drel_ref[...] = jnp.zeros_like(drel_ref)
    dweight_ref[...] = jnp.zeros_like(dweight_ref)
    dhead_own[...] = jnp.zeros_like(dhead_own)
    bias_cols = [bias_ref[kind].T for kind in range(2)]
    ones = jnp.ones((16, length), jnp.bfloat16)

    def act(condition, actions):
        @pl.when(condition)
        def _():
            for action in actions:
                action()

    def span(start, size):
        return pl.ds(pl.multiple_of(start, size), size)

    def sides(first, size, slot):
        mine, other = span(first + core * size, size), span(first + (1 - core) * size, size)
        landed = side_ref.at[:, pl.ds(slot, size)]
        return links.push(dinput_ref.at[:, other], landed, "heads", 1), mine, landed

    def add_side(side, landed=None):
        copy, mine, place = side
        copy.wait()
        for n in range(2):
            dinput_ref[n, mine] = (
                dinput_ref[n, mine].astype(jnp.float32) + place[n].astype(jnp.float32)
            ).astype(jnp.bfloat16)

    core, unit = heads_here & 1, half // 2
    own_first = jnp.where(chip == 0, 0, (rows - 1) * length)
    far_first = jnp.where(chip == 0, (rows - 1) * length, 0)
    own_middle = jnp.where(chip == 0, length, length + half)
    far_middle = jnp.where(chip == 0, length + half, length)
    own_side, far_side = sides(own_first, half, 0), sides(far_first, half, half)
    own_side_two, far_side_two = sides(own_middle, unit, 2 * half), sides(far_middle, unit, 2 * half + unit)
    across = [
        (links.push(dinput_ref.at[:, side[1]], cross_ref.at[:, place], "heads", 2), mine[1], cross_ref.at[:, place])
        for side, mine, place in (
            (far_side, own_side, pl.ds(0, half)), (far_side_two, own_side_two, pl.ds(half, unit))
        )
    ]
    swap_part = span(2 * half + 5 * unit * chip - half * core, unit)
    swap_got = span(2 * half + 5 * unit * chip - half * (1 - core), unit)
    swap = links.push(dinput_ref.at[:, swap_part], swap_ref, "heads", 1)

    def far_over():
        add_side(far_side)
        across[0][0].start()

    def small_middle():
        for copy in small_first:
            copy.wait()
        total = small_got[0]
        for k in range(1, group):
            total = total + small_got[k]
        small_mid[...] = total
        small_more[dp_here] = total
        for copy in small_second:
            copy.start()

    events = {
        (0, heads): [own_side[0].start],
        (1, heads): [far_side[0].start],
        (2, 0): [far_over, lambda: add_side(own_side)],
    }
    if fast:
        for place, actions in {
            (0, 1): [down_two.begin],
            (0, 2): [up_two.begin],
            (0, heads): [up_one.second, out_one.second],
            (1, 0): [small_middle],
            (1, 1): [down_two.second, up_one.third],
            (1, 2): [up_two.second, down_one.begin, out_one.third],
            (2, 0): [down_two.third],
            (2, 1): [up_two.third],
            (2, 2): [down_one.second],
        }.items():
            events[place] = events.get(place, []) + actions

    def one_row(step, carry):
        row = jnp.where(step == 0, 0, rows - step)
        row = jnp.where(chip == 0, row, rows - 1 - row)

        @pl.when(step == 1)
        def _():
            for copy in upper_copies[1:]:
                copy.wait()

        row_part(step, row)
        return carry

    def row_part(step, row):
        here = pl.ds(pl.multiple_of(row * length, length), length)
        content_ref, query_ref = content_all.at[here], query_all.at[here]
        facts_row, facts_col = row_ref[row], col_ref[row]
        roll = roll_matrix(facts_col[:, 3:4], length)
        upper = dot(roll, upper_all[here]).astype(jnp.bfloat16)
        segment_col = facts_col[:, 2:3]
        down = lax.broadcasted_iota(jnp.int32, (half, half), 0)
        along = lax.broadcasted_iota(jnp.int32, (half, half), 1)
        mirror = jnp.where(down + along == half - 1, 1.0, 0.0).astype(jnp.bfloat16)
        lane = lax.broadcasted_iota(jnp.int32, (length, head_size), 1)
        extra = jnp.where(lane == 0, segment_col, jnp.where(lane == 1, 1.0, 0.0)).astype(jnp.bfloat16)
        for head in range(heads):
            own_cols = slice(head * head_size, (head + 1) * head_size)
            cols = lambda kind: slice(kind * width + head * head_size, kind * width + (head + 1) * head_size)
            bias = [bias_ref[kind, head : head + 1] for kind in range(5)]
            keys, values = proj_ref[row, :, cols(1)], proj_ref[row, :, cols(2)]
            keys_extra = jnp.concatenate([keys, extra], -1)
            backward = backward_ref[:, own_cols]
            u_col, w_col = (turned_bias[:, head : head + 1] for turned_bias in bias_cols)
            heads_sums = [jnp.zeros((1, head_size), jnp.float32) for _ in range(5)]
            for stream in range(2):
                query_now = proj_ref[row, :, cols(3 * stream)]
                with_c = query_now.astype(jnp.float32) + bias[2]
                index = stream * heads + head
                upper_now = upper[:, index * head_size : (index + 1) * head_size]
                query_t, upper_t = jnp.concatenate([query_now.T, ones], 0), upper_now.T
                dquery = []
                for block in range(2):
                    part = slice(block * half, (block + 1) * half)
                    low_chances = chance_ref[row, index, block]
                    chances = low_chances.astype(jnp.float32)
                    weighted = chances * dot_nt(upper_now[part], values[part])
                    centre = jnp.sum(weighted, -1, keepdims=True)
                    dscore = (weighted - chances * centre).astype(jnp.bfloat16)
                    dvalue_part = dot(upper_t[:, part], low_chances)
                    by_key = dot(dscore, keys_extra[part])
                    turned = dot(dscore, mirror)
                    wide = pltpu.roll(
                        jnp.concatenate([turned, jnp.zeros((half, half), jnp.float32)], -1),
                        0, 1, stride=1, stride_axis=0,
                    ).astype(jnp.bfloat16)
                    by_place = dot(wide, backward)
                    dkey_part = dot(query_t[:, part], dscore)
                    dkey_part = dkey_part[:head_size] + u_col * dkey_part[head_size : head_size + 1]
                    drel_part = dot(query_t[:, part], wide)
                    drel_ref[own_cols] += drel_part[:head_size] + w_col * drel_part[head_size : head_size + 1]
                    if stream == 0:
                        dkeys_ref[own_cols, part] = dkey_part
                        dvalues_ref[own_cols, part] = dvalue_part
                    else:
                        dkeys_ref[own_cols, part] += dkey_part
                        dvalues_ref[own_cols, part] += dvalue_part
                    with_seg, total = by_key[:, head_size : head_size + 1], by_key[:, head_size + 1 : head_size + 2]
                    seg_i = segment_col[part]
                    seg_one = with_seg + seg_i * (total - 2.0 * with_seg)
                    seg_zero = total - seg_one
                    by_key = by_key[:, :head_size]
                    by_segment = seg_zero * bias[3] + seg_one * bias[4]
                    dquery.append((by_key + by_place + by_segment) * scale)
                    for kind, term in enumerate(
                        (by_key, by_place, by_segment, seg_zero * with_c[part], seg_one * with_c[part])
                    ):
                        heads_sums[kind] = heads_sums[kind] + jnp.sum(term, 0, keepdims=True)
                dcols_ref[:, cols(3 * stream)] = jnp.concatenate(dquery, 0).astype(jnp.bfloat16)
            for kind in range(5):
                dhead_own[kind : kind + 1, own_cols] += heads_sums[kind] * scale
            for when, actions in events.items():
                if when[1] == head:
                    act(step == when[0], actions)
        dcols_ref[:, width : 2 * width] = (dkeys_ref[...] * scale).astype(jnp.bfloat16).T
        dcols_ref[:, 2 * width : 3 * width] = dvalues_ref[...].astype(jnp.bfloat16).T
        unroll = unroll_matrix(facts_row[3:4, :], length)
        joined = dot(unroll, dcols_ref[...]).astype(jnp.bfloat16)
        joined_t = joined.T
        content, query = content_ref[...], query_ref[...]
        dweight_ref[: 3 * width] += dot(joined_t[: 3 * width], content)
        dweight_ref[:width] += dot(joined_t[3 * width :], query)
        dinput_ref[0, here] = dot_nt(joined[:, : 3 * width], weight(0, 3)).astype(jnp.bfloat16)
        dinput_ref[1, here] = dot_nt(joined[:, 3 * width :], weight(0, 1)).astype(jnp.bfloat16)
        for when, actions in events.items():
            if when[1] == heads:
                act(step == when[0], actions)

    lax.fori_loop(0, rows, one_row, 0)
    for side in (far_side_two, own_side_two):
        side[0].start()
    drel = drel_ref[...] * scale
    high = drel.astype(jnp.bfloat16)
    low = (drel - high.astype(jnp.float32)).astype(jnp.bfloat16)
    dweight_ref[3 * width :] = dot(high, turned_ref[...]) + dot(low, turned_ref[...])
    dwide_ref[...] = dweight_ref[...].astype(jnp.bfloat16).T.reshape(dwide_ref.shape)
    if fast:
        place_y, place_z = dp_here & 1, dp_here >> 1
        dweight_first = links.push(dwide_ref.at[:, 1 - place_y], dweight_got, "dp", 1)
        dweight_first.start()
        head_copies = [links.push(dhead_own, head_got.at[dp_here], "dp", k) for k in range(1, parts)]
        for copy in head_copies:
            copy.start()
        head_got[dp_here] = dhead_own[...]
    add_side(far_side_two)
    across[1][0].start()
    add_side(own_side_two)
    if fast:
        down_one.third()
        dweight_first.wait()
        add_planes(dweight_got, lambda z: dwide_ref[z, place_y], dweight_got)
        dweight_second = [
            links.push(dweight_got.at[place_z ^ m], dweight_more.at[m - 1], "dp", 2 * m) for m in range(1, 4)
        ]
        for copy in dweight_second:
            copy.start()
    for side in across:
        add_side(side)
    swap.start()
    if fast:
        up_share, down_share, out_share, proj_share, small_sum, norm_ref = outputs[3:]
        squares = jnp.zeros((1, 1), jnp.float32)
        for copy in small_second:
            copy.wait()
        total = small_more[0]
        for k in range(1, parts):
            total = total + small_more[k]
        small_sum[...] = total
        squares = squares + square_sum(total) / (group * parts)
        for copy in head_copies:
            copy.wait()
        total = head_got[0]
        for k in range(1, parts):
            total = total + head_got[k]
        dhead_ref[...] = total
        squares = squares + square_sum(total) / parts
        for (which, part, _), scatter in zip(plan, scatters):
            total = scatter.last()
            (up_share, down_share, out_share)[which][part] = total
            squares = squares + square_sum(total)
        for copy in dweight_second:
            copy.wait()
        total = dweight_got[place_z].astype(jnp.float32)
        for m in range(1, 4):
            total = total + dweight_more[m - 1].astype(jnp.float32)
        proj_share[...] = total
        squares = squares + square_sum(total)
        tile_ref[...] = jnp.broadcast_to(squares, tile_ref.shape)
        tile_got[heads_here] = tile_ref[...]
        tile_first = [links.push(tile_ref, tile_got.at[heads_here], "heads", k) for k in range(1, group)]
        for copy in tile_first:
            copy.start()
    else:
        dhead_ref[...] = dhead_own[...]
        outputs[3][...] = dwide_ref[...]
    if fast:
        for copy in tile_first:
            copy.wait()
        total = tile_got[0]
        for k in range(1, group):
            total = total + tile_got[k]
        tile_more[dp_here] = total
        tile_ref[...] = total
        tile_second = [links.push(tile_ref, tile_more.at[dp_here], "dp", k) for k in range(1, parts)]
        for copy in tile_second:
            copy.start()
    dresid_copy.wait()
    swap.wait()
    dinput_ref[:, swap_got] = swap_ref[...]
    for n, place in enumerate((content_grad_ref, query_grad_ref)):
        place[...] = dresid_ref[n] + dinput_ref[n, token_part(0)].astype(jnp.float32)
    if fast:
        for copy in tile_second:
            copy.wait()
        total = tile_more[0]
        for k in range(1, parts):
            total = total + tile_more[k]
        norm_ref[...] = jnp.sqrt(total)


def attention_backward(
    kept, table, head_bias, upper, dresid, gradients, small
):
    content_all, query_all, weight_all, chance_all, facts, proj = kept
    rows, length = facts[0].shape[0], facts[0].shape[2]
    group = upper.shape[0]
    fast = weight_all.ndim == 4
    tokens, depth = content_all.shape
    own = tokens // group
    pick, width = weight_all.shape[-2], weight_all.shape[-1] // 4
    parts = depth // pick
    head_size = head_bias.shape[-1]
    half = length // 2
    inside = pl.BlockSpec(memory_space=pltpu.VMEM)
    outside = pl.BlockSpec(memory_space=pl.ANY)
    bfloat, float32 = jnp.bfloat16, jnp.float32
    out_shape = [
        jax.ShapeDtypeStruct((own, depth), float32),
        jax.ShapeDtypeStruct((own, depth), float32),
        jax.ShapeDtypeStruct((8, width), float32),
    ]
    wide_shape = weight_all.shape
    scratch = [
        pltpu.VMEM((tokens, depth), bfloat),
        pltpu.VMEM((tokens, depth), bfloat),
        pltpu.VMEM(weight_all.shape, bfloat),
        pltpu.VMEM((tokens, 2 * width), bfloat),
        pltpu.VMEM((2, tokens, depth), bfloat),
        pltpu.VMEM((4 * width, depth), float32),
        pltpu.VMEM(chance_all.shape, bfloat),
        pltpu.VMEM((length, width), bfloat),
        pltpu.VMEM((width, length), float32),
        pltpu.VMEM((length, 4 * width), bfloat),
        pltpu.VMEM((width, length), float32),
        pltpu.VMEM((width, length), float32),
        pltpu.VMEM(wide_shape, bfloat),
        pltpu.VMEM((2, 2 * own, depth), bfloat),
        pltpu.VMEM((2, own, depth), bfloat),
        pltpu.VMEM((2, half // 2, depth), bfloat),
        pltpu.VMEM((2, own, depth), float32),
        pltpu.VMEM((8, width), float32),
        pltpu.SemaphoreType.DMA((11,)),
        pltpu.SemaphoreType.DMA((80,)),
        pltpu.SemaphoreType.DMA((80,)),
    ]
    if fast:
        planes = parts // 2
        columns = [gradient.shape[-1] for gradient in gradients]
        out_shape += [jax.ShapeDtypeStruct((pick, c), float32) for c in columns]
        out_shape += [
            jax.ShapeDtypeStruct((pick, 4 * width), float32),
            jax.ShapeDtypeStruct(small.shape, float32),
            jax.ShapeDtypeStruct((8, 128), float32),
        ]
        gradients = [g.reshape(planes, 2, group // 2, pick, g.shape[-1]) for g in gradients]
        sizes = [(pick // 2, columns[0])] * 2 + [(pick // 2, columns[1])] * 2 + [(pick, columns[2])]
        for size in sizes:
            scratch += [
                pltpu.VMEM((planes, 2) + size, bfloat),
                pltpu.VMEM((planes, 2) + size, bfloat),
                pltpu.VMEM((planes,) + size, bfloat),
                pltpu.VMEM((planes - 1,) + size, bfloat),
            ]
        scratch += [
            pltpu.VMEM((group,) + small.shape, float32),
            pltpu.VMEM((parts,) + small.shape, float32),
            pltpu.VMEM(small.shape, float32),
            pltpu.VMEM((planes, pick, 4 * width), bfloat),
            pltpu.VMEM((planes - 1, pick, 4 * width), bfloat),
            pltpu.VMEM((parts, 8, width), float32),
            pltpu.VMEM((8, 128), float32),
            pltpu.VMEM((group, 8, 128), float32),
            pltpu.VMEM((parts, 8, 128), float32),
        ]
    else:
        out_shape += [jax.ShapeDtypeStruct(wide_shape, bfloat)]
    return pl.pallas_call(
        functools.partial(attention_backward_kernel, head_size, group, parts, fast),
        in_specs=[outside] * 6 + [inside] * 5 + [outside] * 3 + [inside],
        out_specs=[inside] * len(out_shape),
        out_shape=out_shape,
        scratch_shapes=scratch,
        compiler_params=pltpu.CompilerParams(
            vmem_limit_bytes=VMEM_LIMIT, collective_id=2, has_side_effects=True
        ),
    )(
        content_all, query_all, weight_all, chance_all, upper, dresid, table,
        head_bias, *facts, proj, *gradients, small,
    )


def norm_parts(values):
    centred = values - jnp.mean(values, -1, keepdims=True)
    inverse = lax.rsqrt(jnp.mean(centred * centred, -1, keepdims=True) + NORM_EPSILON)
    return centred * inverse, inverse


def norm_back(upstream, normed, inverse, gain):
    scaled = upstream * gain
    first = jnp.mean(scaled, -1, keepdims=True)
    second = jnp.mean(scaled * normed, -1, keepdims=True)
    return inverse * (scaled - first - normed * second)


def column_sum(values):
    return jnp.sum(values, 0, keepdims=True)


def feed_kernel(group, *refs):
    mixed_ref, refs = refs[0], refs[1:]
    bias_ref, refs = refs[0], refs[1:]
    content_ref, query_ref, dcontent_ref, dquery_ref, norm_ref, up_hbm, down_hbm, out_hbm = refs[:8]
    content_out, query_out, dresid_ref, refs = refs[8], refs[9], refs[10], refs[11:]
    dmixed_ref, refs = refs[0], refs[1:]
    dup_hbm, ddown_hbm, dout_ref, dsmall_ref, refs = refs[0], refs[1], refs[2], refs[3], refs[4:]
    up_ref, down_ref, out_ref, hidden_ref, slope_ref = refs[:5]
    low_ref, low_t_ref, normed_ref, total_ref, up_got, down_got, out_got, out_sent = refs[5:13]
    sems, send_sems, recv_sems = refs[13:]
    own, depth = content_ref.shape
    tokens = 2 * own
    here = lax.axis_index("heads")
    core = here & 1
    chips = group // 2
    loads = [
        pltpu.make_async_copy(out_hbm.at[:, j], out_ref.at[j], sems.at[j]) for j in range(group)
    ]
    loads += [
        pltpu.make_async_copy(up_hbm.at[:, j], up_ref.at[j], sems.at[group + j]) for j in range(group)
    ]
    loads += [
        pltpu.make_async_copy(down_hbm.at[:, j], down_ref.at[j], sems.at[2 * group + j])
        for j in range(group)
    ]
    for load in loads:
        load.start()
    greet("heads", [1])
    gain_one, bias_one, bias_out, gain_two, bias_two = [norm_ref[i : i + 1] for i in range(5)]
    for load in loads[:group]:
        load.wait()
    hidden = up_ref.shape[-1]

    def mixed_piece(k):
        both = mixed_ref[k]
        return jnp.concatenate([both[:, : both.shape[1] // 2], both[:, both.shape[1] // 2 :]], 0)

    def out_block(k):
        return out_ref[here ^ k].reshape(depth, out_ref.shape[-1])

    total = jnp.concatenate([content_ref[...], query_ref[...]], 0).astype(jnp.float32)
    for k in range(group):
        total = total + dot_nt(mixed_piece(k), out_block(k))
    normed, inverse_one = norm_parts(total)
    normed_ref[...] = normed
    middle = normed * gain_one + bias_one
    low_ref[...] = middle.astype(jnp.bfloat16)
    low_t_ref[...] = low_ref[...].T
    total_ref[...] = middle + bias_out
    for load in loads[group:]:
        load.wait()

    def forward(j, carry):
        for part in (slice(0, own), slice(own, tokens)):
            before = dot(low_ref[part], up_ref[j].reshape(depth, hidden)) + bias_ref[j]
            square = before * before
            bent = jnp.tanh(GELU_FACTOR * before * (1.0 + GELU_CUBIC * square))
            half_up = 0.5 * (1.0 + bent)
            hidden_now = (before * half_up).astype(jnp.bfloat16)
            slope_ref[j, part] = half_up + 0.5 * before * (1.0 - bent * bent) * GELU_FACTOR * (
                1.0 + 3.0 * GELU_CUBIC * square
            )
            hidden_ref[j, part] = hidden_now
            total_ref[part] += dot_nt(hidden_now, down_ref[j].reshape(depth, hidden))
        return carry

    lax.fori_loop(0, group, forward, 0)
    normed_two, inverse_two = norm_parts(total_ref[...])
    result = (normed_two * gain_two + bias_two).astype(jnp.bfloat16)
    content_out[...] = result[:own]
    query_out[...] = result[own:]
    upstream = jnp.concatenate([dcontent_ref[...], dquery_ref[...]], 0).astype(jnp.float32)
    dsmall_ref[group + 3 : group + 4] = column_sum(upstream * normed_two)
    dsmall_ref[group + 4 : group + 5] = column_sum(upstream)
    dfinal = norm_back(upstream, normed_two, inverse_two, gain_two)
    dsmall_ref[group + 2 : group + 3] = column_sum(dfinal)
    total_ref[...] = dfinal
    dlow = dfinal.astype(jnp.bfloat16)
    dlow_t = dlow.T

    def to_sibling(source, place, index):
        return pltpu.make_async_remote_copy(
            source, place, send_sems.at[index], recv_sems.at[index],
            device_id={"heads": here ^ 1}, device_id_type=pl.DeviceIdType.MESH,
        )

    def back_block(j):
        ddown = dot(dlow_t, hidden_ref[j])
        bias_grad = jnp.zeros((1, hidden), jnp.float32)
        for part in (slice(0, own), slice(own, tokens)):
            dhidden = dot(dlow[part], down_ref[j].reshape(depth, hidden))
            dbefore = (dhidden * slope_ref[j, part]).astype(jnp.bfloat16)
            bias_grad = bias_grad + column_sum(dbefore.astype(jnp.float32))
            total_ref[part] += dot_nt(dbefore, up_ref[j].reshape(depth, hidden))
            hidden_ref[j, part] = dbefore
        dsmall_ref[pl.ds(j, 1)] = bias_grad
        return dot(low_t_ref[...], hidden_ref[j]), ddown

    def sent(chip):
        j = 2 * chip + 1 - core
        return [
            to_sibling(up_ref.at[j], up_got.at[chip], 2 * chip),
            to_sibling(down_ref.at[j], down_got.at[chip], 2 * chip + 1),
        ]

    def kept(chip):
        j = 2 * chip + core
        return [
            pltpu.make_async_copy(up_ref.at[j], dup_hbm.at[:, chip], sems.at[chip]),
            pltpu.make_async_copy(down_ref.at[j], ddown_hbm.at[:, chip], sems.at[group + chip]),
        ]

    def backward_sent(chip, carry):
        j = 2 * chip + 1 - core
        dup, ddown = back_block(j)
        up_ref[j] = dup.astype(jnp.bfloat16).reshape(up_ref.shape[1:])
        down_ref[j] = ddown.astype(jnp.bfloat16).reshape(down_ref.shape[1:])
        for copy in sent(chip):
            copy.start()
        return carry

    def backward_kept(chip, carry):
        j = 2 * chip + core
        dup, ddown = back_block(j)
        for copy in sent(chip):
            copy.wait_recv()
        dup = dup + up_got[chip].astype(jnp.float32).reshape(depth, hidden)
        ddown = ddown + down_got[chip].astype(jnp.float32).reshape(depth, hidden)
        up_ref[j] = dup.astype(jnp.bfloat16).reshape(up_ref.shape[1:])
        down_ref[j] = ddown.astype(jnp.bfloat16).reshape(down_ref.shape[1:])
        for copy in kept(chip):
            copy.start()
        return carry

    lax.fori_loop(0, chips, backward_sent, 0)
    lax.fori_loop(0, chips, backward_kept, 0)
    dmiddle = total_ref[...]
    normed = normed_ref[...]
    dsmall_ref[group : group + 1] = column_sum(dmiddle * normed)
    dsmall_ref[group + 1 : group + 2] = column_sum(dmiddle)
    dresid = norm_back(dmiddle, normed, inverse_one, gain_one)
    total_ref[...] = dresid
    dresid_copy = pltpu.make_async_copy(total_ref, dresid_ref, sems.at[0])
    dresid_copy.start()
    dlow = dresid.astype(jnp.bfloat16)
    dlow_t = dlow.T
    out_copies = [
        to_sibling(out_sent.at[chip], out_got.at[chip], 2 * chips + chip) for chip in range(chips)
    ]
    for chip in range(chips):
        k = 2 * chip + 1
        mixed = mixed_piece(k)
        out_sent[chip] = dot(dlow_t, mixed).astype(jnp.bfloat16).reshape(out_sent.shape[1:])
        out_copies[chip].start()
    for k in range(group):
        dmixed = dot(dlow, out_block(k)).astype(jnp.bfloat16)
        dmixed_ref[k] = jnp.concatenate([dmixed[:own], dmixed[own:]], -1)
    for chip in range(chips):
        k = 2 * chip
        mixed = mixed_piece(k)
        dout = dot(dlow_t, mixed)
        out_copies[chip].wait_recv()
        dout = dout + out_got[chip].astype(jnp.float32).reshape(dout.shape)
        dout_ref[:, (here ^ k) >> 1] = dout.astype(jnp.bfloat16).reshape(out_sent.shape[1:])
    dsmall_ref[group + 5 :] = jnp.zeros((dsmall_ref.shape[0] - group - 5, depth), jnp.float32)
    dresid_copy.wait()
    for chip in range(chips):
        for copy in sent(chip):
            copy.wait_send()
        out_copies[chip].wait_send()
        for copy in kept(chip):
            copy.wait()


def feed_layer(mixed, bias_all, content, query, dcontent, dquery, norm_param, up, down, out):
    group = mixed.shape[0]
    own, depth = content.shape
    parts, _, pick, hidden = up.shape
    width = out.shape[-1]
    inside = pl.BlockSpec(memory_space=pltpu.VMEM)
    outside = pl.BlockSpec(memory_space=pl.ANY)
    tokens = 2 * own
    results = pl.pallas_call(
        functools.partial(feed_kernel, group),
        in_specs=[inside] * 7 + [outside] * 3,
        out_specs=[inside, inside, outside, inside, outside, outside, inside, inside],
        out_shape=[
            jax.ShapeDtypeStruct((own, depth), jnp.bfloat16),
            jax.ShapeDtypeStruct((own, depth), jnp.bfloat16),
            jax.ShapeDtypeStruct((tokens, depth), jnp.float32),
        ]
        + [
            jax.ShapeDtypeStruct((group, own, 2 * width), jnp.bfloat16),
            jax.ShapeDtypeStruct((parts, group // 2, pick, hidden), jnp.bfloat16),
            jax.ShapeDtypeStruct((parts, group // 2, pick, hidden), jnp.bfloat16),
            jax.ShapeDtypeStruct((parts, group // 2, pick, width), jnp.bfloat16),
            jax.ShapeDtypeStruct((16, depth), jnp.float32),
        ],
        scratch_shapes=[
            pltpu.VMEM((group, parts, pick, hidden), jnp.bfloat16),
            pltpu.VMEM((group, parts, pick, hidden), jnp.bfloat16),
            pltpu.VMEM((group, parts, pick, width), jnp.bfloat16),
            pltpu.VMEM((group, tokens, hidden), jnp.bfloat16),
            pltpu.VMEM((group, tokens, hidden), jnp.float32),
            pltpu.VMEM((tokens, depth), jnp.bfloat16),
            pltpu.VMEM((depth, tokens), jnp.bfloat16),
            pltpu.VMEM((tokens, depth), jnp.float32),
            pltpu.VMEM((tokens, depth), jnp.float32),
            pltpu.VMEM((group // 2, parts, pick, hidden), jnp.bfloat16),
            pltpu.VMEM((group // 2, parts, pick, hidden), jnp.bfloat16),
            pltpu.VMEM((group // 2, parts, pick, width), jnp.bfloat16),
            pltpu.VMEM((group // 2, parts, pick, width), jnp.bfloat16),
            pltpu.SemaphoreType.DMA((3 * group,)),
            pltpu.SemaphoreType.DMA((3 * group // 2,)),
            pltpu.SemaphoreType.DMA((3 * group // 2,)),
        ],
        compiler_params=pltpu.CompilerParams(
            vmem_limit_bytes=VMEM_LIMIT, collective_id=1, has_side_effects=True
        ),
    )(mixed, bias_all, content, query, dcontent, dquery, norm_param, up, down, out)
    return results[0], results[1], results[2].reshape(2, own, depth), results[3], results[4:]


def exchange(value, axis, mask):
    return lax.ppermute(value, axis, [(i, i ^ mask) for i in range(lax.axis_size(axis))])


def total_over(value, axis):
    mask = 1
    while mask < lax.axis_size(axis):
        value = value + exchange(value, axis, mask)
        mask = 2 * mask
    return value


def by_pieces(pick):
    return lax.axis_size("dp") <= 8 and pick % 16 == 0


def reduce_projection(full):
    return lax.psum_scatter(full, "dp", scatter_dimension=0, tiled=True).astype(jnp.float32)


def gather_all(own):
    dp, heads = lax.axis_size("dp"), lax.axis_size("heads")
    rows, columns = own.shape
    full = lax.all_gather(own, ("dp", "heads"), axis=0, tiled=False).reshape(dp, heads, rows, columns)
    if by_pieces(rows):
        return full
    return jnp.swapaxes(full, 0, 1).reshape(1, heads, dp * rows, columns)


def scatter_all(full):
    chip = lax.axis_index("heads") // 2
    mine = lax.dynamic_index_in_dim(full[0], chip, 0, False)
    theirs = lax.dynamic_index_in_dim(full[0], 1 - chip, 0, False)
    mine = mine.astype(jnp.float32) + exchange(theirs, "heads", 2).astype(jnp.float32)
    return lax.psum_scatter(mine, "dp", scatter_dimension=0, tiled=True)


def adam_parts(master, first, second, gradient, factor, decayed):
    clipped = gradient * factor
    new_first = BETA_ONE * first + (1.0 - BETA_ONE) * clipped
    new_second = BETA_TWO * second + (1.0 - BETA_TWO) * clipped * clipped
    first_hat = new_first * (1.0 / (1.0 - BETA_ONE**STEP))
    second_hat = new_second * (1.0 / (1.0 - BETA_TWO**STEP))
    update = first_hat / (jnp.sqrt(second_hat) + ADAM_EPSILON)
    if decayed:
        update = update + WEIGHT_DECAY * master
        return new_first, new_second, master - MATRIX_RATE * update
    return new_first, new_second, master - VECTOR_RATE * update


def update_kernel(group, *refs):
    kept, refs = refs[:4], refs[4:]
    up_share, down_share, out_share, proj_share, dhead_ref, small_ref, norm_ref, refs = *refs[:7], refs[7:]
    weights, refs = refs[:21], refs[21:]
    placed, refs = refs[:4], refs[4:]
    results, grad_norm, stages, sems = refs[:28], refs[28], refs[29:33], refs[33]
    loads = [pltpu.make_async_copy(a, b, sems.at[n]) for n, (a, b) in enumerate(zip(kept, stages))]
    stores = [pltpu.make_async_copy(a, b, sems.at[4 + n]) for n, (a, b) in enumerate(zip(stages, placed))]
    for copy in loads:
        copy.start()
    norm = norm_ref[0:1, 0:1]
    grad_norm[...] = norm
    factor = CLIP_NORM / jnp.maximum(norm, CLIP_NORM)

    def put(index, gradient, decayed, place=lambda ref: ref[...], store=None):
        values = adam_parts(*(place(ref) for ref in weights[3 * index : 3 * index + 3]), gradient, factor, decayed)
        for ref, value in zip(results[4 * index : 4 * index + 4], (gradient,) + values):
            if store is None:
                ref[...] = value
            else:
                store(ref, value)

    width = proj_share.shape[1] // 4
    for kind in range(4):
        def store(ref, value, kind=kind):
            ref[kind] = value

        put(0, proj_share[:, kind * width : (kind + 1) * width], True, lambda ref, kind=kind: ref[kind], store)
    for load, store in zip(loads, stores):
        load.wait()
        store.start()
    put(1, out_share[...].T, True)
    put(2, up_share[...], True)
    put(3, down_share[...], True)
    heads, size = weights[12].shape[1:]
    for head in range(heads):
        def store(ref, value, head=head):
            ref[:, head, :] = value

        put(4, dhead_ref[:5, head * size : (head + 1) * size], False, lambda ref, head=head: ref[:, head, :], store)
    def as_row(ref):
        return ref[...].reshape(1, ref.shape[0])

    def from_row(ref, value):
        ref[...] = value.reshape(ref.shape)

    put(5, small_ref[pl.ds(lax.axis_index("heads"), 1)], False, as_row, from_row)
    put(6, small_ref[group : group + 5], False)
    for store in stores:
        store.wait()


def update_layer(kept, shares, dhead, small_sum, norm_tile, weights):
    inside = pl.BlockSpec(memory_space=pltpu.VMEM)
    outside = pl.BlockSpec(memory_space=pl.ANY)
    up_share, down_share, out_share, proj_share = shares
    out_shape = [jax.ShapeDtypeStruct(a.shape, a.dtype) for a in kept]
    for index in range(7):
        out_shape += [jax.ShapeDtypeStruct(weights[3 * index].shape, jnp.float32)] * 4
    out_shape.append(jax.ShapeDtypeStruct((1, 1), jnp.float32))
    results = pl.pallas_call(
        functools.partial(update_kernel, lax.axis_size("heads")),
        in_specs=[outside] * 4 + [inside] * 28,
        out_specs=[outside] * 4 + [inside] * 29,
        out_shape=out_shape,
        scratch_shapes=[pltpu.VMEM(a.shape, a.dtype) for a in kept] + [pltpu.SemaphoreType.DMA((8,))],
        compiler_params=pltpu.CompilerParams(vmem_limit_bytes=VMEM_LIMIT),
    )(*kept, up_share, down_share, out_share, proj_share, dhead, small_sum, norm_tile, *weights)
    return results[:4], results[4:32], results[32]


def local(
    content_in,
    query_in,
    content_grad,
    query_grad,
    segment_ids,
    doc_lengths,
    factor_order,
    attn_proj,
    attn_proj_first,
    attn_proj_second,
    out_proj,
    out_proj_first,
    out_proj_second,
    up_proj,
    up_proj_first,
    up_proj_second,
    down_proj,
    down_proj_first,
    down_proj_second,
    head_bias,
    head_bias_first,
    head_bias_second,
    up_bias,
    up_bias_first,
    up_bias_second,
    norm_param,
    norm_param_first,
    norm_param_second,
):
    width = content_in.shape[1]
    length = segment_ids.shape[1]
    table = position_table(length, width)
    tables = (jnp.asarray(table), jnp.asarray(table[::-1].copy()))
    kept, bias_all, mixed_pieces, (up_full, down_full, out_full) = attention_forward(
        content_in, query_in, attn_proj, up_proj, down_proj, out_proj, up_bias, doc_lengths, factor_order,
        segment_ids, tables[0], head_bias,
    )
    content_out, query_out, dresid, dmixed_pieces, (dup, ddown, dout, dsmall) = feed_layer(
        mixed_pieces, bias_all, content_in, query_in, content_grad, query_grad, norm_param,
        up_full, down_full, out_full,
    )
    backward = attention_backward(
        kept, tables[1], head_bias, dmixed_pieces, dresid, (dup, ddown, dout), dsmall
    )
    input_grad = backward[:2]
    if by_pieces(attn_proj.shape[1]):
        dhead = backward[2]
        up_share, down_share, out_share, proj_share, small_sum, norm_tile = backward[3:]
    else:
        dp_count, heads_count = lax.axis_size("dp"), lax.axis_size("heads")
        dhead = total_over(backward[2], "dp")
        proj_share = reduce_projection(backward[3])
        up_share, down_share, out_share = scatter_all(dup), scatter_all(ddown), scatter_all(dout)
        small_sum = total_over(total_over(dsmall, "heads"), "dp")
        squares = sum(jnp.sum(share * share) for share in (up_share, down_share, out_share, proj_share))
        squares = squares + jnp.sum(dhead * dhead) / dp_count
        squares = squares + jnp.sum(small_sum * small_sum) / (dp_count * heads_count)
        norm = jnp.sqrt(total_over(total_over(squares.reshape(1, 1), "heads"), "dp"))
        norm_tile = jnp.broadcast_to(norm, (8, 128))
    moments = (
        (attn_proj, attn_proj_first, attn_proj_second),
        (out_proj, out_proj_first, out_proj_second),
        (up_proj, up_proj_first, up_proj_second),
        (down_proj.T, down_proj_first.T, down_proj_second.T),
        (head_bias, head_bias_first, head_bias_second),
        (up_bias, up_bias_first, up_bias_second),
        (norm_param, norm_param_first, norm_param_second),
    )
    placed, updated, grad_norm = update_layer(
        (content_out, query_out) + tuple(input_grad),
        (up_share, down_share, out_share, proj_share),
        dhead, small_sum, norm_tile, [array for group in moments for array in group],
    )
    updated = list(updated)
    for index in range(12, 16):
        updated[index] = updated[index].T
    return (*placed, grad_norm[0, 0], *updated)


def solution(mesh):
    return jax.shard_map(
        local,
        mesh=mesh,
        in_specs=(
            P(("dp", "heads"), None),
            P(("dp", "heads"), None),
            P(("dp", "heads"), None),
            P(("dp", "heads"), None),
            P("dp", None),
            P("dp", None),
            P("dp", None),
            P(None, "dp", "heads"),
            P(None, "dp", "heads"),
            P(None, "dp", "heads"),
            P("heads", "dp"),
            P("heads", "dp"),
            P("heads", "dp"),
            P("dp", "heads"),
            P("dp", "heads"),
            P("dp", "heads"),
            P("heads", "dp"),
            P("heads", "dp"),
            P("heads", "dp"),
            P(None, "heads", None),
            P(None, "heads", None),
            P(None, "heads", None),
            P("heads"),
            P("heads"),
            P("heads"),
            P(),
            P(),
            P(),
        ),
        out_specs=(
            P(("dp", "heads"), None),
            P(("dp", "heads"), None),
            P(("dp", "heads"), None),
            P(("dp", "heads"), None),
            P(),
            P(None, "dp", "heads"),
            P(None, "dp", "heads"),
            P(None, "dp", "heads"),
            P(None, "dp", "heads"),
            P("heads", "dp"),
            P("heads", "dp"),
            P("heads", "dp"),
            P("heads", "dp"),
            P("dp", "heads"),
            P("dp", "heads"),
            P("dp", "heads"),
            P("dp", "heads"),
            P("heads", "dp"),
            P("heads", "dp"),
            P("heads", "dp"),
            P("heads", "dp"),
            P(None, "heads", None),
            P(None, "heads", None),
            P(None, "heads", None),
            P(None, "heads", None),
            P("heads"),
            P("heads"),
            P("heads"),
            P("heads"),
            P(),
            P(),
            P(),
            P(),
        ),
        check_vma=False,
    )
```

```python
import functools

import jax
import jax.numpy as jnp
import ml_dtypes
import numpy as np
from jax import lax
from jax.experimental import pallas as pl
from jax.experimental.pallas import tpu as pltpu
from jax.sharding import PartitionSpec as P

STEP = 10


NORM_EPSILON = 1e-05
CLIP_NORM = 1.0
MATRIX_RATE = 0.08
VECTOR_RATE = 0.5
BETA_ONE = 0.9
BETA_TWO = 0.999
ADAM_EPSILON = 1e-08
WEIGHT_DECAY = 0.01
MASKED_SCORE = -1e30
GELU_FACTOR = 0.7978845608028654
GELU_CUBIC = 0.044715
LOG2E = 1.4426950408889634
VMEM_LIMIT = 56 << 20


def position_table(length, width):
    distance = length // 2 - np.arange(length)
    frequency = 10000.0 ** (-np.arange(0, width, 2) / width)
    angles = distance[:, None] * frequency[None, :]
    return np.concatenate([np.sin(angles), np.cos(angles)], -1).astype(np.float32).astype(ml_dtypes.bfloat16)


def dot(left, right):
    return lax.dot_general(left, right, (((1,), (0,)), ((), ())), preferred_element_type=jnp.float32)


def dot_nt(left, right):
    return lax.dot_general(left, right, (((1,), (1,)), ((), ())), preferred_element_type=jnp.float32)


def split_pair(values):
    high = values.astype(jnp.bfloat16)
    low = (values - high.astype(jnp.float32)).astype(jnp.bfloat16)
    return jnp.concatenate([high, low], -1)


def roll_matrix(token_col, length):
    lanes = lax.broadcasted_iota(jnp.int32, (length, length), 1).astype(jnp.float32)
    return jnp.where(token_col == lanes, 1.0, 0.0).astype(jnp.bfloat16)


def unroll_matrix(token_row, length):
    places = lax.broadcasted_iota(jnp.int32, (length, length), 0).astype(jnp.float32)
    return jnp.where(token_row == places, 1.0, 0.0).astype(jnp.bfloat16)


def write_masks(mask_ref, facts_row, facts_col, half):
    for block in range(2):
        part = slice(block * half, (block + 1) * half)
        code_i, base_i = facts_col[part, 0:1], facts_col[part, 1:2]
        code_j = facts_row[0:1, part]
        same = code_j >= base_i
        mask_ref[0, block] = jnp.where(same & (code_j <= code_i), 0.0, MASKED_SCORE)
        mask_ref[1, block] = jnp.where(same & (code_j < code_i), 0.0, MASKED_SCORE)


def query_sides(query, bias, segment_col, factor):
    wide = query.astype(jnp.float32)
    with_u = split_pair((wide + bias[0]) * factor)
    with_w = split_pair((wide + bias[1]) * factor)
    with_c = wide + bias[2]
    same = jnp.sum(with_c * bias[3], -1, keepdims=True) * factor
    change = jnp.sum(with_c * (bias[4] - bias[3]), -1, keepdims=True) * factor
    return with_u, with_w, with_c, same + change * segment_col, change * (1.0 - 2.0 * segment_col)


def block_scores(with_u, with_w, keys_twice, relative_twice, half):
    content = dot_nt(with_u, keys_twice)
    position = dot_nt(with_w, relative_twice)
    return content + pltpu.roll(position, half, 1, stride=1, stride_axis=0)[:, :half]


def greet(axis, masks):
    barrier = pltpu.get_barrier_semaphore()
    for mask in masks:
        pl.semaphore_signal(
            barrier, inc=1, device_id={axis: lax.axis_index(axis) ^ mask}, device_id_type=pl.DeviceIdType.MESH
        )
    pl.semaphore_wait(barrier, len(masks))


class Links:
    def __init__(self, send_sems, recv_sems):
        self.send_sems, self.recv_sems, self.used = send_sems, recv_sems, 0

    def push(self, source, place, axis, distance):
        index = self.used
        self.used = index + 1
        return pltpu.make_async_remote_copy(
            source, place, self.send_sems.at[index], self.recv_sems.at[index],
            device_id={axis: lax.axis_index(axis) ^ distance}, device_id_type=pl.DeviceIdType.MESH,
        )


def add_planes(place, first, second):
    def one(z, carry):
        place[z] = (first(z).astype(jnp.float32) + second[z].astype(jnp.float32)).astype(place.dtype)
        return carry

    lax.fori_loop(0, place.shape[0], one, 0)


class Scatter:
    def __init__(self, links, sem, source, rows, order, refs):
        self.kept, self.got, self.got_two, self.got_last = refs
        heads_here, dp_here = lax.axis_index("heads"), lax.axis_index("dp")
        x, y, z = heads_here >> 1, dp_here & 1, dp_here >> 1
        if order == "xy":
            own, other, first, second, self.mine = source.at[:, :, x, rows], source.at[:, :, 1 - x, rows], ("heads", 2), ("dp", 1), y
        else:
            own, other, first, second, self.mine = source.at[:, y, :, rows], source.at[:, 1 - y, :, rows], ("dp", 1), ("heads", 2), x
        self.load = pltpu.make_async_copy(own, self.kept, sem)
        self.copy = links.push(other, self.got, *first)
        self.copy_two = links.push(self.kept.at[:, 1 - self.mine], self.got_two, *second)
        self.place = z
        self.copies_last = [
            links.push(self.got_two.at[z ^ m], self.got_last.at[m - 1], "dp", 2 * m)
            for m in range(1, source.shape[0])
        ]

    def begin(self):
        self.load.start()
        self.copy.start()

    def second(self):
        self.load.wait()
        self.copy.wait()
        add_planes(self.kept, lambda z: self.kept[z], self.got)
        self.copy_two.start()

    def third(self):
        self.copy_two.wait()
        add_planes(self.got_two, lambda z: self.kept[z, self.mine], self.got_two)
        for copy in self.copies_last:
            copy.start()

    def last(self):
        for copy in self.copies_last:
            copy.wait()
        total = self.got_two[self.place].astype(jnp.float32)
        for index in range(self.got_last.shape[0]):
            total = total + self.got_last[index].astype(jnp.float32)
        return total


def square_sum(values):
    return jnp.sum(jnp.sum(values * values, -1, keepdims=True), 0, keepdims=True)


def unit_copies(links, source, places, starts, size, base):
    heads_here = lax.axis_index("heads")
    own = places.shape[1]
    copies = []
    for start in starts:
        owner = start // own
        distance = owner ^ heads_here
        index = links.used
        links.used = index + 1
        copies.append(
            pltpu.make_async_remote_copy(
                source.at[pl.ds(pl.multiple_of(start, size), size)],
                places.at[distance, pl.ds(pl.multiple_of(start - owner * own, size), size)],
                links.send_sems.at[index], links.recv_sems.at[base + distance],
                device_id={"heads": owner}, device_id_type=pl.DeviceIdType.MESH,
            )
        )
    return copies


class Gather:
    def __init__(self, links, sem, full, own, rows, order):
        heads_here, dp_here = lax.axis_index("heads"), lax.axis_index("dp")
        x, core, y, z = heads_here >> 1, heads_here & 1, dp_here & 1, dp_here >> 1

        def same(*place):
            part = full.at[place + (rows,)]
            return part, part

        everything = slice(None)
        planes = full.shape[0]
        mine = full.at[z, y, x, core, rows]
        self.keep = pltpu.make_async_copy(own.at[rows], mine, sem)
        self.along_z = [links.push(own.at[rows], mine, "dp", 2 * m) for m in range(1, planes)]
        column = same(everything, y, x, core)
        across = ("heads", 2), ("dp", 1)
        if order == "xy":
            near, wide = same(everything, y, 1 - x, core), same(everything, y, everything, core)
            last = same(everything, 1 - y, everything, core)
        else:
            near, wide = same(everything, 1 - y, x, core), same(everything, everything, x, core)
            last = same(everything, everything, 1 - x, core)
            across = across[1], across[0]
        self.first = links.push(*column, *across[0])
        self.second = links.push(*wide, *across[1])
        self.to_sibling = [links.push(*part, "heads", 1) for part in (column, near, last)]

    def begin(self):
        self.keep.start()
        for copy in self.along_z:
            copy.start()

    def step_one(self):
        self.keep.wait()
        for copy in self.along_z:
            copy.wait()
        self.first.start()
        self.to_sibling[0].start()

    def step_two(self):
        self.first.wait()
        self.second.start()
        self.to_sibling[1].start()

    def step_three(self):
        self.second.wait()
        self.to_sibling[2].start()

    def finish(self):
        for copy in self.to_sibling:
            copy.wait()


def write_facts(lengths_ref, order_ref, segment_ref, row_ref, col_ref):
    rows, length = order_ref.shape
    down = lax.broadcasted_iota(jnp.int32, (length, length), 0).astype(jnp.float32)
    along = lax.broadcasted_iota(jnp.int32, (length, length), 1).astype(jnp.float32)
    places_col, places_row = down[:, 0:1], along[0:1, :]
    row_ref[...] = jnp.zeros_like(row_ref)
    col_ref[...] = jnp.zeros_like(col_ref)

    def as_column(values):
        return jnp.sum(jnp.where(down == along, values, 0.0), 1, keepdims=True)

    for row in range(rows):
        ends, start, end = [], 0, 0
        for document in range(lengths_ref.shape[1]):
            count = lengths_ref[row, document]
            start = start + (count == length // 2).astype(jnp.int32) * end
            end = end + count
            ends.append(end.astype(jnp.float32))
        start = start.astype(jnp.float32)
        order = order_ref[row : row + 1].astype(jnp.float32)
        segment = segment_ref[row : row + 1].astype(jnp.float32)
        order_col, segment_col = as_column(order), as_column(segment)
        for place, turned in ((places_row, False), (places_col, True)):
            token = place + start
            token = jnp.where(token >= length, token - length, token)
            base = jnp.zeros_like(token)
            for end in ends:
                base = base + jnp.where(token >= end, float(length), 0.0)
            if turned:
                rank = jnp.sum(jnp.where(order == token, along, 0.0), 1, keepdims=True)
                kind = jnp.sum(jnp.where(along == token, segment, 0.0), 1, keepdims=True)
                for index, values in enumerate((base + rank, base, kind, token)):
                    col_ref[row, :, index : index + 1] = values
            else:
                rank = jnp.sum(jnp.where(order_col == token, down, 0.0), 0, keepdims=True)
                kind = jnp.sum(jnp.where(down == token, segment_col, 0.0), 0, keepdims=True)
                for index, values in enumerate((base + rank, base, kind, token)):
                    row_ref[row, index : index + 1] = values


def turn(values):
    size = values.shape[1]
    same = lax.broadcasted_iota(jnp.int32, (size, size), 0) == lax.broadcasted_iota(jnp.int32, (size, size), 1)
    identity = jnp.where(same, 1.0, 0.0).astype(jnp.bfloat16)
    return dot_nt(identity, values.astype(jnp.bfloat16)).astype(jnp.bfloat16)


def attention_forward_kernel(head_size, group, parts, fast, *refs):
    content_hbm, query_hbm, weight_in, up_in, down_in, out_in, bias_in, refs = *refs[:7], refs[7:]
    lengths_ref, order_ref, segment_ref, table_ref, head_ref, refs = *refs[:5], refs[5:]
    proj_ref, row_ref, col_ref, bias_all, refs = *refs[:4], refs[4:]
    mixed_pieces, refs = refs[0], refs[1:]
    content_out, query_out, weight_out, chance_out, refs = *refs[:4], refs[4:]
    if fast:
        up_all, down_all, out_all, refs = *refs[:3], refs[3:]
    content_all, query_all, weight_ref, mixed_ref, relative_ref, mask_ref, chance_ref, refs = *refs[:7], refs[7:]
    sems, send_sems, recv_sems, refs = *refs[:3], refs[3:]
    rows, length = row_ref.shape[0], row_ref.shape[2]
    half = length // 2
    tokens, depth = content_hbm.shape
    width = weight_ref.shape[-1] // 4
    heads = width // head_size
    factor = head_size ** (-0.5) * LOG2E
    heads_here, dp_here = lax.axis_index("heads"), lax.axis_index("dp")
    chip = heads_here >> 1
    links = Links(send_sems, recv_sems)

    def token_part(k):
        return pl.ds(pl.multiple_of((heads_here ^ k) * tokens, tokens), tokens)

    streams = ((content_hbm, content_all), (query_hbm, query_all))
    local = [pltpu.make_async_copy(own, full.at[token_part(0)], sems.at[n]) for n, (own, full) in enumerate(streams)]
    if not fast:
        local.append(pltpu.make_async_copy(weight_in, weight_ref, sems.at[2]))
    for copy in local:
        copy.start()
    barrier = pltpu.get_barrier_semaphore()
    peers = [("heads", k) for k in range(1, group)] + [("dp", k) for k in range(1, parts)]
    for axis, k in peers:
        pl.semaphore_signal(
            barrier, inc=1, device_id={axis: lax.axis_index(axis) ^ k}, device_id_type=pl.DeviceIdType.MESH
        )
    if fast:
        weight_send, up_send, down_send, out_send = refs
        weight_send[...] = jnp.concatenate([weight_in[kind] for kind in range(4)], -1).astype(jnp.bfloat16)
    pl.semaphore_wait(barrier, len(peers))
    far = [links.push(own, full.at[token_part(0)], "heads", 2) for own, full in streams]
    near = [links.push(own, full.at[token_part(0)], "heads", 1) for own, full in streams]
    passed = [links.push(full.at[token_part(2)], full.at[token_part(2)], "heads", 1) for _, full in streams]
    bias_copies = [links.push(bias_in, bias_all.at[heads_here], "heads", k) for k in range(1, group)]
    for copy in far + near + bias_copies:
        copy.start()
    if fast:
        y, z = dp_here & 1, dp_here >> 1
        weight_z, weight_y = [], []
        for pair in (pl.ds(0, 2 * width), pl.ds(2 * width, 2 * width)):
            mine = weight_ref.at[z, y, :, pair]
            weight_z.append([links.push(weight_send.at[:, pair], mine, "dp", 2 * m) for m in range(1, parts // 2)])
            column = weight_ref.at[:, y, :, pair]
            weight_y.append(links.push(column, column, "dp", 1))
            for copy in weight_z[-1]:
                copy.start()
        weight_ref[z, y] = weight_send[...]
        up_send[...] = up_in[...].astype(jnp.bfloat16)
        down_send[...] = down_in[...].astype(jnp.bfloat16)
        out_send[...] = turn(out_in[...])
        pick = up_send.shape[0]
        early, late = pl.ds(0, pick // 2), pl.ds(pick // 2, pick // 2)
        up_one = Gather(links, sems.at[3], up_all, up_send, early, "xy")
        up_two = Gather(links, sems.at[4], up_all, up_send, late, "xy")
        down_one = Gather(links, sems.at[5], down_all, down_send, early, "yx")
        down_two = Gather(links, sems.at[6], down_all, down_send, late, "xy")
        out_one = Gather(links, sems.at[7], out_all, out_send, pl.ds(0, pick), "yx")
        gathers = (up_one, up_two, down_one, down_two, out_one)
    bias_all[heads_here] = bias_in[...]
    write_facts(lengths_ref, order_ref, segment_ref, row_ref, col_ref)
    if fast:
        for first, second in zip(weight_z, weight_y):
            for copy in first:
                copy.wait()
            second.start()
        down_one.begin()
        out_one.begin()
        for copy in weight_y[:1]:
            copy.wait()
        up_one.begin()
        weight_y[1].wait()
    for copy in local + near:
        copy.wait()

    def weight(first, last):
        return weight_ref[..., first * width : last * width].reshape(depth, (last - first) * width)

    saves = [
        pltpu.make_async_copy(content_all, content_out, sems.at[0]),
        pltpu.make_async_copy(query_all, query_out, sems.at[1]),
        pltpu.make_async_copy(weight_ref, weight_out, sems.at[2]),
    ]
    saves[2].start()
    relative_ref[...] = dot(table_ref[...], weight(3, 4)).astype(jnp.bfloat16)

    def pass_on():
        for arrived, onward in zip(far, passed):
            arrived.wait()
            onward.start()

    def nothing():
        pass

    events = {(0, 0): [pass_on]}
    if fast:
        events = {
            (0, 0): [pass_on, down_one.step_one, up_two.begin],
            (0, 1): [up_one.step_one, down_two.begin],
            (0, 2): [out_one.step_one, down_one.step_two],
            (1, 0): [up_one.step_two, up_two.step_one],
            (1, 1): [down_two.step_one, out_one.step_two],
            (1, 2): [up_two.step_two, down_one.step_three],
            (2, 0): [down_two.step_two, up_one.step_three],
            (2, 1): [out_one.step_three],
        }

    def one_row(step, carry):
        row = jnp.where(step == 0, 0, rows - step)
        row = jnp.where(chip == 0, row, rows - 1 - row)

        @pl.when(step == 1)
        def _():
            for copy in passed:
                copy.wait()
            for save in saves[:2]:
                save.start()

        here = pl.ds(pl.multiple_of(row * length, length), length)
        facts_row, facts_col = row_ref[row], col_ref[row]
        write_masks(mask_ref, facts_row, facts_col, half)
        roll = roll_matrix(facts_col[:, 3:4], length)
        unroll = unroll_matrix(facts_row[3:4, :], length)
        content, query = content_all[here], query_all[here]
        joined = jnp.concatenate(
            [
                dot(content, weight(0, 3)).astype(jnp.bfloat16),
                dot(query, weight(0, 1)).astype(jnp.bfloat16),
            ],
            -1,
        )
        proj_ref[row] = dot(roll, joined).astype(jnp.bfloat16)
        segment_col, segment_row = facts_col[:, 2:3], facts_row[2:3, :]
        mixed = [[None] * heads, [None] * heads]
        for head in range(heads):
            cols = lambda kind: slice(kind * width + head * head_size, kind * width + (head + 1) * head_size)
            own_cols = slice(head * head_size, (head + 1) * head_size)
            bias = [head_ref[kind, head : head + 1] for kind in range(5)]
            keys, values = proj_ref[row, :, cols(1)], proj_ref[row, :, cols(2)]
            keys_twice = jnp.concatenate([keys, keys], -1)
            relative = relative_ref[:, own_cols]
            relative_twice = jnp.concatenate([relative, relative], -1)
            for stream in range(2):
                with_u, with_w, _, own, slope = query_sides(
                    proj_ref[row, :, cols(3 * stream)], bias, segment_col, factor
                )
                pieces = []
                for block in range(2):
                    part = slice(block * half, (block + 1) * half)
                    scores = block_scores(
                        with_u[part], with_w[part], keys_twice[part], relative_twice, half
                    )
                    scores = scores + own[part] + slope[part] * segment_row[:, part] + mask_ref[stream, block]
                    highest = jnp.maximum(jnp.max(scores, -1, keepdims=True), 0.0)
                    weights = jnp.exp2(scores - highest)
                    totals = jnp.exp2(-highest) + jnp.sum(weights, -1, keepdims=True)
                    chances = (weights * (1.0 / totals)).astype(jnp.bfloat16)
                    chance_ref[row, stream * heads + head, block] = chances
                    pieces.append(dot(chances, values[part]))
                mixed[stream][head] = jnp.concatenate(pieces, 0).astype(jnp.bfloat16)
            for when, actions in events.items():
                if when[1] == head:
                    @pl.when(step == when[0])
                    def _():
                        for action in actions:
                            action()
        both = jnp.concatenate(mixed[0] + mixed[1], -1)
        mixed_ref[here] = dot(unroll, both).astype(jnp.bfloat16)
        chance_copy(row).start()

        @pl.when(step == 1)
        def _():
            for copy in far_units:
                copy.start()

        return carry

    def chance_copy(row):
        return pltpu.make_async_copy(chance_ref.at[row], chance_out.at[row], sems.at[9 + row])

    unit = half // 2
    far_row = jnp.where(chip == 0, (rows - 1) * length, 0)
    far_middle = jnp.where(chip == 0, length + half, length)
    base = links.used
    links.used = base + group
    far_units = unit_copies(links, mixed_ref, mixed_pieces, [far_row + n * unit for n in range(4)], unit, base)
    middle_units = unit_copies(links, mixed_ref, mixed_pieces, [far_middle + n * unit for n in range(2)], unit, base)
    far_pieces = [
        pltpu.make_async_remote_copy(
            mixed_pieces.at[k], mixed_pieces.at[k], send_sems.at[base + k], recv_sems.at[base + k],
            device_id={"heads": heads_here ^ k}, device_id_type=pl.DeviceIdType.MESH,
        )
        for k in (2, 3)
    ]
    lax.fori_loop(0, rows, one_row, 0)
    for copy in middle_units:
        copy.start()
    keep = pltpu.make_async_copy(mixed_ref.at[token_part(0)], mixed_pieces.at[0], sems.at[8])
    keep.start()
    sends = [links.push(mixed_ref.at[token_part(1)], mixed_pieces.at[1], "heads", 1)]
    for copy in sends:
        copy.start()
    if fast:
        up_two.step_three()
        down_two.step_three()
    for copy in [keep] + saves + sends + bias_copies:
        copy.wait()
    for copy in far_units + middle_units:
        copy.wait_send()
    for row in range(rows):
        chance_copy(row).wait()
    for piece in far_pieces:
        piece.wait_recv()
    if fast:
        for gather in gathers:
            gather.finish()


def attention_forward(
    content, query, attn_proj, up_proj, down_proj, out_proj, up_bias, doc_lengths, factor_order, segment_ids,
    table, head_bias,
):
    rows, length = segment_ids.shape
    group, parts = lax.axis_size("heads"), lax.axis_size("dp")
    fast = by_pieces(attn_proj.shape[1])
    own, depth = content.shape
    tokens = own * group
    pick, width = attn_proj.shape[1:]
    hidden = up_proj.shape[1]
    head_size = head_bias.shape[-1]
    half = length // 2
    inside = pl.BlockSpec(memory_space=pltpu.VMEM)
    outside = pl.BlockSpec(memory_space=pl.ANY)
    scalars = pl.BlockSpec(memory_space=pltpu.SMEM)
    bfloat, float32 = jnp.bfloat16, jnp.float32
    weight_shape = (parts // 2, 2, pick, 4 * width) if fast else (depth, 4 * width)
    out_shape = [
        jax.ShapeDtypeStruct((rows, length, 4 * width), bfloat),
        jax.ShapeDtypeStruct((rows, 8, length), float32),
        jax.ShapeDtypeStruct((rows, length, 8), float32),
        jax.ShapeDtypeStruct((group, 1, hidden), float32),
    ]
    out_specs = [inside] * 4 + [outside] * 5
    out_shape += [jax.ShapeDtypeStruct((group, own, 2 * width), bfloat)]
    out_shape += [jax.ShapeDtypeStruct((tokens, depth), bfloat)] * 2
    out_shape += [jax.ShapeDtypeStruct(weight_shape, bfloat)]
    chance_shape = (rows, 2 * width // head_size, 2, half, half)
    out_shape += [jax.ShapeDtypeStruct(chance_shape, bfloat)]
    scratch = [
        pltpu.VMEM((tokens, depth), bfloat),
        pltpu.VMEM((tokens, depth), bfloat),
        pltpu.VMEM(weight_shape, bfloat),
        pltpu.VMEM((tokens, 2 * width), bfloat),
        pltpu.VMEM((length, width), bfloat),
        pltpu.VMEM((2, 2, half, half), float32),
        pltpu.VMEM(chance_shape, bfloat),
        pltpu.SemaphoreType.DMA((9 + rows,)),
        pltpu.SemaphoreType.DMA((72,)),
        pltpu.SemaphoreType.DMA((72,)),
    ]
    if fast:
        weight_spec = inside
        out_specs += [outside] * 3
        out_shape += [
            jax.ShapeDtypeStruct((parts // 2, 2, group // 2, 2, pick, c), bfloat) for c in (hidden, hidden, width)
        ]
        scratch += [
            pltpu.VMEM((pick, 4 * width), bfloat),
            pltpu.VMEM((pick, hidden), bfloat),
            pltpu.VMEM((pick, hidden), bfloat),
            pltpu.VMEM((pick, width), bfloat),
        ]
    else:
        weight_spec = outside
        attn_proj = lax.all_gather(attn_proj.astype(bfloat), "dp", axis=1, tiled=True)
        attn_proj = jnp.swapaxes(attn_proj, 0, 1).reshape(weight_shape)
    results = pl.pallas_call(
        functools.partial(attention_forward_kernel, head_size, group, parts if fast else 1, fast),
        in_specs=[outside, outside, weight_spec] + [inside] * 4 + [scalars] + [inside] * 4,
        out_specs=out_specs,
        out_shape=out_shape,
        scratch_shapes=scratch,
        compiler_params=pltpu.CompilerParams(
            vmem_limit_bytes=VMEM_LIMIT, collective_id=0, has_side_effects=True
        ),
    )(
        content, query, attn_proj, up_proj, down_proj.T, out_proj, up_bias[None], doc_lengths, factor_order,
        segment_ids, table, head_bias,
    )
    proj, facts_row, facts_col, bias_all, mixed_pieces = results[:5]
    content_all, query_all, weight_all, chance_all = results[5:9]
    if fast:
        wide = [full.reshape(parts, group, pick, full.shape[-1]) for full in results[9:]]
    else:
        wide = [gather_all(m) for m in (up_proj.astype(bfloat), down_proj.T.astype(bfloat), out_proj.T.astype(bfloat))]
    kept = (content_all, query_all, weight_all, chance_all, (facts_row, facts_col), proj)
    return kept, bias_all, mixed_pieces, wide


def attention_backward_kernel(head_size, group, parts, fast, *refs):
    content_hbm, query_hbm, weight_hbm, chance_hbm, refs = *refs[:4], refs[4:]
    upper_pieces, dresid_hbm, refs = refs[0], refs[1], refs[2:]
    turned_ref, bias_ref, row_ref, col_ref, proj_ref = refs[:5]
    sources, small_ref, refs = refs[5:8], refs[8], refs[9:]
    outputs, refs = refs[:9] if fast else refs[:4], refs[9:] if fast else refs[4:]
    content_grad_ref, query_grad_ref, dhead_ref = outputs[:3]
    content_all, query_all, weight_ref, upper_all, dinput_ref, dweight_ref = refs[:6]
    chance_ref, backward_ref, drel_ref, dcols_ref, dkeys_ref, dvalues_ref = refs[6:12]
    dwide_ref, side_ref, cross_ref, swap_ref, dresid_ref, dhead_own, refs = *refs[12:18], refs[18:]
    sems, send_sems, recv_sems, refs = *refs[:3], refs[3:]
    rows, length = row_ref.shape[0], row_ref.shape[2]
    half = length // 2
    depth, width = content_all.shape[1], weight_ref.shape[-1] // 4
    heads = width // head_size
    scale = head_size ** (-0.5)
    heads_here, dp_here = lax.axis_index("heads"), lax.axis_index("dp")
    chip = heads_here >> 1
    tokens = upper_pieces.shape[1]
    links = Links(send_sems, recv_sems)

    def token_part(k):
        return pl.ds(pl.multiple_of((heads_here ^ k) * tokens, tokens), tokens)

    copies = [
        pltpu.make_async_copy(content_hbm, content_all, sems.at[0]),
        pltpu.make_async_copy(query_hbm, query_all, sems.at[1]),
        pltpu.make_async_copy(weight_hbm, weight_ref, sems.at[2]),
        pltpu.make_async_copy(upper_pieces.at[0], upper_all.at[token_part(0)], sems.at[3]),
    ]
    for copy in copies:
        copy.start()
    def row_at(step):
        row = jnp.where(step == 0, 0, rows - step)
        return jnp.where(chip == 0, row, rows - 1 - row)

    def chance_copy(row):
        return pltpu.make_async_copy(chance_hbm.at[row], chance_ref.at[row], sems.at[10 + row])

    for step in range(rows):
        chance_copy(row_at(step)).start()
    dresid_copy = pltpu.make_async_copy(dresid_hbm, dresid_ref, sems.at[4])

    def weight(first, last):
        return weight_ref[..., first * width : last * width].reshape(depth, (last - first) * width)

    barrier = pltpu.get_barrier_semaphore()
    peers = [("heads", k) for k in range(1, group)] + [("dp", k) for k in range(1, parts)]
    for axis, k in peers:
        pl.semaphore_signal(
            barrier, inc=1, device_id={axis: lax.axis_index(axis) ^ k}, device_id_type=pl.DeviceIdType.MESH
        )
    pl.semaphore_wait(barrier, len(peers))
    upper_copies = [
        links.push(upper_pieces.at[k], upper_all.at[token_part(0)], "heads", k) for k in range(1, group)
    ]
    for copy in upper_copies:
        copy.start()
    if fast:
        pick = sources[0].shape[3]
        early, late, full = pl.ds(0, pick // 2), pl.ds(pick // 2, pick // 2), pl.ds(0, pick)
        plan = ((0, early, "yx"), (0, late, "yx"), (1, early, "yx"), (1, late, "xy"), (2, full, "yx"))
        scatters = [
            Scatter(links, sems.at[5 + n], sources[which], part, order, refs[4 * n : 4 * n + 4])
            for n, (which, part, order) in enumerate(plan)
        ]
        up_one, up_two, down_one, down_two, out_one = scatters
        small_got, small_more, small_mid, dweight_got, dweight_more, head_got, tile_ref, tile_got, tile_more = refs[20:]
        up_one.begin()
        out_one.begin()
        small_first = [links.push(small_ref, small_got.at[heads_here], "heads", k) for k in range(1, group)]
        for copy in small_first:
            copy.start()
        small_got[heads_here] = small_ref[...]
        small_second = [links.push(small_mid, small_more.at[dp_here], "dp", k) for k in range(1, parts)]
    for copy in copies:
        copy.wait()
    upper_copies[0].wait()
    backward_ref[...] = dot(turned_ref[...], weight(3, 4)).astype(jnp.bfloat16)
    drel_ref[...] = jnp.zeros_like(drel_ref)
    dweight_ref[...] = jnp.zeros_like(dweight_ref)
    dhead_own[...] = jnp.zeros_like(dhead_own)
    bias_cols = [bias_ref[kind].T for kind in range(2)]
    ones = jnp.ones((16, length), jnp.bfloat16)

    def act(condition, actions):
        @pl.when(condition)
        def _():
            for action in actions:
                action()

    def span(start, size):
        return pl.ds(pl.multiple_of(start, size), size)

    def sides(first, size, slot):
        mine, other = span(first + core * size, size), span(first + (1 - core) * size, size)
        landed = side_ref.at[:, pl.ds(slot, size)]
        return links.push(dinput_ref.at[:, other], landed, "heads", 1), mine, landed

    def add_side(side, landed=None):
        copy, mine, place = side
        copy.wait()
        for n in range(2):
            dinput_ref[n, mine] = (
                dinput_ref[n, mine].astype(jnp.float32) + place[n].astype(jnp.float32)
            ).astype(jnp.bfloat16)

    core, unit = heads_here & 1, half // 2
    own_first = jnp.where(chip == 0, 0, (rows - 1) * length)
    far_first = jnp.where(chip == 0, (rows - 1) * length, 0)
    own_middle = jnp.where(chip == 0, length, length + half)
    far_middle = jnp.where(chip == 0, length + half, length)
    own_side, far_side = sides(own_first, half, 0), sides(far_first, half, half)
    own_side_two, far_side_two = sides(own_middle, unit, 2 * half), sides(far_middle, unit, 2 * half + unit)
    across = [
        (links.push(dinput_ref.at[:, side[1]], cross_ref.at[:, place], "heads", 2), mine[1], cross_ref.at[:, place])
        for side, mine, place in (
            (far_side, own_side, pl.ds(0, half)), (far_side_two, own_side_two, pl.ds(half, unit))
        )
    ]
    swap_part = span(2 * half + 5 * unit * chip - half * core, unit)
    swap_got = span(2 * half + 5 * unit * chip - half * (1 - core), unit)
    swap = links.push(dinput_ref.at[:, swap_part], swap_ref, "heads", 1)

    def far_over():
        add_side(far_side)
        across[0][0].start()

    def small_middle():
        for copy in small_first:
            copy.wait()
        total = small_got[0]
        for k in range(1, group):
            total = total + small_got[k]
        small_mid[...] = total
        small_more[dp_here] = total
        for copy in small_second:
            copy.start()

    events = {
        (0, heads): [own_side[0].start],
        (1, heads): [far_side[0].start],
        (2, 0): [far_over, lambda: add_side(own_side)],
    }
    if fast:
        for place, actions in {
            (0, 1): [down_two.begin],
            (0, 2): [up_two.begin],
            (0, heads): [up_one.second, out_one.second],
            (1, 0): [small_middle],
            (1, 1): [down_two.second, up_one.third],
            (1, 2): [up_two.second, down_one.begin, out_one.third],
            (2, 0): [down_two.third],
            (2, 1): [up_two.third],
            (2, 2): [down_one.second],
        }.items():
            events[place] = events.get(place, []) + actions

    def one_row(step, carry):
        row = row_at(step)
        chance_copy(row).wait()

        @pl.when(step == 1)
        def _():
            dresid_copy.start()
            for copy in upper_copies[1:]:
                copy.wait()

        row_part(step, row)
        return carry

    def row_part(step, row):
        here = pl.ds(pl.multiple_of(row * length, length), length)
        content_ref, query_ref = content_all.at[here], query_all.at[here]
        facts_row, facts_col = row_ref[row], col_ref[row]
        roll = roll_matrix(facts_col[:, 3:4], length)
        upper = dot(roll, upper_all[here]).astype(jnp.bfloat16)
        segment_col = facts_col[:, 2:3]
        down = lax.broadcasted_iota(jnp.int32, (half, half), 0)
        along = lax.broadcasted_iota(jnp.int32, (half, half), 1)
        mirror = jnp.where(down + along == half - 1, 1.0, 0.0).astype(jnp.bfloat16)
        lane = lax.broadcasted_iota(jnp.int32, (length, head_size), 1)
        extra = jnp.where(lane == 0, segment_col, jnp.where(lane == 1, 1.0, 0.0)).astype(jnp.bfloat16)
        for head in range(heads):
            own_cols = slice(head * head_size, (head + 1) * head_size)
            cols = lambda kind: slice(kind * width + head * head_size, kind * width + (head + 1) * head_size)
            bias = [bias_ref[kind, head : head + 1] for kind in range(5)]
            keys, values = proj_ref[row, :, cols(1)], proj_ref[row, :, cols(2)]
            keys_extra = jnp.concatenate([keys, extra], -1)
            backward = backward_ref[:, own_cols]
            u_col, w_col = (turned_bias[:, head : head + 1] for turned_bias in bias_cols)
            heads_sums = [jnp.zeros((1, head_size), jnp.float32) for _ in range(5)]
            for stream in range(2):
                query_now = proj_ref[row, :, cols(3 * stream)]
                with_c = query_now.astype(jnp.float32) + bias[2]
                index = stream * heads + head
                upper_now = upper[:, index * head_size : (index + 1) * head_size]
                query_t, upper_t = jnp.concatenate([query_now.T, ones], 0), upper_now.T
                dquery = []
                for block in range(2):
                    part = slice(block * half, (block + 1) * half)
                    low_chances = chance_ref[row, index, block]
                    chances = low_chances.astype(jnp.float32)
                    weighted = chances * dot_nt(upper_now[part], values[part])
                    centre = jnp.sum(weighted, -1, keepdims=True)
                    dscore = (weighted - chances * centre).astype(jnp.bfloat16)
                    dvalue_part = dot(upper_t[:, part], low_chances)
                    by_key = dot(dscore, keys_extra[part])
                    turned = dot(dscore, mirror)
                    wide = pltpu.roll(
                        jnp.concatenate([turned, jnp.zeros((half, half), jnp.float32)], -1),
                        0, 1, stride=1, stride_axis=0,
                    ).astype(jnp.bfloat16)
                    by_place = dot(wide, backward)
                    dkey_part = dot(query_t[:, part], dscore)
                    dkey_part = dkey_part[:head_size] + u_col * dkey_part[head_size : head_size + 1]
                    drel_part = dot(query_t[:, part], wide)
                    drel_ref[own_cols] += drel_part[:head_size] + w_col * drel_part[head_size : head_size + 1]
                    if stream == 0:
                        dkeys_ref[own_cols, part] = dkey_part
                        dvalues_ref[own_cols, part] = dvalue_part
                    else:
                        dkeys_ref[own_cols, part] += dkey_part
                        dvalues_ref[own_cols, part] += dvalue_part
                    with_seg, total = by_key[:, head_size : head_size + 1], by_key[:, head_size + 1 : head_size + 2]
                    seg_i = segment_col[part]
                    seg_one = with_seg + seg_i * (total - 2.0 * with_seg)
                    seg_zero = total - seg_one
                    by_key = by_key[:, :head_size]
                    by_segment = seg_zero * bias[3] + seg_one * bias[4]
                    dquery.append((by_key + by_place + by_segment) * scale)
                    for kind, term in enumerate(
                        (by_key, by_place, by_segment, seg_zero * with_c[part], seg_one * with_c[part])
                    ):
                        heads_sums[kind] = heads_sums[kind] + jnp.sum(term, 0, keepdims=True)
                dcols_ref[:, cols(3 * stream)] = jnp.concatenate(dquery, 0).astype(jnp.bfloat16)
            for kind in range(5):
                dhead_own[kind : kind + 1, own_cols] += heads_sums[kind] * scale
            for when, actions in events.items():
                if when[1] == head:
                    act(step == when[0], actions)
        dcols_ref[:, width : 2 * width] = (dkeys_ref[...] * scale).astype(jnp.bfloat16).T
        dcols_ref[:, 2 * width : 3 * width] = dvalues_ref[...].astype(jnp.bfloat16).T
        unroll = unroll_matrix(facts_row[3:4, :], length)
        joined = dot(unroll, dcols_ref[...]).astype(jnp.bfloat16)
        joined_t = joined.T
        content, query = content_ref[...], query_ref[...]
        dweight_ref[: 3 * width] += dot(joined_t[: 3 * width], content)
        dweight_ref[:width] += dot(joined_t[3 * width :], query)
        dinput_ref[0, here] = dot_nt(joined[:, : 3 * width], weight(0, 3)).astype(jnp.bfloat16)
        dinput_ref[1, here] = dot_nt(joined[:, 3 * width :], weight(0, 1)).astype(jnp.bfloat16)
        for when, actions in events.items():
            if when[1] == heads:
                act(step == when[0], actions)

    lax.fori_loop(0, rows, one_row, 0)
    for side in (far_side_two, own_side_two):
        side[0].start()
    drel = drel_ref[...] * scale
    high = drel.astype(jnp.bfloat16)
    low = (drel - high.astype(jnp.float32)).astype(jnp.bfloat16)
    dweight_ref[3 * width :] = dot(high, turned_ref[...]) + dot(low, turned_ref[...])
    dwide_ref[...] = dweight_ref[...].astype(jnp.bfloat16).T.reshape(dwide_ref.shape)
    if fast:
        place_y, place_z = dp_here & 1, dp_here >> 1
        dweight_first = links.push(dwide_ref.at[:, 1 - place_y], dweight_got, "dp", 1)
        dweight_first.start()
        head_copies = [links.push(dhead_own, head_got.at[dp_here], "dp", k) for k in range(1, parts)]
        for copy in head_copies:
            copy.start()
        head_got[dp_here] = dhead_own[...]
    add_side(far_side_two)
    across[1][0].start()
    add_side(own_side_two)
    if fast:
        down_one.third()
        dweight_first.wait()
        add_planes(dweight_got, lambda z: dwide_ref[z, place_y], dweight_got)
        dweight_second = [
            links.push(dweight_got.at[place_z ^ m], dweight_more.at[m - 1], "dp", 2 * m) for m in range(1, 4)
        ]
        for copy in dweight_second:
            copy.start()
    for side in across:
        add_side(side)
    swap.start()
    if fast:
        up_share, down_share, out_share, proj_share, small_sum, norm_ref = outputs[3:]
        squares = jnp.zeros((1, 1), jnp.float32)
        for copy in small_second:
            copy.wait()
        total = small_more[0]
        for k in range(1, parts):
            total = total + small_more[k]
        small_sum[...] = total
        squares = squares + square_sum(total) / (group * parts)
        for copy in head_copies:
            copy.wait()
        total = head_got[0]
        for k in range(1, parts):
            total = total + head_got[k]
        dhead_ref[...] = total
        squares = squares + square_sum(total) / parts
        for (which, part, _), scatter in zip(plan, scatters):
            total = scatter.last()
            (up_share, down_share, out_share)[which][part] = total
            squares = squares + square_sum(total)
        for copy in dweight_second:
            copy.wait()
        total = dweight_got[place_z].astype(jnp.float32)
        for m in range(1, 4):
            total = total + dweight_more[m - 1].astype(jnp.float32)
        proj_share[...] = total
        squares = squares + square_sum(total)
        tile_ref[...] = jnp.broadcast_to(squares, tile_ref.shape)
        tile_got[heads_here] = tile_ref[...]
        tile_first = [links.push(tile_ref, tile_got.at[heads_here], "heads", k) for k in range(1, group)]
        for copy in tile_first:
            copy.start()
    else:
        dhead_ref[...] = dhead_own[...]
        outputs[3][...] = dwide_ref[...]
    if fast:
        for copy in tile_first:
            copy.wait()
        total = tile_got[0]
        for k in range(1, group):
            total = total + tile_got[k]
        tile_more[dp_here] = total
        tile_ref[...] = total
        tile_second = [links.push(tile_ref, tile_more.at[dp_here], "dp", k) for k in range(1, parts)]
        for copy in tile_second:
            copy.start()
    dresid_copy.wait()
    swap.wait()
    dinput_ref[:, swap_got] = swap_ref[...]
    for n, place in enumerate((content_grad_ref, query_grad_ref)):
        place[...] = dresid_ref[n] + dinput_ref[n, token_part(0)].astype(jnp.float32)
    if fast:
        for copy in tile_second:
            copy.wait()
        total = tile_more[0]
        for k in range(1, parts):
            total = total + tile_more[k]
        norm_ref[...] = jnp.sqrt(total)


def attention_backward(
    kept, table, head_bias, upper, dresid, gradients, small
):
    content_all, query_all, weight_all, chance_all, facts, proj = kept
    rows, length = facts[0].shape[0], facts[0].shape[2]
    group = upper.shape[0]
    fast = weight_all.ndim == 4
    tokens, depth = content_all.shape
    own = tokens // group
    pick, width = weight_all.shape[-2], weight_all.shape[-1] // 4
    parts = depth // pick
    head_size = head_bias.shape[-1]
    half = length // 2
    inside = pl.BlockSpec(memory_space=pltpu.VMEM)
    outside = pl.BlockSpec(memory_space=pl.ANY)
    bfloat, float32 = jnp.bfloat16, jnp.float32
    out_shape = [
        jax.ShapeDtypeStruct((own, depth), float32),
        jax.ShapeDtypeStruct((own, depth), float32),
        jax.ShapeDtypeStruct((8, width), float32),
    ]
    wide_shape = weight_all.shape
    scratch = [
        pltpu.VMEM((tokens, depth), bfloat),
        pltpu.VMEM((tokens, depth), bfloat),
        pltpu.VMEM(weight_all.shape, bfloat),
        pltpu.VMEM((tokens, 2 * width), bfloat),
        pltpu.VMEM((2, tokens, depth), bfloat),
        pltpu.VMEM((4 * width, depth), float32),
        pltpu.VMEM(chance_all.shape, bfloat),
        pltpu.VMEM((length, width), bfloat),
        pltpu.VMEM((width, length), float32),
        pltpu.VMEM((length, 4 * width), bfloat),
        pltpu.VMEM((width, length), float32),
        pltpu.VMEM((width, length), float32),
        pltpu.VMEM(wide_shape, bfloat),
        pltpu.VMEM((2, 2 * own, depth), bfloat),
        pltpu.VMEM((2, own, depth), bfloat),
        pltpu.VMEM((2, half // 2, depth), bfloat),
        pltpu.VMEM((2, own, depth), float32),
        pltpu.VMEM((8, width), float32),
        pltpu.SemaphoreType.DMA((10 + rows,)),
        pltpu.SemaphoreType.DMA((80,)),
        pltpu.SemaphoreType.DMA((80,)),
    ]
    if fast:
        planes = parts // 2
        columns = [gradient.shape[-1] for gradient in gradients]
        out_shape += [jax.ShapeDtypeStruct((pick, c), float32) for c in columns]
        out_shape += [
            jax.ShapeDtypeStruct((pick, 4 * width), float32),
            jax.ShapeDtypeStruct(small.shape, float32),
            jax.ShapeDtypeStruct((8, 128), float32),
        ]
        gradients = [g.reshape(planes, 2, group // 2, pick, g.shape[-1]) for g in gradients]
        sizes = [(pick // 2, columns[0])] * 2 + [(pick // 2, columns[1])] * 2 + [(pick, columns[2])]
        for size in sizes:
            scratch += [
                pltpu.VMEM((planes, 2) + size, bfloat),
                pltpu.VMEM((planes, 2) + size, bfloat),
                pltpu.VMEM((planes,) + size, bfloat),
                pltpu.VMEM((planes - 1,) + size, bfloat),
            ]
        scratch += [
            pltpu.VMEM((group,) + small.shape, float32),
            pltpu.VMEM((parts,) + small.shape, float32),
            pltpu.VMEM(small.shape, float32),
            pltpu.VMEM((planes, pick, 4 * width), bfloat),
            pltpu.VMEM((planes - 1, pick, 4 * width), bfloat),
            pltpu.VMEM((parts, 8, width), float32),
            pltpu.VMEM((8, 128), float32),
            pltpu.VMEM((group, 8, 128), float32),
            pltpu.VMEM((parts, 8, 128), float32),
        ]
    else:
        out_shape += [jax.ShapeDtypeStruct(wide_shape, bfloat)]
    return pl.pallas_call(
        functools.partial(attention_backward_kernel, head_size, group, parts, fast),
        in_specs=[outside] * 6 + [inside] * 5 + [outside] * 3 + [inside],
        out_specs=[inside] * len(out_shape),
        out_shape=out_shape,
        scratch_shapes=scratch,
        compiler_params=pltpu.CompilerParams(
            vmem_limit_bytes=VMEM_LIMIT, collective_id=2, has_side_effects=True
        ),
    )(
        content_all, query_all, weight_all, chance_all, upper, dresid, table,
        head_bias, *facts, proj, *gradients, small,
    )


def norm_parts(values):
    centred = values - jnp.mean(values, -1, keepdims=True)
    inverse = lax.rsqrt(jnp.mean(centred * centred, -1, keepdims=True) + NORM_EPSILON)
    return centred * inverse, inverse


def norm_back(upstream, normed, inverse, gain):
    scaled = upstream * gain
    first = jnp.mean(scaled, -1, keepdims=True)
    second = jnp.mean(scaled * normed, -1, keepdims=True)
    return inverse * (scaled - first - normed * second)


def column_sum(values):
    return jnp.sum(values, 0, keepdims=True)


def feed_kernel(group, *refs):
    mixed_ref, refs = refs[0], refs[1:]
    bias_ref, refs = refs[0], refs[1:]
    content_ref, query_ref, dcontent_ref, dquery_ref, norm_ref, up_hbm, down_hbm, out_hbm = refs[:8]
    content_out, query_out, dresid_ref, refs = refs[8], refs[9], refs[10], refs[11:]
    dmixed_ref, refs = refs[0], refs[1:]
    dup_hbm, ddown_hbm, dout_ref, dsmall_ref, refs = refs[0], refs[1], refs[2], refs[3], refs[4:]
    up_ref, down_ref, out_ref, hidden_ref, slope_ref = refs[:5]
    low_ref, low_t_ref, normed_ref, total_ref, up_got, down_got, out_got, out_sent = refs[5:13]
    sems, send_sems, recv_sems = refs[13:]
    own, depth = content_ref.shape
    tokens = 2 * own
    here = lax.axis_index("heads")
    core = here & 1
    chips = group // 2
    loads = [
        pltpu.make_async_copy(out_hbm.at[:, j], out_ref.at[j], sems.at[j]) for j in range(group)
    ]
    loads += [
        pltpu.make_async_copy(up_hbm.at[:, j], up_ref.at[j], sems.at[group + j]) for j in range(group)
    ]
    loads += [
        pltpu.make_async_copy(down_hbm.at[:, j], down_ref.at[j], sems.at[2 * group + j])
        for j in range(group)
    ]
    for load in loads:
        load.start()
    greet("heads", [1])
    gain_one, bias_one, bias_out, gain_two, bias_two = [norm_ref[i : i + 1] for i in range(5)]
    for load in loads[:group]:
        load.wait()
    hidden = up_ref.shape[-1]

    def mixed_piece(k):
        both = mixed_ref[k]
        return jnp.concatenate([both[:, : both.shape[1] // 2], both[:, both.shape[1] // 2 :]], 0)

    def out_block(k):
        return out_ref[here ^ k].reshape(depth, out_ref.shape[-1])

    total = jnp.concatenate([content_ref[...], query_ref[...]], 0).astype(jnp.float32)
    for k in range(group):
        total = total + dot_nt(mixed_piece(k), out_block(k))
    normed, inverse_one = norm_parts(total)
    normed_ref[...] = normed
    middle = normed * gain_one + bias_one
    low_ref[...] = middle.astype(jnp.bfloat16)
    low_t_ref[...] = low_ref[...].T
    total_ref[...] = middle + bias_out

    def forward(j, carry):
        pltpu.make_async_copy(up_hbm.at[:, j], up_ref.at[j], sems.at[group + j]).wait()
        pltpu.make_async_copy(down_hbm.at[:, j], down_ref.at[j], sems.at[2 * group + j]).wait()
        for part in (slice(0, own), slice(own, tokens)):
            before = dot(low_ref[part], up_ref[j].reshape(depth, hidden)) + bias_ref[j]
            square = before * before
            bent = jnp.tanh(GELU_FACTOR * before * (1.0 + GELU_CUBIC * square))
            half_up = 0.5 * (1.0 + bent)
            hidden_now = (before * half_up).astype(jnp.bfloat16)
            slope_ref[j, part] = half_up + 0.5 * before * (1.0 - bent * bent) * GELU_FACTOR * (
                1.0 + 3.0 * GELU_CUBIC * square
            )
            hidden_ref[j, part] = hidden_now
            total_ref[part] += dot_nt(hidden_now, down_ref[j].reshape(depth, hidden))
        return carry

    lax.fori_loop(0, group, forward, 0)
    normed_two, inverse_two = norm_parts(total_ref[...])
    result = (normed_two * gain_two + bias_two).astype(jnp.bfloat16)
    content_out[...] = result[:own]
    query_out[...] = result[own:]
    upstream = jnp.concatenate([dcontent_ref[...], dquery_ref[...]], 0).astype(jnp.float32)
    dsmall_ref[group + 3 : group + 4] = column_sum(upstream * normed_two)
    dsmall_ref[group + 4 : group + 5] = column_sum(upstream)
    dfinal = norm_back(upstream, normed_two, inverse_two, gain_two)
    dsmall_ref[group + 2 : group + 3] = column_sum(dfinal)
    total_ref[...] = dfinal
    dlow = dfinal.astype(jnp.bfloat16)
    dlow_t = dlow.T

    def to_sibling(source, place, index):
        return pltpu.make_async_remote_copy(
            source, place, send_sems.at[index], recv_sems.at[index],
            device_id={"heads": here ^ 1}, device_id_type=pl.DeviceIdType.MESH,
        )

    def back_block(j):
        ddown = dot(dlow_t, hidden_ref[j])
        bias_grad = jnp.zeros((1, hidden), jnp.float32)
        for part in (slice(0, own), slice(own, tokens)):
            dhidden = dot(dlow[part], down_ref[j].reshape(depth, hidden))
            dbefore = (dhidden * slope_ref[j, part]).astype(jnp.bfloat16)
            bias_grad = bias_grad + column_sum(dbefore.astype(jnp.float32))
            total_ref[part] += dot_nt(dbefore, up_ref[j].reshape(depth, hidden))
            hidden_ref[j, part] = dbefore
        dsmall_ref[pl.ds(j, 1)] = bias_grad
        return dot(low_t_ref[...], hidden_ref[j]), ddown

    def sent(chip):
        j = 2 * chip + 1 - core
        return [
            to_sibling(up_ref.at[j], up_got.at[chip], 2 * chip),
            to_sibling(down_ref.at[j], down_got.at[chip], 2 * chip + 1),
        ]

    def kept(chip):
        j = 2 * chip + core
        return [
            pltpu.make_async_copy(up_ref.at[j], dup_hbm.at[:, chip], sems.at[chip]),
            pltpu.make_async_copy(down_ref.at[j], ddown_hbm.at[:, chip], sems.at[group + chip]),
        ]

    def backward_sent(chip, carry):
        j = 2 * chip + 1 - core
        dup, ddown = back_block(j)
        up_ref[j] = dup.astype(jnp.bfloat16).reshape(up_ref.shape[1:])
        down_ref[j] = ddown.astype(jnp.bfloat16).reshape(down_ref.shape[1:])
        for copy in sent(chip):
            copy.start()
        return carry

    def backward_kept(chip, carry):
        j = 2 * chip + core
        dup, ddown = back_block(j)
        for copy in sent(chip):
            copy.wait_recv()
        dup = dup + up_got[chip].astype(jnp.float32).reshape(depth, hidden)
        ddown = ddown + down_got[chip].astype(jnp.float32).reshape(depth, hidden)
        up_ref[j] = dup.astype(jnp.bfloat16).reshape(up_ref.shape[1:])
        down_ref[j] = ddown.astype(jnp.bfloat16).reshape(down_ref.shape[1:])
        for copy in kept(chip):
            copy.start()
        return carry

    lax.fori_loop(0, chips, backward_sent, 0)
    lax.fori_loop(0, chips, backward_kept, 0)
    dmiddle = total_ref[...]
    normed = normed_ref[...]
    dsmall_ref[group : group + 1] = column_sum(dmiddle * normed)
    dsmall_ref[group + 1 : group + 2] = column_sum(dmiddle)
    dresid = norm_back(dmiddle, normed, inverse_one, gain_one)
    total_ref[...] = dresid
    dresid_copy = pltpu.make_async_copy(total_ref, dresid_ref, sems.at[0])
    dresid_copy.start()
    dlow = dresid.astype(jnp.bfloat16)
    dlow_t = dlow.T
    out_copies = [
        to_sibling(out_sent.at[chip], out_got.at[chip], 2 * chips + chip) for chip in range(chips)
    ]
    for chip in range(chips):
        k = 2 * chip + 1
        mixed = mixed_piece(k)
        out_sent[chip] = dot(dlow_t, mixed).astype(jnp.bfloat16).reshape(out_sent.shape[1:])
        out_copies[chip].start()
    for k in range(group):
        dmixed = dot(dlow, out_block(k)).astype(jnp.bfloat16)
        dmixed_ref[k] = jnp.concatenate([dmixed[:own], dmixed[own:]], -1)
    for chip in range(chips):
        k = 2 * chip
        mixed = mixed_piece(k)
        dout = dot(dlow_t, mixed)
        out_copies[chip].wait_recv()
        dout = dout + out_got[chip].astype(jnp.float32).reshape(dout.shape)
        dout_ref[:, (here ^ k) >> 1] = dout.astype(jnp.bfloat16).reshape(out_sent.shape[1:])
    dsmall_ref[group + 5 :] = jnp.zeros((dsmall_ref.shape[0] - group - 5, depth), jnp.float32)
    dresid_copy.wait()
    for chip in range(chips):
        for copy in sent(chip):
            copy.wait_send()
        out_copies[chip].wait_send()
        for copy in kept(chip):
            copy.wait()


def feed_layer(mixed, bias_all, content, query, dcontent, dquery, norm_param, up, down, out):
    group = mixed.shape[0]
    own, depth = content.shape
    parts, _, pick, hidden = up.shape
    width = out.shape[-1]
    inside = pl.BlockSpec(memory_space=pltpu.VMEM)
    outside = pl.BlockSpec(memory_space=pl.ANY)
    tokens = 2 * own
    results = pl.pallas_call(
        functools.partial(feed_kernel, group),
        in_specs=[inside] * 7 + [outside] * 3,
        out_specs=[inside, inside, outside, inside, outside, outside, inside, inside],
        out_shape=[
            jax.ShapeDtypeStruct((own, depth), jnp.bfloat16),
            jax.ShapeDtypeStruct((own, depth), jnp.bfloat16),
            jax.ShapeDtypeStruct((tokens, depth), jnp.float32),
        ]
        + [
            jax.ShapeDtypeStruct((group, own, 2 * width), jnp.bfloat16),
            jax.ShapeDtypeStruct((parts, group // 2, pick, hidden), jnp.bfloat16),
            jax.ShapeDtypeStruct((parts, group // 2, pick, hidden), jnp.bfloat16),
            jax.ShapeDtypeStruct((parts, group // 2, pick, width), jnp.bfloat16),
            jax.ShapeDtypeStruct((16, depth), jnp.float32),
        ],
        scratch_shapes=[
            pltpu.VMEM((group, parts, pick, hidden), jnp.bfloat16),
            pltpu.VMEM((group, parts, pick, hidden), jnp.bfloat16),
            pltpu.VMEM((group, parts, pick, width), jnp.bfloat16),
            pltpu.VMEM((group, tokens, hidden), jnp.bfloat16),
            pltpu.VMEM((group, tokens, hidden), jnp.float32),
            pltpu.VMEM((tokens, depth), jnp.bfloat16),
            pltpu.VMEM((depth, tokens), jnp.bfloat16),
            pltpu.VMEM((tokens, depth), jnp.float32),
            pltpu.VMEM((tokens, depth), jnp.float32),
            pltpu.VMEM((group // 2, parts, pick, hidden), jnp.bfloat16),
            pltpu.VMEM((group // 2, parts, pick, hidden), jnp.bfloat16),
            pltpu.VMEM((group // 2, parts, pick, width), jnp.bfloat16),
            pltpu.VMEM((group // 2, parts, pick, width), jnp.bfloat16),
            pltpu.SemaphoreType.DMA((3 * group,)),
            pltpu.SemaphoreType.DMA((3 * group // 2,)),
            pltpu.SemaphoreType.DMA((3 * group // 2,)),
        ],
        compiler_params=pltpu.CompilerParams(
            vmem_limit_bytes=VMEM_LIMIT, collective_id=1, has_side_effects=True
        ),
    )(mixed, bias_all, content, query, dcontent, dquery, norm_param, up, down, out)
    return results[0], results[1], results[2].reshape(2, own, depth), results[3], results[4:]


def exchange(value, axis, mask):
    return lax.ppermute(value, axis, [(i, i ^ mask) for i in range(lax.axis_size(axis))])


def total_over(value, axis):
    mask = 1
    while mask < lax.axis_size(axis):
        value = value + exchange(value, axis, mask)
        mask = 2 * mask
    return value


def by_pieces(pick):
    return lax.axis_size("dp") <= 8 and pick % 16 == 0


def reduce_projection(full):
    return lax.psum_scatter(full, "dp", scatter_dimension=0, tiled=True).astype(jnp.float32)


def gather_all(own):
    dp, heads = lax.axis_size("dp"), lax.axis_size("heads")
    rows, columns = own.shape
    full = lax.all_gather(own, ("dp", "heads"), axis=0, tiled=False).reshape(dp, heads, rows, columns)
    if by_pieces(rows):
        return full
    return jnp.swapaxes(full, 0, 1).reshape(1, heads, dp * rows, columns)


def scatter_all(full):
    chip = lax.axis_index("heads") // 2
    mine = lax.dynamic_index_in_dim(full[0], chip, 0, False)
    theirs = lax.dynamic_index_in_dim(full[0], 1 - chip, 0, False)
    mine = mine.astype(jnp.float32) + exchange(theirs, "heads", 2).astype(jnp.float32)
    return lax.psum_scatter(mine, "dp", scatter_dimension=0, tiled=True)


def adam_parts(master, first, second, gradient, factor, decayed):
    clipped = gradient * factor
    new_first = BETA_ONE * first + (1.0 - BETA_ONE) * clipped
    new_second = BETA_TWO * second + (1.0 - BETA_TWO) * clipped * clipped
    first_hat = new_first * (1.0 / (1.0 - BETA_ONE**STEP))
    second_hat = new_second * (1.0 / (1.0 - BETA_TWO**STEP))
    update = first_hat / (jnp.sqrt(second_hat) + ADAM_EPSILON)
    if decayed:
        update = update + WEIGHT_DECAY * master
        return new_first, new_second, master - MATRIX_RATE * update
    return new_first, new_second, master - VECTOR_RATE * update


def update_kernel(group, *refs):
    kept, refs = refs[:4], refs[4:]
    up_share, down_share, out_share, proj_share, dhead_ref, small_ref, norm_ref, refs = *refs[:7], refs[7:]
    weights, refs = refs[:21], refs[21:]
    placed, refs = refs[:4], refs[4:]
    results, grad_norm, stages, sems = refs[:28], refs[28], refs[29:33], refs[33]
    loads = [pltpu.make_async_copy(a, b, sems.at[n]) for n, (a, b) in enumerate(zip(kept, stages))]
    stores = [pltpu.make_async_copy(a, b, sems.at[4 + n]) for n, (a, b) in enumerate(zip(stages, placed))]
    for copy in loads:
        copy.start()
    norm = norm_ref[0:1, 0:1]
    grad_norm[...] = norm
    factor = CLIP_NORM / jnp.maximum(norm, CLIP_NORM)

    def put(index, gradient, decayed, place=lambda ref: ref[...], store=None):
        values = adam_parts(*(place(ref) for ref in weights[3 * index : 3 * index + 3]), gradient, factor, decayed)
        for ref, value in zip(results[4 * index : 4 * index + 4], (gradient,) + values):
            if store is None:
                ref[...] = value
            else:
                store(ref, value)

    width = proj_share.shape[1] // 4
    for kind in range(4):
        def store(ref, value, kind=kind):
            ref[kind] = value

        put(0, proj_share[:, kind * width : (kind + 1) * width], True, lambda ref, kind=kind: ref[kind], store)
    for load, store in zip(loads, stores):
        load.wait()
        store.start()
    put(1, out_share[...].T, True)
    put(2, up_share[...], True)
    put(3, down_share[...], True)
    heads, size = weights[12].shape[1:]
    for head in range(heads):
        def store(ref, value, head=head):
            ref[:, head, :] = value

        put(4, dhead_ref[:5, head * size : (head + 1) * size], False, lambda ref, head=head: ref[:, head, :], store)
    def as_row(ref):
        return ref[...].reshape(1, ref.shape[0])

    def from_row(ref, value):
        ref[...] = value.reshape(ref.shape)

    put(5, small_ref[pl.ds(lax.axis_index("heads"), 1)], False, as_row, from_row)
    put(6, small_ref[group : group + 5], False)
    for store in stores:
        store.wait()


def update_layer(kept, shares, dhead, small_sum, norm_tile, weights):
    inside = pl.BlockSpec(memory_space=pltpu.VMEM)
    outside = pl.BlockSpec(memory_space=pl.ANY)
    up_share, down_share, out_share, proj_share = shares
    out_shape = [jax.ShapeDtypeStruct(a.shape, a.dtype) for a in kept]
    for index in range(7):
        out_shape += [jax.ShapeDtypeStruct(weights[3 * index].shape, jnp.float32)] * 4
    out_shape.append(jax.ShapeDtypeStruct((1, 1), jnp.float32))
    results = pl.pallas_call(
        functools.partial(update_kernel, lax.axis_size("heads")),
        in_specs=[outside] * 4 + [inside] * 28,
        out_specs=[outside] * 4 + [inside] * 29,
        out_shape=out_shape,
        scratch_shapes=[pltpu.VMEM(a.shape, a.dtype) for a in kept] + [pltpu.SemaphoreType.DMA((8,))],
        compiler_params=pltpu.CompilerParams(vmem_limit_bytes=VMEM_LIMIT),
    )(*kept, up_share, down_share, out_share, proj_share, dhead, small_sum, norm_tile, *weights)
    return results[:4], results[4:32], results[32]


def local(
    content_in,
    query_in,
    content_grad,
    query_grad,
    segment_ids,
    doc_lengths,
    factor_order,
    attn_proj,
    attn_proj_first,
    attn_proj_second,
    out_proj,
    out_proj_first,
    out_proj_second,
    up_proj,
    up_proj_first,
    up_proj_second,
    down_proj,
    down_proj_first,
    down_proj_second,
    head_bias,
    head_bias_first,
    head_bias_second,
    up_bias,
    up_bias_first,
    up_bias_second,
    norm_param,
    norm_param_first,
    norm_param_second,
):
    width = content_in.shape[1]
    length = segment_ids.shape[1]
    table = position_table(length, width)
    tables = (jnp.asarray(table), jnp.asarray(table[::-1].copy()))
    kept, bias_all, mixed_pieces, (up_full, down_full, out_full) = attention_forward(
        content_in, query_in, attn_proj, up_proj, down_proj, out_proj, up_bias, doc_lengths, factor_order,
        segment_ids, tables[0], head_bias,
    )
    content_out, query_out, dresid, dmixed_pieces, (dup, ddown, dout, dsmall) = feed_layer(
        mixed_pieces, bias_all, content_in, query_in, content_grad, query_grad, norm_param,
        up_full, down_full, out_full,
    )
    backward = attention_backward(
        kept, tables[1], head_bias, dmixed_pieces, dresid, (dup, ddown, dout), dsmall
    )
    input_grad = backward[:2]
    if by_pieces(attn_proj.shape[1]):
        dhead = backward[2]
        up_share, down_share, out_share, proj_share, small_sum, norm_tile = backward[3:]
    else:
        dp_count, heads_count = lax.axis_size("dp"), lax.axis_size("heads")
        dhead = total_over(backward[2], "dp")
        proj_share = reduce_projection(backward[3])
        up_share, down_share, out_share = scatter_all(dup), scatter_all(ddown), scatter_all(dout)
        small_sum = total_over(total_over(dsmall, "heads"), "dp")
        squares = sum(jnp.sum(share * share) for share in (up_share, down_share, out_share, proj_share))
        squares = squares + jnp.sum(dhead * dhead) / dp_count
        squares = squares + jnp.sum(small_sum * small_sum) / (dp_count * heads_count)
        norm = jnp.sqrt(total_over(total_over(squares.reshape(1, 1), "heads"), "dp"))
        norm_tile = jnp.broadcast_to(norm, (8, 128))
    moments = (
        (attn_proj, attn_proj_first, attn_proj_second),
        (out_proj, out_proj_first, out_proj_second),
        (up_proj, up_proj_first, up_proj_second),
        (down_proj.T, down_proj_first.T, down_proj_second.T),
        (head_bias, head_bias_first, head_bias_second),
        (up_bias, up_bias_first, up_bias_second),
        (norm_param, norm_param_first, norm_param_second),
    )
    placed, updated, grad_norm = update_layer(
        (content_out, query_out) + tuple(input_grad),
        (up_share, down_share, out_share, proj_share),
        dhead, small_sum, norm_tile, [array for group in moments for array in group],
    )
    updated = list(updated)
    for index in range(12, 16):
        updated[index] = updated[index].T
    return (*placed, grad_norm[0, 0], *updated)


def solution(mesh):
    return jax.shard_map(
        local,
        mesh=mesh,
        in_specs=(
            P(("dp", "heads"), None),
            P(("dp", "heads"), None),
            P(("dp", "heads"), None),
            P(("dp", "heads"), None),
            P("dp", None),
            P("dp", None),
            P("dp", None),
            P(None, "dp", "heads"),
            P(None, "dp", "heads"),
            P(None, "dp", "heads"),
            P("heads", "dp"),
            P("heads", "dp"),
            P("heads", "dp"),
            P("dp", "heads"),
            P("dp", "heads"),
            P("dp", "heads"),
            P("heads", "dp"),
            P("heads", "dp"),
            P("heads", "dp"),
            P(None, "heads", None),
            P(None, "heads", None),
            P(None, "heads", None),
            P("heads"),
            P("heads"),
            P("heads"),
            P(),
            P(),
            P(),
        ),
        out_specs=(
            P(("dp", "heads"), None),
            P(("dp", "heads"), None),
            P(("dp", "heads"), None),
            P(("dp", "heads"), None),
            P(),
            P(None, "dp", "heads"),
            P(None, "dp", "heads"),
            P(None, "dp", "heads"),
            P(None, "dp", "heads"),
            P("heads", "dp"),
            P("heads", "dp"),
            P("heads", "dp"),
            P("heads", "dp"),
            P("dp", "heads"),
            P("dp", "heads"),
            P("dp", "heads"),
            P("dp", "heads"),
            P("heads", "dp"),
            P("heads", "dp"),
            P("heads", "dp"),
            P("heads", "dp"),
            P(None, "heads", None),
            P(None, "heads", None),
            P(None, "heads", None),
            P(None, "heads", None),
            P("heads"),
            P("heads"),
            P("heads"),
            P("heads"),
            P(),
            P(),
            P(),
            P(),
        ),
        check_vma=False,
    )
```
